32 devices in a mesh: seq: 8 (over z, y), rows: 4 (over x, core).
Axes of the slice: x: 2, y: 2, z: 4, core: 2. Of those that a mesh axis runs over, the one named last changes fastest.
Arguments:
- inputs: bfloat16 [16, 2048, 1280], P('rows', 'seq'), may hold values from -6 to 6
- cell_ids: int32 [16, 2048], P('rows'), may hold values from 0 to 6, as said below
- valid_counts: int32 [16], P('rows'), may hold values from 1920 to 2048, as said below
- cotangent: bfloat16 [16, 2048, 1280], P('rows', 'seq'), may hold values from -6 to 6
- attention_gain: float32 [1280], replicated, may hold values from 0.5 to 1.5
- qkv_weight: bfloat16 [1280, 3840], replicated, may hold values from -0.15625 to 0.15625
- out_weight: bfloat16 [1280, 1280], replicated, may hold values from -2 to 2
- feed_gain: float32 [1280], replicated, may hold values from 0.5 to 1.5
- up_weight: bfloat16 [1280, 5120], replicated, may hold values from -0.15625 to 0.15625
- down_weight: bfloat16 [5120, 1280], replicated, may hold values from -0.078125 to 0.078125
Outputs:
- outputs: bfloat16 [16, 2048, 1280], P('rows', 'seq')
- input_grad: bfloat16 [16, 2048, 1280], P('rows', 'seq')
- attention_gain_grad: float32 [1280], P('seq')
- qkv_weight_grad: float32 [1280, 3840], P('seq')
- out_weight_grad: float32 [1280, 1280], P('seq')
- feed_gain_grad: float32 [1280], P('seq')
- up_weight_grad: float32 [1280, 5120], P('seq')
- down_weight_grad: float32 [5120, 1280], P('seq')
The draws below stay inside these ranges and needn't reach their ends.
Inputs may be any that keep to these rules, and one draw needn't show every extreme that they name: `cell_ids`: along each row the ids start at 0 and never fall. In each group of 4 rows held at one index of rows, one row, drawn from the seed, is a single cell without padding; every other row holds at most 7 cells (ids 0 to 6); a cell may lie wholly in padding. `valid_counts`: positions from this count on are padding.
All inputs are finite; a program needn't handle non-finite values.
Results may differ from the reference program's by a relative error of at most 0.019.
Values may be sent and summed in bfloat16 or wider, within the bound.
A program may use at most 512 MiB of HBM per device.

```python
import jax
import jax.numpy as jnp
from jax import lax

D = 1280
HEADS = 20
HDIM = 64
FF = 5120
SEQ_LEN = 2048
ROWS_DEV = 4
BLOCK = 256
ROWS = 16


cell_breaks = 6


def single_row(key):
    chosen = jax.random.randint(key, (ROWS // ROWS_DEV,), 0, ROWS_DEV)
    offsets = jnp.arange(ROWS, dtype=jnp.int32) % ROWS_DEV
    return offsets == jnp.repeat(chosen, ROWS_DEV)


def draw_cell_ids(key, part):
    whole_row = single_row(key)
    key = jax.random.fold_in(key, 11)
    row_keys = jax.random.split(key, ROWS)
    orders = jax.vmap(lambda one_key: jax.random.permutation(one_key, SEQ_LEN - 1))(row_keys)
    chosen_places = orders[:, :cell_breaks].astype(jnp.int32) + 1
    places = jnp.arange(SEQ_LEN, dtype=jnp.int32)
    starts = jnp.any(chosen_places[:, :, None] == places[None, None, :], axis=1)
    starts = starts & jnp.logical_not(whole_row)[:, None]
    return jnp.cumsum(starts.astype(jnp.int32), axis=1).astype(jnp.int32)


def draw_valid_counts(key, part):
    whole_row = single_row(key)
    key = jax.random.fold_in(key, 12)
    cut_count = jax.random.randint(key, (ROWS,), 0, BLOCK // 2 + 1)
    return jnp.where(whole_row, SEQ_LEN, SEQ_LEN - cut_count).astype(jnp.int32)


def block_scale(rng, extent, shards, least, largest):
    factor_of, own = 1.0, jax.random.fold_in(rng, 6)
    for axis_at, shards_of in shards:
        steps = jnp.exp(jax.random.uniform(jax.random.fold_in(own, axis_at), (shards_of,), jnp.float32, least / len(shards), largest / len(shards)))
        factor_of = factor_of * jnp.repeat(steps, extent[axis_at] // shards_of).reshape([-1 if axis == axis_at else 1 for axis in range(len(extent))])
    return factor_of


def centred(rng, shape, deviation, limit, pieces=(), held_as=jnp.bfloat16):
    array = deviation * jax.random.normal(rng, shape, jnp.float32)
    if pieces:
        array = array * block_scale(rng, shape, pieces, -0.22, 0.18)
    return jnp.clip(array, -limit, limit).astype(held_as)


def setup_inputs(seed: int = 0) -> dict:
    key_of = jax.random.split(jax.random.key(seed), 11)
    return {
        "inputs": centred(key_of[0], (ROWS, SEQ_LEN, D), 1.0, 6.0, ((0, 4), (1, 8))),
        "cell_ids": draw_cell_ids(jax.random.fold_in(key_of[10], 71), 0),
        "valid_counts": draw_valid_counts(jax.random.fold_in(key_of[10], 71), 0),
        "cotangent": centred(key_of[3], (ROWS, SEQ_LEN, D), 1.0, 6.0, ((0, 4), (1, 8))),
        "attention_gain": jnp.clip(1.0 + 0.1 * jax.random.normal(key_of[4], (D,), jnp.float32), 0.5, 1.5),
        "qkv_weight": centred(key_of[5], (D, 3 * D), D ** -0.5, 0.15625),
        "out_weight": centred(key_of[6], (D, D), (max(D // 128, 4)) ** -0.5, 2.0),
        "feed_gain": jnp.clip(1.0 + 0.1 * jax.random.normal(key_of[7], (D,), jnp.float32), 0.5, 1.5),
        "up_weight": centred(key_of[8], (D, FF), D ** -0.5, 0.15625),
        "down_weight": centred(key_of[9], (FF, D), FF ** -0.5, 0.078125),
    }


epsilon = 1e-05
masked_score = -1e+30

@jax.custom_vjp
def low(v):
    return lax.optimization_barrier(v.astype(jnp.bfloat16)).astype(jnp.float32)

@jax.custom_vjp
def low_back(v):
    return v

def low_keep(v):
    return (low(v), None)

def low_pass(kept, grad):
    return (grad,)

def back_keep(v):
    return (v, None)

def back_low(kept, grad):
    return (low(grad),)
low.defvjp(low_keep, low_pass)
low_back.defvjp(back_keep, back_low)

def norm_rows(values, gain_vector):
    center = values - lax.optimization_barrier(jnp.mean(values, axis=-1, keepdims=True))
    spread = lax.optimization_barrier(jnp.mean(center * center, axis=-1, keepdims=True))
    return center * lax.rsqrt(spread + epsilon) * gain_vector

def layer_rows(row_values, row_tags, attention_gain, qkv_weight, out_weight, feed_gain, up_weight, down_weight):
    highest = lax.Precision.HIGHEST
    score_scale = HDIM ** (-0.5)
    first_norm = low(norm_rows(row_values, attention_gain))
    projected = low(low_back(jnp.dot(first_norm, qkv_weight, precision=highest)))
    queries = projected[:, :D].reshape(SEQ_LEN, HEADS, HDIM)
    keys_all = projected[:, D:2 * D].reshape(SEQ_LEN, HEADS, HDIM)
    values_all = projected[:, 2 * D:].reshape(SEQ_LEN, HEADS, HDIM)
    places = jnp.arange(SEQ_LEN, dtype=jnp.int32)
    allowed = (row_tags[:, None] == row_tags[None, :]) & (row_tags[None, :] >= 0) | (places[:, None] == places[None, :])
    raw = low_back(jnp.einsum('ihe,jhe->hij', queries, keys_all, precision=highest))
    scores = jnp.where(allowed[None], raw * score_scale, masked_score)
    row_peak = lax.optimization_barrier(jnp.max(scores, axis=-1, keepdims=True))
    powers = jnp.exp(scores - row_peak)
    weights = low(powers / lax.optimization_barrier(jnp.sum(powers, axis=-1, keepdims=True)))
    mixture = jnp.einsum('hij,jhe->ihe', weights, values_all, precision=highest).reshape(SEQ_LEN, D)
    mixture = low(low_back(mixture))
    attended = low_back(jnp.dot(mixture, out_weight, precision=highest))
    middle = row_values + attended
    second_norm = low(norm_rows(middle, feed_gain))
    hidden_up = low_back(jnp.dot(second_norm, up_weight, precision=highest))
    activated = low(jax.nn.gelu(hidden_up, approximate=False))
    return middle + jnp.dot(activated, down_weight, precision=highest)

def reference(inputs, cell_ids, valid_counts, cotangent, attention_gain, qkv_weight, out_weight, feed_gain, up_weight, down_weight):
    places = jnp.arange(SEQ_LEN, dtype=jnp.int32)
    token_tags = jnp.where(places[None, :] < valid_counts[:, None], cell_ids, -1).astype(jnp.int32)
    params = (attention_gain.astype(jnp.float32), qkv_weight.astype(jnp.float32), out_weight.astype(jnp.float32), feed_gain.astype(jnp.float32), up_weight.astype(jnp.float32), down_weight.astype(jnp.float32))

    def forward(values, *weights_all):

        def one_row(running, items):
            return (running, layer_rows(items[0], items[1], *weights_all))
        _, results = lax.scan(jax.checkpoint(one_row), jnp.zeros((), jnp.float32), (values, token_tags))
        return results
    outputs, pullback = jax.vjp(forward, inputs.astype(jnp.float32), *params)
    grads = pullback(cotangent.astype(jnp.float32))
    return (outputs.astype(jnp.bfloat16), grads[0].astype(jnp.bfloat16), grads[1], grads[2], grads[3], grads[4], grads[5], grads[6])
```

```python
import functools

import jax
import jax.numpy as jnp
from jax import lax
from jax.experimental import pallas as pl
from jax.experimental.pallas import tpu as pltpu
from jax.sharding import PartitionSpec as P

HDIM = 64
CORES = 2
epsilon = 1e-05
masked_score = -1e30
score_scale = HDIM ** (-0.5)
log2e = 1.4426950408889634
bf16 = jnp.bfloat16
f32 = jnp.float32
AXES = ("seq", "rows")
vmem_bytes = 56 * 2**20


def dot(a, b, ca, cb):
    return lax.dot_general(a, b, (((ca,), (cb,)), ((), ())), preferred_element_type=f32)


def attend_kernel(tile, key_tags, query_tags, q_ref, k_ref, v_ref, o_ref, lse_ref, v_turned):
    tokens = q_ref.shape[0]
    v_turned[...] = v_ref[...].T
    lane = lax.broadcasted_iota(jnp.int32, (tile, 2 * HDIM), 1)

    def body(step, _):
        part = pl.ds(pl.multiple_of(step * tile, tile), tile)
        q = q_ref[part, :]
        allowed = key_tags[...] == query_tags[:, part]
        pieces = []
        for head in range(2):
            own = jnp.where((lane // HDIM) == head, q, bf16(0))
            scores = dot(k_ref[...], own, 1, 1)
            scores = jnp.where(allowed, scores, masked_score)
            peak = jnp.max(scores, axis=0, keepdims=True)
            powers = jnp.exp2((scores - peak) * (score_scale * log2e))
            total = jnp.sum(powers, axis=0, keepdims=True)
            mixed = dot(v_turned[head * HDIM : (head + 1) * HDIM, :], powers.astype(bf16), 1, 0)
            pieces.append(mixed * (1.0 / total))
            lse_ref[head : head + 1, part] = peak * (score_scale * log2e) + jnp.log2(total)
        o_ref[part, :] = jnp.concatenate(pieces, axis=0).T.astype(bf16)
        return 0

    lax.fori_loop(0, tokens // tile, body, 0)


def attend(qkv, key_tags, query_tags):
    tokens, width = qkv.shape
    pairs = width // (6 * HDIM)
    tile = min(512, tokens)
    lanes = 2 * HDIM
    return pl.pallas_call(
        functools.partial(attend_kernel, tile),
        grid=(pairs,),
        in_specs=[
            pl.BlockSpec((tokens, 1), lambda i: (0, 0)),
            pl.BlockSpec((1, tokens), lambda i: (0, 0)),
            pl.BlockSpec((tokens, lanes), lambda i: (0, i)),
            pl.BlockSpec((tokens, lanes), lambda i: (0, pairs + i)),
            pl.BlockSpec((tokens, lanes), lambda i: (0, 2 * pairs + i)),
        ],
        out_specs=[
            pl.BlockSpec((tokens, lanes), lambda i: (0, i)),
            pl.BlockSpec((None, 2, tokens), lambda i: (i, 0, 0)),
        ],
        out_shape=[
            jax.ShapeDtypeStruct((tokens, pairs * lanes), bf16),
            jax.ShapeDtypeStruct((pairs, 2, tokens), f32),
        ],
        scratch_shapes=[pltpu.VMEM((lanes, tokens), bf16)],
        compiler_params=pltpu.CompilerParams(vmem_limit_bytes=vmem_bytes),
        cost_estimate=pl.CostEstimate(
            flops=16 * pairs * tokens * tokens * HDIM,
            bytes_accessed=8 * tokens * pairs * lanes,
            transcendentals=2 * pairs * tokens * tokens,
        ),
        name="attend",
    )(key_tags, query_tags, qkv, qkv, qkv)


def attend_back_kernel(
    tile, key_tags, query_tags, q_ref, k_ref, v_ref, do_ref, lse_ref, delta_ref, dq_ref, dk_ref, dv_ref, k_turned, dq_turned
):
    tokens = q_ref.shape[0]
    k_turned[...] = k_ref[...].T
    dq_turned[...] = jnp.zeros_like(dq_turned)
    first = lax.broadcasted_iota(jnp.int32, (tile, 2 * HDIM), 1) < HDIM

    def body(step, _):
        part = pl.ds(pl.multiple_of(step * tile, tile), tile)
        k, v = k_ref[part, :], v_ref[part, :]
        q, do = q_ref[...], do_ref[...]
        allowed = key_tags[part, :] == query_tags[...]
        dk, dv = [], []
        for head in range(2):
            own = first if head == 0 else jnp.logical_not(first)
            own_rows = slice(head * HDIM, (head + 1) * HDIM)
            scores = dot(jnp.where(own, k, bf16(0)), q, 1, 1)
            scores = jnp.where(allowed, scores, masked_score)
            chances = jnp.exp2(scores * (score_scale * log2e) - lse_ref[head : head + 1, :])
            weight_grad = dot(jnp.where(own, v, bf16(0)), do, 1, 1)
            score_grad = (chances * (weight_grad - delta_ref[head : head + 1, :])).astype(bf16)
            dv.append(dot(chances.astype(bf16), do, 1, 0))
            dk.append(dot(score_grad, q, 1, 0))
            dq_turned[own_rows, :] += dot(k_turned[own_rows, part], score_grad, 1, 0)
        dk_ref[part, :] = (jnp.where(first, dk[0], dk[1]) * score_scale).astype(bf16)
        dv_ref[part, :] = jnp.where(first, dv[0], dv[1]).astype(bf16)
        return 0

    lax.fori_loop(0, tokens // tile, body, 0)
    dq_ref[...] = (dq_turned[...] * score_scale).T.astype(bf16)


def attend_back(qkv, do, lse, delta, key_tags, query_tags, start, count):
    tokens, width = qkv.shape
    pairs = width // (6 * HDIM)
    tile = min(512, tokens)
    lanes = 2 * HDIM

    def columns(place):
        return pl.BlockSpec((tokens, lanes), lambda i: (0, place * pairs + start + i))

    stat = pl.BlockSpec((None, 2, tokens), lambda i: (start + i, 0, 0))
    return pl.pallas_call(
        functools.partial(attend_back_kernel, tile),
        grid=(count,),
        in_specs=[
            pl.BlockSpec((tokens, 1), lambda i: (0, 0)),
            pl.BlockSpec((1, tokens), lambda i: (0, 0)),
            columns(0),
            columns(1),
            columns(2),
            columns(0),
            stat,
            stat,
        ],
        out_specs=[pl.BlockSpec((tokens, lanes), lambda i: (0, i))] * 3,
        out_shape=[jax.ShapeDtypeStruct((tokens, count * lanes), bf16)] * 3,
        scratch_shapes=[pltpu.VMEM((lanes, tokens), bf16), pltpu.VMEM((lanes, tokens), f32)],
        compiler_params=pltpu.CompilerParams(vmem_limit_bytes=vmem_bytes),
        cost_estimate=pl.CostEstimate(
            flops=40 * count * tokens * tokens * HDIM,
            bytes_accessed=14 * tokens * count * lanes,
            transcendentals=2 * count * tokens * tokens,
        ),
        name="attend_back",
    )(key_tags, query_tags, qkv, qkv, qkv, do, lse, delta)


def hidden_kernel(n_ref, cot_ref, up_ref, down_ref, act_ref, d_up_ref):
    up = dot(n_ref[...], up_ref[...], 1, 0)
    d_act = dot(cot_ref[...], down_ref[...], 1, 1)
    half = 0.5 + 0.5 * lax.erf(up * (0.5**0.5))
    density = jnp.exp(-0.5 * up * up) * 0.3989422804014327
    act_ref[...] = (up * half).astype(bf16)
    d_up_ref[...] = (d_act * (half + up * density)).astype(bf16)


def hidden(n2, cotangent, up_weight, down_weight):
    tokens, width = n2.shape
    wide = up_weight.shape[1]
    tile = 256
    return pl.pallas_call(
        hidden_kernel,
        grid=(wide // tile,),
        in_specs=[
            pl.BlockSpec((tokens, width), lambda i: (0, 0)),
            pl.BlockSpec((tokens, width), lambda i: (0, 0)),
            pl.BlockSpec((width, tile), lambda i: (0, i)),
            pl.BlockSpec((tile, width), lambda i: (i, 0)),
        ],
        out_specs=[pl.BlockSpec((tokens, tile), lambda i: (0, i))] * 2,
        out_shape=[jax.ShapeDtypeStruct((tokens, wide), bf16)] * 2,
        compiler_params=pltpu.CompilerParams(vmem_limit_bytes=vmem_bytes),
        cost_estimate=pl.CostEstimate(
            flops=4 * tokens * width * wide,
            bytes_accessed=4 * tokens * (width + wide) + 4 * width * wide,
            transcendentals=2 * tokens * wide,
        ),
        name="hidden",
    )(n2, cotangent, up_weight, down_weight)


def norm_parts(values):
    center = values - jnp.mean(values, axis=-1, keepdims=True)
    spread = jnp.mean(center * center, axis=-1, keepdims=True)
    scale = lax.rsqrt(spread + epsilon)
    return center * scale, scale


def norm_back(grad, gain, unit, scale):
    e = grad * gain
    return scale * (
        e - jnp.mean(e, axis=-1, keepdims=True) - unit * jnp.mean(e * unit, axis=-1, keepdims=True)
    )


def build(n_seq, n_rows):
    devices = n_seq * n_rows
    highs = n_rows // CORES
    seq_bits = n_seq.bit_length() - 1
    high_bits = highs.bit_length() - 1

    def permute(value, target):
        pairs = []
        for s in range(n_seq):
            for r in range(n_rows):
                to_s, to_r = target(s, r)
                pairs.append((s * n_rows + r, to_s * n_rows + to_r))
        return lax.ppermute(value, AXES, pairs)

    def other_core(value):
        return permute(value, lambda s, r: (s, r ^ 1))

    def per_device(
        inputs, cell_ids, valid_counts, cotangent, attention_gain, qkv_weight, out_weight, feed_gain, up_weight, down_weight
    ):
        row_count, block, width = inputs.shape
        seq_len = cell_ids.shape[1]
        heads = width // HDIM
        seq_at, rows_at = lax.axis_index("seq"), lax.axis_index("rows")
        core = rows_at % CORES
        chips = n_seq // (CORES * row_count)
        group = chips * CORES
        sub = block // group
        tokens = n_seq * sub
        member = (seq_at % chips) * CORES + core
        group_heads = heads // group
        padded_heads = group_heads + group_heads % 2
        group_width = group_heads * HDIM
        padded = padded_heads * HDIM - group_width

        def to_member(value, hop):
            def target(s, r):
                place = ((s % chips) * CORES + r % CORES + hop) % group
                return (s // chips * chips + place // CORES, r // CORES * CORES + place % CORES)

            return permute(value, target)

        def pick(value, place, axis):
            return lax.dynamic_index_in_dim(value, place, axis, keepdims=False)

        def ordered(own, received, axis):
            return jnp.where(
                core == 0,
                jnp.concatenate([own, received], axis),
                jnp.concatenate([received, own], axis),
            )

        def to_rows(value):
            halves = value.reshape(row_count, CORES, block // CORES, width)
            received = other_core(pick(halves, 1 - core, 1))
            both = ordered(pick(halves, core, 1), received, 0)
            both = both.reshape(n_seq, sub, width) if chips == 1 else both.reshape(
                CORES * row_count, chips, sub, width
            ).reshape(n_seq, sub, width)
            return lax.all_to_all(both, "seq", 0, 0, tiled=True).reshape(tokens, width)

        def from_rows(value):
            both = lax.all_to_all(value.reshape(n_seq, sub, width), "seq", 0, 0, tiled=True)
            both = both.reshape(CORES, row_count, block // CORES, width)
            received = other_core(pick(both, 1 - core, 0))
            own = pick(both, core, 0)
            return ordered(own[:, None], received[:, None], 1).reshape(row_count, block, width)

        places = jnp.arange(seq_len, dtype=jnp.int32)
        tags = jnp.where(places[None, :] < valid_counts[:, None], cell_ids, -1 - places[None, :])
        tags = ordered(tags, other_core(tags), 0)
        tags = pick(tags, seq_at // chips, 0).reshape(n_seq, CORES, chips, sub)
        tags = tags.transpose(2, 1, 0, 3).reshape(group, tokens)
        order = (member - jnp.arange(group, dtype=jnp.int32)) % group
        tags = jnp.take(tags, order, axis=0).reshape(1, seq_len)
        query_tags, key_tags = tags, tags.reshape(seq_len, 1)

        def pad_heads(value, axis):
            if not padded:
                return value
            fill = [(0, 0)] * value.ndim
            fill[axis] = (0, padded)
            return jnp.pad(value, fill)

        qkv_split = qkv_weight.reshape(width, 3, group, group_width)
        out_split = out_weight.reshape(group, group_width, width)

        def qkv_of(hop):
            piece = pick(qkv_split, (member + hop) % group, 2)
            return pad_heads(piece, 2).reshape(width, -1)

        def out_of(hop):
            return pad_heads(pick(out_split, (member + hop) % group, 0), 0)

        qkv_parts = [qkv_of(hop) for hop in range(group)]
        out_parts = [out_of(hop) for hop in range(group)]

        start = to_rows(inputs).astype(f32)
        cot = to_rows(cotangent)
        unit1, scale1 = norm_parts(start)
        n1 = (unit1 * attention_gain).astype(bf16)
        n1_all = jnp.concatenate([n1] + [to_member(n1, hop) for hop in range(1, group)], 0)
        qkv = dot(n1_all, qkv_parts[0], 1, 0).astype(bf16)
        mixed, lse = attend(qkv, key_tags, query_tags)
        mixed_parts = [mixed[:tokens]] + [
            to_member(mixed[hop * tokens : (hop + 1) * tokens], group - hop) for hop in range(1, group)
        ]
        middle = start
        for part, weight in zip(mixed_parts, out_parts):
            middle = middle + dot(part, weight, 1, 0)
        unit2, scale2 = norm_parts(middle)
        n2 = (unit2 * feed_gain).astype(bf16)
        act, d_up = hidden(n2, cot, up_weight, down_weight)
        outputs = from_rows((middle + dot(act, down_weight, 1, 0)).astype(bf16))

        def halve(value, lead):
            value = value.reshape((2,) * (seq_bits + high_bits) + value.shape[lead:])
            steps = [("rows", b + 1, seq_bits + high_bits - 1 - b) for b in reversed(range(high_bits))]
            steps += [("seq", b, seq_bits - 1 - b) for b in range(seq_bits)]
            gone = []
            for axis_name, bit, axis in steps:
                at = rows_at if axis_name == "rows" else seq_at
                mine = (at >> bit) & 1
                place = axis - sum(1 for g in gone if g < axis)
                gone.append(axis)
                sent = pick(value, 1 - mine, place)
                if axis_name == "rows":
                    received = permute(sent, lambda s, r: (s, r ^ (1 << bit)))
                else:
                    received = permute(sent, lambda s, r: (s ^ (1 << bit), r))
                value = (pick(value, mine, place).astype(f32) + received.astype(f32)).astype(bf16)
            return value

        def gather_rows(value):
            for b in range(high_bits):
                bit = 1 << (b + 1)
                received = permute(value, lambda s, r: (s, r ^ bit))
                mine = (rows_at >> (b + 1)) & 1
                value = jnp.where(
                    mine == 0,
                    jnp.concatenate([value, received], 0),
                    jnp.concatenate([received, value], 0),
                )
            return value

        def reduce_halves(value, rows):
            parts = n_seq * highs
            value = halve(value.reshape(parts, rows // parts, -1), 1)
            return gather_rows(value)

        def weight_total(left, right):
            rows, columns = left.shape[1], right.shape[1]
            right = right.reshape(right.shape[0], CORES, columns // CORES)
            sent = dot(left, pick(right, 1 - core, 1), 0, 0).astype(bf16)
            kept = dot(left, pick(right, core, 1), 0, 0)
            kept = (kept + other_core(sent).astype(f32)).astype(bf16)
            part = reduce_halves(kept, rows)
            return ordered(part, other_core(part), 1).astype(f32)

        down_total = weight_total(act, cot)
        up_total = weight_total(n2, d_up)

        d_n2 = dot(d_up, up_weight, 1, 1)
        d_middle = cot.astype(f32) + norm_back(d_n2, feed_gain, unit2, scale2)
        d_attn = d_middle.astype(bf16)
        d_attn_all = jnp.concatenate([d_attn] + [to_member(d_attn, hop) for hop in range(1, group)], 0)
        d_mixed = dot(d_attn_all, out_parts[0], 1, 1).astype(bf16)
        if group == 2:
            mixed_own = ordered(mixed_parts[0], mixed_parts[1], 1)
        else:
            slots = jnp.stack([part[:, :group_width] for part in mixed_parts])
            back = (jnp.arange(group, dtype=jnp.int32) - member) % group
            mixed_own = jnp.take(slots, back, axis=0).transpose(1, 0, 2).reshape(tokens, width)
        out_total = weight_total(mixed_own, d_attn)
        delta = jnp.sum(
            (d_mixed.astype(f32) * mixed.astype(f32)).reshape(seq_len, padded_heads, HDIM), axis=-1
        )
        delta = delta.T.reshape(padded_heads // 2, 2, seq_len)
        d_qkv = attend_back(qkv, d_mixed, lse, delta, key_tags, query_tags, 0, padded_heads // 2)
        d_qkv = jnp.concatenate(d_qkv, axis=1)
        if group == 2:
            part = reduce_halves(dot(n1_all, d_qkv, 0, 0).astype(bf16), width)
            part = part.reshape(-1, 3, group_width)
            qkv_total = ordered(part[:, :, None], other_core(part)[:, :, None], 2)
            qkv_total = qkv_total.reshape(-1, 3 * width).astype(f32)
        else:
            grad = dot(n1_all, d_qkv, 0, 0).reshape(width, 3, 1, -1)[..., :group_width]
            grad = lax.dynamic_update_slice_in_dim(
                jnp.zeros((width, 3, group, group_width), f32), grad, member, 2
            )
            grad = grad.reshape(width, 3, CORES, width // CORES)
            kept = pick(grad, core, 2) + other_core(pick(grad, 1 - core, 2).astype(bf16)).astype(f32)
            part = reduce_halves(kept.reshape(width, -1).astype(bf16), width)
            part = part.reshape(-1, 3, width // CORES)
            qkv_total = ordered(part[:, :, None], other_core(part)[:, :, None], 2)
            qkv_total = qkv_total.reshape(-1, 3 * width).astype(f32)

        d_parts = [d_qkv[:tokens]] + [
            to_member(d_qkv[hop * tokens : (hop + 1) * tokens], group - hop) for hop in range(1, group)
        ]
        d_n1 = jnp.zeros((tokens, width), f32)
        for part, weight in zip(d_parts, qkv_parts):
            d_n1 = d_n1 + dot(part, weight, 1, 1)
        input_grad = d_middle + norm_back(d_n1, attention_gain, unit1, scale1)
        input_grad = from_rows(input_grad.astype(bf16))

        shard = width // n_seq

        def gain_total(weight, total, gain):
            rows = lax.dynamic_slice_in_dim(weight, seq_at * shard, shard, 0).astype(f32)
            return jnp.sum(rows * total, axis=1) / lax.dynamic_slice_in_dim(gain, seq_at * shard, shard, 0)

        return (
            outputs,
            input_grad,
            gain_total(qkv_weight, qkv_total, attention_gain),
            qkv_total,
            out_total,
            gain_total(up_weight, up_total, feed_gain),
            up_total,
            down_total,
        )

    return per_device


def solution(mesh):
    placed = (
        P("rows", "seq", None),
        P("rows", None),
        P("rows"),
        P("rows", "seq", None),
        P(),
        P(),
        P(),
        P(),
        P(),
        P(),
    )
    return jax.shard_map(
        build(mesh.shape["seq"], mesh.shape["rows"]),
        mesh=mesh,
        in_specs=placed,
        out_specs=(
            P("rows", "seq", None),
            P("rows", "seq", None),
            P("seq"),
            P("seq", None),
            P("seq", None),
            P("seq"),
            P("seq", None),
            P("seq", None),
        ),
        check_vma=False,
    )
```

```python
import functools

import jax
import jax.numpy as jnp
from jax import lax
from jax.experimental import pallas as pl
from jax.experimental.pallas import tpu as pltpu
from jax.sharding import PartitionSpec as P

HDIM = 64
CORES = 2
epsilon = 1e-05
masked_score = -1e30
score_scale = HDIM ** (-0.5)
log2e = 1.4426950408889634
bf16 = jnp.bfloat16
f32 = jnp.float32
AXES = ("seq", "rows")
vmem_bytes = 60 * 2**20
feed_vmem_bytes = 62 * 2**20
feed_tile = 512
MESH = pl.DeviceIdType.MESH


def dot(a, b, ca, cb):
    return lax.dot_general(a, b, (((ca,), (cb,)), ((), ())), preferred_element_type=f32)


def attend_kernel(tile, key_tags, query_tags, q_ref, k_ref, v_ref, o_ref, lse_ref, v_turned):
    tokens = q_ref.shape[0]
    v_turned[...] = v_ref[...].T
    lane = lax.broadcasted_iota(jnp.int32, (tile, 2 * HDIM), 1)

    def body(step, _):
        part = pl.ds(pl.multiple_of(step * tile, tile), tile)
        q = q_ref[part, :]
        allowed = key_tags[...] == query_tags[:, part]
        pieces = []
        for head in range(2):
            own = jnp.where((lane // HDIM) == head, q, bf16(0))
            scores = dot(k_ref[...], own, 1, 1)
            scores = jnp.where(allowed, scores, masked_score)
            peak = jnp.max(scores, axis=0, keepdims=True)
            powers = jnp.exp2((scores - peak) * (score_scale * log2e))
            total = jnp.sum(powers, axis=0, keepdims=True)
            mixed = dot(v_turned[head * HDIM : (head + 1) * HDIM, :], powers.astype(bf16), 1, 0)
            pieces.append(mixed * (1.0 / total))
            lse_ref[head : head + 1, part] = peak * (score_scale * log2e) + jnp.log2(total)
        o_ref[part, :] = jnp.concatenate(pieces, axis=0).T.astype(bf16)
        return 0

    lax.fori_loop(0, tokens // tile, body, 0)


def attend(qkv, key_tags, query_tags):
    tokens, width = qkv.shape
    lanes = 2 * HDIM
    pairs = width // (3 * lanes)
    tile = min(512, tokens)

    def columns(place):
        return pl.BlockSpec((tokens, lanes), lambda i: (0, 3 * i + place))

    return pl.pallas_call(
        functools.partial(attend_kernel, tile),
        grid=(pairs,),
        in_specs=[
            pl.BlockSpec((tokens, 1), lambda i: (0, 0)),
            pl.BlockSpec((1, tokens), lambda i: (0, 0)),
            columns(0),
            columns(1),
            columns(2),
        ],
        out_specs=[
            pl.BlockSpec((tokens, lanes), lambda i: (0, i)),
            pl.BlockSpec((None, 2, tokens), lambda i: (i, 0, 0)),
        ],
        out_shape=[
            jax.ShapeDtypeStruct((tokens, pairs * lanes), bf16),
            jax.ShapeDtypeStruct((pairs, 2, tokens), f32),
        ],
        scratch_shapes=[pltpu.VMEM((lanes, tokens), bf16)],
        compiler_params=pltpu.CompilerParams(vmem_limit_bytes=vmem_bytes),
        cost_estimate=pl.CostEstimate(
            flops=32 * pairs * tokens * tokens * HDIM,
            bytes_accessed=8 * tokens * pairs * lanes,
            transcendentals=2 * pairs * tokens * tokens,
        ),
        name="attend",
    )(key_tags, query_tags, qkv, qkv, qkv)


def attend_back_kernel(
    tile, key_tags, query_tags, q_ref, k_ref, v_ref, o_ref, do_ref, lse_ref, grad_ref, k_turned, dq_turned, delta
):
    tokens = q_ref.shape[0]
    lanes = 2 * HDIM
    k_turned[...] = k_ref[...].T
    dq_turned[...] = (o_ref[...].astype(f32) * do_ref[...].astype(f32)).T
    for head in range(2):
        rows = dq_turned[head * HDIM : (head + 1) * HDIM, :]
        delta[head : head + 1, :] = jnp.sum(rows, axis=0, keepdims=True)
    dq_turned[...] = jnp.zeros_like(dq_turned)
    first = lax.broadcasted_iota(jnp.int32, (tile, lanes), 1) < HDIM

    def body(step, _):
        part = pl.ds(pl.multiple_of(step * tile, tile), tile)
        k, v = k_ref[part, :], v_ref[part, :]
        q, do = q_ref[...], do_ref[...]
        allowed = key_tags[part, :] == query_tags[...]
        dk, dv = [], []
        for head in range(2):
            own = first if head == 0 else jnp.logical_not(first)
            own_rows = slice(head * HDIM, (head + 1) * HDIM)
            scores = dot(jnp.where(own, k, bf16(0)), q, 1, 1)
            scores = jnp.where(allowed, scores, masked_score)
            chances = jnp.exp2(scores * (score_scale * log2e) - lse_ref[head : head + 1, :])
            weight_grad = dot(jnp.where(own, v, bf16(0)), do, 1, 1)
            score_grad = (chances * (weight_grad - delta[head : head + 1, :])).astype(bf16)
            dv.append(dot(chances.astype(bf16), do, 1, 0))
            dk.append(dot(score_grad, q, 1, 0))
            dq_turned[own_rows, :] += dot(k_turned[own_rows, part], score_grad, 1, 0)
        grad_ref[part, lanes : 2 * lanes] = (jnp.where(first, dk[0], dk[1]) * score_scale).astype(bf16)
        grad_ref[part, 2 * lanes :] = jnp.where(first, dv[0], dv[1]).astype(bf16)
        return 0

    lax.fori_loop(0, tokens // tile, body, 0)
    grad_ref[:, :lanes] = (dq_turned[...] * score_scale).T.astype(bf16)


def attend_back(qkv, mixed, d_mixed, lse, key_tags, query_tags, start, count):
    tokens = qkv.shape[0]
    tile = min(512, tokens)
    lanes = 2 * HDIM

    def columns(place):
        return pl.BlockSpec((tokens, lanes), lambda i: (0, 3 * (start + i) + place))

    pair = pl.BlockSpec((tokens, lanes), lambda i: (0, start + i))
    return pl.pallas_call(
        functools.partial(attend_back_kernel, tile),
        grid=(count,),
        in_specs=[
            pl.BlockSpec((tokens, 1), lambda i: (0, 0)),
            pl.BlockSpec((1, tokens), lambda i: (0, 0)),
            columns(0),
            columns(1),
            columns(2),
            pair,
            pair,
            pl.BlockSpec((None, 2, tokens), lambda i: (start + i, 0, 0)),
        ],
        out_specs=pl.BlockSpec((tokens, 3 * lanes), lambda i: (0, i)),
        out_shape=jax.ShapeDtypeStruct((tokens, 3 * count * lanes), bf16),
        scratch_shapes=[
            pltpu.VMEM((lanes, tokens), bf16),
            pltpu.VMEM((lanes, tokens), f32),
            pltpu.VMEM((2, tokens), f32),
        ],
        compiler_params=pltpu.CompilerParams(vmem_limit_bytes=vmem_bytes),
        cost_estimate=pl.CostEstimate(
            flops=80 * count * tokens * tokens * HDIM,
            bytes_accessed=16 * tokens * count * lanes,
            transcendentals=2 * count * tokens * tokens,
        ),
        name="attend_back",
    )(key_tags, query_tags, qkv, qkv, qkv, mixed, d_mixed, lse)


def copy_kernel(core_ref, from_ref, to_ref):
    to_ref[...] = from_ref[...]


def gather_pairs(core, qkv_weight):
    width, lanes = qkv_weight.shape[0], 2 * HDIM
    pairs = width // (CORES * lanes)
    return pl.pallas_call(
        copy_kernel,
        grid_spec=pltpu.PrefetchScalarGridSpec(
            num_scalar_prefetch=1,
            grid=(pairs, 3),
            in_specs=[
                pl.BlockSpec((width, lanes), lambda i, j, core: (0, (j * CORES + core[0]) * pairs + i))
            ],
            out_specs=pl.BlockSpec((width, lanes), lambda i, j, core: (0, 3 * i + j)),
        ),
        out_shape=jax.ShapeDtypeStruct((width, 3 * pairs * lanes), qkv_weight.dtype),
        cost_estimate=pl.CostEstimate(flops=0, bytes_accessed=12 * width * pairs * lanes, transcendentals=0),
        name="gather_pairs",
    )(core, qkv_weight)


def norm_parts(values):
    center = values - jnp.mean(values, axis=-1, keepdims=True)
    spread = jnp.mean(center * center, axis=-1, keepdims=True)
    scale = lax.rsqrt(spread + epsilon)
    return center * scale, scale


def norm_back(grad, gain, unit, scale):
    e = grad * gain
    return scale * (
        e - jnp.mean(e, axis=-1, keepdims=True) - unit * jnp.mean(e * unit, axis=-1, keepdims=True)
    )


def feed_kernel(rows, core_ref, middle_ref, cot_ref, gain_ref, up_ref, down_ref,
    out_ref, d_middle_ref, d_attn_ref, down_sent, down_kept, up_sent, up_kept, n2, n2_turned, total, d_n2):
    step, last = pl.program_id(0), pl.num_programs(0) - 1
    tokens, width = n2.shape
    half = width // 2

    @pl.when(step == 0)
    def _():
        def body(i, _):
            part = pl.ds(pl.multiple_of(i * rows, rows), rows)
            unit, _s = norm_parts(middle_ref[part, :])
            n2[part, :] = (unit * gain_ref[...]).astype(bf16)
            return 0
        lax.fori_loop(0, tokens // rows, body, 0)
        n2_turned[...] = n2[...].T

    up_w, down_w = up_ref[...], down_ref[...]
    up = dot(n2[...], up_w, 1, 0)
    d_act = dot(cot_ref[...], down_w, 1, 1)
    share = 0.5 + 0.5 * lax.erf(up * (0.5**0.5))
    density = jnp.exp(-0.5 * up * up) * 0.3989422804014327
    act = (up * share).astype(bf16)
    d_up = (d_act * (share + up * density)).astype(bf16)
    y = dot(act, down_w, 1, 0)
    d = dot(d_up, up_w, 1, 1)

    @pl.when(step == 0)
    def _():
        total[...] = middle_ref[...] + y
        d_n2[...] = d

    @pl.when(step > 0)
    def _():
        total[...] += y
        d_n2[...] += d

    up_grad = dot(n2_turned[...], d_up, 1, 0).astype(bf16)

    @pl.when(step <= last // 2)
    def _():
        up_sent[...] = up_grad

    @pl.when(step > last // 2)
    def _():
        up_kept[...] = up_grad

    down_grad = dot(act, cot_ref[...], 0, 0).astype(bf16)

    @pl.when(core_ref[0] == 0)
    def _():
        down_kept[...] = down_grad[:, :half]
        down_sent[...] = down_grad[:, half:]

    @pl.when(core_ref[0] != 0)
    def _():
        down_kept[...] = down_grad[:, half:]
        down_sent[...] = down_grad[:, :half]

    @pl.when(step == last)
    def _():
        def body(i, _):
            part = pl.ds(pl.multiple_of(i * rows, rows), rows)
            out_ref[part, :] = total[part, :].astype(bf16)
            unit, scale = norm_parts(middle_ref[part, :])
            grad = cot_ref[part, :].astype(f32) + norm_back(d_n2[part, :], gain_ref[...], unit, scale)
            d_middle_ref[part, :] = grad
            d_attn_ref[part, :] = grad.astype(bf16)
            return 0
        lax.fori_loop(0, tokens // rows, body, 0)


def feed(core, middle, cot, gain, up_weight, down_weight, tile=512):
    tokens, width = middle.shape
    wide = up_weight.shape[1]
    steps = wide // tile
    halves = steps // 2
    place = lambda i, core: (i + (1 - core[0]) * halves) % steps
    whole = lambda dtype: jax.ShapeDtypeStruct((tokens, width), dtype)
    fixed = lambda shape: pl.BlockSpec(shape, lambda i, core: (0, 0), pipeline_mode=pl.Buffered(1))
    return pl.pallas_call(
        functools.partial(feed_kernel, 128),
        grid_spec=pltpu.PrefetchScalarGridSpec(
            num_scalar_prefetch=1,
            grid=(steps,),
            in_specs=[
                fixed((tokens, width)),
                fixed((tokens, width)),
                fixed((1, width)),
                pl.BlockSpec((width, tile), lambda i, core: (0, place(i, core))),
                pl.BlockSpec((tile, width), lambda i, core: (place(i, core), 0)),
            ],
            out_specs=[
                fixed((tokens, width)),
                fixed((tokens, width)),
                fixed((tokens, width)),
                pl.BlockSpec((tile, width // 2), lambda i, core: (place(i, core), 0)),
                pl.BlockSpec((tile, width // 2), lambda i, core: (place(i, core), 0)),
                pl.BlockSpec((width, tile), lambda i, core: (0, jnp.minimum(i, halves - 1))),
                pl.BlockSpec((width, tile), lambda i, core: (0, jnp.maximum(i - halves, 0))),
            ],
            scratch_shapes=[
                pltpu.VMEM((tokens, width), bf16),
                pltpu.VMEM((width, tokens), bf16),
                pltpu.VMEM((tokens, width), f32),
                pltpu.VMEM((tokens, width), f32),
            ],
        ),
        out_shape=[
            whole(bf16), whole(f32), whole(bf16),
            jax.ShapeDtypeStruct((wide, width // 2), bf16),
            jax.ShapeDtypeStruct((wide, width // 2), bf16),
            jax.ShapeDtypeStruct((width, wide // 2), bf16),
            jax.ShapeDtypeStruct((width, wide // 2), bf16),
        ],
        compiler_params=pltpu.CompilerParams(vmem_limit_bytes=vmem_bytes),
        name="feed",
    )(core, middle, cot, gain.reshape(1, width), up_weight, down_weight)


def feed_kernel(rows, core_ref, middle_ref, cot_ref, gain_ref, up_ref, down_ref,
    out_ref, d_middle_ref, d_attn_ref, down_sent, down_kept, up_sent, up_kept, n2, n2_turned, total, d_n2):
    step, last = pl.program_id(0), pl.num_programs(0) - 1
    tokens, width = n2.shape
    half = width // 2

    @pl.when(step == 0)
    def _():
        def body(i, _):
            part = pl.ds(pl.multiple_of(i * rows, rows), rows)
            unit, _s = norm_parts(middle_ref[part, :])
            n2[part, :] = (unit * gain_ref[...]).astype(bf16)
            return 0
        lax.fori_loop(0, tokens // rows, body, 0)
        n2_turned[...] = n2[...].T

    up_w, down_w = up_ref[...], down_ref[...]
    up = dot(n2[...], up_w, 1, 0)
    d_act = dot(cot_ref[...], down_w, 1, 1)
    share = 0.5 + 0.5 * lax.erf(up * (0.5**0.5))
    density = jnp.exp(-0.5 * up * up) * 0.3989422804014327
    act = (up * share).astype(bf16)
    d_up = (d_act * (share + up * density)).astype(bf16)
    y = dot(act, down_w, 1, 0)
    d = dot(d_up, up_w, 1, 1)

    @pl.when(step == 0)
    def _():
        total[...] = middle_ref[...] + y
        d_n2[...] = d

    @pl.when(step > 0)
    def _():
        total[...] += y
        d_n2[...] += d

    up_grad = dot(n2_turned[...], d_up, 1, 0).astype(bf16)

    @pl.when(step <= last // 2)
    def _():
        up_sent[...] = up_grad

    @pl.when(step > last // 2)
    def _():
        up_kept[...] = up_grad

    down_grad = dot(act, cot_ref[...], 0, 0).astype(bf16)

    @pl.when(core_ref[0] == 0)
    def _():
        down_kept[...] = down_grad[:, :half]
        down_sent[...] = down_grad[:, half:]

    @pl.when(core_ref[0] != 0)
    def _():
        down_kept[...] = down_grad[:, half:]
        down_sent[...] = down_grad[:, :half]

    @pl.when(step == last)
    def _():
        def body(i, _):
            part = pl.ds(pl.multiple_of(i * rows, rows), rows)
            out_ref[part, :] = total[part, :].astype(bf16)
            unit, scale = norm_parts(middle_ref[part, :])
            grad = cot_ref[part, :].astype(f32) + norm_back(d_n2[part, :], gain_ref[...], unit, scale)
            d_middle_ref[part, :] = grad
            d_attn_ref[part, :] = grad.astype(bf16)
            return 0
        lax.fori_loop(0, tokens // rows, body, 0)


def feed(core, middle, cot, gain, up_weight, down_weight, tile=512):
    tokens, width = middle.shape
    wide = up_weight.shape[1]
    steps = wide // tile
    halves = steps // 2
    place = lambda i, core: (i + (1 - core[0]) * halves) % steps
    whole = lambda dtype: jax.ShapeDtypeStruct((tokens, width), dtype)
    fixed = lambda shape: pl.BlockSpec(shape, lambda i, core: (0, 0), pipeline_mode=pl.Buffered(1))
    return pl.pallas_call(
        functools.partial(feed_kernel, 128),
        grid_spec=pltpu.PrefetchScalarGridSpec(
            num_scalar_prefetch=1,
            grid=(steps,),
            in_specs=[
                fixed((tokens, width)),
                fixed((tokens, width)),
                fixed((1, width)),
                pl.BlockSpec((width, tile), lambda i, core: (0, place(i, core))),
                pl.BlockSpec((tile, width), lambda i, core: (place(i, core), 0)),
            ],
            out_specs=[
                fixed((tokens, width)),
                fixed((tokens, width)),
                fixed((tokens, width)),
                pl.BlockSpec((tile, width // 2), lambda i, core: (place(i, core), 0)),
                pl.BlockSpec((tile, width // 2), lambda i, core: (place(i, core), 0)),
                pl.BlockSpec((width, tile), lambda i, core: (0, jnp.minimum(i, halves - 1))),
                pl.BlockSpec((width, tile), lambda i, core: (0, jnp.maximum(i - halves, 0))),
            ],
            scratch_shapes=[
                pltpu.VMEM((tokens, width), bf16),
                pltpu.VMEM((width, tokens), bf16),
                pltpu.VMEM((tokens, width), f32),
                pltpu.VMEM((tokens, width), f32),
            ],
        ),
        out_shape=[
            whole(bf16), whole(f32), whole(bf16),
            jax.ShapeDtypeStruct((wide, width // 2), bf16),
            jax.ShapeDtypeStruct((wide, width // 2), bf16),
            jax.ShapeDtypeStruct((width, wide // 2), bf16),
            jax.ShapeDtypeStruct((width, wide // 2), bf16),
        ],
        compiler_params=pltpu.CompilerParams(vmem_limit_bytes=vmem_bytes),
        name="feed",
    )(core, middle, cot, gain.reshape(1, width), up_weight, down_weight)


def add_split_kernel(has_two, bit_ref, *refs):
    ins, outs = refs[: 2 if has_two else 1], refs[2 if has_two else 1 :]
    value = ins[0][...]
    if has_two:
        value = (value.astype(f32) + ins[1][...].astype(f32)).astype(bf16)
    if len(outs) == 1:
        outs[0][...] = value
    else:
        sends = pl.program_id(0) == 0

        @pl.when(sends)
        def _():
            outs[0][...] = value

        @pl.when(jnp.logical_not(sends))
        def _():
            outs[1][...] = value


def add_split(kept, received, inner, bit):
    rows, columns = kept.shape
    values = [kept] if received is None else [kept, received.reshape(rows, columns)]
    if bit is None:
        if received is None:
            return None, kept
        count = 4 if rows % 64 == 0 else 1
        block = pl.BlockSpec((rows // count, columns), lambda i, bit: (i, 0))
        grid, ins, outs = (count,), [block] * 2, block
        shapes = jax.ShapeDtypeStruct((rows, columns), bf16)
        bit = jnp.zeros((), jnp.int32)
    else:
        outer = rows // (2 * inner)
        cut = 1
        while inner // cut * columns > 2**19 and inner % (32 * cut) == 0:
            cut *= 2
        values = [value.reshape(outer, 2, inner, columns) for value in values]
        ins = [
            pl.BlockSpec(
                (None, None, inner // cut, columns),
                lambda w, i, j, bit: (i, jnp.where(w == 0, 1 - bit[0], bit[0]), j, 0),
            )
        ] * len(values)
        outs = [
            pl.BlockSpec(
                (None, inner // cut, columns),
                lambda w, i, j, bit: (jnp.where(w == 0, i, outer - 1), jnp.where(w == 0, j, cut - 1), 0),
            ),
            pl.BlockSpec(
                (None, inner // cut, columns),
                lambda w, i, j, bit: (jnp.where(w == 0, 0, i), jnp.where(w == 0, 0, j), 0),
            ),
        ]
        grid = (2, outer, cut)
        shapes = [jax.ShapeDtypeStruct((outer, inner, columns), bf16)] * 2
    done = pl.pallas_call(
        functools.partial(add_split_kernel, len(values) == 2),
        grid_spec=pltpu.PrefetchScalarGridSpec(
            num_scalar_prefetch=1, grid=grid, in_specs=ins, out_specs=outs
        ),
        out_shape=shapes,
        cost_estimate=pl.CostEstimate(flops=rows * columns, bytes_accessed=6 * rows * columns, transcendentals=0),
        name="add_split",
    )(bit.reshape(1), *values)
    if not isinstance(done, (list, tuple)):
        return None, done
    return done[0].reshape(rows // 2, columns), done[1].reshape(rows // 2, columns)


piece_rows = 32


def feed_kernel(
    tiles,
    rows,
    middle_ref,
    cot_ref,
    gain_ref,
    up_ref,
    down_ref,
    out_ref,
    d_middle_ref,
    d_attn_ref,
    down_part,
    up_part,
    n2,
    n2_turned,
    total,
    down_keep,
    down_send,
    down_recv,
    up_keep,
    up_send,
    up_recv,
    down_far_keep,
    down_far_send,
    down_far_recv,
    up_far_keep,
    up_far_send,
    up_far_recv,
    core_send_sem,
    core_recv_sem,
    far_send_sem,
    far_recv_sem,
    core_free,
    far_free,
):
    step = pl.program_id(0)
    tokens, width = n2.shape
    half = width // 2
    seq_at, rows_at = lax.axis_index("seq"), lax.axis_index("rows")
    core, high, low = rows_at % 2, (rows_at // 2) % 2, seq_at % 2
    core_peer = (seq_at, rows_at + 1 - 2 * core)
    far_peers = ((seq_at, rows_at + 2 - 4 * high), (seq_at + 1 - 2 * low, rows_at))

    def copies(slot, far):
        if far:
            refs = ((down_far_send, down_far_recv), (up_far_send, up_far_recv))
            sems, peers = (far_send_sem, far_recv_sem), far_peers
        else:
            refs = ((down_send, down_recv), (up_send, up_recv))
            sems, peers = (core_send_sem, core_recv_sem), (core_peer, core_peer)
        return [
            pltpu.make_async_remote_copy(
                src_ref=refs[kind][0].at[slot],
                dst_ref=refs[kind][1].at[slot],
                send_sem=sems[0].at[kind, slot],
                recv_sem=sems[1].at[kind, slot],
                device_id=peers[kind],
                device_id_type=MESH,
            )
            for kind in range(2)
        ]

    def signal(sem, peer):
        pl.semaphore_signal(sem, inc=1, device_id=peer, device_id_type=MESH)

    @pl.when(step == 0)
    def _():
        barrier = pltpu.get_barrier_semaphore()
        for peer in (core_peer,) + far_peers:
            signal(barrier, peer)
        pl.semaphore_wait(barrier, 3)

        def body(i, _):
            part = pl.ds(pl.multiple_of(i * rows, rows), rows)
            unit, _s = norm_parts(middle_ref[part, :])
            n2[part, :] = (unit * gain_ref[...]).astype(bf16)
            return 0

        lax.fori_loop(0, tokens // rows, body, 0)
        n2_turned[...] = n2[...].T
        total[...] = middle_ref[...]
        d_middle_ref[...] = jnp.zeros_like(d_middle_ref)

    @pl.when(step < tiles)
    def _():
        up_w, down_w = up_ref[...], down_ref[...]
        up = dot(n2[...], up_w, 1, 0)
        d_act = dot(cot_ref[...], down_w, 1, 1)
        share = 0.5 + 0.5 * lax.erf(up * (0.5**0.5))
        density = jnp.exp(-0.5 * up * up) * 0.3989422804014327
        act = (up * share).astype(bf16)
        d_up = (d_act * (share + up * density)).astype(bf16)
        total[...] += dot(act, down_w, 1, 0)
        d_middle_ref[...] += dot(d_up, up_w, 1, 1)
        slot = step % 2

        @pl.when(step >= 2)
        def _():
            for copy in copies(slot, False):
                copy.wait_send()

        up_grad = dot(n2_turned[...], d_up, 1, 0).astype(bf16)
        cut = up_grad.shape[1] // 2

        @pl.when(core == 0)
        def _():
            up_keep[slot] = up_grad[:, :cut].reshape(up_keep.shape[1:])
            up_send[slot] = up_grad[:, cut:].reshape(up_keep.shape[1:])

        @pl.when(core != 0)
        def _():
            up_keep[slot] = up_grad[:, cut:].reshape(up_keep.shape[1:])
            up_send[slot] = up_grad[:, :cut].reshape(up_keep.shape[1:])

        down_grad = dot(act, cot_ref[...], 0, 0).astype(bf16)

        @pl.when(core == 0)
        def _():
            down_keep[slot] = down_grad[:, :half].reshape(down_keep.shape[1:])
            down_send[slot] = down_grad[:, half:].reshape(down_keep.shape[1:])

        @pl.when(core != 0)
        def _():
            down_keep[slot] = down_grad[:, half:].reshape(down_keep.shape[1:])
            down_send[slot] = down_grad[:, :half].reshape(down_keep.shape[1:])

    def add(a, b):
        return (a.astype(f32) + b.astype(f32)).astype(bf16)

    def last_add():
        slot = step % 2
        for copy in copies(slot, True):
            copy.wait_recv()
        down_part[...] = add(down_far_keep[slot], down_far_recv[slot]).reshape(down_part.shape)
        up_part[...] = add(up_far_keep[slot], up_far_recv[slot]).reshape(up_part.shape)

        @pl.when(step < tiles)
        def _():
            signal(far_free.at[0], far_peers[0])
            signal(far_free.at[1], far_peers[1])

    def pass_on():
        slot = (step + 1) % 2
        for copy in copies(slot, False):
            copy.wait_recv()

        @pl.when(step >= 3)
        def _():
            for copy in copies(slot, True):
                copy.wait_send()
            pl.semaphore_wait(far_free.at[0], 1)
            pl.semaphore_wait(far_free.at[1], 1)

        down_far_send[slot] = add(down_keep[slot, :, 1 - high], down_recv[slot, :, 1 - high])
        down_far_keep[slot] = add(down_keep[slot, :, high], down_recv[slot, :, high])
        up_far_send[slot] = add(up_keep[slot, :, 1 - low], up_recv[slot, :, 1 - low])
        up_far_keep[slot] = add(up_keep[slot, :, low], up_recv[slot, :, low])
        for copy in copies(slot, True):
            copy.start()

        @pl.when(step < tiles - 1)
        def _():
            signal(core_free, core_peer)

    @pl.when((step >= 2) & (step <= tiles))
    def _():
        last_add()

    @pl.when((step >= 1) & (step <= tiles))
    def _():
        pass_on()

    @pl.when(step < tiles)
    def _():
        @pl.when(step >= 2)
        def _():
            pl.semaphore_wait(core_free, 1)

        for copy in copies(step % 2, False):
            copy.start()

    @pl.when(step == tiles)
    def _():
        def body(i, _):
            part = pl.ds(pl.multiple_of(i * rows, rows), rows)
            out_ref[part, :] = total[part, :].astype(bf16)
            unit, scale = norm_parts(middle_ref[part, :])
            grad = cot_ref[part, :].astype(f32) + norm_back(d_middle_ref[part, :], gain_ref[...], unit, scale)
            d_middle_ref[part, :] = grad
            d_attn_ref[part, :] = grad.astype(bf16)
            return 0

        lax.fori_loop(0, tokens // rows, body, 0)

    @pl.when(step == tiles + 1)
    def _():
        last_add()
        for slot in range(2):
            for far in (False, True):
                for copy in copies(slot, far):
                    copy.wait_send()


def feed(middle, cot, gain, up_weight, down_weight, n_seq):
    tokens, width = middle.shape
    wide = up_weight.shape[1]
    tile = feed_tile
    tiles = wide // tile
    half, shard = width // 2, width // n_seq
    whole = lambda dtype: jax.ShapeDtypeStruct((tokens, width), dtype)
    fixed = lambda shape: pl.BlockSpec(shape, lambda i: (0, 0), pipeline_mode=pl.Buffered(1))
    at = lambda i: jnp.minimum(i, tiles - 1)
    done = lambda i: jnp.maximum(i - 2, 0)
    down_shape = (2, tile // (2 * piece_rows), 2, piece_rows, half)
    up_shape = (2, n_seq // 2, 2, shard, tile // 2)
    near = [pltpu.VMEM(down_shape, bf16)] * 3 + [pltpu.VMEM(up_shape, bf16)] * 3
    far = [pltpu.VMEM(down_shape[:2] + down_shape[3:], bf16)] * 3 + [pltpu.VMEM(up_shape[:2] + up_shape[3:], bf16)] * 3
    return pl.pallas_call(
        functools.partial(feed_kernel, tiles, 128),
        grid=(tiles + 2,),
        in_specs=[
            fixed((tokens, width)),
            fixed((tokens, width)),
            fixed((1, width)),
            pl.BlockSpec((width, tile), lambda i: (0, at(i))),
            pl.BlockSpec((tile, width), lambda i: (at(i), 0)),
        ],
        out_specs=[
            fixed((tokens, width)),
            fixed((tokens, width)),
            fixed((tokens, width)),
            pl.BlockSpec((tile // 2, half), lambda i: (done(i), 0)),
            pl.BlockSpec((width // 2, tile // 2), lambda i: (0, done(i))),
        ],
        scratch_shapes=[
            pltpu.VMEM((tokens, width), bf16),
            pltpu.VMEM((width, tokens), bf16),
            pltpu.VMEM((tokens, width), f32),
        ]
        + near
        + far
        + [pltpu.SemaphoreType.DMA((2, 2))] * 4
        + [pltpu.SemaphoreType.REGULAR, pltpu.SemaphoreType.REGULAR((2,))],
        out_shape=[
            whole(bf16),
            whole(f32),
            whole(bf16),
            jax.ShapeDtypeStruct((wide // 2, half), bf16),
            jax.ShapeDtypeStruct((width // 2, wide // 2), bf16),
        ],
        compiler_params=pltpu.CompilerParams(
            vmem_limit_bytes=feed_vmem_bytes, collective_id=1, has_side_effects=True
        ),
        cost_estimate=pl.CostEstimate(
            flops=12 * tokens * width * wide,
            bytes_accessed=16 * tokens * width + 6 * width * wide,
            transcendentals=2 * tokens * wide,
        ),
        name="feed",
    )(middle, cot, gain.reshape(1, width), up_weight, down_weight)


def add_split_kernel(has_two, bit_ref, *refs):
    ins, outs = refs[: 2 if has_two else 1], refs[2 if has_two else 1 :]
    value = ins[0][...]
    if has_two:
        value = (value.astype(f32) + ins[1][...].astype(f32)).astype(bf16)
    if len(outs) == 1:
        outs[0][...] = value
    else:
        sends = pl.program_id(0) == 0

        @pl.when(sends)
        def _():
            outs[0][...] = value

        @pl.when(jnp.logical_not(sends))
        def _():
            outs[1][...] = value


def add_split(kept, received, inner, bit):
    rows, columns = kept.shape
    values = [kept] if received is None else [kept, received.reshape(rows, columns)]
    if bit is None:
        if received is None:
            return None, kept
        count = 4 if rows % 64 == 0 else 1
        block = pl.BlockSpec((rows // count, columns), lambda i, bit: (i, 0))
        grid, ins, outs = (count,), [block] * 2, block
        shapes = jax.ShapeDtypeStruct((rows, columns), bf16)
        bit = jnp.zeros((), jnp.int32)
    else:
        outer = rows // (2 * inner)
        cut = 1
        while inner // cut * columns > 2**19 and inner % (32 * cut) == 0:
            cut *= 2
        values = [value.reshape(outer, 2, inner, columns) for value in values]
        ins = [
            pl.BlockSpec(
                (None, None, inner // cut, columns),
                lambda w, i, j, bit: (i, jnp.where(w == 0, 1 - bit[0], bit[0]), j, 0),
            )
        ] * len(values)
        outs = [
            pl.BlockSpec(
                (None, inner // cut, columns),
                lambda w, i, j, bit: (jnp.where(w == 0, i, outer - 1), jnp.where(w == 0, j, cut - 1), 0),
            ),
            pl.BlockSpec(
                (None, inner // cut, columns),
                lambda w, i, j, bit: (jnp.where(w == 0, 0, i), jnp.where(w == 0, 0, j), 0),
            ),
        ]
        grid = (2, outer, cut)
        shapes = [jax.ShapeDtypeStruct((outer, inner, columns), bf16)] * 2
    done = pl.pallas_call(
        functools.partial(add_split_kernel, len(values) == 2),
        grid_spec=pltpu.PrefetchScalarGridSpec(
            num_scalar_prefetch=1, grid=grid, in_specs=ins, out_specs=outs
        ),
        out_shape=shapes,
        cost_estimate=pl.CostEstimate(flops=rows * columns, bytes_accessed=6 * rows * columns, transcendentals=0),
        name="add_split",
    )(bit.reshape(1), *values)
    if not isinstance(done, (list, tuple)):
        return None, done
    return done[0].reshape(rows // 2, columns), done[1].reshape(rows // 2, columns)


def tie(*values):
    return lax.optimization_barrier(values)


def build(n_seq, n_rows):
    highs = n_rows // CORES
    seq_bits = n_seq.bit_length() - 1
    high_bits = highs.bit_length() - 1
    bits = seq_bits + high_bits

    def permute(value, target):
        pairs = []
        for s in range(n_seq):
            for r in range(n_rows):
                to_s, to_r = target(s, r)
                pairs.append((s * n_rows + r, to_s * n_rows + to_r))
        return lax.ppermute(value, AXES, pairs)

    def other_core(value):
        return permute(value, lambda s, r: (s, r ^ 1))

    def pick(value, place, axis):
        return lax.dynamic_index_in_dim(value, place, axis, keepdims=False)

    def bit_of(step):
        name, bit = step
        return (lax.axis_index(name) >> bit) & 1

    def across(value, step):
        name, bit = step
        if name == "rows":
            return permute(value, lambda s, r: (s, r ^ (1 << bit)))
        return permute(value, lambda s, r: (s ^ (1 << bit), r))

    high_steps = [("rows", bit + 1) for bit in reversed(range(high_bits))]
    seq_steps = [("seq", bit) for bit in range(seq_bits)]

    class Sum:
        def __init__(self, kept, received, order):
            self.rows, self.columns = kept.shape
            self.kept, self.received = kept, received
            self.left = [step for step in seq_steps[::-1] + high_steps if step in order]
            self.order = list(order)

        def finish(self):
            step = self.order[0] if self.order else None
            inner = self.rows
            if step is not None:
                axis = self.left.index(step)
                inner = self.rows >> (axis + 1)
            self.sent, self.kept = add_split(self.kept, self.received, inner, step and bit_of(step))
            self.received = None

        def begin(self):
            step = self.order.pop(0)
            self.left.remove(step)
            self.rows //= 2
            self.received = across(self.sent, step)

        def finished(self):
            while self.order:
                self.finish()
                self.begin()
            self.finish()
            return self.kept

    rows_first = high_steps + seq_steps[1:2] + seq_steps[:1] + seq_steps[2:]
    down_order = [step for step in seq_steps + high_steps if step != ("rows", 1)]
    up_order = [step for step in high_steps + seq_steps if step != ("seq", 0)]

    def gather_high(value, pieces=0):
        for step in high_steps[::-1]:
            if pieces and step == ("rows", 1):
                continue
            received = across(value, step)
            value = jnp.where(
                bit_of(step) == 0,
                jnp.concatenate([value, received], 0),
                jnp.concatenate([received, value], 0),
            )
        if pieces:
            value = value.reshape(-1, 1, pieces, value.shape[1])
            received = across(value, ("rows", 1))
            value = jnp.where(
                bit_of(("rows", 1)) == 0,
                jnp.concatenate([value, received], 1),
                jnp.concatenate([received, value], 1),
            )
            value = value.reshape(-1, value.shape[-1])
        return value

    def per_device(
        inputs, cell_ids, valid_counts, cotangent, attention_gain, qkv_weight, out_weight, feed_gain, up_weight, down_weight
    ):
        row_count, block, width = inputs.shape
        seq_len = cell_ids.shape[1]
        heads = width // HDIM
        lanes = 2 * HDIM
        seq_at, rows_at = lax.axis_index("seq"), lax.axis_index("rows")
        core = rows_at % CORES
        chips = n_seq // (CORES * row_count)
        group = chips * CORES
        sub = block // group
        tokens = n_seq * sub
        member = (seq_at % chips) * CORES + core
        group_heads = heads // group
        pairs = -(-group_heads // 2)
        group_width = group_heads * HDIM
        padded = pairs * lanes - group_width

        def to_member(value, hop):
            def target(s, r):
                place = ((s % chips) * CORES + r % CORES + hop) % group
                return (s // chips * chips + place // CORES, r // CORES * CORES + place % CORES)

            return permute(value, target)

        def ordered(own, received, axis):
            return jnp.where(
                core == 0,
                jnp.concatenate([own, received], axis),
                jnp.concatenate([received, own], axis),
            )

        def to_rows(value):
            halves = value.reshape(row_count, CORES, block // CORES, width)
            received = other_core(pick(halves, 1 - core, 1))
            both = ordered(pick(halves, core, 1), received, 0).reshape(n_seq, sub, width)
            return lax.all_to_all(both, "seq", 0, 0, tiled=True).reshape(tokens, width)

        def from_rows(value):
            both = lax.all_to_all(value.reshape(n_seq, sub, width), "seq", 0, 0, tiled=True)
            both = both.reshape(CORES, row_count, block // CORES, width)
            received = other_core(pick(both, 1 - core, 0))
            own = pick(both, core, 0)
            return ordered(own[:, None], received[:, None], 1).reshape(row_count, block, width)

        places = jnp.arange(seq_len, dtype=jnp.int32)
        tags = jnp.where(places[None, :] < valid_counts[:, None], cell_ids, -1 - places[None, :])
        tags = ordered(tags, other_core(tags), 0)
        tags = pick(tags, seq_at // chips, 0).reshape(n_seq, CORES, chips, sub)
        tags = tags.transpose(2, 1, 0, 3).reshape(group, tokens)
        order = (member - jnp.arange(group, dtype=jnp.int32)) % group
        tags = jnp.take(tags, order, axis=0).reshape(1, seq_len)
        query_tags, key_tags = tags, tags.reshape(seq_len, 1)

        def pad_heads(value, axis):
            if not padded:
                return value
            fill = [(0, 0)] * value.ndim
            fill[axis] = (0, padded)
            return jnp.pad(value, fill)

        def qkv_of(hop):
            if group == CORES:
                return gather_pairs(((core + hop) % CORES).reshape(1), qkv_weight)
            piece = pick(qkv_weight.reshape(width, 3, group, group_width), (member + hop) % group, 2)
            piece = pad_heads(piece, 2).reshape(width, 3, pairs, lanes)
            return piece.transpose(0, 2, 1, 3).reshape(width, 3 * pairs * lanes)

        def out_of(hop):
            at = (member + hop) % group * group_width
            return pad_heads(lax.dynamic_slice_in_dim(out_weight, at, group_width, 0), 0)

        start = to_rows(inputs)
        qkv_parts = [qkv_of(hop) for hop in range(group)]
        out_parts = [out_of(hop) for hop in range(group)]
        start = start.astype(f32)
        unit1, scale1 = norm_parts(start)
        n1 = (unit1 * attention_gain).astype(bf16)
        n1_all = jnp.concatenate([n1] + [to_member(n1, hop) for hop in range(1, group)], 0)
        cotangent, _ = tie(cotangent, start[:1])
        cot = to_rows(cotangent)
        qkv = dot(n1_all, qkv_parts[0], 1, 0).astype(bf16)
        mixed, lse = attend(qkv, key_tags, query_tags)
        mixed_parts = [mixed[:tokens]] + [
            to_member(mixed[hop * tokens : (hop + 1) * tokens], group - hop) for hop in range(1, group)
        ]
        middle = start
        for part, weight in zip(mixed_parts, out_parts):
            middle = middle + dot(part, weight, 1, 0)
        outputs, d_middle, d_attn, down_part, up_part = feed(middle, cot, feed_gain, up_weight, down_weight, n_seq)

        d_attn_all = jnp.concatenate([d_attn] + [to_member(d_attn, hop) for hop in range(1, group)], 0)

        out_low = from_rows(outputs)

        half = width // CORES
        if group == CORES:
            mixed_own = ordered(mixed_parts[0], mixed_parts[1], 1)
        else:
            slots = jnp.stack([part[:, :group_width] for part in mixed_parts])
            back = (jnp.arange(group, dtype=jnp.int32) - member) % group
            mixed_own = jnp.take(slots, back, axis=0).transpose(1, 0, 2).reshape(tokens, width)
        out_sent = dot(mixed_own, lax.dynamic_slice_in_dim(d_attn, (1 - core) * half, half, 1), 0, 0)
        out_kept = dot(mixed_own, lax.dynamic_slice_in_dim(d_attn, core * half, half, 1), 0, 0)
        out_received = other_core(out_sent.astype(bf16))
        d_mixed = dot(d_attn_all, out_parts[0], 1, 1).astype(bf16)

        down = Sum(down_part, None, down_order)
        up = Sum(up_part, None, up_order)
        out = Sum(out_kept.astype(bf16), out_received, rows_first)

        def before_next(*sums):
            nonlocal d_mixed
            for each in sums:
                each.finish()
            values = tie(d_mixed, *[v for each in sums for v in (each.sent, each.kept)])
            d_mixed = values[0]
            for at, each in enumerate(sums):
                each.sent, each.kept = values[1 + 2 * at : 3 + 2 * at]
                each.begin()

        def back(at):
            return attend_back(qkv, mixed, d_mixed, lse, key_tags, query_tags, at, 1)

        cut = max(1, 3 * pairs // 5)
        before_next(down, up)
        d_qkv, qkv_sums, d_parts = [], [], [[] for _ in range(group)]

        def take_piece(pieces):
            piece = jnp.concatenate(pieces, axis=1)
            d_parts[0].append(piece[:tokens])
            for hop in range(1, group):
                d_parts[hop].append(to_member(piece[hop * tokens : (hop + 1) * tokens], group - hop))
            return dot(n1_all, piece, 0, 0)

        grads = []
        for at in range(pairs):
            d_qkv.append(back(at))
            d_mixed, d_qkv[at] = tie(d_mixed, d_qkv[at])
            if at + 1 == cut:
                grads.append(take_piece(d_qkv))
            if at == min(0, pairs - 1):
                before_next(out)
            if at == min(1, pairs - 1):
                before_next(down, up)
            if at == min(3, pairs - 1):
                before_next(down, up, out)
        if pairs > cut:
            grads.append(take_piece(d_qkv[cut:]))
        if group == CORES:
            qkv_sums = [Sum(grad.astype(bf16), None, rows_first) for grad in grads]
        else:
            grad = jnp.concatenate(grads, 1)
            grad = grad.reshape(width, pairs, 3, lanes).transpose(0, 2, 1, 3)
            grad = grad.reshape(width, 3, 1, pairs * lanes)[..., :group_width]
            grad = lax.dynamic_update_slice_in_dim(
                jnp.zeros((width, 3, group, group_width), f32), grad, member, 2
            ).reshape(width, 3, CORES, half)
            kept = pick(grad, core, 2).astype(bf16).reshape(width, 3 * half)
            sent = pick(grad, 1 - core, 2).astype(bf16).reshape(width, 3 * half)
            qkv_sums = [Sum(kept, other_core(sent), rows_first)]

        d_n1 = jnp.zeros((tokens, width), f32)
        for part, weight in zip(d_parts, qkv_parts):
            d_n1 = d_n1 + dot(jnp.concatenate(part, 1), weight, 1, 1)
        input_grad = d_middle + norm_back(d_n1, attention_gain, unit1, scale1)
        input_grad = from_rows(input_grad.astype(bf16))

        down_total = gather_high(down.finished(), piece_rows)
        down_total = ordered(down_total, other_core(down_total), 1).astype(f32)
        tile = feed_tile // CORES
        up_total = gather_high(up.finished()).reshape(width // n_seq, -1, 1, tile)
        up_total = ordered(up_total, other_core(up_total), 2).reshape(width // n_seq, -1).astype(f32)
        out_total = gather_high(out.finished())
        out_total = ordered(out_total, other_core(out_total), 1).astype(f32)
        qkv_part = gather_high(jnp.concatenate([each.finished() for each in qkv_sums], 1))
        if group == CORES:
            qkv_part = qkv_part.reshape(-1, pairs, 3, lanes).transpose(0, 2, 1, 3)
        qkv_part = qkv_part.reshape(-1, 3, half)
        qkv_total = ordered(qkv_part[:, :, None], other_core(qkv_part)[:, :, None], 2)
        qkv_total = qkv_total.reshape(-1, 3 * width).astype(f32)

        shard = width // n_seq

        def gain_total(weight, total, gain):
            rows = lax.dynamic_slice_in_dim(weight, seq_at * shard, shard, 0).astype(f32)
            return jnp.sum(rows * total, axis=1) / lax.dynamic_slice_in_dim(gain, seq_at * shard, shard, 0)

        return (
            out_low,
            input_grad,
            gain_total(qkv_weight, qkv_total, attention_gain),
            qkv_total,
            out_total,
            gain_total(up_weight, up_total, feed_gain),
            up_total,
            down_total,
        )

    return per_device


def solution(mesh):
    placed = (
        P("rows", "seq", None),
        P("rows", None),
        P("rows"),
        P("rows", "seq", None),
        P(),
        P(),
        P(),
        P(),
        P(),
        P(),
    )
    return jax.shard_map(
        build(mesh.shape["seq"], mesh.shape["rows"]),
        mesh=mesh,
        in_specs=placed,
        out_specs=(
            P("rows", "seq", None),
            P("rows", "seq", None),
            P("seq"),
            P("seq", None),
            P("seq", None),
            P("seq"),
            P("seq", None),
            P("seq", None),
        ),
        check_vma=False,
    )
```

```python
import functools

import jax
import jax.numpy as jnp
from jax import lax
from jax.experimental import pallas as pl
from jax.experimental.pallas import tpu as pltpu
from jax.sharding import PartitionSpec as P

HDIM = 64
CORES = 2
epsilon = 1e-05
masked_score = -1e30
score_scale = HDIM ** (-0.5)
log2e = 1.4426950408889634
bf16 = jnp.bfloat16
f32 = jnp.float32
AXES = ("seq", "rows")
vmem_bytes = 60 * 2**20
feed_vmem_bytes = 62 * 2**20
feed_tile = 512
MESH = pl.DeviceIdType.MESH


def dot(a, b, ca, cb):
    return lax.dot_general(a, b, (((ca,), (cb,)), ((), ())), preferred_element_type=f32)


def attend_kernel(tile, key_tags, query_tags, q_ref, k_ref, v_ref, o_ref, lse_ref, v_turned):
    tokens = q_ref.shape[0]
    v_turned[...] = v_ref[...].T
    lane = lax.broadcasted_iota(jnp.int32, (tile, 2 * HDIM), 1)

    def body(step, _):
        part = pl.ds(pl.multiple_of(step * tile, tile), tile)
        q = q_ref[part, :]
        allowed = key_tags[...] == query_tags[:, part]
        pieces = []
        for head in range(2):
            own = jnp.where((lane // HDIM) == head, q, bf16(0))
            scores = dot(k_ref[...], own, 1, 1)
            scores = jnp.where(allowed, scores, masked_score)
            peak = jnp.max(scores, axis=0, keepdims=True)
            powers = jnp.exp2((scores - peak) * (score_scale * log2e))
            total = jnp.sum(powers, axis=0, keepdims=True)
            mixed = dot(v_turned[head * HDIM : (head + 1) * HDIM, :], powers.astype(bf16), 1, 0)
            pieces.append(mixed * (1.0 / total))
            lse_ref[head : head + 1, part] = peak * (score_scale * log2e) + jnp.log2(total)
        o_ref[part, :] = jnp.concatenate(pieces, axis=0).T.astype(bf16)
        return 0

    lax.fori_loop(0, tokens // tile, body, 0)


def attend(qkv, key_tags, query_tags):
    tokens, width = qkv.shape
    lanes = 2 * HDIM
    pairs = width // (3 * lanes)
    tile = min(512, tokens)

    def columns(place):
        return pl.BlockSpec((tokens, lanes), lambda i: (0, 3 * i + place))

    return pl.pallas_call(
        functools.partial(attend_kernel, tile),
        grid=(pairs,),
        in_specs=[
            pl.BlockSpec((tokens, 1), lambda i: (0, 0)),
            pl.BlockSpec((1, tokens), lambda i: (0, 0)),
            columns(0),
            columns(1),
            columns(2),
        ],
        out_specs=[
            pl.BlockSpec((tokens, lanes), lambda i: (0, i)),
            pl.BlockSpec((None, 2, tokens), lambda i: (i, 0, 0)),
        ],
        out_shape=[
            jax.ShapeDtypeStruct((tokens, pairs * lanes), bf16),
            jax.ShapeDtypeStruct((pairs, 2, tokens), f32),
        ],
        scratch_shapes=[pltpu.VMEM((lanes, tokens), bf16)],
        compiler_params=pltpu.CompilerParams(vmem_limit_bytes=vmem_bytes),
        cost_estimate=pl.CostEstimate(
            flops=32 * pairs * tokens * tokens * HDIM,
            bytes_accessed=8 * tokens * pairs * lanes,
            transcendentals=2 * pairs * tokens * tokens,
        ),
        name="attend",
    )(key_tags, query_tags, qkv, qkv, qkv)


def attend_back_kernel(
    tile, key_tags, query_tags, q_ref, k_ref, v_ref, o_ref, do_ref, lse_ref, grad_ref, k_turned, dq_turned, delta
):
    tokens = q_ref.shape[0]
    lanes = 2 * HDIM
    k_turned[...] = k_ref[...].T
    dq_turned[...] = (o_ref[...].astype(f32) * do_ref[...].astype(f32)).T
    for head in range(2):
        rows = dq_turned[head * HDIM : (head + 1) * HDIM, :]
        delta[head : head + 1, :] = jnp.sum(rows, axis=0, keepdims=True)
    dq_turned[...] = jnp.zeros_like(dq_turned)
    first = lax.broadcasted_iota(jnp.int32, (tile, lanes), 1) < HDIM

    def body(step, _):
        part = pl.ds(pl.multiple_of(step * tile, tile), tile)
        k, v = k_ref[part, :], v_ref[part, :]
        q, do = q_ref[...], do_ref[...]
        allowed = key_tags[part, :] == query_tags[...]
        dk, dv = [], []
        for head in range(2):
            own = first if head == 0 else jnp.logical_not(first)
            own_rows = slice(head * HDIM, (head + 1) * HDIM)
            scores = dot(jnp.where(own, k, bf16(0)), q, 1, 1)
            scores = jnp.where(allowed, scores, masked_score)
            chances = jnp.exp2(scores * (score_scale * log2e) - lse_ref[head : head + 1, :])
            weight_grad = dot(jnp.where(own, v, bf16(0)), do, 1, 1)
            score_grad = (chances * (weight_grad - delta[head : head + 1, :])).astype(bf16)
            dv.append(dot(chances.astype(bf16), do, 1, 0))
            dk.append(dot(score_grad, q, 1, 0))
            dq_turned[own_rows, :] += dot(k_turned[own_rows, part], score_grad, 1, 0)
        grad_ref[part, lanes : 2 * lanes] = (jnp.where(first, dk[0], dk[1]) * score_scale).astype(bf16)
        grad_ref[part, 2 * lanes :] = jnp.where(first, dv[0], dv[1]).astype(bf16)
        return 0

    lax.fori_loop(0, tokens // tile, body, 0)
    grad_ref[:, :lanes] = (dq_turned[...] * score_scale).T.astype(bf16)


def attend_back(qkv, mixed, d_mixed, lse, key_tags, query_tags, start, count):
    tokens = qkv.shape[0]
    tile = min(512, tokens)
    lanes = 2 * HDIM

    def columns(place):
        return pl.BlockSpec((tokens, lanes), lambda i: (0, 3 * (start + i) + place))

    pair = pl.BlockSpec((tokens, lanes), lambda i: (0, start + i))
    return pl.pallas_call(
        functools.partial(attend_back_kernel, tile),
        grid=(count,),
        in_specs=[
            pl.BlockSpec((tokens, 1), lambda i: (0, 0)),
            pl.BlockSpec((1, tokens), lambda i: (0, 0)),
            columns(0),
            columns(1),
            columns(2),
            pair,
            pair,
            pl.BlockSpec((None, 2, tokens), lambda i: (start + i, 0, 0)),
        ],
        out_specs=pl.BlockSpec((tokens, 3 * lanes), lambda i: (0, i)),
        out_shape=jax.ShapeDtypeStruct((tokens, 3 * count * lanes), bf16),
        scratch_shapes=[
            pltpu.VMEM((lanes, tokens), bf16),
            pltpu.VMEM((lanes, tokens), f32),
            pltpu.VMEM((2, tokens), f32),
        ],
        compiler_params=pltpu.CompilerParams(vmem_limit_bytes=vmem_bytes),
        cost_estimate=pl.CostEstimate(
            flops=80 * count * tokens * tokens * HDIM,
            bytes_accessed=16 * tokens * count * lanes,
            transcendentals=2 * count * tokens * tokens,
        ),
        name="attend_back",
    )(key_tags, query_tags, qkv, qkv, qkv, mixed, d_mixed, lse)


def copy_kernel(core_ref, from_ref, to_ref):
    to_ref[...] = from_ref[...]


def gather_pairs(core, qkv_weight):
    width, lanes = qkv_weight.shape[0], 2 * HDIM
    pairs = width // (CORES * lanes)
    return pl.pallas_call(
        copy_kernel,
        grid_spec=pltpu.PrefetchScalarGridSpec(
            num_scalar_prefetch=1,
            grid=(pairs, 3),
            in_specs=[
                pl.BlockSpec((width, lanes), lambda i, j, core: (0, (j * CORES + core[0]) * pairs + i))
            ],
            out_specs=pl.BlockSpec((width, lanes), lambda i, j, core: (0, 3 * i + j)),
        ),
        out_shape=jax.ShapeDtypeStruct((width, 3 * pairs * lanes), qkv_weight.dtype),
        cost_estimate=pl.CostEstimate(flops=0, bytes_accessed=12 * width * pairs * lanes, transcendentals=0),
        name="gather_pairs",
    )(core, qkv_weight)


def norm_parts(values):
    center = values - jnp.mean(values, axis=-1, keepdims=True)
    spread = jnp.mean(center * center, axis=-1, keepdims=True)
    scale = lax.rsqrt(spread + epsilon)
    return center * scale, scale


def norm_back(grad, gain, unit, scale):
    e = grad * gain
    return scale * (
        e - jnp.mean(e, axis=-1, keepdims=True) - unit * jnp.mean(e * unit, axis=-1, keepdims=True)
    )


piece_rows = 32


def feed_kernel(
    tiles,
    rows,
    middle_ref,
    cot_ref,
    gain_ref,
    up_ref,
    down_ref,
    out_ref,
    d_middle_ref,
    d_attn_ref,
    down_part,
    up_part,
    n2,
    n2_turned,
    total,
    down_keep,
    down_send,
    down_recv,
    up_keep,
    up_send,
    up_recv,
    down_far_keep,
    down_far_send,
    down_far_recv,
    up_far_keep,
    up_far_send,
    up_far_recv,
    core_send_sem,
    core_recv_sem,
    far_send_sem,
    far_recv_sem,
    core_free,
    far_free,
):
    step = pl.program_id(0)
    tokens, width = n2.shape
    half = width // 2
    seq_at, rows_at = lax.axis_index("seq"), lax.axis_index("rows")
    core, high, low = rows_at % 2, (rows_at // 2) % 2, seq_at % 2
    core_peer = (seq_at, rows_at + 1 - 2 * core)
    far_peers = ((seq_at, rows_at + 2 - 4 * high), (seq_at + 1 - 2 * low, rows_at))

    def copies(slot, far):
        if far:
            refs = ((down_far_send, down_far_recv), (up_far_send, up_far_recv))
            sems, peers = (far_send_sem, far_recv_sem), far_peers
        else:
            refs = ((down_send, down_recv), (up_send, up_recv))
            sems, peers = (core_send_sem, core_recv_sem), (core_peer, core_peer)
        return [
            pltpu.make_async_remote_copy(
                src_ref=refs[kind][0].at[slot],
                dst_ref=refs[kind][1].at[slot],
                send_sem=sems[0].at[kind, slot],
                recv_sem=sems[1].at[kind, slot],
                device_id=peers[kind],
                device_id_type=MESH,
            )
            for kind in range(2)
        ]

    def signal(sem, peer):
        pl.semaphore_signal(sem, inc=1, device_id=peer, device_id_type=MESH)

    @pl.when(step == 0)
    def _():
        barrier = pltpu.get_barrier_semaphore()
        for peer in (core_peer,) + far_peers:
            signal(barrier, peer)
        pl.semaphore_wait(barrier, 3)

        def body(i, _):
            part = pl.ds(pl.multiple_of(i * rows, rows), rows)
            unit, _s = norm_parts(middle_ref[part, :])
            n2[part, :] = (unit * gain_ref[...]).astype(bf16)
            return 0

        lax.fori_loop(0, tokens // rows, body, 0)
        n2_turned[...] = n2[...].T
        total[...] = middle_ref[...]
        d_middle_ref[...] = jnp.zeros_like(d_middle_ref)

    @pl.when(step < tiles)
    def _():
        up_w, down_w = up_ref[...], down_ref[...]
        up = dot(n2[...], up_w, 1, 0)
        d_act = dot(cot_ref[...], down_w, 1, 1)
        share = 0.5 + 0.5 * lax.erf(up * (0.5**0.5))
        density = jnp.exp(-0.5 * up * up) * 0.3989422804014327
        act = (up * share).astype(bf16)
        d_up = (d_act * (share + up * density)).astype(bf16)
        total[...] += dot(act, down_w, 1, 0)
        d_middle_ref[...] += dot(d_up, up_w, 1, 1)
        slot = step % 2

        @pl.when(step >= 2)
        def _():
            for copy in copies(slot, False):
                copy.wait_send()

        up_grad = dot(n2_turned[...], d_up, 1, 0).astype(bf16)
        cut = up_grad.shape[1] // 2

        @pl.when(core == 0)
        def _():
            up_keep[slot] = up_grad[:, :cut].reshape(up_keep.shape[1:])
            up_send[slot] = up_grad[:, cut:].reshape(up_keep.shape[1:])

        @pl.when(core != 0)
        def _():
            up_keep[slot] = up_grad[:, cut:].reshape(up_keep.shape[1:])
            up_send[slot] = up_grad[:, :cut].reshape(up_keep.shape[1:])

        down_grad = dot(act, cot_ref[...], 0, 0).astype(bf16)

        @pl.when(core == 0)
        def _():
            down_keep[slot] = down_grad[:, :half].reshape(down_keep.shape[1:])
            down_send[slot] = down_grad[:, half:].reshape(down_keep.shape[1:])

        @pl.when(core != 0)
        def _():
            down_keep[slot] = down_grad[:, half:].reshape(down_keep.shape[1:])
            down_send[slot] = down_grad[:, :half].reshape(down_keep.shape[1:])

    def add(a, b):
        return (a.astype(f32) + b.astype(f32)).astype(bf16)

    def last_add():
        slot = step % 2
        for copy in copies(slot, True):
            copy.wait_recv()
        down_part[...] = add(down_far_keep[slot], down_far_recv[slot]).reshape(down_part.shape)
        up_part[...] = add(up_far_keep[slot], up_far_recv[slot]).reshape(up_part.shape)

        @pl.when(step < tiles)
        def _():
            signal(far_free.at[0], far_peers[0])
            signal(far_free.at[1], far_peers[1])

    def pass_on():
        slot = (step + 1) % 2
        for copy in copies(slot, False):
            copy.wait_recv()

        @pl.when(step >= 3)
        def _():
            for copy in copies(slot, True):
                copy.wait_send()
            pl.semaphore_wait(far_free.at[0], 1)
            pl.semaphore_wait(far_free.at[1], 1)

        down_far_send[slot] = add(down_keep[slot, :, 1 - high], down_recv[slot, :, 1 - high])
        down_far_keep[slot] = add(down_keep[slot, :, high], down_recv[slot, :, high])
        up_far_send[slot] = add(up_keep[slot, :, 1 - low], up_recv[slot, :, 1 - low])
        up_far_keep[slot] = add(up_keep[slot, :, low], up_recv[slot, :, low])
        for copy in copies(slot, True):
            copy.start()

        @pl.when(step < tiles - 1)
        def _():
            signal(core_free, core_peer)

    @pl.when((step >= 2) & (step <= tiles))
    def _():
        last_add()

    @pl.when((step >= 1) & (step <= tiles))
    def _():
        pass_on()

    @pl.when(step < tiles)
    def _():
        @pl.when(step >= 2)
        def _():
            pl.semaphore_wait(core_free, 1)

        for copy in copies(step % 2, False):
            copy.start()

    @pl.when(step == tiles)
    def _():
        def body(i, _):
            part = pl.ds(pl.multiple_of(i * rows, rows), rows)
            out_ref[part, :] = total[part, :].astype(bf16)
            unit, scale = norm_parts(middle_ref[part, :])
            grad = cot_ref[part, :].astype(f32) + norm_back(d_middle_ref[part, :], gain_ref[...], unit, scale)
            d_middle_ref[part, :] = grad
            d_attn_ref[part, :] = grad.astype(bf16)
            return 0

        lax.fori_loop(0, tokens // rows, body, 0)

    @pl.when(step == tiles + 1)
    def _():
        last_add()
        for slot in range(2):
            for far in (False, True):
                for copy in copies(slot, far):
                    copy.wait_send()


def feed(middle, cot, gain, up_weight, down_weight, n_seq):
    tokens, width = middle.shape
    wide = up_weight.shape[1]
    tile = feed_tile
    tiles = wide // tile
    half, shard = width // 2, width // n_seq
    whole = lambda dtype: jax.ShapeDtypeStruct((tokens, width), dtype)
    fixed = lambda shape: pl.BlockSpec(shape, lambda i: (0, 0), pipeline_mode=pl.Buffered(1))
    at = lambda i: jnp.minimum(i, tiles - 1)
    done = lambda i: jnp.maximum(i - 2, 0)
    down_shape = (2, tile // (2 * piece_rows), 2, piece_rows, half)
    up_shape = (2, n_seq // 2, 2, shard, tile // 2)
    near = [pltpu.VMEM(down_shape, bf16)] * 3 + [pltpu.VMEM(up_shape, bf16)] * 3
    far = [pltpu.VMEM(down_shape[:2] + down_shape[3:], bf16)] * 3 + [pltpu.VMEM(up_shape[:2] + up_shape[3:], bf16)] * 3
    return pl.pallas_call(
        functools.partial(feed_kernel, tiles, 128),
        grid=(tiles + 2,),
        in_specs=[
            fixed((tokens, width)),
            fixed((tokens, width)),
            fixed((1, width)),
            pl.BlockSpec((width, tile), lambda i: (0, at(i))),
            pl.BlockSpec((tile, width), lambda i: (at(i), 0)),
        ],
        out_specs=[
            fixed((tokens, width)),
            fixed((tokens, width)),
            fixed((tokens, width)),
            pl.BlockSpec((tile // 2, half), lambda i: (done(i), 0)),
            pl.BlockSpec((width // 2, tile // 2), lambda i: (0, done(i))),
        ],
        scratch_shapes=[
            pltpu.VMEM((tokens, width), bf16),
            pltpu.VMEM((width, tokens), bf16),
            pltpu.VMEM((tokens, width), f32),
        ]
        + near
        + far
        + [pltpu.SemaphoreType.DMA((2, 2))] * 4
        + [pltpu.SemaphoreType.REGULAR, pltpu.SemaphoreType.REGULAR((2,))],
        out_shape=[
            whole(bf16),
            whole(f32),
            whole(bf16),
            jax.ShapeDtypeStruct((wide // 2, half), bf16),
            jax.ShapeDtypeStruct((width // 2, wide // 2), bf16),
        ],
        compiler_params=pltpu.CompilerParams(
            vmem_limit_bytes=feed_vmem_bytes, collective_id=1, has_side_effects=True
        ),
        cost_estimate=pl.CostEstimate(
            flops=12 * tokens * width * wide,
            bytes_accessed=16 * tokens * width + 6 * width * wide,
            transcendentals=2 * tokens * wide,
        ),
        name="feed",
    )(middle, cot, gain.reshape(1, width), up_weight, down_weight)


class Stream:
    def __init__(self, levels, rows, columns):
        self.levels, self.rows, self.columns = levels, rows, columns

    def shape(self, level):
        outer = 2 ** (len(self.levels) - 1 - level)
        return (max(outer // 2, 1), min(outer, 2), self.rows, self.columns)

    def scratch(self):
        shapes = []
        for level in range(len(self.levels)):
            shape = self.shape(level)
            shapes += [pltpu.VMEM(shape, bf16), pltpu.VMEM(shape, bf16), pltpu.VMEM((2,) + shape, bf16)]
        return shapes


def streams_of(block_rows, width, pairs):
    lanes = 2 * HDIM
    return (
        Stream(("x", "y", "z1", "z2"), width // 16, 4 * lanes),
        Stream(("y", "z1", "z2"), block_rows // 2, lanes),
        Stream(("x", "z1", "z2"), width // 16, block_rows * 8 // CORES // pairs),
    )


def back_kernel(pairs, tile, streams, row_count, *refs):
    (
        key_tags, query_tags, q_ref, k_ref, v_ref, o_ref, do_ref, lse_ref, turned_ref, own_weight, other_weight,
        gain_ref, out_kept, out_came, down_ref, up_ref, start_ref, d_middle_ref, outputs_ref,
    ) = refs[:19]
    grad_out, outputs_out, *gathered = refs[19:24]
    rest = list(refs[24:])
    take = lambda count: [rest.pop(0) for _ in range(count)]
    k_turned, dq_turned, delta, d_pair, d_came, d_n1, staged, start_part, middle_part = take(9)
    levels = []
    for stream in streams:
        levels.append([take(3) for _ in stream.levels])
    joined = take(len(streams))
    (
        send_sems, recv_sems, join_send, join_recv, core_send, core_recv, local_sems,
        pair_send, pair_recv, home_send, home_recv, home_local, part_sems, result_send, result_recv, result_local,
    ) = rest

    step = pl.program_id(0)
    tokens, lanes = q_ref.shape
    own_tokens = tokens // CORES
    seq_at, rows_at = lax.axis_index("seq"), lax.axis_index("rows")
    core, high = rows_at % 2, (rows_at // 2) % 2
    places = {"x": high, "y": seq_at % 2, "z1": (seq_at // 2) % 2, "z2": seq_at // 4}
    peers = {
        "x": (seq_at, rows_at + 2 - 4 * high),
        "y": (seq_at + 1 - 2 * places["y"], rows_at),
        "z1": (seq_at + 2 - 4 * places["z1"], rows_at),
        "z2": (seq_at + 4 - 8 * places["z2"], rows_at),
        "core": (seq_at, rows_at + 1 - 2 * core),
    }
    n_seq = 2 * row_count
    sub = start_part.shape[1]

    def remote(source, target, send, recv, peer):
        return pltpu.make_async_remote_copy(
            src_ref=source, dst_ref=target, send_sem=send, recv_sem=recv, device_id=peer, device_id_type=MESH
        )

    def add(a, b):
        return (a.astype(f32) + b.astype(f32)).astype(bf16)

    def level_copy(at, level, item):
        send, _, came = levels[at][level]
        slot = item % 2
        return remote(
            send, came.at[slot], send_sems.at[at, level], recv_sems.at[at, level, slot], peers[streams[at].levels[level]]
        )

    def join_copy(at, item):
        part = joined[at].at[item, high]
        return remote(part, part, join_send.at[at], join_recv.at[at, item % 2], peers["x"])

    def core_copy(at, item):
        return remote(
            joined[at].at[item],
            gathered[at].at[item, core],
            core_send.at[at],
            core_recv.at[at, item % 2],
            peers["core"],
        )

    def local_copy(at, item):
        return pltpu.make_async_copy(joined[at].at[item], gathered[at].at[item, core], local_sems.at[at])

    def pair_copy(item):
        slot = item % 2
        return remote(
            d_pair.at[slot, pl.ds(own_tokens, own_tokens)],
            d_came.at[slot],
            pair_send.at[slot],
            pair_recv.at[slot],
            peers["core"],
        )

    home = seq_at // row_count

    def to_home(block, own, result):
        if result:
            source, target = outputs_ref.at[pl.ds(block * sub, sub)], outputs_out
            sems = result_send, result_recv, result_local
        else:
            source, target = staged.at[block], grad_out
            sems = home_send, home_recv, home_local
        row = seq_at % row_count
        if own:
            return pltpu.make_async_copy(source, target.at[row, core], sems[2])
        return remote(source, target.at[row, core], sems[0].at[block], sems[1].at[row, core], (block, rows_at - core + home))

    def start_home(block, result):
        @pl.when(is_own(block))
        def _():
            to_home(block, True, result).start()

        @pl.when(jnp.logical_not(is_own(block)))
        def _():
            to_home(block, False, result).start()

    def wait_home(result):
        for block in range(n_seq):
            @pl.when(is_own(block))
            def _():
                to_home(block, True, result).wait()

            @pl.when(jnp.logical_not(is_own(block)))
            def _():
                to_home(block, False, result).wait_send()
        source, target = (outputs_ref.at[pl.ds(0, sub)], outputs_out) if result else (staged.at[0], grad_out)
        sems = (result_send, result_recv) if result else (home_send, home_recv)
        for row in range(row_count):
            for c in range(CORES):
                @pl.when(jnp.logical_not((seq_at == core * row_count + row) & (core == c)))
                def _():
                    remote(source, target.at[row, c], sems[0].at[0], sems[1].at[row, c], peers["core"]).wait_recv()

    def is_own(block):
        return (seq_at == block) & (home == core)

    @pl.when(step == 0)
    def _():
        barrier = pltpu.get_barrier_semaphore()
        for s in range(n_seq):
            for c in range(CORES):
                @pl.when(jnp.logical_not((seq_at == s) & (core == c)))
                def _():
                    pl.semaphore_signal(barrier, inc=1, device_id=(s, rows_at - core + c), device_id_type=MESH)
        pl.semaphore_signal(barrier, inc=1, device_id=peers["x"], device_id_type=MESH)
        pl.semaphore_wait(barrier, n_seq * CORES)
        d_n1[...] = jnp.zeros_like(d_n1)
        for block in range(n_seq):
            start_home(block, True)

    @pl.when(step < pairs)
    def _():
        slot = step % 2
        k_turned[...] = k_ref[...].T
        dq_turned[...] = (o_ref[...].astype(f32) * do_ref[...].astype(f32)).T
        for head in range(2):
            own_rows = dq_turned[head * HDIM : (head + 1) * HDIM, :]
            delta[head : head + 1, :] = jnp.sum(own_rows, axis=0, keepdims=True)
        dq_turned[...] = jnp.zeros_like(dq_turned)
        first = lax.broadcasted_iota(jnp.int32, (tile, lanes), 1) < HDIM

        def body(i, _):
            part = pl.ds(pl.multiple_of(i * tile, tile), tile)
            k, v = k_ref[part, :], v_ref[part, :]
            q, do = q_ref[...], do_ref[...]
            allowed = key_tags[part, :] == query_tags[...]
            dk, dv = [], []
            for head in range(2):
                own = first if head == 0 else jnp.logical_not(first)
                own_rows = slice(head * HDIM, (head + 1) * HDIM)
                scores = dot(jnp.where(own, k, bf16(0)), q, 1, 1)
                scores = jnp.where(allowed, scores, masked_score)
                chances = jnp.exp2(scores * (score_scale * log2e) - lse_ref[head : head + 1, :])
                weight_grad = dot(jnp.where(own, v, bf16(0)), do, 1, 1)
                score_grad = (chances * (weight_grad - delta[head : head + 1, :])).astype(bf16)
                dv.append(dot(chances.astype(bf16), do, 1, 0))
                dk.append(dot(score_grad, q, 1, 0))
                dq_turned[own_rows, :] += dot(k_turned[own_rows, part], score_grad, 1, 0)
            d_pair[slot, part, lanes : 2 * lanes] = (jnp.where(first, dk[0], dk[1]) * score_scale).astype(bf16)
            d_pair[slot, part, 2 * lanes :] = jnp.where(first, dv[0], dv[1]).astype(bf16)
            return 0

        lax.fori_loop(0, tokens // tile, body, 0)
        d_pair[slot, :, :lanes] = (dq_turned[...] * score_scale).T.astype(bf16)

    def add_pair():
        item = step - 1
        slot = item % 2
        pair_copy(item).wait()
        d_n1[...] += dot(d_pair[slot, :own_tokens, :], own_weight[...], 1, 1) + dot(
            d_came[slot], other_weight[...], 1, 1
        )

    @pl.when((step >= 1) & (step <= pairs))
    def _():
        add_pair()

    @pl.when(step < pairs)
    def _():
        pair_copy(step).start()

    def part_copies(block):
        rows = pl.ds(block * start_part.shape[1], start_part.shape[1])
        slot = block % 2
        return (
            pltpu.make_async_copy(start_ref.at[rows], start_part.at[slot], part_sems.at[0, slot]),
            pltpu.make_async_copy(d_middle_ref.at[rows], middle_part.at[slot], part_sems.at[1, slot]),
        )

    @pl.when(step == pairs)
    def _():
        for copy in part_copies(0):
            copy.start()
        for block in range(n_seq):
            if block + 1 < n_seq:
                for copy in part_copies(block + 1):
                    copy.start()
            for copy in part_copies(block):
                copy.wait()
            unit, scale = norm_parts(start_part[block % 2].astype(f32))
            grad = norm_back(d_n1[block * sub : (block + 1) * sub, :], gain_ref[...], unit, scale)
            staged[block] = (middle_part[block % 2] + grad).astype(bf16)
            start_home(block, False)

    for at, stream in enumerate(streams):
        depth = len(stream.levels)

        def item_at(lag):
            return step - lag, (step >= lag) & (step - lag < pairs)

        item, here = item_at(depth + 2)

        @pl.when(here)
        def _(at=at, item=item):
            core_copy(at, item).wait()
            local_copy(at, item).wait()

        item, here = item_at(depth + 1)

        @pl.when(here)
        def _(at=at, item=item):
            join_copy(at, item).wait()
            core_copy(at, item).start()
            local_copy(at, item).start()

        for level in reversed(range(depth)):
            item, here = item_at(level + 1)

            @pl.when(here)
            def _(at=at, item=item, level=level, stream=stream, depth=depth):
                _, keep, came = levels[at][level]
                slot = item % 2
                level_copy(at, level, item).wait_recv()
                if level == depth - 1:
                    joined[at][item, high] = add(keep[0, 0], came[slot, 0, 0])
                    join_copy(at, item).start()
                    return

                @pl.when(item > 0)
                def _():
                    level_copy(at, level + 1, item - 1).wait_send()

                next_send, next_keep, _ = levels[at][level + 1]
                place = places[stream.levels[level + 1]]
                next_send[...] = add(keep[:, 1 - place], came[slot, :, 1 - place]).reshape(next_send.shape)
                next_keep[...] = add(keep[:, place], came[slot, :, place]).reshape(next_keep.shape)
                level_copy(at, level + 1, item).start()

    @pl.when(step < pairs)
    def _():
        @pl.when(step > 0)
        def _():
            for at in range(len(streams)):
                level_copy(at, 0, step - 1).wait_send()

        send, keep, _ = levels[0][0]
        grad = dot(turned_ref[...], d_pair[step % 2], 1, 0).astype(bf16)
        grad = grad.reshape(n_seq, 2, send.shape[2], 3 * lanes)
        shape = send.shape[:3] + (3 * lanes,)

        @pl.when(high == 0)
        def _():
            send[:, :, :, : 3 * lanes] = grad[:, 1].reshape(shape)
            keep[:, :, :, : 3 * lanes] = grad[:, 0].reshape(shape)

        @pl.when(high != 0)
        def _():
            send[:, :, :, : 3 * lanes] = grad[:, 0].reshape(shape)
            keep[:, :, :, : 3 * lanes] = grad[:, 1].reshape(shape)

        shape = send.shape[:3] + (lanes,)
        send[:, :, :, 3 * lanes :] = add(out_kept[:, 1 - high], out_came[:, 1 - high]).reshape(shape)
        keep[:, :, :, 3 * lanes :] = add(out_kept[:, high], out_came[:, high]).reshape(shape)
        for at, (ref, place) in enumerate(((down_ref, places["y"]), (up_ref, high)), 1):
            send, keep, _ = levels[at][0]
            send[...] = ref[:, 1 - place].reshape(send.shape)
            keep[...] = ref[:, place].reshape(keep.shape)
        for at in range(len(streams)):
            level_copy(at, 0, step).start()

    @pl.when(step == pl.num_programs(0) - 1)
    def _():
        for at, stream in enumerate(streams):
            for level in range(len(stream.levels)):
                level_copy(at, level, pairs - 1).wait_send()
        wait_home(False)
        wait_home(True)


def back(
    qkv, mixed, d_mixed, lse, key_tags, query_tags, n1_turned, weights, gain, out_kept, out_came, down_part, up_part,
    start, d_middle, outputs, row_count,
):
    tokens = qkv.shape[0]
    width = n1_turned.shape[0]
    own_tokens = tokens // CORES
    lanes = 2 * HDIM
    pairs = qkv.shape[1] // (3 * lanes)
    n_seq = 2 * row_count
    tile = 256
    sub = own_tokens // n_seq
    streams = streams_of(down_part.shape[0] * 2 // n_seq, width, pairs)
    last = pairs - 1
    now = lambda i: jnp.minimum(i, last)
    before = lambda i: jnp.clip(i - 1, 0, last)
    fixed = lambda shape: pl.BlockSpec(shape, lambda i: (0,) * len(shape), pipeline_mode=pl.Buffered(1))

    def columns(place):
        return pl.BlockSpec((tokens, lanes), lambda i: (0, 3 * now(i) + place))

    pair = pl.BlockSpec((tokens, lanes), lambda i: (0, now(i)))
    weight = pl.BlockSpec((width, 3 * lanes), lambda i: (0, before(i)))
    hbm = pl.BlockSpec(memory_space=pl.ANY)

    def piece(value, place):
        parts = (value.shape[0] // (2 * place), 2, place, value.shape[1] // pairs)
        whole = value.reshape(parts[:3] + value.shape[1:])
        return whole, pl.BlockSpec(parts, lambda i: (0, 0, 0, now(i)))

    outs = [piece(value, width // 16) for value in (out_kept, out_came)]
    down = piece(down_part, streams[1].rows)
    up = piece(up_part, streams[2].rows)
    count = len(streams)
    deepest = max(len(stream.levels) for stream in streams)
    return pl.pallas_call(
        functools.partial(back_kernel, pairs, tile, streams, row_count),
        grid=(pairs + deepest + 2,),
        in_specs=[
            fixed((tokens, 1)),
            fixed((1, tokens)),
            columns(0),
            columns(1),
            columns(2),
            pair,
            pair,
            pl.BlockSpec((None, 2, tokens), lambda i: (now(i), 0, 0)),
            fixed((width, tokens)),
            weight,
            weight,
            fixed((1, width)),
            outs[0][1],
            outs[1][1],
            down[1],
            up[1],
            hbm,
            hbm,
            hbm,
        ],
        out_specs=[hbm] * 5,
        out_shape=[jax.ShapeDtypeStruct((row_count, CORES, sub, width), bf16)] * 2
        + [jax.ShapeDtypeStruct((pairs, CORES, 2, stream.rows, stream.columns), bf16) for stream in streams],
        scratch_shapes=[
            pltpu.VMEM((lanes, tokens), bf16),
            pltpu.VMEM((lanes, tokens), f32),
            pltpu.VMEM((2, tokens), f32),
            pltpu.VMEM((2, tokens, 3 * lanes), bf16),
            pltpu.VMEM((2, own_tokens, 3 * lanes), bf16),
            pltpu.VMEM((own_tokens, width), f32),
            pltpu.VMEM((n_seq, sub, width), bf16),
            pltpu.VMEM((2, sub, width), bf16),
            pltpu.VMEM((2, sub, width), f32),
        ]
        + [shape for stream in streams for shape in stream.scratch()]
        + [pltpu.VMEM((pairs, 2, stream.rows, stream.columns), bf16) for stream in streams]
        + [
            pltpu.SemaphoreType.DMA((count, deepest)),
            pltpu.SemaphoreType.DMA((count, deepest, 2)),
            pltpu.SemaphoreType.DMA((count,)),
            pltpu.SemaphoreType.DMA((count, 2)),
            pltpu.SemaphoreType.DMA((count,)),
            pltpu.SemaphoreType.DMA((count, 2)),
            pltpu.SemaphoreType.DMA((count,)),
            pltpu.SemaphoreType.DMA((2,)),
            pltpu.SemaphoreType.DMA((2,)),
            pltpu.SemaphoreType.DMA((n_seq,)),
            pltpu.SemaphoreType.DMA((row_count, CORES)),
            pltpu.SemaphoreType.DMA,
            pltpu.SemaphoreType.DMA((2, 2)),
            pltpu.SemaphoreType.DMA((n_seq,)),
            pltpu.SemaphoreType.DMA((row_count, CORES)),
            pltpu.SemaphoreType.DMA,
        ],
        compiler_params=pltpu.CompilerParams(
            vmem_limit_bytes=feed_vmem_bytes, collective_id=2, has_side_effects=True
        ),
        cost_estimate=pl.CostEstimate(
            flops=80 * pairs * tokens * tokens * HDIM,
            bytes_accessed=16 * tokens * pairs * lanes,
            transcendentals=2 * pairs * tokens * tokens,
        ),
        name="back",
    )(
        key_tags, query_tags, qkv, qkv, qkv, mixed, d_mixed, lse, n1_turned, weights[0], weights[1],
        gain.reshape(1, width), outs[0][0], outs[1][0], down[0], up[0], start, d_middle, outputs,
    )


def collect_kernel(pairs, seq_ref, *refs):
    qkv_parts, down_parts, up_parts = refs[:3]
    qkv_weights, up_weight, first_gain, second_gain = refs[3:9], refs[9], refs[10], refs[11]
    qkv_out, out_out, down_out, up_out, first_out, second_out = refs[12:]
    item = pl.program_id(0)
    lanes = 2 * HDIM
    rows = qkv_parts.shape[2]
    width = out_out.shape[1]
    half = width // CORES
    tile = feed_tile // CORES

    @pl.when(item == 0)
    def _():
        first_out[...] = jnp.zeros_like(first_out)
        second_out[...] = jnp.zeros_like(second_out)

    for core in range(CORES):
        place = pl.multiple_of(core * half + item * lanes, lanes)
        for high in range(2):
            own = slice(high * rows, (high + 1) * rows)
            part = qkv_parts[core, high].astype(f32)
            for kind in range(3):
                value = part[:, kind * lanes : (kind + 1) * lanes]
                qkv_out[own, pl.ds(kind * width + place, lanes)] = value
                weight = qkv_weights[kind * CORES + core][own, :].astype(f32)
                first_out[own, :] += jnp.sum(value * weight, axis=1, keepdims=True)
            out_out[own, pl.ds(place, lanes)] = part[:, 3 * lanes :]
            part = up_parts[core, high].astype(f32)
            for at in range(part.shape[1] // tile):
                value = part[:, at * tile : (at + 1) * tile]
                columns = slice(at * feed_tile + core * tile, at * feed_tile + (core + 1) * tile)
                up_out[own, columns] = value
                second_out[own, :] += jnp.sum(value * up_weight[own, columns].astype(f32), axis=1, keepdims=True)
            part = down_parts[core, high].astype(f32)
            for at in range(part.shape[0] // piece_rows):
                start = (2 * at + high) * piece_rows
                down_out[start : start + piece_rows, pl.ds(place, lanes)] = part[at * piece_rows : (at + 1) * piece_rows]

    @pl.when(item == pairs - 1)
    def _():
        first_out[...] = first_out[...] / first_gain[...]
        second_out[...] = second_out[...] / second_gain[...]


def collect(seq_at, qkv_parts, down_parts, up_parts, qkv_weight, up_weight, first_gain, second_gain):
    pairs, _, _, rows, _ = qkv_parts.shape
    width, lanes = qkv_weight.shape[0], 2 * HDIM
    shard, wide = 2 * rows, up_weight.shape[1]
    down_rows = 2 * down_parts.shape[3]

    def parts(value):
        return pl.BlockSpec((None,) + value.shape[1:], lambda i, seq: (i, 0, 0, 0, 0))

    def weight(kind, core):
        return pl.BlockSpec((shard, lanes), lambda i, seq: (seq[0], (kind * CORES + core) * pairs + i))

    gain = pl.BlockSpec((shard, 1), lambda i, seq: (seq[0], 0))
    whole = lambda shape: pl.BlockSpec(shape, lambda i, seq: (0, 0))
    return pl.pallas_call(
        functools.partial(collect_kernel, pairs),
        grid_spec=pltpu.PrefetchScalarGridSpec(
            num_scalar_prefetch=1,
            grid=(pairs,),
            in_specs=[parts(qkv_parts), parts(down_parts), parts(up_parts)]
            + [weight(kind, core) for kind in range(3) for core in range(CORES)]
            + [pl.BlockSpec((shard, wide // pairs), lambda i, seq: (seq[0], i)), gain, gain],
            out_specs=[
                whole((shard, 3 * width)),
                whole((shard, width)),
                whole((down_rows, width)),
                pl.BlockSpec((shard, wide // pairs), lambda i, seq: (0, i)),
                whole((shard, 1)),
                whole((shard, 1)),
            ],
        ),
        out_shape=[
            jax.ShapeDtypeStruct((shard, 3 * width), f32),
            jax.ShapeDtypeStruct((shard, width), f32),
            jax.ShapeDtypeStruct((down_rows, width), f32),
            jax.ShapeDtypeStruct((shard, wide), f32),
            jax.ShapeDtypeStruct((shard, 1), f32),
            jax.ShapeDtypeStruct((shard, 1), f32),
        ],
        compiler_params=pltpu.CompilerParams(vmem_limit_bytes=vmem_bytes),
        name="collect",
    )(
        seq_at.reshape(1), qkv_parts, down_parts, up_parts, *[qkv_weight] * 6, up_weight,
        first_gain.reshape(width, 1), second_gain.reshape(width, 1),
    )


def add_split_kernel(has_two, bit_ref, *refs):
    ins, outs = refs[: 2 if has_two else 1], refs[2 if has_two else 1 :]
    value = ins[0][...]
    if has_two:
        value = (value.astype(f32) + ins[1][...].astype(f32)).astype(bf16)
    if len(outs) == 1:
        outs[0][...] = value
    else:
        sends = pl.program_id(0) == 0

        @pl.when(sends)
        def _():
            outs[0][...] = value

        @pl.when(jnp.logical_not(sends))
        def _():
            outs[1][...] = value


def add_split(kept, received, inner, bit):
    rows, columns = kept.shape
    values = [kept] if received is None else [kept, received.reshape(rows, columns)]
    if bit is None:
        if received is None:
            return None, kept
        count = 4 if rows % 64 == 0 else 1
        block = pl.BlockSpec((rows // count, columns), lambda i, bit: (i, 0))
        grid, ins, outs = (count,), [block] * 2, block
        shapes = jax.ShapeDtypeStruct((rows, columns), bf16)
        bit = jnp.zeros((), jnp.int32)
    else:
        outer = rows // (2 * inner)
        cut = 1
        while inner // cut * columns > 2**19 and inner % (32 * cut) == 0:
            cut *= 2
        values = [value.reshape(outer, 2, inner, columns) for value in values]
        ins = [
            pl.BlockSpec(
                (None, None, inner // cut, columns),
                lambda w, i, j, bit: (i, jnp.where(w == 0, 1 - bit[0], bit[0]), j, 0),
            )
        ] * len(values)
        outs = [
            pl.BlockSpec(
                (None, inner // cut, columns),
                lambda w, i, j, bit: (jnp.where(w == 0, i, outer - 1), jnp.where(w == 0, j, cut - 1), 0),
            ),
            pl.BlockSpec(
                (None, inner // cut, columns),
                lambda w, i, j, bit: (jnp.where(w == 0, 0, i), jnp.where(w == 0, 0, j), 0),
            ),
        ]
        grid = (2, outer, cut)
        shapes = [jax.ShapeDtypeStruct((outer, inner, columns), bf16)] * 2
    done = pl.pallas_call(
        functools.partial(add_split_kernel, len(values) == 2),
        grid_spec=pltpu.PrefetchScalarGridSpec(
            num_scalar_prefetch=1, grid=grid, in_specs=ins, out_specs=outs
        ),
        out_shape=shapes,
        cost_estimate=pl.CostEstimate(flops=rows * columns, bytes_accessed=6 * rows * columns, transcendentals=0),
        name="add_split",
    )(bit.reshape(1), *values)
    if not isinstance(done, (list, tuple)):
        return None, done
    return done[0].reshape(rows // 2, columns), done[1].reshape(rows // 2, columns)


def tie(*values):
    return lax.optimization_barrier(values)


def build(n_seq, n_rows):
    highs = n_rows // CORES
    seq_bits = n_seq.bit_length() - 1
    high_bits = highs.bit_length() - 1
    bits = seq_bits + high_bits

    def permute(value, target):
        pairs = []
        for s in range(n_seq):
            for r in range(n_rows):
                to_s, to_r = target(s, r)
                pairs.append((s * n_rows + r, to_s * n_rows + to_r))
        return lax.ppermute(value, AXES, pairs)

    def other_core(value):
        return permute(value, lambda s, r: (s, r ^ 1))

    def pick(value, place, axis):
        return lax.dynamic_index_in_dim(value, place, axis, keepdims=False)

    def bit_of(step):
        name, bit = step
        return (lax.axis_index(name) >> bit) & 1

    def across(value, step):
        name, bit = step
        if name == "rows":
            return permute(value, lambda s, r: (s, r ^ (1 << bit)))
        return permute(value, lambda s, r: (s ^ (1 << bit), r))

    high_steps = [("rows", bit + 1) for bit in reversed(range(high_bits))]
    seq_steps = [("seq", bit) for bit in range(seq_bits)]

    class Sum:
        def __init__(self, kept, received, order):
            self.rows, self.columns = kept.shape
            self.kept, self.received = kept, received
            self.left = [step for step in seq_steps[::-1] + high_steps if step in order]
            self.order = list(order)

        def finish(self):
            step = self.order[0] if self.order else None
            inner = self.rows
            if step is not None:
                axis = self.left.index(step)
                inner = self.rows >> (axis + 1)
            self.sent, self.kept = add_split(self.kept, self.received, inner, step and bit_of(step))
            self.received = None

        def begin(self):
            step = self.order.pop(0)
            self.left.remove(step)
            self.rows //= 2
            self.received = across(self.sent, step)

        def finished(self):
            while self.order:
                self.finish()
                self.begin()
            self.finish()
            return self.kept

    rows_first = high_steps + seq_steps[1:2] + seq_steps[:1] + seq_steps[2:]
    down_order = [step for step in seq_steps + high_steps if step != ("rows", 1)]
    up_order = [step for step in high_steps + seq_steps if step != ("seq", 0)]

    def gather_high(value, pieces=0):
        for step in high_steps[::-1]:
            if pieces and step == ("rows", 1):
                continue
            received = across(value, step)
            value = jnp.where(
                bit_of(step) == 0,
                jnp.concatenate([value, received], 0),
                jnp.concatenate([received, value], 0),
            )
        if pieces:
            value = value.reshape(-1, 1, pieces, value.shape[1])
            received = across(value, ("rows", 1))
            value = jnp.where(
                bit_of(("rows", 1)) == 0,
                jnp.concatenate([value, received], 1),
                jnp.concatenate([received, value], 1),
            )
            value = value.reshape(-1, value.shape[-1])
        return value

    def back_by_steps(
        qkv, mixed, d_mixed, lse, key_tags, query_tags, n1_all, qkv_parts, attention_gain,
        out_kept, out_received, down_part, up_part, start, d_middle, to_member, ordered, from_rows, sizes,
    ):
        group, member, core, pairs, group_width, tokens, width = sizes
        lanes, half = 2 * HDIM, width // CORES
        unit1, scale1 = norm_parts(start)
        down = Sum(down_part, None, down_order)
        up = Sum(up_part, None, up_order)
        out = Sum(out_kept, out_received, rows_first)

        def before_next(*sums):
            nonlocal d_mixed
            for each in sums:
                each.finish()
            values = tie(d_mixed, *[v for each in sums for v in (each.sent, each.kept)])
            d_mixed = values[0]
            for at, each in enumerate(sums):
                each.sent, each.kept = values[1 + 2 * at : 3 + 2 * at]
                each.begin()

        def back_at(at):
            return attend_back(qkv, mixed, d_mixed, lse, key_tags, query_tags, at, 1)

        cut = max(1, 3 * pairs // 5)
        before_next(down, up)
        d_qkv, qkv_sums, d_parts = [], [], [[] for _ in range(group)]

        def take_piece(pieces):
            piece = jnp.concatenate(pieces, axis=1)
            d_parts[0].append(piece[:tokens])
            for hop in range(1, group):
                d_parts[hop].append(to_member(piece[hop * tokens : (hop + 1) * tokens], group - hop))
            return dot(n1_all, piece, 0, 0)

        grads = []
        for at in range(pairs):
            d_qkv.append(back_at(at))
            d_mixed, d_qkv[at] = tie(d_mixed, d_qkv[at])
            if at + 1 == cut:
                grads.append(take_piece(d_qkv))
            if at == min(0, pairs - 1):
                before_next(out)
            if at == min(1, pairs - 1):
                before_next(down, up)
            if at == min(3, pairs - 1):
                before_next(down, up, out)
        if pairs > cut:
            grads.append(take_piece(d_qkv[cut:]))
        if group == CORES:
            qkv_sums = [Sum(grad.astype(bf16), None, rows_first) for grad in grads]
        else:
            grad = jnp.concatenate(grads, 1)
            grad = grad.reshape(width, pairs, 3, lanes).transpose(0, 2, 1, 3)
            grad = grad.reshape(width, 3, 1, pairs * lanes)[..., :group_width]
            grad = lax.dynamic_update_slice_in_dim(
                jnp.zeros((width, 3, group, group_width), f32), grad, member, 2
            ).reshape(width, 3, CORES, half)
            kept = pick(grad, core, 2).astype(bf16).reshape(width, 3 * half)
            sent = pick(grad, 1 - core, 2).astype(bf16).reshape(width, 3 * half)
            qkv_sums = [Sum(kept, other_core(sent), rows_first)]

        d_n1 = jnp.zeros((tokens, width), f32)
        for part, weight in zip(d_parts, qkv_parts):
            d_n1 = d_n1 + dot(jnp.concatenate(part, 1), weight, 1, 1)
        input_grad = d_middle + norm_back(d_n1, attention_gain, unit1, scale1)
        input_grad = from_rows(input_grad.astype(bf16))

        down_total = gather_high(down.finished(), piece_rows)
        down_total = ordered(down_total, other_core(down_total), 1).astype(f32)
        tile = feed_tile // CORES
        up_total = gather_high(up.finished()).reshape(width // n_seq, -1, 1, tile)
        up_total = ordered(up_total, other_core(up_total), 2).reshape(width // n_seq, -1).astype(f32)
        out_total = gather_high(out.finished())
        out_total = ordered(out_total, other_core(out_total), 1).astype(f32)
        qkv_part = gather_high(jnp.concatenate([each.finished() for each in qkv_sums], 1))
        if group == CORES:
            qkv_part = qkv_part.reshape(-1, pairs, 3, lanes).transpose(0, 2, 1, 3)
        qkv_part = qkv_part.reshape(-1, 3, half)
        qkv_total = ordered(qkv_part[:, :, None], other_core(qkv_part)[:, :, None], 2)
        qkv_total = qkv_total.reshape(-1, 3 * width).astype(f32)

        return input_grad, qkv_total, out_total, down_total, up_total

    def per_device(
        inputs, cell_ids, valid_counts, cotangent, attention_gain, qkv_weight, out_weight, feed_gain, up_weight, down_weight
    ):
        row_count, block, width = inputs.shape
        seq_len = cell_ids.shape[1]
        heads = width // HDIM
        lanes = 2 * HDIM
        seq_at, rows_at = lax.axis_index("seq"), lax.axis_index("rows")
        core = rows_at % CORES
        chips = n_seq // (CORES * row_count)
        group = chips * CORES
        sub = block // group
        tokens = n_seq * sub
        member = (seq_at % chips) * CORES + core
        group_heads = heads // group
        pairs = -(-group_heads // 2)
        group_width = group_heads * HDIM
        padded = pairs * lanes - group_width

        def to_member(value, hop):
            def target(s, r):
                place = ((s % chips) * CORES + r % CORES + hop) % group
                return (s // chips * chips + place // CORES, r // CORES * CORES + place % CORES)

            return permute(value, target)

        def ordered(own, received, axis):
            return jnp.where(
                core == 0,
                jnp.concatenate([own, received], axis),
                jnp.concatenate([received, own], axis),
            )

        def to_rows(value):
            halves = value.reshape(row_count, CORES, block // CORES, width)
            received = other_core(pick(halves, 1 - core, 1))
            both = ordered(pick(halves, core, 1), received, 0).reshape(n_seq, sub, width)
            return lax.all_to_all(both, "seq", 0, 0, tiled=True).reshape(tokens, width)

        def from_rows(value):
            both = lax.all_to_all(value.reshape(n_seq, sub, width), "seq", 0, 0, tiled=True)
            both = both.reshape(CORES, row_count, block // CORES, width)
            received = other_core(pick(both, 1 - core, 0))
            own = pick(both, core, 0)
            return ordered(own[:, None], received[:, None], 1).reshape(row_count, block, width)

        places = jnp.arange(seq_len, dtype=jnp.int32)
        tags = jnp.where(places[None, :] < valid_counts[:, None], cell_ids, -1 - places[None, :])
        tags = ordered(tags, other_core(tags), 0)
        tags = pick(tags, seq_at // chips, 0).reshape(n_seq, CORES, chips, sub)
        tags = tags.transpose(2, 1, 0, 3).reshape(group, tokens)
        order = (member - jnp.arange(group, dtype=jnp.int32)) % group
        tags = jnp.take(tags, order, axis=0).reshape(1, seq_len)
        query_tags, key_tags = tags, tags.reshape(seq_len, 1)

        def pad_heads(value, axis):
            if not padded:
                return value
            fill = [(0, 0)] * value.ndim
            fill[axis] = (0, padded)
            return jnp.pad(value, fill)

        def qkv_of(hop):
            if group == CORES:
                return gather_pairs(((core + hop) % CORES).reshape(1), qkv_weight)
            piece = pick(qkv_weight.reshape(width, 3, group, group_width), (member + hop) % group, 2)
            piece = pad_heads(piece, 2).reshape(width, 3, pairs, lanes)
            return piece.transpose(0, 2, 1, 3).reshape(width, 3 * pairs * lanes)

        def out_of(hop):
            at = (member + hop) % group * group_width
            return pad_heads(lax.dynamic_slice_in_dim(out_weight, at, group_width, 0), 0)

        start = to_rows(inputs)
        qkv_parts = [qkv_of(hop) for hop in range(group)]
        out_parts = [out_of(hop) for hop in range(group)]
        start_low = start
        start = start.astype(f32)
        unit1, scale1 = norm_parts(start)
        n1 = (unit1 * attention_gain).astype(bf16)
        n1_all = jnp.concatenate([n1] + [to_member(n1, hop) for hop in range(1, group)], 0)
        cotangent, _ = tie(cotangent, start[:1])
        cot = to_rows(cotangent)
        qkv = dot(n1_all, qkv_parts[0], 1, 0).astype(bf16)
        mixed, lse = attend(qkv, key_tags, query_tags)
        mixed_parts = [mixed[:tokens]] + [
            to_member(mixed[hop * tokens : (hop + 1) * tokens], group - hop) for hop in range(1, group)
        ]
        middle = start
        for part, weight in zip(mixed_parts, out_parts):
            middle = middle + dot(part, weight, 1, 0)
        outputs, d_middle, d_attn, down_part, up_part = feed(middle, cot, feed_gain, up_weight, down_weight, n_seq)

        d_attn_all = jnp.concatenate([d_attn] + [to_member(d_attn, hop) for hop in range(1, group)], 0)


        half = width // CORES
        if group == CORES:
            mixed_own = ordered(mixed_parts[0], mixed_parts[1], 1)
        else:
            slots = jnp.stack([part[:, :group_width] for part in mixed_parts])
            turn = (jnp.arange(group, dtype=jnp.int32) - member) % group
            mixed_own = jnp.take(slots, turn, axis=0).transpose(1, 0, 2).reshape(tokens, width)
        out_grad = dot(mixed_own, d_attn, 0, 0).astype(bf16)
        out_kept = lax.dynamic_slice_in_dim(out_grad, core * half, half, 1)
        out_received = other_core(lax.dynamic_slice_in_dim(out_grad, (1 - core) * half, half, 1))
        d_mixed = dot(d_attn_all, out_parts[0], 1, 1).astype(bf16)

        if chips == 1 and highs == 2:
            input_grad, out_low, qkv_out, down_all, up_all = back(
                qkv, mixed, d_mixed, lse, key_tags, query_tags, n1_all.T, qkv_parts, attention_gain,
                out_kept, out_received, down_part, up_part, start_low, d_middle, outputs, row_count,
            )
            qkv_total, out_total, down_total, up_total, first, second = collect(
                seq_at, qkv_out, down_all, up_all, qkv_weight, up_weight, attention_gain, feed_gain
            )
            return (
                out_low.reshape(inputs.shape),
                input_grad.reshape(inputs.shape),
                first.reshape(-1),
                qkv_total,
                out_total,
                second.reshape(-1),
                up_total,
                down_total,
            )
        out_low = from_rows(outputs)
        input_grad, qkv_total, out_total, down_total, up_total = back_by_steps(
            qkv, mixed, d_mixed, lse, key_tags, query_tags, n1_all, qkv_parts, attention_gain,
            out_kept, out_received, down_part, up_part, start, d_middle, to_member, ordered, from_rows,
            (group, member, core, pairs, group_width, tokens, width),
        )

        shard = width // n_seq

        def gain_total(weight, total, gain):
            rows = lax.dynamic_slice_in_dim(weight, seq_at * shard, shard, 0).astype(f32)
            return jnp.sum(rows * total, axis=1) / lax.dynamic_slice_in_dim(gain, seq_at * shard, shard, 0)

        return (
            out_low,
            input_grad,
            gain_total(qkv_weight, qkv_total, attention_gain),
            qkv_total,
            out_total,
            gain_total(up_weight, up_total, feed_gain),
            up_total,
            down_total,
        )

    return per_device


def solution(mesh):
    placed = (
        P("rows", "seq", None),
        P("rows", None),
        P("rows"),
        P("rows", "seq", None),
        P(),
        P(),
        P(),
        P(),
        P(),
        P(),
    )
    return jax.shard_map(
        build(mesh.shape["seq"], mesh.shape["rows"]),
        mesh=mesh,
        in_specs=placed,
        out_specs=(
            P("rows", "seq", None),
            P("rows", "seq", None),
            P("seq"),
            P("seq", None),
            P("seq", None),
            P("seq"),
            P("seq", None),
            P("seq", None),
        ),
        check_vma=False,
    )
```

```python
import functools

import jax
import jax.numpy as jnp
from jax import lax
from jax.experimental import pallas as pl
from jax.experimental.pallas import tpu as pltpu
from jax.sharding import PartitionSpec as P

HDIM = 64
CORES = 2
epsilon = 1e-05
masked_score = -1e30
score_scale = HDIM ** (-0.5)
log2e = 1.4426950408889634
bf16 = jnp.bfloat16
f32 = jnp.float32
AXES = ("seq", "rows")
vmem_bytes = 60 * 2**20
feed_vmem_bytes = 62 * 2**20
feed_tile = 512
max_cells = 7
MESH = pl.DeviceIdType.MESH


def dot(a, b, ca, cb):
    return lax.dot_general(a, b, (((ca,), (cb,)), ((), ())), preferred_element_type=f32)


def attend_kernel(tile, key_tags, query_tags, q_ref, k_ref, v_ref, o_ref, lse_ref, v_turned):
    tokens = q_ref.shape[0]
    v_turned[...] = v_ref[...].T
    lane = lax.broadcasted_iota(jnp.int32, (tile, 2 * HDIM), 1)

    def body(step, _):
        part = pl.ds(pl.multiple_of(step * tile, tile), tile)
        q = q_ref[part, :]
        allowed = key_tags[...] == query_tags[:, part]
        pieces = []
        for head in range(2):
            own = jnp.where((lane // HDIM) == head, q, bf16(0))
            scores = dot(k_ref[...], own, 1, 1)
            scores = jnp.where(allowed, scores, masked_score)
            peak = jnp.max(scores, axis=0, keepdims=True)
            powers = jnp.exp2((scores - peak) * (score_scale * log2e))
            total = jnp.sum(powers, axis=0, keepdims=True)
            mixed = dot(v_turned[head * HDIM : (head + 1) * HDIM, :], powers.astype(bf16), 1, 0)
            pieces.append(mixed * (1.0 / total))
            lse_ref[head : head + 1, part] = peak * (score_scale * log2e) + jnp.log2(total)
        o_ref[part, :] = jnp.concatenate(pieces, axis=0).T.astype(bf16)
        return 0

    lax.fori_loop(0, tokens // tile, body, 0)


def attend(qkv, key_tags, query_tags):
    tokens, width = qkv.shape
    lanes = 2 * HDIM
    pairs = width // (3 * lanes)
    tile = min(512, tokens)

    def columns(place):
        return pl.BlockSpec((tokens, lanes), lambda i: (0, 3 * i + place))

    return pl.pallas_call(
        functools.partial(attend_kernel, tile),
        grid=(pairs,),
        in_specs=[
            pl.BlockSpec((tokens, 1), lambda i: (0, 0)),
            pl.BlockSpec((1, tokens), lambda i: (0, 0)),
            columns(0),
            columns(1),
            columns(2),
        ],
        out_specs=[
            pl.BlockSpec((tokens, lanes), lambda i: (0, i)),
            pl.BlockSpec((None, 2, tokens), lambda i: (i, 0, 0)),
        ],
        out_shape=[
            jax.ShapeDtypeStruct((tokens, pairs * lanes), bf16),
            jax.ShapeDtypeStruct((pairs, 2, tokens), f32),
        ],
        scratch_shapes=[pltpu.VMEM((lanes, tokens), bf16)],
        compiler_params=pltpu.CompilerParams(vmem_limit_bytes=vmem_bytes),
        cost_estimate=pl.CostEstimate(
            flops=32 * pairs * tokens * tokens * HDIM,
            bytes_accessed=8 * tokens * pairs * lanes,
            transcendentals=2 * pairs * tokens * tokens,
        ),
        name="attend",
    )(key_tags, query_tags, qkv, qkv, qkv)


def attend_back_kernel(
    tile, key_tags, query_tags, q_ref, k_ref, v_ref, o_ref, do_ref, lse_ref, grad_ref, k_turned, dq_turned, delta
):
    tokens = q_ref.shape[0]
    lanes = 2 * HDIM
    k_turned[...] = k_ref[...].T
    dq_turned[...] = (o_ref[...].astype(f32) * do_ref[...].astype(f32)).T
    for head in range(2):
        rows = dq_turned[head * HDIM : (head + 1) * HDIM, :]
        delta[head : head + 1, :] = jnp.sum(rows, axis=0, keepdims=True)
    dq_turned[...] = jnp.zeros_like(dq_turned)
    first = lax.broadcasted_iota(jnp.int32, (tile, lanes), 1) < HDIM

    def body(step, _):
        part = pl.ds(pl.multiple_of(step * tile, tile), tile)
        k, v = k_ref[part, :], v_ref[part, :]
        q, do = q_ref[...], do_ref[...]
        allowed = key_tags[part, :] == query_tags[...]
        dk, dv = [], []
        for head in range(2):
            own = first if head == 0 else jnp.logical_not(first)
            own_rows = slice(head * HDIM, (head + 1) * HDIM)
            scores = dot(jnp.where(own, k, bf16(0)), q, 1, 1)
            scores = jnp.where(allowed, scores, masked_score)
            chances = jnp.exp2(scores * (score_scale * log2e) - lse_ref[head : head + 1, :])
            weight_grad = dot(jnp.where(own, v, bf16(0)), do, 1, 1)
            score_grad = (chances * (weight_grad - delta[head : head + 1, :])).astype(bf16)
            dv.append(dot(chances.astype(bf16), do, 1, 0))
            dk.append(dot(score_grad, q, 1, 0))
            dq_turned[own_rows, :] += dot(k_turned[own_rows, part], score_grad, 1, 0)
        grad_ref[part, lanes : 2 * lanes] = (jnp.where(first, dk[0], dk[1]) * score_scale).astype(bf16)
        grad_ref[part, 2 * lanes :] = jnp.where(first, dv[0], dv[1]).astype(bf16)
        return 0

    lax.fori_loop(0, tokens // tile, body, 0)
    grad_ref[:, :lanes] = (dq_turned[...] * score_scale).T.astype(bf16)


def attend_back(qkv, mixed, d_mixed, lse, key_tags, query_tags, start, count):
    tokens = qkv.shape[0]
    tile = min(512, tokens)
    lanes = 2 * HDIM

    def columns(place):
        return pl.BlockSpec((tokens, lanes), lambda i: (0, 3 * (start + i) + place))

    pair = pl.BlockSpec((tokens, lanes), lambda i: (0, start + i))
    return pl.pallas_call(
        functools.partial(attend_back_kernel, tile),
        grid=(count,),
        in_specs=[
            pl.BlockSpec((tokens, 1), lambda i: (0, 0)),
            pl.BlockSpec((1, tokens), lambda i: (0, 0)),
            columns(0),
            columns(1),
            columns(2),
            pair,
            pair,
            pl.BlockSpec((None, 2, tokens), lambda i: (start + i, 0, 0)),
        ],
        out_specs=pl.BlockSpec((tokens, 3 * lanes), lambda i: (0, i)),
        out_shape=jax.ShapeDtypeStruct((tokens, 3 * count * lanes), bf16),
        scratch_shapes=[
            pltpu.VMEM((lanes, tokens), bf16),
            pltpu.VMEM((lanes, tokens), f32),
            pltpu.VMEM((2, tokens), f32),
        ],
        compiler_params=pltpu.CompilerParams(vmem_limit_bytes=vmem_bytes),
        cost_estimate=pl.CostEstimate(
            flops=80 * count * tokens * tokens * HDIM,
            bytes_accessed=16 * tokens * count * lanes,
            transcendentals=2 * count * tokens * tokens,
        ),
        name="attend_back",
    )(key_tags, query_tags, qkv, qkv, qkv, mixed, d_mixed, lse)


def copy_kernel(core_ref, from_ref, to_ref):
    to_ref[...] = from_ref[...]


def gather_pairs(core, qkv_weight):
    width, lanes = qkv_weight.shape[0], 2 * HDIM
    pairs = width // (CORES * lanes)
    return pl.pallas_call(
        copy_kernel,
        grid_spec=pltpu.PrefetchScalarGridSpec(
            num_scalar_prefetch=1,
            grid=(pairs, 3),
            in_specs=[
                pl.BlockSpec((width, lanes), lambda i, j, core: (0, (j * CORES + core[0]) * pairs + i))
            ],
            out_specs=pl.BlockSpec((width, lanes), lambda i, j, core: (0, 3 * i + j)),
        ),
        out_shape=jax.ShapeDtypeStruct((width, 3 * pairs * lanes), qkv_weight.dtype),
        cost_estimate=pl.CostEstimate(flops=0, bytes_accessed=12 * width * pairs * lanes, transcendentals=0),
        name="gather_pairs",
    )(core, qkv_weight)


def norm_parts(values):
    center = values - jnp.mean(values, axis=-1, keepdims=True)
    spread = jnp.mean(center * center, axis=-1, keepdims=True)
    scale = lax.rsqrt(spread + epsilon)
    return center * scale, scale


def norm_back(grad, gain, unit, scale):
    e = grad * gain
    return scale * (
        e - jnp.mean(e, axis=-1, keepdims=True) - unit * jnp.mean(e * unit, axis=-1, keepdims=True)
    )


def all_signal(n_seq, seq_at, rows_at, extra=()):
    core = rows_at % CORES
    barrier = pltpu.get_barrier_semaphore()
    for s in range(n_seq):
        for c in range(CORES):
            @pl.when(jnp.logical_not((seq_at == s) & (core == c)))
            def _():
                pl.semaphore_signal(barrier, inc=1, device_id=(s, rows_at - core + c), device_id_type=MESH)
    for peer in extra:
        pl.semaphore_signal(barrier, inc=1, device_id=peer, device_id_type=MESH)
    pl.semaphore_wait(barrier, n_seq * CORES - 1 + len(extra))


class ToRows:
    def __init__(self, source, target, send, recv, local, row_count, seq_at, rows_at):
        self.source, self.target, self.send, self.recv, self.local = source, target, send, recv, local
        self.row_count, self.seq_at, self.rows_at = row_count, seq_at, rows_at
        self.core = rows_at % CORES

    def copy(self, row, c):
        chip = self.core * self.row_count + row
        return pltpu.make_async_remote_copy(
            src_ref=self.source.at[row, c],
            dst_ref=self.target.at[self.seq_at],
            send_sem=self.send.at[row, c],
            recv_sem=self.recv.at[self.seq_at],
            device_id=(chip, self.rows_at - self.core + c),
            device_id_type=MESH,
        )

    def own(self, row, c):
        return pltpu.make_async_copy(self.source.at[row, c], self.target.at[self.seq_at], self.local)

    def each(self, own, other):
        for row_turn in range(self.row_count):
            for core_turn in range(CORES):
                row = (row_turn + self.seq_at) % self.row_count
                c = (core_turn + self.seq_at // self.row_count) % CORES
                here = (self.core * self.row_count + row == self.seq_at) & (self.core == c)

                @pl.when(here)
                def _():
                    own(row, c)

                @pl.when(jnp.logical_not(here))
                def _():
                    other(row, c)

    def start(self):
        self.each(lambda row, c: self.own(row, c).start(), lambda row, c: self.copy(row, c).start())

    def wait_block(self, s):
        here = (s == self.seq_at) & (self.seq_at // self.row_count == self.core)

        @pl.when(here)
        def _():
            self.own(0, 0).wait()

        @pl.when(jnp.logical_not(here))
        def _():
            pltpu.make_async_remote_copy(
                src_ref=self.source.at[0, 0],
                dst_ref=self.target.at[s],
                send_sem=self.send.at[0, 0],
                recv_sem=self.recv.at[s],
                device_id=(self.seq_at, self.rows_at + 1 - 2 * self.core),
                device_id_type=MESH,
            ).wait_recv()

    def wait_sends(self):
        self.each(lambda row, c: None, lambda row, c: self.copy(row, c).wait_send())


def begin_kernel(
    row_count, pairs, x_ref, weight_ref, gain_ref, x_out, n1_out, qkv_out, own_out, other_out,
    x_part, n1, qkv, weight, other_weight,
    x_send, x_recv, x_local, n1_send, n1_recv, weight_sems, out_sems, x_sems, qkv_sems, n1_sems,
):
    seq_at, rows_at = lax.axis_index("seq"), lax.axis_index("rows")
    core = rows_at % CORES
    n_seq, sub, width = x_part.shape
    lanes = 2 * HDIM
    tokens = n_seq * sub
    moves = ToRows(x_ref, x_part, x_send, x_recv, x_local, row_count, seq_at, rows_at)

    def weight_copies(item, which):
        pair, kind = item // 3, item % 3
        to = pl.ds(pl.multiple_of(item * lanes, lanes), lanes)

        def columns(c):
            return pl.ds(pl.multiple_of((kind * CORES + c) * pairs * lanes + pair * lanes, lanes), lanes)

        source = weight_ref.at[:, columns(1 - core if which else core)]
        return pltpu.make_async_copy(source, (weight, other_weight)[which].at[:, to], weight_sems.at[which, item])

    def each_weight(act, which):
        def body(item, _):
            act(weight_copies(item, which))
            return 0

        lax.fori_loop(0, 3 * pairs, body, 0)

    each_weight(lambda copy: copy.start(), 0)
    all_signal(n_seq, seq_at, rows_at)
    moves.start()
    each_weight(lambda copy: copy.start(), 1)
    each_weight(lambda copy: copy.wait(), 0)
    weights_out = (
        pltpu.make_async_copy(weight, own_out, out_sems.at[0]),
        pltpu.make_async_copy(other_weight, other_out, out_sems.at[1]),
    )
    weights_out[0].start()
    each_weight(lambda copy: copy.wait(), 1)
    weights_out[1].start()

    def block_of(place):
        near = (place % 2) * ((place + 1) // 2) + (1 - place % 2) * ((n_seq - place // 2) % n_seq)
        return (seq_at + near) % n_seq

    def rows_of(s, other):
        return pl.ds(pl.multiple_of(s * sub + other * tokens, sub), sub)

    def n1_copy(s):
        return pltpu.make_async_remote_copy(
            src_ref=n1.at[rows_of(s, 0)],
            dst_ref=n1.at[rows_of(s, 1)],
            send_sem=n1_send.at[s],
            recv_sem=n1_recv.at[s],
            device_id=(seq_at, rows_at + 1 - 2 * core),
            device_id_type=MESH,
        )

    def x_copy(s):
        return pltpu.make_async_copy(x_part.at[s], x_out.at[s], x_sems.at[s])

    def out_copies(s, other):
        rows = rows_of(s, other)
        return (
            pltpu.make_async_copy(qkv.at[rows], qkv_out.at[rows], qkv_sems.at[other, s]),
            pltpu.make_async_copy(n1.at[rows], n1_out.at[rows], n1_sems.at[other, s]),
        )

    def product(first, second, other):
        both = jnp.concatenate([n1[rows_of(first, other), :], n1[rows_of(second, other), :]], 0)
        found = dot(both, weight[...], 1, 0).astype(bf16)
        for at, s in enumerate((first, second)):
            qkv[rows_of(s, other), :] = found[at * sub : (at + 1) * sub]
            for copy in out_copies(s, other):
                copy.start()

    def body(group, _):
        @pl.when(group < n_seq // 2)
        def _():
            places = block_of(2 * group), block_of(2 * group + 1)
            for s in places:
                moves.wait_block(s)
                x_copy(s).start()
                unit, _s = norm_parts(x_part[s].astype(f32))
                n1[rows_of(s, 0), :] = (unit * gain_ref[...]).astype(bf16)
                n1_copy(s).start()
            product(*places, 0)

        @pl.when(group > 0)
        def _():
            places = block_of(2 * group - 2), block_of(2 * group - 1)
            for s in places:
                n1_copy(s).wait()
            product(*places, 1)

        return 0

    lax.fori_loop(0, n_seq // 2 + 1, body, 0)

    def finish(s, _):
        x_copy(s).wait()
        for other in range(2):
            for copy in out_copies(s, other):
                copy.wait()
        return 0

    lax.fori_loop(0, n_seq, finish, 0)
    moves.wait_sends()
    for copy in weights_out:
        copy.wait()


def begin(inputs, qkv_weight, gain):
    row_count, block, width = inputs.shape
    n_seq = CORES * row_count
    lanes = 2 * HDIM
    pairs = width // (CORES * lanes)
    sub = block // CORES
    tokens = n_seq * sub
    hbm = pl.BlockSpec(memory_space=pl.ANY)
    return pl.pallas_call(
        functools.partial(begin_kernel, row_count, pairs),
        in_specs=[hbm, hbm, pl.BlockSpec(memory_space=pltpu.VMEM)],
        out_specs=[hbm] * 5,
        out_shape=[
            jax.ShapeDtypeStruct((n_seq, sub, width), bf16),
            jax.ShapeDtypeStruct((CORES * tokens, width), bf16),
            jax.ShapeDtypeStruct((CORES * tokens, 3 * pairs * lanes), bf16),
            jax.ShapeDtypeStruct((width, 3 * pairs * lanes), bf16),
            jax.ShapeDtypeStruct((width, 3 * pairs * lanes), bf16),
        ],
        scratch_shapes=[
            pltpu.VMEM((n_seq, sub, width), bf16),
            pltpu.VMEM((CORES * tokens, width), bf16),
            pltpu.VMEM((CORES * tokens, 3 * pairs * lanes), bf16),
            pltpu.VMEM((width, 3 * pairs * lanes), bf16),
            pltpu.VMEM((width, 3 * pairs * lanes), bf16),
            pltpu.SemaphoreType.DMA((row_count, CORES)),
            pltpu.SemaphoreType.DMA((n_seq,)),
            pltpu.SemaphoreType.DMA,
            pltpu.SemaphoreType.DMA((n_seq,)),
            pltpu.SemaphoreType.DMA((n_seq,)),
            pltpu.SemaphoreType.DMA((2, 3 * pairs)),
            pltpu.SemaphoreType.DMA((2,)),
            pltpu.SemaphoreType.DMA((n_seq,)),
            pltpu.SemaphoreType.DMA((CORES, n_seq)),
            pltpu.SemaphoreType.DMA((CORES, n_seq)),
        ],
        compiler_params=pltpu.CompilerParams(
            vmem_limit_bytes=vmem_bytes, collective_id=3, has_side_effects=True
        ),
        name="begin",
    )(inputs.reshape(row_count, CORES, sub, width), qkv_weight, gain.reshape(1, width))


def with_cells(value, tags, head, is_key):
    lane = lax.broadcasted_iota(jnp.int32, value.shape, 1)
    cell = lane - (1 - head) * HDIM
    if is_key:
        marks = jnp.where((cell == tags) | (cell >= max_cells), 0.0, -1.0)
    else:
        marks = jnp.where(cell == tags, -masked_score, 0.0)
    return jnp.where((lane // HDIM) == head, value, marks.astype(bf16))


def attend_row_kernel(
    tile, row_count, tags, row_tags, q_ref, k_ref, v_ref, cot_ref, o_ref, lse_ref, cot_out, own_out,
    v_turned, keys, scores_ref, mixed_ref, parts,
    cot_send, cot_recv, cot_local, part_send, part_recv, part_local,
):
    item, last = pl.program_id(0), pl.num_programs(0) - 1
    seq_at, rows_at = lax.axis_index("seq"), lax.axis_index("rows")
    core = rows_at % CORES
    tokens, lanes = q_ref.shape
    own_tokens = tokens // CORES
    n_seq = cot_out.shape[0]
    moves = ToRows(cot_ref, cot_out, cot_send, cot_recv, cot_local, row_count, seq_at, rows_at)

    def part_copies(at):
        slot = at % 2
        half = pl.num_programs(0) * lanes
        columns = pl.ds(pl.multiple_of(core * half + at * lanes, lanes), lanes)
        return (
            pltpu.make_async_remote_copy(
                src_ref=parts.at[slot, pl.ds(own_tokens, own_tokens)],
                dst_ref=own_out.at[:, columns],
                send_sem=part_send.at[slot],
                recv_sem=part_recv.at[at],
                device_id=(seq_at, rows_at + 1 - 2 * core),
                device_id_type=MESH,
            ),
            pltpu.make_async_copy(parts.at[slot, pl.ds(0, own_tokens)], own_out.at[:, columns], part_local.at[slot]),
        )

    def part_came(at):
        half = pl.num_programs(0) * lanes
        columns = pl.ds(pl.multiple_of((1 - core) * half + at * lanes, lanes), lanes)
        return pltpu.make_async_remote_copy(
            src_ref=parts.at[0, pl.ds(own_tokens, own_tokens)],
            dst_ref=own_out.at[:, columns],
            send_sem=part_send.at[0],
            recv_sem=part_recv.at[at],
            device_id=(seq_at, rows_at + 1 - 2 * core),
            device_id_type=MESH,
        )

    @pl.when(item == 0)
    def _():
        all_signal(n_seq, seq_at, rows_at)
        moves.start()

    for head in range(2):
        keys[head] = with_cells(k_ref[...], tags[...], head, True)
        v_turned[head, :HDIM, :] = v_ref[...].T[head * HDIM : (head + 1) * HDIM, :]
        v_turned[head, HDIM:, :] = jnp.ones((16, tokens), bf16)

    def begin_scores(step, head):
        part = pl.ds(pl.multiple_of(step * tile, tile), tile)
        scores_ref[head] = dot(keys[head], with_cells(q_ref[part, :], tags[part, :], head, False), 1, 1)

    def finish(step, head):
        part = pl.ds(pl.multiple_of(step * tile, tile), tile)
        scores = scores_ref[head]
        peak = jnp.max(scores, axis=0, keepdims=True)
        powers = jnp.exp2((scores - peak) * (score_scale * log2e))
        mixed = dot(v_turned[head], powers.astype(bf16), 1, 0)
        total = mixed[HDIM : HDIM + 1, :]
        mixed_ref[head * HDIM : (head + 1) * HDIM, part] = mixed[:HDIM, :] * (1.0 / total)
        lse = peak * (score_scale * log2e) + jnp.log2(total)
        lse_ref[head : head + 1, part] = jnp.where(row_tags[:, part] < 0, -masked_score, lse)

    steps = tokens // tile
    begin_scores(0, 0)

    def body(step, _):
        begin_scores(step, 1)
        finish(step, 0)
        begin_scores(jnp.minimum(step + 1, steps - 1), 0)
        finish(step, 1)
        return 0

    lax.fori_loop(0, steps, body, 0)
    found = jnp.where(tags[...] < 0, v_ref[...], mixed_ref[...].T.astype(bf16))
    o_ref[...] = found

    @pl.when(item >= 2)
    def _():
        remote, local = part_copies(item - 2)
        remote.wait_send()
        local.wait()

    parts[item % 2] = found
    for copy in part_copies(item):
        copy.start()

    @pl.when(item == last)
    def _():
        for at in range(2):
            remote, local = part_copies(last - at)
            remote.wait_send()
            local.wait()
        for at in range(part_recv.shape[0]):
            part_came(at).wait_recv()
        for s in range(n_seq):
            moves.wait_block(s)
        moves.wait_sends()


def attend_row(qkv, tags, row_tags, cotangent):
    tokens, width = qkv.shape
    row_count, block, model = cotangent.shape
    lanes = 2 * HDIM
    pairs = width // (3 * lanes)
    tile = 512
    n_seq, sub = CORES * row_count, block // CORES
    hbm = pl.BlockSpec(memory_space=pl.ANY)

    def columns(place):
        return pl.BlockSpec((tokens, lanes), lambda i: (0, 3 * i + place))

    return pl.pallas_call(
        functools.partial(attend_row_kernel, tile, row_count),
        grid=(pairs,),
        in_specs=[
            pl.BlockSpec((tokens, 1), lambda i: (0, 0)),
            pl.BlockSpec((1, tokens), lambda i: (0, 0)),
            columns(0),
            columns(1),
            columns(2),
            hbm,
        ],
        out_specs=[
            pl.BlockSpec((tokens, lanes), lambda i: (0, i)),
            pl.BlockSpec((None, 2, tokens), lambda i: (i, 0, 0)),
            hbm,
            hbm,
        ],
        out_shape=[
            jax.ShapeDtypeStruct((tokens, pairs * lanes), bf16),
            jax.ShapeDtypeStruct((pairs, 2, tokens), f32),
            jax.ShapeDtypeStruct((n_seq, sub, model), bf16),
            jax.ShapeDtypeStruct((tokens // CORES, model), bf16),
        ],
        scratch_shapes=[
            pltpu.VMEM((2, HDIM + 16, tokens), bf16),
            pltpu.VMEM((2, tokens, lanes), bf16),
            pltpu.VMEM((2, tokens, tile), f32),
            pltpu.VMEM((lanes, tokens), f32),
            pltpu.VMEM((2, tokens, lanes), bf16),
            pltpu.SemaphoreType.DMA((row_count, CORES)),
            pltpu.SemaphoreType.DMA((n_seq,)),
            pltpu.SemaphoreType.DMA,
            pltpu.SemaphoreType.DMA((2,)),
            pltpu.SemaphoreType.DMA((pairs,)),
            pltpu.SemaphoreType.DMA((2,)),
        ],
        compiler_params=pltpu.CompilerParams(
            vmem_limit_bytes=vmem_bytes, collective_id=4, has_side_effects=True
        ),
        name="attend_row",
    )(tags, row_tags, qkv, qkv, qkv, cotangent.reshape(row_count, CORES, sub, model))


piece_rows = 16


def feed_kernel(
    tiles,
    rows,
    middle_ref,
    cot_ref,
    gain_ref,
    up_ref,
    down_ref,
    out_ref,
    d_middle_ref,
    d_attn_out,
    down_part,
    up_part,
    n2,
    n2_turned,
    total,
    d_attn,
    down_keep,
    down_send,
    down_recv,
    up_keep,
    up_send,
    up_recv,
    down_far_keep,
    down_far_send,
    down_far_recv,
    up_far_keep,
    up_far_send,
    up_far_recv,
    core_send_sem,
    core_recv_sem,
    far_send_sem,
    far_recv_sem,
    core_free,
    far_free,
    d_attn_sems,
):
    step = pl.program_id(0)
    tokens, width = n2.shape
    half = width // 2
    seq_at, rows_at = lax.axis_index("seq"), lax.axis_index("rows")
    core, high, low = rows_at % 2, (rows_at // 2) % 2, seq_at % 2
    core_peer = (seq_at, rows_at + 1 - 2 * core)
    far_peers = ((seq_at, rows_at + 2 - 4 * high), (seq_at + 1 - 2 * low, rows_at))

    def copies(slot, far):
        if far:
            refs = ((down_far_send, down_far_recv), (up_far_send, up_far_recv))
            sems, peers = (far_send_sem, far_recv_sem), far_peers
        else:
            refs = ((down_send, down_recv), (up_send, up_recv))
            sems, peers = (core_send_sem, core_recv_sem), (core_peer, core_peer)
        return [
            pltpu.make_async_remote_copy(
                src_ref=refs[kind][0].at[slot],
                dst_ref=refs[kind][1].at[slot],
                send_sem=sems[0].at[kind, slot],
                recv_sem=sems[1].at[kind, slot],
                device_id=peers[kind],
                device_id_type=MESH,
            )
            for kind in range(2)
        ]

    def signal(sem, peer):
        pl.semaphore_signal(sem, inc=1, device_id=peer, device_id_type=MESH)

    @pl.when(step == 0)
    def _():
        barrier = pltpu.get_barrier_semaphore()
        for peer in (core_peer,) + far_peers:
            signal(barrier, peer)
        pl.semaphore_wait(barrier, 3)

        def body(i, _):
            part = pl.ds(pl.multiple_of(i * rows, rows), rows)
            unit, _s = norm_parts(middle_ref[part, :])
            n2[part, :] = (unit * gain_ref[...]).astype(bf16)
            return 0

        lax.fori_loop(0, tokens // rows, body, 0)
        n2_turned[...] = n2[...].T
        total[...] = middle_ref[...]
        d_middle_ref[...] = jnp.zeros_like(d_middle_ref)

    @pl.when(step < tiles)
    def _():
        up_w, down_w = up_ref[...], down_ref[...]
        up = dot(n2[...], up_w, 1, 0)
        d_act = dot(cot_ref[...], down_w, 1, 1)
        share = 0.5 + 0.5 * lax.erf(up * (0.5**0.5))
        density = jnp.exp(-0.5 * up * up) * 0.3989422804014327
        act = (up * share).astype(bf16)
        d_up = (d_act * (share + up * density)).astype(bf16)
        total[...] += dot(act, down_w, 1, 0)
        d_middle_ref[...] += dot(d_up, up_w, 1, 1)
        slot = step % 2

        @pl.when(step >= 2)
        def _():
            for copy in copies(slot, False):
                copy.wait_send()

        up_grad = dot(n2_turned[...], d_up, 1, 0).astype(bf16)
        cut = up_grad.shape[1] // 2

        @pl.when(core == 0)
        def _():
            up_keep[slot] = up_grad[:, :cut].reshape(up_keep.shape[1:])
            up_send[slot] = up_grad[:, cut:].reshape(up_keep.shape[1:])

        @pl.when(core != 0)
        def _():
            up_keep[slot] = up_grad[:, cut:].reshape(up_keep.shape[1:])
            up_send[slot] = up_grad[:, :cut].reshape(up_keep.shape[1:])

        down_grad = dot(act, cot_ref[...], 0, 0).astype(bf16)

        @pl.when(core == 0)
        def _():
            down_keep[slot] = down_grad[:, :half].reshape(down_keep.shape[1:])
            down_send[slot] = down_grad[:, half:].reshape(down_keep.shape[1:])

        @pl.when(core != 0)
        def _():
            down_keep[slot] = down_grad[:, half:].reshape(down_keep.shape[1:])
            down_send[slot] = down_grad[:, :half].reshape(down_keep.shape[1:])

    def add(a, b):
        return (a.astype(f32) + b.astype(f32)).astype(bf16)

    def last_add():
        slot = step % 2
        for copy in copies(slot, True):
            copy.wait_recv()
        down_part[...] = add(down_far_keep[slot], down_far_recv[slot]).reshape(down_part.shape)
        up_part[...] = add(up_far_keep[slot], up_far_recv[slot]).reshape(up_part.shape)

        @pl.when(step < tiles)
        def _():
            signal(far_free.at[0], far_peers[0])
            signal(far_free.at[1], far_peers[1])

    def pass_on():
        slot = (step + 1) % 2
        for copy in copies(slot, False):
            copy.wait_recv()

        @pl.when(step >= 3)
        def _():
            for copy in copies(slot, True):
                copy.wait_send()
            pl.semaphore_wait(far_free.at[0], 1)
            pl.semaphore_wait(far_free.at[1], 1)

        down_far_send[slot] = add(down_keep[slot, :, 1 - high], down_recv[slot, :, 1 - high])
        down_far_keep[slot] = add(down_keep[slot, :, high], down_recv[slot, :, high])
        up_far_send[slot] = add(up_keep[slot, :, 1 - low], up_recv[slot, :, 1 - low])
        up_far_keep[slot] = add(up_keep[slot, :, low], up_recv[slot, :, low])
        for copy in copies(slot, True):
            copy.start()

        @pl.when(step < tiles - 1)
        def _():
            signal(core_free, core_peer)

    @pl.when((step >= 2) & (step <= tiles))
    def _():
        last_add()

    @pl.when((step >= 1) & (step <= tiles))
    def _():
        pass_on()

    @pl.when(step < tiles)
    def _():
        @pl.when(step >= 2)
        def _():
            pl.semaphore_wait(core_free, 1)

        for copy in copies(step % 2, False):
            copy.start()

    @pl.when(step == tiles)
    def _():
        def body(i, _):
            part = pl.ds(pl.multiple_of(i * rows, rows), rows)
            out_ref[part, :] = total[part, :].astype(bf16)
            unit, scale = norm_parts(middle_ref[part, :])
            grad = cot_ref[part, :].astype(f32) + norm_back(d_middle_ref[part, :], gain_ref[...], unit, scale)
            d_middle_ref[part, :] = grad
            d_attn[part, :] = grad.astype(bf16)
            return 0

        lax.fori_loop(0, tokens // rows, body, 0)

    d_attn_copies = lambda: (
        pltpu.make_async_copy(d_attn, d_attn_out.at[0], d_attn_sems.at[0]),
        pltpu.make_async_remote_copy(
            src_ref=d_attn,
            dst_ref=d_attn_out.at[1],
            send_sem=d_attn_sems.at[1],
            recv_sem=d_attn_sems.at[2],
            device_id=core_peer,
            device_id_type=MESH,
        ),
    )

    @pl.when(step == tiles)
    def _():
        for copy in d_attn_copies():
            copy.start()

    @pl.when(step == tiles + 1)
    def _():
        last_add()
        for copy in d_attn_copies():
            copy.wait()
        for slot in range(2):
            for far in (False, True):
                for copy in copies(slot, far):
                    copy.wait_send()


def feed(middle, cot, gain, up_weight, down_weight, n_seq):
    tokens, width = middle.shape
    wide = up_weight.shape[1]
    tile = feed_tile
    tiles = wide // tile
    half, shard = width // 2, width // n_seq
    whole = lambda dtype: jax.ShapeDtypeStruct((tokens, width), dtype)
    fixed = lambda shape: pl.BlockSpec(shape, lambda i: (0, 0), pipeline_mode=pl.Buffered(1))
    at = lambda i: jnp.minimum(i, tiles - 1)
    late = lambda i: jnp.maximum(i - 2, 0)
    down_shape = (2, tile // (2 * piece_rows), 2, piece_rows, half)
    up_shape = (2, n_seq // 2, 2, shard, tile // 2)
    near = [pltpu.VMEM(down_shape, bf16)] * 3 + [pltpu.VMEM(up_shape, bf16)] * 3
    far = [pltpu.VMEM(down_shape[:2] + down_shape[3:], bf16)] * 3 + [pltpu.VMEM(up_shape[:2] + up_shape[3:], bf16)] * 3
    return pl.pallas_call(
        functools.partial(feed_kernel, tiles, 128),
        grid=(tiles + 2,),
        in_specs=[
            fixed((tokens, width)),
            fixed((tokens, width)),
            fixed((1, width)),
            pl.BlockSpec((width, tile), lambda i: (0, at(i))),
            pl.BlockSpec((tile, width), lambda i: (at(i), 0)),
        ],
        out_specs=[
            fixed((tokens, width)),
            fixed((tokens, width)),
            pl.BlockSpec(memory_space=pl.ANY),
            pl.BlockSpec((tile // 2, half), lambda i: (late(i), 0)),
            pl.BlockSpec((width // 2, tile // 2), lambda i: (0, late(i))),
        ],
        scratch_shapes=[
            pltpu.VMEM((tokens, width), bf16),
            pltpu.VMEM((width, tokens), bf16),
            pltpu.VMEM((tokens, width), f32),
            pltpu.VMEM((tokens, width), bf16),
        ]
        + near
        + far
        + [pltpu.SemaphoreType.DMA((2, 2))] * 4
        + [pltpu.SemaphoreType.REGULAR, pltpu.SemaphoreType.REGULAR((2,)), pltpu.SemaphoreType.DMA((3,))],
        out_shape=[
            whole(bf16),
            whole(f32),
            jax.ShapeDtypeStruct((2, tokens, width), bf16),
            jax.ShapeDtypeStruct((wide // 2, half), bf16),
            jax.ShapeDtypeStruct((width // 2, wide // 2), bf16),
        ],
        compiler_params=pltpu.CompilerParams(
            vmem_limit_bytes=feed_vmem_bytes, collective_id=1, has_side_effects=True
        ),
        cost_estimate=pl.CostEstimate(
            flops=12 * tokens * width * wide,
            bytes_accessed=16 * tokens * width + 6 * width * wide,
            transcendentals=2 * tokens * wide,
        ),
        name="feed",
    )(middle, cot, gain.reshape(1, width), up_weight, down_weight)


class Stream:
    def __init__(self, levels, rows, columns, first, count):
        self.levels, self.rows, self.columns, self.first, self.count = levels, rows, columns, first, count

    def shape(self, level):
        outer = 2 ** (len(self.levels) - 1 - level)
        return (max(outer // 2, 1), min(outer, 2), self.rows, self.columns)

    def scratch(self):
        shapes = []
        for level in range(len(self.levels)):
            shape = self.shape(level)
            shapes += [pltpu.VMEM(shape, bf16), pltpu.VMEM(shape, bf16), pltpu.VMEM((2,) + shape, bf16)]
        return shapes


down_pieces = 4


def streams_of(width, wide, n_seq, pairs):
    lanes = 2 * HDIM
    rows = width // (2 * n_seq)
    return (
        Stream(("x", "y", "z1", "z2"), rows, 4 * lanes, 1, pairs),
        Stream(("y", "z1", "z2"), wide // (2 * n_seq * down_pieces), width // CORES, 0, down_pieces),
        Stream(("x", "z1", "z2"), rows, wide // CORES // down_pieces, 0, down_pieces),
    )


def back_kernel(pairs, tile, streams, row_count, *refs):
    (
        key_tags, query_tags, q_ref, k_ref, v_ref, o_ref, do_ref, lse_ref, n1_ref, own_weight, other_weight,
        gain_ref, out_kept, out_came, down_ref, up_ref, start_ref, d_middle_ref, outputs_ref,
    ) = refs[:19]
    grad_out, outputs_out, *gathered = refs[19:24]
    rest = list(refs[24:])
    take = lambda count: [rest.pop(0) for _ in range(count)]
    k_turned, dq_turned, delta, d_pair, d_came, d_n1, staged, start_part, middle_part = take(9)
    levels = []
    for stream in streams:
        levels.append([take(3) for _ in stream.levels])
    joined = take(len(streams))
    (
        send_sems, recv_sems, join_send, join_recv, core_send, core_recv, local_sems,
        pair_send, pair_recv, home_send, home_recv, home_local, part_sems, result_send, result_recv, result_local,
    ) = rest

    step = pl.program_id(0)
    tokens, lanes = q_ref.shape
    own_tokens = tokens // CORES
    seq_at, rows_at = lax.axis_index("seq"), lax.axis_index("rows")
    core, high = rows_at % 2, (rows_at // 2) % 2
    places = {"x": high, "y": seq_at % 2, "z1": (seq_at // 2) % 2, "z2": seq_at // 4}
    peers = {
        "x": (seq_at, rows_at + 2 - 4 * high),
        "y": (seq_at + 1 - 2 * places["y"], rows_at),
        "z1": (seq_at + 2 - 4 * places["z1"], rows_at),
        "z2": (seq_at + 4 - 8 * places["z2"], rows_at),
        "core": (seq_at, rows_at + 1 - 2 * core),
    }
    n_seq = 2 * row_count
    sub = start_part.shape[1]

    def remote(source, target, send, recv, peer):
        return pltpu.make_async_remote_copy(
            src_ref=source, dst_ref=target, send_sem=send, recv_sem=recv, device_id=peer, device_id_type=MESH
        )

    def add(a, b):
        return (a.astype(f32) + b.astype(f32)).astype(bf16)

    def level_copy(at, level, item):
        send, _, came = levels[at][level]
        slot = item % 2
        return remote(
            send, came.at[slot], send_sems.at[at, level], recv_sems.at[at, level, slot], peers[streams[at].levels[level]]
        )

    def join_copy(at, item):
        part = joined[at].at[item, high]
        return remote(part, part, join_send.at[at], join_recv.at[at, item % 2], peers["x"])

    def core_copy(at, item):
        return remote(
            joined[at].at[item],
            gathered[at].at[item, core],
            core_send.at[at],
            core_recv.at[at, item % 2],
            peers["core"],
        )

    def local_copy(at, item):
        return pltpu.make_async_copy(joined[at].at[item], gathered[at].at[item, core], local_sems.at[at])

    def pair_copy(item):
        slot = item % 2
        return remote(
            d_pair.at[slot, pl.ds(own_tokens, own_tokens)],
            d_came.at[slot],
            pair_send.at[slot],
            pair_recv.at[slot],
            peers["core"],
        )

    home = seq_at // row_count

    def to_home(block, own, result):
        if result:
            source, target = outputs_ref.at[pl.ds(block * sub, sub)], outputs_out
            sems = result_send, result_recv, result_local
        else:
            source, target = staged.at[block], grad_out
            sems = home_send, home_recv, home_local
        row = seq_at % row_count
        if own:
            return pltpu.make_async_copy(source, target.at[row, core], sems[2])
        return remote(source, target.at[row, core], sems[0].at[block], sems[1].at[row, core], (block, rows_at - core + home))

    def start_home(block, result):
        @pl.when(is_own(block))
        def _():
            to_home(block, True, result).start()

        @pl.when(jnp.logical_not(is_own(block)))
        def _():
            to_home(block, False, result).start()

    def wait_home(result):
        for block in range(n_seq):
            @pl.when(is_own(block))
            def _():
                to_home(block, True, result).wait()

            @pl.when(jnp.logical_not(is_own(block)))
            def _():
                to_home(block, False, result).wait_send()
        source, target = (outputs_ref.at[pl.ds(0, sub)], outputs_out) if result else (staged.at[0], grad_out)
        sems = (result_send, result_recv) if result else (home_send, home_recv)
        for row in range(row_count):
            for c in range(CORES):
                @pl.when(jnp.logical_not((seq_at == core * row_count + row) & (core == c)))
                def _():
                    remote(source, target.at[row, c], sems[0].at[0], sems[1].at[row, c], peers["core"]).wait_recv()

    def is_own(block):
        return (seq_at == block) & (home == core)

    @pl.when(step == 0)
    def _():
        barrier = pltpu.get_barrier_semaphore()
        for s in range(n_seq):
            for c in range(CORES):
                @pl.when(jnp.logical_not((seq_at == s) & (core == c)))
                def _():
                    pl.semaphore_signal(barrier, inc=1, device_id=(s, rows_at - core + c), device_id_type=MESH)
        pl.semaphore_signal(barrier, inc=1, device_id=peers["x"], device_id_type=MESH)
        pl.semaphore_wait(barrier, n_seq * CORES)
        d_n1[...] = jnp.zeros_like(d_n1)
        for block in range(n_seq):
            start_home(block, True)

    working, second = step < 2 * pairs, step % 2

    @pl.when(working & (second == 0))
    def _():
        k_turned[...] = k_ref[...].T
        dq_turned[...] = (o_ref[...].astype(f32) * do_ref[...].astype(f32)).T
        for head in range(2):
            own_rows = dq_turned[head * HDIM : (head + 1) * HDIM, :]
            delta[head : head + 1, :] = jnp.sum(own_rows, axis=0, keepdims=True)
        dq_turned[...] = jnp.zeros_like(dq_turned)

    @pl.when(working)
    def _():
        slot = step // 2 % 2
        half_steps = tokens // tile // 2
        first = lax.broadcasted_iota(jnp.int32, (tile, lanes), 1) < HDIM

        def body(i, _):
            part = pl.ds(pl.multiple_of((i + second * half_steps) * tile, tile), tile)
            k, v = k_ref[part, :], v_ref[part, :]
            q, do = q_ref[...], do_ref[...]
            tag = key_tags[part, :]
            allowed = tag == query_tags[...]
            dk, dv = [], []
            for head in range(2):
                own = first if head == 0 else jnp.logical_not(first)
                own_rows = slice(head * HDIM, (head + 1) * HDIM)
                scores = dot(jnp.where(own, k, bf16(0)), q, 1, 1)
                scores = jnp.where(allowed, scores, masked_score)
                chances = jnp.exp2(scores * (score_scale * log2e) - lse_ref[head : head + 1, :])
                weight_grad = dot(jnp.where(own, v, bf16(0)), do, 1, 1)
                score_grad = (chances * (weight_grad - delta[head : head + 1, :])).astype(bf16)
                dv.append(dot(chances.astype(bf16), do, 1, 0))
                dk.append(dot(score_grad, q, 1, 0))
                dq_turned[own_rows, :] += dot(k_turned[own_rows, part], score_grad, 1, 0)
            d_pair[slot, part, lanes : 2 * lanes] = (jnp.where(first, dk[0], dk[1]) * score_scale).astype(bf16)
            d_v = jnp.where(first, dv[0], dv[1]).astype(bf16)
            d_pair[slot, part, 2 * lanes :] = jnp.where(tag < 0, do_ref[part, :], d_v)
            return 0

        lax.fori_loop(0, half_steps, body, 0)

    @pl.when(working & (second == 1))
    def _():
        d_pair[step // 2 % 2, :, :lanes] = (dq_turned[...] * score_scale).T.astype(bf16)

    def add_pair():
        item = step // 2 - 1
        slot = item % 2
        pair_copy(item).wait()
        d_n1[...] += dot(d_pair[slot, :own_tokens, :], own_weight[...], 1, 1) + dot(
            d_came[slot], other_weight[...], 1, 1
        )

    @pl.when((step >= 2) & (step <= 2 * pairs) & (second == 0))
    def _():
        add_pair()

    @pl.when(working & (second == 1))
    def _():
        pair_copy(step // 2).start()

    def part_copies(block):
        rows = pl.ds(block * start_part.shape[1], start_part.shape[1])
        slot = block % 2
        return (
            pltpu.make_async_copy(start_ref.at[rows], start_part.at[slot], part_sems.at[0, slot]),
            pltpu.make_async_copy(d_middle_ref.at[rows], middle_part.at[slot], part_sems.at[1, slot]),
        )

    @pl.when(step == 2 * pairs)
    def _():
        for copy in part_copies(0):
            copy.start()
        for block in range(n_seq):
            if block + 1 < n_seq:
                for copy in part_copies(block + 1):
                    copy.start()
            for copy in part_copies(block):
                copy.wait()
            unit, scale = norm_parts(start_part[block % 2].astype(f32))
            grad = norm_back(d_n1[block * sub : (block + 1) * sub, :], gain_ref[...], unit, scale)
            staged[block] = (middle_part[block % 2] + grad).astype(bf16)
            start_home(block, False)

    for at, stream in enumerate(streams):
        depth = len(stream.levels)

        def item_at(lag, stream=stream):
            since = step - stream.first - lag
            return since // 2, (since >= 0) & (since % 2 == 0) & (since < 2 * stream.count)

        item, here = item_at(depth + 2)

        @pl.when(here)
        def _(at=at, item=item):
            core_copy(at, item).wait()
            local_copy(at, item).wait()

        item, here = item_at(depth + 1)

        @pl.when(here)
        def _(at=at, item=item):
            join_copy(at, item).wait()
            core_copy(at, item).start()
            local_copy(at, item).start()

        for level in reversed(range(depth)):
            item, here = item_at(level + 1)

            @pl.when(here)
            def _(at=at, item=item, level=level, stream=stream, depth=depth):
                _, keep, came = levels[at][level]
                slot = item % 2
                level_copy(at, level, item).wait_recv()
                if level == depth - 1:
                    joined[at][item, high] = add(keep[0, 0], came[slot, 0, 0])
                    join_copy(at, item).start()
                    return

                @pl.when(item > 0)
                def _():
                    level_copy(at, level + 1, item - 1).wait_send()

                next_send, next_keep, _ = levels[at][level + 1]
                place = places[stream.levels[level + 1]]
                next_send[...] = add(keep[:, 1 - place], came[slot, :, 1 - place]).reshape(next_send.shape)
                next_keep[...] = add(keep[:, place], came[slot, :, place]).reshape(next_keep.shape)
                level_copy(at, level + 1, item).start()

    def begin_piece(fills):
        for at, fill in fills.items():
            stream = streams[at]
            item = (step - stream.first) // 2

            @pl.when((step % 2 == stream.first) & (item < stream.count))
            def _(at=at, fill=fill, item=item):
                @pl.when(item > 0)
                def _():
                    level_copy(at, 0, item - 1).wait_send()

                fill(*levels[at][0][:2])
                level_copy(at, 0, item).start()

    def fill_pair(send, keep):
        grad = dot(n1_ref[...], d_pair[step // 2 % 2], 0, 0).astype(bf16)
        grad = grad.reshape(n_seq, 2, send.shape[2], 3 * lanes)
        shape = send.shape[:3] + (3 * lanes,)

        @pl.when(high == 0)
        def _():
            send[:, :, :, : 3 * lanes] = grad[:, 1].reshape(shape)
            keep[:, :, :, : 3 * lanes] = grad[:, 0].reshape(shape)

        @pl.when(high != 0)
        def _():
            send[:, :, :, : 3 * lanes] = grad[:, 0].reshape(shape)
            keep[:, :, :, : 3 * lanes] = grad[:, 1].reshape(shape)

        shape = send.shape[:3] + (lanes,)
        send[:, :, :, 3 * lanes :] = add(out_kept[:, 1 - high], out_came[:, 1 - high]).reshape(shape)
        keep[:, :, :, 3 * lanes :] = add(out_kept[:, high], out_came[:, high]).reshape(shape)

    def fill_from(ref, place):
        def fill(send, keep):
            send[...] = ref[:, 1 - place].reshape(send.shape)
            keep[...] = ref[:, place].reshape(keep.shape)

        return fill

    begin_piece({0: fill_pair, 1: fill_from(down_ref, places["y"]), 2: fill_from(up_ref, high)})

    @pl.when(step == pl.num_programs(0) - 1)
    def _():
        for at, stream in enumerate(streams):
            for level in range(len(stream.levels)):
                level_copy(at, level, stream.count - 1).wait_send()
        wait_home(False)
        wait_home(True)


def back(
    qkv, mixed, d_mixed, lse, key_tags, query_tags, n1, weights, gain, out_kept, out_came, down_part, up_part,
    start, d_middle, outputs, row_count,
):
    tokens = qkv.shape[0]
    width = n1.shape[1]
    own_tokens = tokens // CORES
    lanes = 2 * HDIM
    pairs = qkv.shape[1] // (3 * lanes)
    n_seq = 2 * row_count
    tile = 256
    sub = own_tokens // n_seq
    streams = streams_of(width, down_part.shape[0] * 2, n_seq, pairs)
    last = pairs - 1
    now = lambda i: jnp.minimum(i // 2, last)
    before = lambda i: jnp.clip(i // 2 - 1, 0, last)
    early = lambda i: jnp.minimum(i // 2, down_pieces - 1)
    fixed = lambda shape: pl.BlockSpec(shape, lambda i: (0,) * len(shape), pipeline_mode=pl.Buffered(1))

    def columns(place):
        return pl.BlockSpec((tokens, lanes), lambda i: (0, 3 * now(i) + place))

    pair = pl.BlockSpec((tokens, lanes), lambda i: (0, now(i)))
    weight = pl.BlockSpec((width, 3 * lanes), lambda i: (0, before(i)))
    hbm = pl.BlockSpec(memory_space=pl.ANY)

    rows = streams[0].rows

    def out_piece(value):
        whole = value.reshape(n_seq, 2, rows, value.shape[1])
        return whole, pl.BlockSpec((n_seq, 2, rows, lanes), lambda i: (0, 0, 0, now(i)))

    outs = [out_piece(value) for value in (out_kept, out_came)]
    down = down_part.reshape(n_seq // 2, 2, -1, width // CORES)
    up = up_part.reshape(n_seq // 2, 2, rows, -1)
    down_spec = pl.BlockSpec((n_seq // 2, 2, streams[1].rows, width // CORES), lambda i: (0, 0, early(i), 0))
    up_spec = pl.BlockSpec((n_seq // 2, 2, rows, streams[2].columns), lambda i: (0, 0, 0, early(i)))
    count = len(streams)
    deepest = max(len(stream.levels) for stream in streams)
    return pl.pallas_call(
        functools.partial(back_kernel, pairs, tile, streams, row_count),
        grid=(2 * pairs + deepest + 2,),
        in_specs=[
            fixed((tokens, 1)),
            fixed((1, tokens)),
            columns(0),
            columns(1),
            columns(2),
            pair,
            pair,
            pl.BlockSpec((None, 2, tokens), lambda i: (now(i), 0, 0)),
            fixed((tokens, width)),
            weight,
            weight,
            fixed((1, width)),
            outs[0][1],
            outs[1][1],
            down_spec,
            up_spec,
            hbm,
            hbm,
            hbm,
        ],
        out_specs=[hbm] * 5,
        out_shape=[jax.ShapeDtypeStruct((row_count, CORES, sub, width), bf16)] * 2
        + [jax.ShapeDtypeStruct((stream.count, CORES, 2, stream.rows, stream.columns), bf16) for stream in streams],
        scratch_shapes=[
            pltpu.VMEM((lanes, tokens), bf16),
            pltpu.VMEM((lanes, tokens), f32),
            pltpu.VMEM((2, tokens), f32),
            pltpu.VMEM((2, tokens, 3 * lanes), bf16),
            pltpu.VMEM((2, own_tokens, 3 * lanes), bf16),
            pltpu.VMEM((own_tokens, width), f32),
            pltpu.VMEM((n_seq, sub, width), bf16),
            pltpu.VMEM((2, sub, width), bf16),
            pltpu.VMEM((2, sub, width), f32),
        ]
        + [shape for stream in streams for shape in stream.scratch()]
        + [pltpu.VMEM((stream.count, 2, stream.rows, stream.columns), bf16) for stream in streams]
        + [
            pltpu.SemaphoreType.DMA((count, deepest)),
            pltpu.SemaphoreType.DMA((count, deepest, 2)),
            pltpu.SemaphoreType.DMA((count,)),
            pltpu.SemaphoreType.DMA((count, 2)),
            pltpu.SemaphoreType.DMA((count,)),
            pltpu.SemaphoreType.DMA((count, 2)),
            pltpu.SemaphoreType.DMA((count,)),
            pltpu.SemaphoreType.DMA((2,)),
            pltpu.SemaphoreType.DMA((2,)),
            pltpu.SemaphoreType.DMA((n_seq,)),
            pltpu.SemaphoreType.DMA((row_count, CORES)),
            pltpu.SemaphoreType.DMA,
            pltpu.SemaphoreType.DMA((2, 2)),
            pltpu.SemaphoreType.DMA((n_seq,)),
            pltpu.SemaphoreType.DMA((row_count, CORES)),
            pltpu.SemaphoreType.DMA,
        ],
        compiler_params=pltpu.CompilerParams(
            vmem_limit_bytes=feed_vmem_bytes, collective_id=2, has_side_effects=True
        ),
        cost_estimate=pl.CostEstimate(
            flops=80 * pairs * tokens * tokens * HDIM,
            bytes_accessed=16 * tokens * pairs * lanes,
            transcendentals=2 * pairs * tokens * tokens,
        ),
        name="back",
    )(
        key_tags, query_tags, qkv, qkv, qkv, mixed, d_mixed, lse, n1, weights[0], weights[1],
        gain.reshape(1, width), outs[0][0], outs[1][0], down, up, start, d_middle, outputs,
    )


def collect_kernel(pairs, seq_ref, *refs):
    qkv_parts, down_parts, up_parts = refs[:3]
    qkv_weights, up_weight, first_gain, second_gain = refs[3:9], refs[9], refs[10], refs[11]
    qkv_out, out_out, down_out, up_out, first_out, second_out = refs[12:]
    item = pl.program_id(0)
    lanes = 2 * HDIM
    rows = qkv_parts.shape[2]
    width = out_out.shape[1]
    half = width // CORES
    tile = feed_tile // CORES

    @pl.when(item == 0)
    def _():
        first_out[...] = jnp.zeros_like(first_out)
        second_out[...] = jnp.zeros_like(second_out)

    for core in range(CORES):
        place = pl.multiple_of(core * half + item * lanes, lanes)
        for high in range(2):
            own = slice(high * rows, (high + 1) * rows)
            part = qkv_parts[core, high].astype(f32)
            for kind in range(3):
                value = part[:, kind * lanes : (kind + 1) * lanes]
                qkv_out[own, pl.ds(kind * width + place, lanes)] = value
                weight = qkv_weights[kind * CORES + core][own, :].astype(f32)
                first_out[own, :] += jnp.sum(value * weight, axis=1, keepdims=True)
            out_out[own, pl.ds(place, lanes)] = part[:, 3 * lanes :]

    @pl.when(item < down_pieces)
    def _():
        for core in range(CORES):
            for high in range(2):
                own = slice(high * rows, (high + 1) * rows)
                for at in range(up_parts.shape[3] // lanes):
                    column = item * up_parts.shape[3] + at * lanes
                    column = column // tile * feed_tile + core * tile + column % tile
                    columns = pl.ds(pl.multiple_of(column, lanes), lanes)
                    value = up_parts[core, high, :, at * lanes : (at + 1) * lanes].astype(f32)
                    up_out[own, columns] = value
                    second_out[own, :] += jnp.sum(value * up_weight[own, columns].astype(f32), axis=1, keepdims=True)
                count = down_parts.shape[2] // piece_rows
                for at in range(count):
                    start = ((item * count + at) * 2 + high) * piece_rows
                    value = down_parts[core, high, at * piece_rows : (at + 1) * piece_rows, :].astype(f32)
                    down_out[pl.ds(pl.multiple_of(start, piece_rows), piece_rows), core * half : (core + 1) * half] = value

    @pl.when(item == pairs - 1)
    def _():
        first_out[...] = first_out[...] / first_gain[...]
        second_out[...] = second_out[...] / second_gain[...]


def collect(seq_at, qkv_parts, down_parts, up_parts, qkv_weight, up_weight, first_gain, second_gain):
    pairs, _, _, rows, _ = qkv_parts.shape
    width, lanes = qkv_weight.shape[0], 2 * HDIM
    shard, wide = 2 * rows, up_weight.shape[1]
    down_rows = 2 * down_pieces * down_parts.shape[3]

    def parts(value):
        return pl.BlockSpec(
            (None,) + value.shape[1:], lambda i, seq: (jnp.minimum(i, value.shape[0] - 1), 0, 0, 0, 0)
        )

    def weight(kind, core):
        return pl.BlockSpec((shard, lanes), lambda i, seq: (seq[0], (kind * CORES + core) * pairs + i))

    gain = pl.BlockSpec((shard, 1), lambda i, seq: (seq[0], 0))
    whole = lambda shape: pl.BlockSpec(shape, lambda i, seq: (0, 0))
    return pl.pallas_call(
        functools.partial(collect_kernel, pairs),
        grid_spec=pltpu.PrefetchScalarGridSpec(
            num_scalar_prefetch=1,
            grid=(pairs,),
            in_specs=[parts(qkv_parts), parts(down_parts), parts(up_parts)]
            + [weight(kind, core) for kind in range(3) for core in range(CORES)]
            + [pl.BlockSpec((shard, wide), lambda i, seq: (seq[0], 0)), gain, gain],
            out_specs=[
                whole((shard, 3 * width)),
                whole((shard, width)),
                whole((down_rows, width)),
                whole((shard, wide)),
                whole((shard, 1)),
                whole((shard, 1)),
            ],
        ),
        out_shape=[
            jax.ShapeDtypeStruct((shard, 3 * width), f32),
            jax.ShapeDtypeStruct((shard, width), f32),
            jax.ShapeDtypeStruct((down_rows, width), f32),
            jax.ShapeDtypeStruct((shard, wide), f32),
            jax.ShapeDtypeStruct((shard, 1), f32),
            jax.ShapeDtypeStruct((shard, 1), f32),
        ],
        compiler_params=pltpu.CompilerParams(vmem_limit_bytes=vmem_bytes),
        name="collect",
    )(
        seq_at.reshape(1), qkv_parts, down_parts, up_parts, *[qkv_weight] * 6, up_weight,
        first_gain.reshape(width, 1), second_gain.reshape(width, 1),
    )


def add_split_kernel(has_two, bit_ref, *refs):
    ins, outs = refs[: 2 if has_two else 1], refs[2 if has_two else 1 :]
    value = ins[0][...]
    if has_two:
        value = (value.astype(f32) + ins[1][...].astype(f32)).astype(bf16)
    if len(outs) == 1:
        outs[0][...] = value
    else:
        sends = pl.program_id(0) == 0

        @pl.when(sends)
        def _():
            outs[0][...] = value

        @pl.when(jnp.logical_not(sends))
        def _():
            outs[1][...] = value


def add_split(kept, received, inner, bit):
    rows, columns = kept.shape
    values = [kept] if received is None else [kept, received.reshape(rows, columns)]
    if bit is None:
        if received is None:
            return None, kept
        count = 4 if rows % 64 == 0 else 1
        block = pl.BlockSpec((rows // count, columns), lambda i, bit: (i, 0))
        grid, ins, outs = (count,), [block] * 2, block
        shapes = jax.ShapeDtypeStruct((rows, columns), bf16)
        bit = jnp.zeros((), jnp.int32)
    else:
        outer = rows // (2 * inner)
        cut = 1
        while inner // cut * columns > 2**19 and inner % (32 * cut) == 0:
            cut *= 2
        values = [value.reshape(outer, 2, inner, columns) for value in values]
        ins = [
            pl.BlockSpec(
                (None, None, inner // cut, columns),
                lambda w, i, j, bit: (i, jnp.where(w == 0, 1 - bit[0], bit[0]), j, 0),
            )
        ] * len(values)
        outs = [
            pl.BlockSpec(
                (None, inner // cut, columns),
                lambda w, i, j, bit: (jnp.where(w == 0, i, outer - 1), jnp.where(w == 0, j, cut - 1), 0),
            ),
            pl.BlockSpec(
                (None, inner // cut, columns),
                lambda w, i, j, bit: (jnp.where(w == 0, 0, i), jnp.where(w == 0, 0, j), 0),
            ),
        ]
        grid = (2, outer, cut)
        shapes = [jax.ShapeDtypeStruct((outer, inner, columns), bf16)] * 2
    done = pl.pallas_call(
        functools.partial(add_split_kernel, len(values) == 2),
        grid_spec=pltpu.PrefetchScalarGridSpec(
            num_scalar_prefetch=1, grid=grid, in_specs=ins, out_specs=outs
        ),
        out_shape=shapes,
        cost_estimate=pl.CostEstimate(flops=rows * columns, bytes_accessed=6 * rows * columns, transcendentals=0),
        name="add_split",
    )(bit.reshape(1), *values)
    if not isinstance(done, (list, tuple)):
        return None, done
    return done[0].reshape(rows // 2, columns), done[1].reshape(rows // 2, columns)


def tie(*values):
    return lax.optimization_barrier(values)


def build(n_seq, n_rows):
    highs = n_rows // CORES
    seq_bits = n_seq.bit_length() - 1
    high_bits = highs.bit_length() - 1
    bits = seq_bits + high_bits

    def permute(value, target):
        pairs = []
        for s in range(n_seq):
            for r in range(n_rows):
                to_s, to_r = target(s, r)
                pairs.append((s * n_rows + r, to_s * n_rows + to_r))
        return lax.ppermute(value, AXES, pairs)

    def other_core(value):
        return permute(value, lambda s, r: (s, r ^ 1))

    def pick(value, place, axis):
        return lax.dynamic_index_in_dim(value, place, axis, keepdims=False)

    def bit_of(step):
        name, bit = step
        return (lax.axis_index(name) >> bit) & 1

    def across(value, step):
        name, bit = step
        if name == "rows":
            return permute(value, lambda s, r: (s, r ^ (1 << bit)))
        return permute(value, lambda s, r: (s ^ (1 << bit), r))

    high_steps = [("rows", bit + 1) for bit in reversed(range(high_bits))]
    seq_steps = [("seq", bit) for bit in range(seq_bits)]

    class Sum:
        def __init__(self, kept, received, order):
            self.rows, self.columns = kept.shape
            self.kept, self.received = kept, received
            self.left = [step for step in seq_steps[::-1] + high_steps if step in order]
            self.order = list(order)

        def finish(self):
            step = self.order[0] if self.order else None
            inner = self.rows
            if step is not None:
                axis = self.left.index(step)
                inner = self.rows >> (axis + 1)
            self.sent, self.kept = add_split(self.kept, self.received, inner, step and bit_of(step))
            self.received = None

        def begin(self):
            step = self.order.pop(0)
            self.left.remove(step)
            self.rows //= 2
            self.received = across(self.sent, step)

        def finished(self):
            while self.order:
                self.finish()
                self.begin()
            self.finish()
            return self.kept

    rows_first = high_steps + seq_steps[1:2] + seq_steps[:1] + seq_steps[2:]
    down_order = [step for step in seq_steps + high_steps if step != ("rows", 1)]
    up_order = [step for step in high_steps + seq_steps if step != ("seq", 0)]

    def gather_high(value, pieces=0):
        for step in high_steps[::-1]:
            if pieces and step == ("rows", 1):
                continue
            received = across(value, step)
            value = jnp.where(
                bit_of(step) == 0,
                jnp.concatenate([value, received], 0),
                jnp.concatenate([received, value], 0),
            )
        if pieces:
            value = value.reshape(-1, 1, pieces, value.shape[1])
            received = across(value, ("rows", 1))
            value = jnp.where(
                bit_of(("rows", 1)) == 0,
                jnp.concatenate([value, received], 1),
                jnp.concatenate([received, value], 1),
            )
            value = value.reshape(-1, value.shape[-1])
        return value

    def back_by_steps(
        qkv, mixed, d_mixed, lse, key_tags, query_tags, n1_all, qkv_parts, attention_gain,
        out_kept, out_received, down_part, up_part, start, d_middle, to_member, ordered, from_rows, sizes,
    ):
        group, member, core, pairs, group_width, tokens, width = sizes
        lanes, half = 2 * HDIM, width // CORES
        unit1, scale1 = norm_parts(start)
        down = Sum(down_part, None, down_order)
        up = Sum(up_part, None, up_order)
        out = Sum(out_kept, out_received, rows_first)

        def before_next(*sums):
            nonlocal d_mixed
            for each in sums:
                each.finish()
            values = tie(d_mixed, *[v for each in sums for v in (each.sent, each.kept)])
            d_mixed = values[0]
            for at, each in enumerate(sums):
                each.sent, each.kept = values[1 + 2 * at : 3 + 2 * at]
                each.begin()

        def back_at(at):
            return attend_back(qkv, mixed, d_mixed, lse, key_tags, query_tags, at, 1)

        cut = max(1, 3 * pairs // 5)
        before_next(down, up)
        d_qkv, qkv_sums, d_parts = [], [], [[] for _ in range(group)]

        def take_piece(pieces):
            piece = jnp.concatenate(pieces, axis=1)
            d_parts[0].append(piece[:tokens])
            for hop in range(1, group):
                d_parts[hop].append(to_member(piece[hop * tokens : (hop + 1) * tokens], group - hop))
            return dot(n1_all, piece, 0, 0)

        grads = []
        for at in range(pairs):
            d_qkv.append(back_at(at))
            d_mixed, d_qkv[at] = tie(d_mixed, d_qkv[at])
            if at + 1 == cut:
                grads.append(take_piece(d_qkv))
            if at == min(0, pairs - 1):
                before_next(out)
            if at == min(1, pairs - 1):
                before_next(down, up)
            if at == min(3, pairs - 1):
                before_next(down, up, out)
        if pairs > cut:
            grads.append(take_piece(d_qkv[cut:]))
        if group == CORES:
            qkv_sums = [Sum(grad.astype(bf16), None, rows_first) for grad in grads]
        else:
            grad = jnp.concatenate(grads, 1)
            grad = grad.reshape(width, pairs, 3, lanes).transpose(0, 2, 1, 3)
            grad = grad.reshape(width, 3, 1, pairs * lanes)[..., :group_width]
            grad = lax.dynamic_update_slice_in_dim(
                jnp.zeros((width, 3, group, group_width), f32), grad, member, 2
            ).reshape(width, 3, CORES, half)
            kept = pick(grad, core, 2).astype(bf16).reshape(width, 3 * half)
            sent = pick(grad, 1 - core, 2).astype(bf16).reshape(width, 3 * half)
            qkv_sums = [Sum(kept, other_core(sent), rows_first)]

        d_n1 = jnp.zeros((tokens, width), f32)
        for part, weight in zip(d_parts, qkv_parts):
            d_n1 = d_n1 + dot(jnp.concatenate(part, 1), weight, 1, 1)
        input_grad = d_middle + norm_back(d_n1, attention_gain, unit1, scale1)
        input_grad = from_rows(input_grad.astype(bf16))

        down_total = gather_high(down.finished(), piece_rows)
        down_total = ordered(down_total, other_core(down_total), 1).astype(f32)
        tile = feed_tile // CORES
        up_total = gather_high(up.finished()).reshape(width // n_seq, -1, 1, tile)
        up_total = ordered(up_total, other_core(up_total), 2).reshape(width // n_seq, -1).astype(f32)
        out_total = gather_high(out.finished())
        out_total = ordered(out_total, other_core(out_total), 1).astype(f32)
        qkv_part = gather_high(jnp.concatenate([each.finished() for each in qkv_sums], 1))
        if group == CORES:
            qkv_part = qkv_part.reshape(-1, pairs, 3, lanes).transpose(0, 2, 1, 3)
        qkv_part = qkv_part.reshape(-1, 3, half)
        qkv_total = ordered(qkv_part[:, :, None], other_core(qkv_part)[:, :, None], 2)
        qkv_total = qkv_total.reshape(-1, 3 * width).astype(f32)

        return input_grad, qkv_total, out_total, down_total, up_total

    def per_device(
        inputs, cell_ids, valid_counts, cotangent, attention_gain, qkv_weight, out_weight, feed_gain, up_weight, down_weight
    ):
        row_count, block, width = inputs.shape
        seq_len = cell_ids.shape[1]
        heads = width // HDIM
        lanes = 2 * HDIM
        seq_at, rows_at = lax.axis_index("seq"), lax.axis_index("rows")
        core = rows_at % CORES
        chips = n_seq // (CORES * row_count)
        group = chips * CORES
        sub = block // group
        tokens = n_seq * sub
        member = (seq_at % chips) * CORES + core
        group_heads = heads // group
        pairs = -(-group_heads // 2)
        group_width = group_heads * HDIM
        padded = pairs * lanes - group_width

        def to_member(value, hop):
            def target(s, r):
                place = ((s % chips) * CORES + r % CORES + hop) % group
                return (s // chips * chips + place // CORES, r // CORES * CORES + place % CORES)

            return permute(value, target)

        def ordered(own, received, axis):
            return jnp.where(
                core == 0,
                jnp.concatenate([own, received], axis),
                jnp.concatenate([received, own], axis),
            )

        def to_rows(value):
            halves = value.reshape(row_count, CORES, block // CORES, width)
            received = other_core(pick(halves, 1 - core, 1))
            both = ordered(pick(halves, core, 1), received, 0).reshape(n_seq, sub, width)
            return lax.all_to_all(both, "seq", 0, 0, tiled=True).reshape(tokens, width)

        def from_rows(value):
            both = lax.all_to_all(value.reshape(n_seq, sub, width), "seq", 0, 0, tiled=True)
            both = both.reshape(CORES, row_count, block // CORES, width)
            received = other_core(pick(both, 1 - core, 0))
            own = pick(both, core, 0)
            return ordered(own[:, None], received[:, None], 1).reshape(row_count, block, width)

        places = jnp.arange(seq_len, dtype=jnp.int32)
        tags = jnp.where(places[None, :] < valid_counts[:, None], cell_ids, -1 - places[None, :])
        tags = ordered(tags, other_core(tags), 0)
        tags = pick(tags, seq_at // chips, 0).reshape(n_seq, CORES, chips, sub)
        tags = tags.transpose(2, 1, 0, 3).reshape(group, tokens)
        order = (member - jnp.arange(group, dtype=jnp.int32)) % group
        tags = jnp.take(tags, order, axis=0).reshape(1, seq_len)
        query_tags, key_tags = tags, tags.reshape(seq_len, 1)

        def pad_heads(value, axis):
            if not padded:
                return value
            fill = [(0, 0)] * value.ndim
            fill[axis] = (0, padded)
            return jnp.pad(value, fill)

        def qkv_of(hop):
            if group == CORES:
                return gather_pairs(((core + hop) % CORES).reshape(1), qkv_weight)
            piece = pick(qkv_weight.reshape(width, 3, group, group_width), (member + hop) % group, 2)
            piece = pad_heads(piece, 2).reshape(width, 3, pairs, lanes)
            return piece.transpose(0, 2, 1, 3).reshape(width, 3 * pairs * lanes)

        def out_of(hop):
            at = (member + hop) % group * group_width
            return pad_heads(lax.dynamic_slice_in_dim(out_weight, at, group_width, 0), 0)

        if chips == 1 and highs == 2:
            half = width // CORES
            x_row, n1, qkv, own_weight, other_weight = begin(inputs, qkv_weight, attention_gain)
            start = x_row.reshape(tokens, width)
            mixed, lse, cot, mixed_own = attend_row(qkv, key_tags, query_tags, cotangent)
            middle = start.astype(f32) + dot(mixed_own, out_weight, 1, 0)
            outputs, d_middle, d_attn, down_part, up_part = feed(
                middle, cot.reshape(tokens, width), feed_gain, up_weight, down_weight, n_seq
            )
            out_grad = dot(mixed_own, d_attn[0], 0, 0).astype(bf16)
            out_kept = lax.dynamic_slice_in_dim(out_grad, core * half, half, 1)
            out_received = other_core(lax.dynamic_slice_in_dim(out_grad, (1 - core) * half, half, 1))
            out_own = lax.dynamic_slice_in_dim(out_weight, core * half, half, 0)
            d_mixed = dot(d_attn.reshape(seq_len, width), out_own, 1, 1).astype(bf16)
            input_grad, out_low, qkv_out, down_all, up_all = back(
                qkv, mixed, d_mixed, lse, key_tags, query_tags, n1, (own_weight, other_weight), attention_gain,
                out_kept, out_received, down_part, up_part, start, d_middle, outputs, row_count,
            )
            qkv_total, out_total, down_total, up_total, first, second = collect(
                seq_at, qkv_out, down_all, up_all, qkv_weight, up_weight, attention_gain, feed_gain
            )
            return (
                out_low.reshape(inputs.shape),
                input_grad.reshape(inputs.shape),
                first.reshape(-1),
                qkv_total,
                out_total,
                second.reshape(-1),
                up_total,
                down_total,
            )

        start = to_rows(inputs)
        qkv_parts = [qkv_of(hop) for hop in range(group)]
        out_parts = [out_of(hop) for hop in range(group)]
        start = start.astype(f32)
        unit1, scale1 = norm_parts(start)
        n1 = (unit1 * attention_gain).astype(bf16)
        n1_all = jnp.concatenate([n1] + [to_member(n1, hop) for hop in range(1, group)], 0)
        cotangent, _ = tie(cotangent, start[:1])
        cot = to_rows(cotangent)
        qkv = dot(n1_all, qkv_parts[0], 1, 0).astype(bf16)
        mixed, lse = attend(qkv, key_tags, query_tags)
        mixed_parts = [mixed[:tokens]] + [
            to_member(mixed[hop * tokens : (hop + 1) * tokens], group - hop) for hop in range(1, group)
        ]
        middle = start
        for part, weight in zip(mixed_parts, out_parts):
            middle = middle + dot(part, weight, 1, 0)
        outputs, d_middle, d_attn, down_part, up_part = feed(middle, cot, feed_gain, up_weight, down_weight, n_seq)
        d_attn = d_attn[0]

        d_attn_all = jnp.concatenate([d_attn] + [to_member(d_attn, hop) for hop in range(1, group)], 0)


        half = width // CORES
        if group == CORES:
            mixed_own = ordered(mixed_parts[0], mixed_parts[1], 1)
        else:
            slots = jnp.stack([part[:, :group_width] for part in mixed_parts])
            turn = (jnp.arange(group, dtype=jnp.int32) - member) % group
            mixed_own = jnp.take(slots, turn, axis=0).transpose(1, 0, 2).reshape(tokens, width)
        out_grad = dot(mixed_own, d_attn, 0, 0).astype(bf16)
        out_kept = lax.dynamic_slice_in_dim(out_grad, core * half, half, 1)
        out_received = other_core(lax.dynamic_slice_in_dim(out_grad, (1 - core) * half, half, 1))
        d_mixed = dot(d_attn_all, out_parts[0], 1, 1).astype(bf16)

        out_low = from_rows(outputs)
        input_grad, qkv_total, out_total, down_total, up_total = back_by_steps(
            qkv, mixed, d_mixed, lse, key_tags, query_tags, n1_all, qkv_parts, attention_gain,
            out_kept, out_received, down_part, up_part, start, d_middle, to_member, ordered, from_rows,
            (group, member, core, pairs, group_width, tokens, width),
        )

        shard = width // n_seq

        def gain_total(weight, total, gain):
            rows = lax.dynamic_slice_in_dim(weight, seq_at * shard, shard, 0).astype(f32)
            return jnp.sum(rows * total, axis=1) / lax.dynamic_slice_in_dim(gain, seq_at * shard, shard, 0)

        return (
            out_low,
            input_grad,
            gain_total(qkv_weight, qkv_total, attention_gain),
            qkv_total,
            out_total,
            gain_total(up_weight, up_total, feed_gain),
            up_total,
            down_total,
        )

    return per_device


def solution(mesh):
    placed = (
        P("rows", "seq", None),
        P("rows", None),
        P("rows"),
        P("rows", "seq", None),
        P(),
        P(),
        P(),
        P(),
        P(),
        P(),
    )
    return jax.shard_map(
        build(mesh.shape["seq"], mesh.shape["rows"]),
        mesh=mesh,
        in_specs=placed,
        out_specs=(
            P("rows", "seq", None),
            P("rows", "seq", None),
            P("seq"),
            P("seq", None),
            P("seq", None),
            P("seq"),
            P("seq", None),
            P("seq", None),
        ),
        check_vma=False,
    )
```

```python
import functools

import jax
import jax.numpy as jnp
from jax import lax
from jax.experimental import pallas as pl
from jax.experimental.pallas import tpu as pltpu
from jax.sharding import PartitionSpec as P

HDIM = 64
CORES = 2
epsilon = 1e-05
masked_score = -1e30
score_scale = HDIM ** (-0.5)
log2e = 1.4426950408889634
bf16 = jnp.bfloat16
f32 = jnp.float32
AXES = ("seq", "rows")
vmem_bytes = 60 * 2**20
feed_vmem_bytes = 62 * 2**20
feed_tile = 512
max_cells = 7
MESH = pl.DeviceIdType.MESH


def dot(a, b, ca, cb):
    return lax.dot_general(a, b, (((ca,), (cb,)), ((), ())), preferred_element_type=f32)


def attend_kernel(tile, key_tags, query_tags, q_ref, k_ref, v_ref, o_ref, lse_ref, v_turned):
    tokens = q_ref.shape[0]
    v_turned[...] = v_ref[...].T
    lane = lax.broadcasted_iota(jnp.int32, (tile, 2 * HDIM), 1)

    def body(step, _):
        part = pl.ds(pl.multiple_of(step * tile, tile), tile)
        q = q_ref[part, :]
        allowed = key_tags[...] == query_tags[:, part]
        pieces = []
        for head in range(2):
            own = jnp.where((lane // HDIM) == head, q, bf16(0))
            scores = dot(k_ref[...], own, 1, 1)
            scores = jnp.where(allowed, scores, masked_score)
            peak = jnp.max(scores, axis=0, keepdims=True)
            powers = jnp.exp2((scores - peak) * (score_scale * log2e))
            total = jnp.sum(powers, axis=0, keepdims=True)
            mixed = dot(v_turned[head * HDIM : (head + 1) * HDIM, :], powers.astype(bf16), 1, 0)
            pieces.append(mixed * (1.0 / total))
            lse_ref[head : head + 1, part] = peak * (score_scale * log2e) + jnp.log2(total)
        o_ref[part, :] = jnp.concatenate(pieces, axis=0).T.astype(bf16)
        return 0

    lax.fori_loop(0, tokens // tile, body, 0)


def attend(qkv, key_tags, query_tags):
    tokens, width = qkv.shape
    lanes = 2 * HDIM
    pairs = width // (3 * lanes)
    tile = min(512, tokens)

    def columns(place):
        return pl.BlockSpec((tokens, lanes), lambda i: (0, 3 * i + place))

    return pl.pallas_call(
        functools.partial(attend_kernel, tile),
        grid=(pairs,),
        in_specs=[
            pl.BlockSpec((tokens, 1), lambda i: (0, 0)),
            pl.BlockSpec((1, tokens), lambda i: (0, 0)),
            columns(0),
            columns(1),
            columns(2),
        ],
        out_specs=[
            pl.BlockSpec((tokens, lanes), lambda i: (0, i)),
            pl.BlockSpec((None, 2, tokens), lambda i: (i, 0, 0)),
        ],
        out_shape=[
            jax.ShapeDtypeStruct((tokens, pairs * lanes), bf16),
            jax.ShapeDtypeStruct((pairs, 2, tokens), f32),
        ],
        scratch_shapes=[pltpu.VMEM((lanes, tokens), bf16)],
        compiler_params=pltpu.CompilerParams(vmem_limit_bytes=vmem_bytes),
        cost_estimate=pl.CostEstimate(
            flops=32 * pairs * tokens * tokens * HDIM,
            bytes_accessed=8 * tokens * pairs * lanes,
            transcendentals=2 * pairs * tokens * tokens,
        ),
        name="attend",
    )(key_tags, query_tags, qkv, qkv, qkv)


def attend_back_kernel(
    tile, key_tags, query_tags, q_ref, k_ref, v_ref, o_ref, do_ref, lse_ref, grad_ref, k_turned, dq_turned, delta
):
    tokens = q_ref.shape[0]
    lanes = 2 * HDIM
    k_turned[...] = k_ref[...].T
    dq_turned[...] = (o_ref[...].astype(f32) * do_ref[...].astype(f32)).T
    for head in range(2):
        rows = dq_turned[head * HDIM : (head + 1) * HDIM, :]
        delta[head : head + 1, :] = jnp.sum(rows, axis=0, keepdims=True)
    dq_turned[...] = jnp.zeros_like(dq_turned)
    first = lax.broadcasted_iota(jnp.int32, (tile, lanes), 1) < HDIM

    def body(step, _):
        part = pl.ds(pl.multiple_of(step * tile, tile), tile)
        k, v = k_ref[part, :], v_ref[part, :]
        q, do = q_ref[...], do_ref[...]
        allowed = key_tags[part, :] == query_tags[...]
        dk, dv = [], []
        for head in range(2):
            own = first if head == 0 else jnp.logical_not(first)
            own_rows = slice(head * HDIM, (head + 1) * HDIM)
            scores = dot(jnp.where(own, k, bf16(0)), q, 1, 1)
            scores = jnp.where(allowed, scores, masked_score)
            chances = jnp.exp2(scores * (score_scale * log2e) - lse_ref[head : head + 1, :])
            weight_grad = dot(jnp.where(own, v, bf16(0)), do, 1, 1)
            score_grad = (chances * (weight_grad - delta[head : head + 1, :])).astype(bf16)
            dv.append(dot(chances.astype(bf16), do, 1, 0))
            dk.append(dot(score_grad, q, 1, 0))
            dq_turned[own_rows, :] += dot(k_turned[own_rows, part], score_grad, 1, 0)
        grad_ref[part, lanes : 2 * lanes] = (jnp.where(first, dk[0], dk[1]) * score_scale).astype(bf16)
        grad_ref[part, 2 * lanes :] = jnp.where(first, dv[0], dv[1]).astype(bf16)
        return 0

    lax.fori_loop(0, tokens // tile, body, 0)
    grad_ref[:, :lanes] = (dq_turned[...] * score_scale).T.astype(bf16)


def attend_back(qkv, mixed, d_mixed, lse, key_tags, query_tags, start, count):
    tokens = qkv.shape[0]
    tile = min(512, tokens)
    lanes = 2 * HDIM

    def columns(place):
        return pl.BlockSpec((tokens, lanes), lambda i: (0, 3 * (start + i) + place))

    pair = pl.BlockSpec((tokens, lanes), lambda i: (0, start + i))
    return pl.pallas_call(
        functools.partial(attend_back_kernel, tile),
        grid=(count,),
        in_specs=[
            pl.BlockSpec((tokens, 1), lambda i: (0, 0)),
            pl.BlockSpec((1, tokens), lambda i: (0, 0)),
            columns(0),
            columns(1),
            columns(2),
            pair,
            pair,
            pl.BlockSpec((None, 2, tokens), lambda i: (start + i, 0, 0)),
        ],
        out_specs=pl.BlockSpec((tokens, 3 * lanes), lambda i: (0, i)),
        out_shape=jax.ShapeDtypeStruct((tokens, 3 * count * lanes), bf16),
        scratch_shapes=[
            pltpu.VMEM((lanes, tokens), bf16),
            pltpu.VMEM((lanes, tokens), f32),
            pltpu.VMEM((2, tokens), f32),
        ],
        compiler_params=pltpu.CompilerParams(vmem_limit_bytes=vmem_bytes),
        cost_estimate=pl.CostEstimate(
            flops=80 * count * tokens * tokens * HDIM,
            bytes_accessed=16 * tokens * count * lanes,
            transcendentals=2 * count * tokens * tokens,
        ),
        name="attend_back",
    )(key_tags, query_tags, qkv, qkv, qkv, mixed, d_mixed, lse)


def copy_kernel(core_ref, from_ref, to_ref):
    to_ref[...] = from_ref[...]


def gather_pairs(core, qkv_weight):
    width, lanes = qkv_weight.shape[0], 2 * HDIM
    pairs = width // (CORES * lanes)
    return pl.pallas_call(
        copy_kernel,
        grid_spec=pltpu.PrefetchScalarGridSpec(
            num_scalar_prefetch=1,
            grid=(pairs, 3),
            in_specs=[
                pl.BlockSpec((width, lanes), lambda i, j, core: (0, (j * CORES + core[0]) * pairs + i))
            ],
            out_specs=pl.BlockSpec((width, lanes), lambda i, j, core: (0, 3 * i + j)),
        ),
        out_shape=jax.ShapeDtypeStruct((width, 3 * pairs * lanes), qkv_weight.dtype),
        cost_estimate=pl.CostEstimate(flops=0, bytes_accessed=12 * width * pairs * lanes, transcendentals=0),
        name="gather_pairs",
    )(core, qkv_weight)


def norm_parts(values):
    center = values - jnp.mean(values, axis=-1, keepdims=True)
    spread = jnp.mean(center * center, axis=-1, keepdims=True)
    scale = lax.rsqrt(spread + epsilon)
    return center * scale, scale


def norm_back(grad, gain, unit, scale):
    e = grad * gain
    return scale * (
        e - jnp.mean(e, axis=-1, keepdims=True) - unit * jnp.mean(e * unit, axis=-1, keepdims=True)
    )


def all_signal(n_seq, seq_at, rows_at, extra=()):
    core = rows_at % CORES
    barrier = pltpu.get_barrier_semaphore()
    for s in range(n_seq):
        for c in range(CORES):
            @pl.when(jnp.logical_not((seq_at == s) & (core == c)))
            def _():
                pl.semaphore_signal(barrier, inc=1, device_id=(s, rows_at - core + c), device_id_type=MESH)
    for peer in extra:
        pl.semaphore_signal(barrier, inc=1, device_id=peer, device_id_type=MESH)
    pl.semaphore_wait(barrier, n_seq * CORES - 1 + len(extra))


class ToRows:
    def __init__(self, source, target, send, recv, local, row_count, seq_at, rows_at):
        self.source, self.target, self.send, self.recv, self.local = source, target, send, recv, local
        self.row_count, self.seq_at, self.rows_at = row_count, seq_at, rows_at
        self.core = rows_at % CORES

    def copy(self, row, c):
        chip = self.core * self.row_count + row
        return pltpu.make_async_remote_copy(
            src_ref=self.source.at[row, c],
            dst_ref=self.target.at[self.seq_at],
            send_sem=self.send.at[row, c],
            recv_sem=self.recv.at[self.seq_at],
            device_id=(chip, self.rows_at - self.core + c),
            device_id_type=MESH,
        )

    def own(self, row, c):
        return pltpu.make_async_copy(self.source.at[row, c], self.target.at[self.seq_at], self.local)

    def each(self, own, other):
        for row_turn in range(self.row_count):
            for core_turn in range(CORES):
                row = (row_turn + self.seq_at) % self.row_count
                c = (core_turn + self.seq_at // self.row_count) % CORES
                here = (self.core * self.row_count + row == self.seq_at) & (self.core == c)

                @pl.when(here)
                def _():
                    own(row, c)

                @pl.when(jnp.logical_not(here))
                def _():
                    other(row, c)

    def start(self):
        self.each(lambda row, c: self.own(row, c).start(), lambda row, c: self.copy(row, c).start())

    def wait_block(self, s):
        here = (s == self.seq_at) & (self.seq_at // self.row_count == self.core)

        @pl.when(here)
        def _():
            self.own(0, 0).wait()

        @pl.when(jnp.logical_not(here))
        def _():
            pltpu.make_async_remote_copy(
                src_ref=self.source.at[0, 0],
                dst_ref=self.target.at[s],
                send_sem=self.send.at[0, 0],
                recv_sem=self.recv.at[s],
                device_id=(self.seq_at, self.rows_at + 1 - 2 * self.core),
                device_id_type=MESH,
            ).wait_recv()

    def wait_sends(self):
        self.each(lambda row, c: None, lambda row, c: self.copy(row, c).wait_send())


def begin_kernel(
    row_count, pairs, x_ref, weight_ref, gain_ref, x_out, n1_out, qkv_out, own_out, other_out,
    x_part, n1, qkv, weight, other_weight,
    x_send, x_recv, x_local, n1_send, n1_recv, weight_sems, out_sems, x_sems, qkv_sems, n1_sems,
):
    seq_at, rows_at = lax.axis_index("seq"), lax.axis_index("rows")
    core = rows_at % CORES
    n_seq, sub, width = x_part.shape
    lanes = 2 * HDIM
    tokens = n_seq * sub
    moves = ToRows(x_ref, x_part, x_send, x_recv, x_local, row_count, seq_at, rows_at)

    def weight_copies(item, which):
        pair, kind = item // 3, item % 3
        to = pl.ds(pl.multiple_of(item * lanes, lanes), lanes)

        def columns(c):
            return pl.ds(pl.multiple_of((kind * CORES + c) * pairs * lanes + pair * lanes, lanes), lanes)

        source = weight_ref.at[:, columns(1 - core if which else core)]
        return pltpu.make_async_copy(source, (weight, other_weight)[which].at[:, to], weight_sems.at[which, item])

    def each_weight(act, which):
        def body(item, _):
            act(weight_copies(item, which))
            return 0

        lax.fori_loop(0, 3 * pairs, body, 0)

    each_weight(lambda copy: copy.start(), 0)
    all_signal(n_seq, seq_at, rows_at)
    moves.start()
    each_weight(lambda copy: copy.start(), 1)
    each_weight(lambda copy: copy.wait(), 0)
    weights_out = (
        pltpu.make_async_copy(weight, own_out, out_sems.at[0]),
        pltpu.make_async_copy(other_weight, other_out, out_sems.at[1]),
    )
    weights_out[0].start()
    each_weight(lambda copy: copy.wait(), 1)
    weights_out[1].start()

    def block_of(place):
        near = (place % 2) * ((place + 1) // 2) + (1 - place % 2) * ((n_seq - place // 2) % n_seq)
        return (seq_at + near) % n_seq

    def rows_of(s, other):
        return pl.ds(pl.multiple_of(s * sub + other * tokens, sub), sub)

    def n1_copy(s):
        return pltpu.make_async_remote_copy(
            src_ref=n1.at[rows_of(s, 0)],
            dst_ref=n1.at[rows_of(s, 1)],
            send_sem=n1_send.at[s],
            recv_sem=n1_recv.at[s],
            device_id=(seq_at, rows_at + 1 - 2 * core),
            device_id_type=MESH,
        )

    def x_copy(s):
        return pltpu.make_async_copy(x_part.at[s], x_out.at[s], x_sems.at[s])

    def out_copies(s, other):
        rows = rows_of(s, other)
        return (
            pltpu.make_async_copy(qkv.at[rows], qkv_out.at[rows], qkv_sems.at[other, s]),
            pltpu.make_async_copy(n1.at[rows], n1_out.at[rows], n1_sems.at[other, s]),
        )

    def product(first, second, other):
        both = jnp.concatenate([n1[rows_of(first, other), :], n1[rows_of(second, other), :]], 0)
        found = dot(both, weight[...], 1, 0).astype(bf16)
        for at, s in enumerate((first, second)):
            qkv[rows_of(s, other), :] = found[at * sub : (at + 1) * sub]
            for copy in out_copies(s, other):
                copy.start()

    def body(group, _):
        @pl.when(group < n_seq // 2)
        def _():
            places = block_of(2 * group), block_of(2 * group + 1)
            for s in places:
                moves.wait_block(s)
                x_copy(s).start()
                unit, _s = norm_parts(x_part[s].astype(f32))
                n1[rows_of(s, 0), :] = (unit * gain_ref[...]).astype(bf16)
                n1_copy(s).start()
            product(*places, 0)

        @pl.when(group > 0)
        def _():
            places = block_of(2 * group - 2), block_of(2 * group - 1)
            for s in places:
                n1_copy(s).wait()
            product(*places, 1)

        return 0

    lax.fori_loop(0, n_seq // 2 + 1, body, 0)

    def finish(s, _):
        x_copy(s).wait()
        for other in range(2):
            for copy in out_copies(s, other):
                copy.wait()
        return 0

    lax.fori_loop(0, n_seq, finish, 0)
    moves.wait_sends()
    for copy in weights_out:
        copy.wait()


def begin(inputs, qkv_weight, gain):
    row_count, block, width = inputs.shape
    n_seq = CORES * row_count
    lanes = 2 * HDIM
    pairs = width // (CORES * lanes)
    sub = block // CORES
    tokens = n_seq * sub
    hbm = pl.BlockSpec(memory_space=pl.ANY)
    return pl.pallas_call(
        functools.partial(begin_kernel, row_count, pairs),
        in_specs=[hbm, hbm, pl.BlockSpec(memory_space=pltpu.VMEM)],
        out_specs=[hbm] * 5,
        out_shape=[
            jax.ShapeDtypeStruct((n_seq, sub, width), bf16),
            jax.ShapeDtypeStruct((CORES * tokens, width), bf16),
            jax.ShapeDtypeStruct((CORES * tokens, 3 * pairs * lanes), bf16),
            jax.ShapeDtypeStruct((width, 3 * pairs * lanes), bf16),
            jax.ShapeDtypeStruct((width, 3 * pairs * lanes), bf16),
        ],
        scratch_shapes=[
            pltpu.VMEM((n_seq, sub, width), bf16),
            pltpu.VMEM((CORES * tokens, width), bf16),
            pltpu.VMEM((CORES * tokens, 3 * pairs * lanes), bf16),
            pltpu.VMEM((width, 3 * pairs * lanes), bf16),
            pltpu.VMEM((width, 3 * pairs * lanes), bf16),
            pltpu.SemaphoreType.DMA((row_count, CORES)),
            pltpu.SemaphoreType.DMA((n_seq,)),
            pltpu.SemaphoreType.DMA,
            pltpu.SemaphoreType.DMA((n_seq,)),
            pltpu.SemaphoreType.DMA((n_seq,)),
            pltpu.SemaphoreType.DMA((2, 3 * pairs)),
            pltpu.SemaphoreType.DMA((2,)),
            pltpu.SemaphoreType.DMA((n_seq,)),
            pltpu.SemaphoreType.DMA((CORES, n_seq)),
            pltpu.SemaphoreType.DMA((CORES, n_seq)),
        ],
        compiler_params=pltpu.CompilerParams(
            vmem_limit_bytes=vmem_bytes, collective_id=3, has_side_effects=True
        ),
        name="begin",
    )(inputs.reshape(row_count, CORES, sub, width), qkv_weight, gain.reshape(1, width))


def with_cells(value, tags, head, is_key):
    lane = lax.broadcasted_iota(jnp.int32, value.shape, 1)
    cell = lane - (1 - head) * HDIM
    if is_key:
        marks = jnp.where((cell == tags) | (cell >= max_cells), 0.0, -1.0)
    else:
        marks = jnp.where(cell == tags, -masked_score, 0.0)
    return jnp.where((lane // HDIM) == head, value, marks.astype(bf16))


def attend_row_kernel(
    tile, row_count, tags, row_tags, q_ref, k_ref, v_ref, cot_ref, o_ref, lse_ref, cot_out, own_out,
    v_turned, keys, scores_ref, mixed_ref, parts,
    cot_send, cot_recv, cot_local, part_send, part_recv, part_local,
):
    item, last = pl.program_id(0), pl.num_programs(0) - 1
    seq_at, rows_at = lax.axis_index("seq"), lax.axis_index("rows")
    core = rows_at % CORES
    tokens, lanes = q_ref.shape
    own_tokens = tokens // CORES
    n_seq = cot_out.shape[0]
    moves = ToRows(cot_ref, cot_out, cot_send, cot_recv, cot_local, row_count, seq_at, rows_at)

    def part_copies(at):
        slot = at % 2
        half = pl.num_programs(0) * lanes
        columns = pl.ds(pl.multiple_of(core * half + at * lanes, lanes), lanes)
        return (
            pltpu.make_async_remote_copy(
                src_ref=parts.at[slot, pl.ds(own_tokens, own_tokens)],
                dst_ref=own_out.at[:, columns],
                send_sem=part_send.at[slot],
                recv_sem=part_recv.at[at],
                device_id=(seq_at, rows_at + 1 - 2 * core),
                device_id_type=MESH,
            ),
            pltpu.make_async_copy(parts.at[slot, pl.ds(0, own_tokens)], own_out.at[:, columns], part_local.at[slot]),
        )

    def part_came(at):
        half = pl.num_programs(0) * lanes
        columns = pl.ds(pl.multiple_of((1 - core) * half + at * lanes, lanes), lanes)
        return pltpu.make_async_remote_copy(
            src_ref=parts.at[0, pl.ds(own_tokens, own_tokens)],
            dst_ref=own_out.at[:, columns],
            send_sem=part_send.at[0],
            recv_sem=part_recv.at[at],
            device_id=(seq_at, rows_at + 1 - 2 * core),
            device_id_type=MESH,
        )

    @pl.when(item == 0)
    def _():
        all_signal(n_seq, seq_at, rows_at)
        moves.start()

    for head in range(2):
        keys[head] = with_cells(k_ref[...], tags[...], head, True)
        v_turned[head, :HDIM, :] = v_ref[...].T[head * HDIM : (head + 1) * HDIM, :]
        v_turned[head, HDIM:, :] = jnp.ones((16, tokens), bf16)

    def begin_scores(step, head):
        part = pl.ds(pl.multiple_of(step * tile, tile), tile)
        scores_ref[head] = dot(keys[head], with_cells(q_ref[part, :], tags[part, :], head, False), 1, 1)

    def finish(step, head):
        part = pl.ds(pl.multiple_of(step * tile, tile), tile)
        scores = scores_ref[head]
        peak = jnp.max(scores, axis=0, keepdims=True)
        powers = jnp.exp2((scores - peak) * (score_scale * log2e))
        mixed = dot(v_turned[head], powers.astype(bf16), 1, 0)
        total = mixed[HDIM : HDIM + 1, :]
        mixed_ref[head * HDIM : (head + 1) * HDIM, part] = mixed[:HDIM, :] * (1.0 / total)
        lse = peak * (score_scale * log2e) + jnp.log2(total)
        lse_ref[head : head + 1, part] = jnp.where(row_tags[:, part] < 0, -masked_score, lse)

    steps = tokens // tile
    begin_scores(0, 0)

    def body(step, _):
        begin_scores(step, 1)
        finish(step, 0)
        begin_scores(jnp.minimum(step + 1, steps - 1), 0)
        finish(step, 1)
        return 0

    lax.fori_loop(0, steps, body, 0)
    found = jnp.where(tags[...] < 0, v_ref[...], mixed_ref[...].T.astype(bf16))
    o_ref[...] = found

    @pl.when(item >= 2)
    def _():
        remote, local = part_copies(item - 2)
        remote.wait_send()
        local.wait()

    parts[item % 2] = found
    for copy in part_copies(item):
        copy.start()

    @pl.when(item == last)
    def _():
        for at in range(2):
            remote, local = part_copies(last - at)
            remote.wait_send()
            local.wait()
        for at in range(part_recv.shape[0]):
            part_came(at).wait_recv()
        for s in range(n_seq):
            moves.wait_block(s)
        moves.wait_sends()


def attend_row(qkv, tags, row_tags, cotangent):
    tokens, width = qkv.shape
    row_count, block, model = cotangent.shape
    lanes = 2 * HDIM
    pairs = width // (3 * lanes)
    tile = 512
    n_seq, sub = CORES * row_count, block // CORES
    hbm = pl.BlockSpec(memory_space=pl.ANY)

    def columns(place):
        return pl.BlockSpec((tokens, lanes), lambda i: (0, 3 * i + place))

    return pl.pallas_call(
        functools.partial(attend_row_kernel, tile, row_count),
        grid=(pairs,),
        in_specs=[
            pl.BlockSpec((tokens, 1), lambda i: (0, 0)),
            pl.BlockSpec((1, tokens), lambda i: (0, 0)),
            columns(0),
            columns(1),
            columns(2),
            hbm,
        ],
        out_specs=[
            pl.BlockSpec((tokens, lanes), lambda i: (0, i)),
            pl.BlockSpec((None, 2, tokens), lambda i: (i, 0, 0)),
            hbm,
            hbm,
        ],
        out_shape=[
            jax.ShapeDtypeStruct((tokens, pairs * lanes), bf16),
            jax.ShapeDtypeStruct((pairs, 2, tokens), f32),
            jax.ShapeDtypeStruct((n_seq, sub, model), bf16),
            jax.ShapeDtypeStruct((tokens // CORES, model), bf16),
        ],
        scratch_shapes=[
            pltpu.VMEM((2, HDIM + 16, tokens), bf16),
            pltpu.VMEM((2, tokens, lanes), bf16),
            pltpu.VMEM((2, tokens, tile), f32),
            pltpu.VMEM((lanes, tokens), f32),
            pltpu.VMEM((2, tokens, lanes), bf16),
            pltpu.SemaphoreType.DMA((row_count, CORES)),
            pltpu.SemaphoreType.DMA((n_seq,)),
            pltpu.SemaphoreType.DMA,
            pltpu.SemaphoreType.DMA((2,)),
            pltpu.SemaphoreType.DMA((pairs,)),
            pltpu.SemaphoreType.DMA((2,)),
        ],
        compiler_params=pltpu.CompilerParams(
            vmem_limit_bytes=vmem_bytes, collective_id=4, has_side_effects=True
        ),
        name="attend_row",
    )(tags, row_tags, qkv, qkv, qkv, cotangent.reshape(row_count, CORES, sub, model))


piece_rows = 16


def feed_kernel(
    tiles,
    rows,
    middle_ref,
    cot_ref,
    gain_ref,
    up_ref,
    down_ref,
    mixed_ref,
    out_weight_ref,
    out_ref,
    d_middle_ref,
    d_attn_out,
    d_mixed_out,
    out_kept,
    out_came,
    down_part,
    up_part,
    n2,
    total,
    d_attn,
    d_attn_other,
    out_weight,
    out_keep,
    out_send,
    d_mixed,
    down_keep,
    down_send,
    down_recv,
    up_keep,
    up_send,
    up_recv,
    down_far_keep,
    down_far_send,
    down_far_recv,
    up_far_keep,
    up_far_send,
    up_far_recv,
    up_last_keep,
    up_last_send,
    up_last_recv,
    core_send_sem,
    core_recv_sem,
    far_send_sem,
    far_recv_sem,
    core_free,
    far_free,
    d_attn_sems,
    last_send_sem,
    last_recv_sem,
    out_sems,
):
    step = pl.program_id(0)
    tokens, width = n2.shape
    half = width // 2
    seq_at, rows_at = lax.axis_index("seq"), lax.axis_index("rows")
    core, high, low, mid = rows_at % 2, (rows_at // 2) % 2, seq_at % 2, (seq_at // 2) % 2
    core_peer = (seq_at, rows_at + 1 - 2 * core)
    far_peers = ((seq_at, rows_at + 2 - 4 * high), (seq_at + 1 - 2 * low, rows_at))
    last_peer = (seq_at + 2 - 4 * mid, rows_at)

    def copies(slot, far):
        if far:
            refs = ((down_far_send, down_far_recv), (up_far_send, up_far_recv))
            sems, peers = (far_send_sem, far_recv_sem), far_peers
        else:
            refs = ((down_send, down_recv), (up_send, up_recv))
            sems, peers = (core_send_sem, core_recv_sem), (core_peer, core_peer)
        return [
            pltpu.make_async_remote_copy(
                src_ref=refs[kind][0].at[slot],
                dst_ref=refs[kind][1].at[slot],
                send_sem=sems[0].at[kind, slot],
                recv_sem=sems[1].at[kind, slot],
                device_id=peers[kind],
                device_id_type=MESH,
            )
            for kind in range(2)
        ]

    def signal(sem, peer):
        pl.semaphore_signal(sem, inc=1, device_id=peer, device_id_type=MESH)

    @pl.when(step == 0)
    def _():
        barrier = pltpu.get_barrier_semaphore()
        for peer in (core_peer,) + far_peers + (last_peer,):
            signal(barrier, peer)
        pl.semaphore_wait(barrier, 4)

        def body(i, _):
            part = pl.ds(pl.multiple_of(i * rows, rows), rows)
            unit, _s = norm_parts(middle_ref[part, :])
            n2[part, :] = (unit * gain_ref[...]).astype(bf16)
            return 0

        lax.fori_loop(0, tokens // rows, body, 0)
        total[...] = middle_ref[...]
        d_middle_ref[...] = jnp.zeros_like(d_middle_ref)

    @pl.when(step < tiles)
    def _():
        up_w, down_w = up_ref[...], down_ref[...]
        up = dot(n2[...], up_w, 1, 0)
        d_act = dot(cot_ref[...], down_w, 1, 1)
        share = 0.5 + 0.5 * lax.erf(up * (0.5**0.5))
        density = jnp.exp(-0.5 * up * up) * 0.3989422804014327
        act = (up * share).astype(bf16)
        d_up = (d_act * (share + up * density)).astype(bf16)
        total[...] += dot(act, down_w, 1, 0)
        d_middle_ref[...] += dot(d_up, up_w, 1, 1)
        slot = step % 2

        @pl.when(step >= 2)
        def _():
            for copy in copies(slot, False):
                copy.wait_send()

        up_grad = dot(n2[...], d_up, 0, 0).astype(bf16)
        cut = up_grad.shape[1] // 2

        @pl.when(core == 0)
        def _():
            up_keep[slot] = up_grad[:, :cut].reshape(up_keep.shape[1:])
            up_send[slot] = up_grad[:, cut:].reshape(up_keep.shape[1:])

        @pl.when(core != 0)
        def _():
            up_keep[slot] = up_grad[:, cut:].reshape(up_keep.shape[1:])
            up_send[slot] = up_grad[:, :cut].reshape(up_keep.shape[1:])

        down_grad = dot(act, cot_ref[...], 0, 0).astype(bf16)

        @pl.when(core == 0)
        def _():
            down_keep[slot] = down_grad[:, :half].reshape(down_keep.shape[1:])
            down_send[slot] = down_grad[:, half:].reshape(down_keep.shape[1:])

        @pl.when(core != 0)
        def _():
            down_keep[slot] = down_grad[:, half:].reshape(down_keep.shape[1:])
            down_send[slot] = down_grad[:, :half].reshape(down_keep.shape[1:])

    def add(a, b):
        return (a.astype(f32) + b.astype(f32)).astype(bf16)

    def last_copy(slot):
        return pltpu.make_async_remote_copy(
            src_ref=up_last_send.at[slot],
            dst_ref=up_last_recv.at[slot],
            send_sem=last_send_sem.at[slot],
            recv_sem=last_recv_sem.at[slot],
            device_id=last_peer,
            device_id_type=MESH,
        )

    def last_add():
        slot = (step + 1) % 2
        last_copy(slot).wait_recv()
        up_part[...] = add(up_last_keep[slot], up_last_recv[slot]).reshape(up_part.shape)

    def far_add():
        slot = step % 2
        for copy in copies(slot, True):
            copy.wait_recv()
        down_part[...] = add(down_far_keep[slot], down_far_recv[slot]).reshape(down_part.shape)

        @pl.when(step >= 4)
        def _():
            last_copy(slot).wait_send()

        up_last_send[slot] = add(up_far_keep[slot, :, 1 - mid], up_far_recv[slot, :, 1 - mid])
        up_last_keep[slot] = add(up_far_keep[slot, :, mid], up_far_recv[slot, :, mid])
        last_copy(slot).start()

        @pl.when(step < tiles)
        def _():
            signal(far_free.at[0], far_peers[0])
            signal(far_free.at[1], far_peers[1])

    def pass_on():
        slot = (step + 1) % 2
        for copy in copies(slot, False):
            copy.wait_recv()

        @pl.when(step >= 3)
        def _():
            for copy in copies(slot, True):
                copy.wait_send()
            pl.semaphore_wait(far_free.at[0], 1)
            pl.semaphore_wait(far_free.at[1], 1)

        down_far_send[slot] = add(down_keep[slot, :, 1 - high], down_recv[slot, :, 1 - high])
        down_far_keep[slot] = add(down_keep[slot, :, high], down_recv[slot, :, high])
        shape = up_far_send.shape[1:]
        up_far_send[slot] = add(up_keep[slot, :, 1 - low], up_recv[slot, :, 1 - low]).reshape(shape)
        up_far_keep[slot] = add(up_keep[slot, :, low], up_recv[slot, :, low]).reshape(shape)
        for copy in copies(slot, True):
            copy.start()

        @pl.when(step < tiles - 1)
        def _():
            signal(core_free, core_peer)

    @pl.when((step >= 3) & (step <= tiles + 1))
    def _():
        last_add()

    @pl.when((step >= 2) & (step <= tiles))
    def _():
        far_add()

    @pl.when((step >= 1) & (step <= tiles))
    def _():
        pass_on()

    @pl.when(step < tiles)
    def _():
        @pl.when(step >= 2)
        def _():
            pl.semaphore_wait(core_free, 1)

        for copy in copies(step % 2, False):
            copy.start()

    @pl.when(step == tiles)
    def _():
        def body(i, _):
            part = pl.ds(pl.multiple_of(i * rows, rows), rows)
            out_ref[part, :] = total[part, :].astype(bf16)
            unit, scale = norm_parts(middle_ref[part, :])
            grad = cot_ref[part, :].astype(f32) + norm_back(d_middle_ref[part, :], gain_ref[...], unit, scale)
            d_middle_ref[part, :] = grad
            d_attn[part, :] = grad.astype(bf16)
            return 0

        lax.fori_loop(0, tokens // rows, body, 0)

    def to_core(source, target, at):
        return pltpu.make_async_remote_copy(
            src_ref=source,
            dst_ref=target,
            send_sem=d_attn_sems.at[at],
            recv_sem=d_attn_sems.at[at + 1],
            device_id=core_peer,
            device_id_type=MESH,
        )

    d_attn_copy = lambda: to_core(d_attn, d_attn_other, 0)
    out_copy = lambda: to_core(out_send, out_came, 2)
    mixed_copy = lambda: pltpu.make_async_copy(mixed_ref, n2, out_sems.at[0])
    weight_copy = lambda: pltpu.make_async_copy(
        out_weight_ref.at[pl.ds(pl.multiple_of(core * half, half), half)], out_weight, out_sems.at[1]
    )
    d_attn_save = lambda: pltpu.make_async_copy(d_attn, d_attn_out, out_sems.at[2])
    out_save = lambda: pltpu.make_async_copy(out_keep, out_kept, out_sems.at[3])
    d_mixed_save = lambda: pltpu.make_async_copy(d_mixed, d_mixed_out, out_sems.at[4])

    @pl.when(step == tiles)
    def _():
        d_attn_copy().start()
        d_attn_save().start()
        mixed_copy().start()
        weight_copy().start()

    @pl.when(step == tiles + 1)
    def _():
        mixed_copy().wait()
        grad = dot(n2[...], d_attn[...], 0, 0).astype(bf16)

        @pl.when(core == 0)
        def _():
            out_keep[...] = grad[:, :half]
            out_send[...] = grad[:, half:]

        @pl.when(core != 0)
        def _():
            out_keep[...] = grad[:, half:]
            out_send[...] = grad[:, :half]

        out_copy().start()
        out_save().start()
        far_add()

    @pl.when(step == tiles + 2)
    def _():
        weight_copy().wait()
        d_attn_copy().wait()
        d_mixed[:tokens, :] = dot(d_attn[...], out_weight[...], 1, 1).astype(bf16)
        d_mixed[tokens:, :] = dot(d_attn_other[...], out_weight[...], 1, 1).astype(bf16)
        d_mixed_save().start()
        last_add()
        out_copy().wait()
        for copy in (d_attn_save(), out_save(), d_mixed_save()):
            copy.wait()
        for slot in range(2):
            last_copy(slot).wait_send()
            for far in (False, True):
                for copy in copies(slot, far):
                    copy.wait_send()


def feed(middle, cot, gain, up_weight, down_weight, mixed_own, out_weight, n_seq):
    tokens, width = middle.shape
    wide = up_weight.shape[1]
    tile = feed_tile
    tiles = wide // tile
    half, shard = width // 2, width // n_seq
    whole = lambda dtype: jax.ShapeDtypeStruct((tokens, width), dtype)
    fixed = lambda shape: pl.BlockSpec(shape, lambda i: (0, 0), pipeline_mode=pl.Buffered(1))
    at = lambda i: jnp.minimum(i, tiles - 1)
    hbm = pl.BlockSpec(memory_space=pl.ANY)
    late = lambda i: jnp.clip(i - 2, 0, tiles - 1)
    down_shape = (2, tile // (2 * piece_rows), 2, piece_rows, half)
    up_shape = (2, n_seq // 2, 2, shard, tile // 2)
    near = [pltpu.VMEM(down_shape, bf16)] * 3 + [pltpu.VMEM(up_shape, bf16)] * 3
    up_far = (2, n_seq // 4, 2, shard, tile // 2)
    far = [pltpu.VMEM(down_shape[:2] + down_shape[3:], bf16)] * 3 + [pltpu.VMEM(up_far, bf16)] * 3
    far += [pltpu.VMEM(up_far[:2] + up_far[3:], bf16)] * 3
    return pl.pallas_call(
        functools.partial(feed_kernel, tiles, 128),
        grid=(tiles + 3,),
        in_specs=[
            fixed((tokens, width)),
            fixed((tokens, width)),
            fixed((1, width)),
            pl.BlockSpec((width, tile), lambda i: (0, at(i))),
            pl.BlockSpec((tile, width), lambda i: (at(i), 0)),
            hbm,
            hbm,
        ],
        out_specs=[
            fixed((tokens, width)),
            fixed((tokens, width)),
            hbm,
            hbm,
            hbm,
            hbm,
            pl.BlockSpec((tile // 2, half), lambda i: (late(i), 0)),
            pl.BlockSpec((width // 4, tile // 2), lambda i: (0, jnp.maximum(i - 3, 0))),
        ],
        scratch_shapes=[
            pltpu.VMEM((tokens, width), bf16),
            pltpu.VMEM((tokens, width), f32),
            pltpu.VMEM((tokens, width), bf16),
            pltpu.VMEM((tokens, width), bf16),
            pltpu.VMEM((half, width), bf16),
            pltpu.VMEM((width, half), bf16),
            pltpu.VMEM((width, half), bf16),
            pltpu.VMEM((2 * tokens, half), bf16),
        ]
        + near
        + far
        + [pltpu.SemaphoreType.DMA((2, 2))] * 4
        + [pltpu.SemaphoreType.REGULAR, pltpu.SemaphoreType.REGULAR((2,)), pltpu.SemaphoreType.DMA((4,))]
        + [pltpu.SemaphoreType.DMA((2,))] * 2
        + [pltpu.SemaphoreType.DMA((5,))],
        out_shape=[
            whole(bf16),
            whole(f32),
            whole(bf16),
            jax.ShapeDtypeStruct((2 * tokens, half), bf16),
            jax.ShapeDtypeStruct((width, half), bf16),
            jax.ShapeDtypeStruct((width, half), bf16),
            jax.ShapeDtypeStruct((wide // 2, half), bf16),
            jax.ShapeDtypeStruct((width // 4, wide // 2), bf16),
        ],
        compiler_params=pltpu.CompilerParams(
            vmem_limit_bytes=feed_vmem_bytes, collective_id=1, has_side_effects=True
        ),
        cost_estimate=pl.CostEstimate(
            flops=12 * tokens * width * wide,
            bytes_accessed=16 * tokens * width + 6 * width * wide,
            transcendentals=2 * tokens * wide,
        ),
        name="feed",
    )(middle, cot, gain.reshape(1, width), up_weight, down_weight, mixed_own, out_weight)


class Stream:
    def __init__(self, levels, rows, columns, first, count, lag):
        self.levels, self.rows, self.columns, self.first, self.count = levels, rows, columns, first, count
        self.lag = lag

    def shape(self, level):
        outer = 2 ** (len(self.levels) - 1 - level)
        return (max(outer // 2, 1), min(outer, 2), self.rows, self.columns)

    def scratch(self):
        shapes = []
        for level in range(len(self.levels)):
            shape = self.shape(level)
            shapes += [pltpu.VMEM(shape, bf16), pltpu.VMEM(shape, bf16), pltpu.VMEM((2,) + shape, bf16)]
        return shapes


down_pieces = 4


def streams_of(width, wide, n_seq, pairs):
    lanes = 2 * HDIM
    rows = width // (2 * n_seq)
    return (
        Stream(("x", "y", "z1", "z2"), rows, 4 * lanes, 1, pairs, 2),
        Stream(("y", "z1", "z2"), wide // (2 * n_seq * down_pieces), width // CORES, 2, down_pieces, 1),
        Stream(("x", "z2"), rows, wide // CORES // down_pieces, 2, down_pieces, 1),
    )


def back_kernel(pairs, tile, streams, row_count, *refs):
    (
        key_tags, query_tags, q_ref, k_ref, v_ref, o_ref, do_ref, lse_ref, n1_ref, own_weight, other_weight,
        gain_ref, out_kept, out_came, down_ref, up_ref, start_ref, d_middle_ref, outputs_ref,
    ) = refs[:19]
    grad_out, outputs_out, *gathered = refs[19:24]
    rest = list(refs[24:])
    take = lambda count: [rest.pop(0) for _ in range(count)]
    k_turned, dq_turned, delta, d_pair, d_came, d_n1, staged, start_part, middle_part = take(9)
    levels = []
    for stream in streams:
        levels.append([take(3) for _ in stream.levels])
    joined = take(len(streams))
    (
        send_sems, recv_sems, join_send, join_recv, core_send, core_recv, local_sems,
        pair_send, pair_recv, home_send, home_recv, home_local, part_sems, result_send, result_recv, result_local,
    ) = rest

    step = pl.program_id(0)
    tokens, lanes = q_ref.shape
    own_tokens = tokens // CORES
    seq_at, rows_at = lax.axis_index("seq"), lax.axis_index("rows")
    core, high = rows_at % 2, (rows_at // 2) % 2
    places = {"x": high, "y": seq_at % 2, "z1": (seq_at // 2) % 2, "z2": seq_at // 4}
    peers = {
        "x": (seq_at, rows_at + 2 - 4 * high),
        "y": (seq_at + 1 - 2 * places["y"], rows_at),
        "z1": (seq_at + 2 - 4 * places["z1"], rows_at),
        "z2": (seq_at + 4 - 8 * places["z2"], rows_at),
        "core": (seq_at, rows_at + 1 - 2 * core),
    }
    n_seq = 2 * row_count
    sub = start_part.shape[1]

    def remote(source, target, send, recv, peer):
        return pltpu.make_async_remote_copy(
            src_ref=source, dst_ref=target, send_sem=send, recv_sem=recv, device_id=peer, device_id_type=MESH
        )

    def add(a, b):
        return (a.astype(f32) + b.astype(f32)).astype(bf16)

    def level_copy(at, level, item):
        send, _, came = levels[at][level]
        slot = item % 2
        return remote(
            send, came.at[slot], send_sems.at[at, level], recv_sems.at[at, level, slot], peers[streams[at].levels[level]]
        )

    def join_copy(at, item):
        part = joined[at].at[item, high]
        return remote(part, part, join_send.at[at], join_recv.at[at, item % 2], peers["x"])

    def core_copy(at, item):
        return remote(
            joined[at].at[item],
            gathered[at].at[item, core],
            core_send.at[at],
            core_recv.at[at, item % 2],
            peers["core"],
        )

    def local_copy(at, item):
        return pltpu.make_async_copy(joined[at].at[item], gathered[at].at[item, core], local_sems.at[at])

    def pair_copy(item):
        slot = item % 2
        return remote(
            d_pair.at[slot, pl.ds(own_tokens, own_tokens)],
            d_came.at[slot],
            pair_send.at[slot],
            pair_recv.at[slot],
            peers["core"],
        )

    home = seq_at // row_count

    def to_home(block, own, result):
        if result:
            source, target = outputs_ref.at[pl.ds(pl.multiple_of(block * sub, sub), sub)], outputs_out
            sems = result_send, result_recv, result_local
        else:
            source, target = staged.at[block], grad_out
            sems = home_send, home_recv, home_local
        row = seq_at % row_count
        if own:
            return pltpu.make_async_copy(source, target.at[row, core], sems[2])
        return remote(source, target.at[row, core], sems[0].at[block], sems[1].at[row, core], (block, rows_at - core + home))

    def start_home(block, result):
        @pl.when(is_own(block))
        def _():
            to_home(block, True, result).start()

        @pl.when(jnp.logical_not(is_own(block)))
        def _():
            to_home(block, False, result).start()

    def wait_home(result):
        for block in range(n_seq):
            @pl.when(is_own(block))
            def _():
                to_home(block, True, result).wait()

            @pl.when(jnp.logical_not(is_own(block)))
            def _():
                to_home(block, False, result).wait_send()
        source, target = (outputs_ref.at[pl.ds(0, sub)], outputs_out) if result else (staged.at[0], grad_out)
        sems = (result_send, result_recv) if result else (home_send, home_recv)
        for row in range(row_count):
            for c in range(CORES):
                @pl.when(jnp.logical_not((seq_at == core * row_count + row) & (core == c)))
                def _():
                    remote(source, target.at[row, c], sems[0].at[0], sems[1].at[row, c], peers["core"]).wait_recv()

    def is_own(block):
        return (seq_at == block) & (home == core)

    @pl.when(step == 0)
    def _():
        barrier = pltpu.get_barrier_semaphore()
        for s in range(n_seq):
            for c in range(CORES):
                @pl.when(jnp.logical_not((seq_at == s) & (core == c)))
                def _():
                    pl.semaphore_signal(barrier, inc=1, device_id=(s, rows_at - core + c), device_id_type=MESH)
        pl.semaphore_signal(barrier, inc=1, device_id=peers["x"], device_id_type=MESH)
        pl.semaphore_wait(barrier, n_seq * CORES)
        d_n1[...] = jnp.zeros_like(d_n1)

    @pl.when(step < n_seq)
    def _():
        start_home((seq_at + step) % n_seq, True)

    working, second = step < 2 * pairs, step % 2

    @pl.when(working & (second == 0))
    def _():
        k_turned[...] = k_ref[...].T
        dq_turned[...] = (o_ref[...].astype(f32) * do_ref[...].astype(f32)).T
        for head in range(2):
            own_rows = dq_turned[head * HDIM : (head + 1) * HDIM, :]
            delta[head : head + 1, :] = jnp.sum(own_rows, axis=0, keepdims=True)
        dq_turned[...] = jnp.zeros_like(dq_turned)

    @pl.when(working)
    def _():
        slot = step // 2 % 2
        half_steps = tokens // tile // 2
        first = lax.broadcasted_iota(jnp.int32, (tile, lanes), 1) < HDIM

        def body(i, _):
            part = pl.ds(pl.multiple_of((i + second * half_steps) * tile, tile), tile)
            k, v = k_ref[part, :], v_ref[part, :]
            q, do = q_ref[...], do_ref[...]
            tag = key_tags[part, :]
            allowed = tag == query_tags[...]
            dk, dv = [], []
            for head in range(2):
                own = first if head == 0 else jnp.logical_not(first)
                own_rows = slice(head * HDIM, (head + 1) * HDIM)
                scores = dot(jnp.where(own, k, bf16(0)), q, 1, 1)
                scores = jnp.where(allowed, scores, masked_score)
                chances = jnp.exp2(scores * (score_scale * log2e) - lse_ref[head : head + 1, :])
                weight_grad = dot(jnp.where(own, v, bf16(0)), do, 1, 1)
                score_grad = (chances * (weight_grad - delta[head : head + 1, :])).astype(bf16)
                dv.append(dot(chances.astype(bf16), do, 1, 0))
                dk.append(dot(score_grad, q, 1, 0))
                dq_turned[own_rows, :] += dot(k_turned[own_rows, part], score_grad, 1, 0)
            d_pair[slot, part, lanes : 2 * lanes] = (jnp.where(first, dk[0], dk[1]) * score_scale).astype(bf16)
            d_v = jnp.where(first, dv[0], dv[1]).astype(bf16)
            d_pair[slot, part, 2 * lanes :] = jnp.where(tag < 0, do_ref[part, :], d_v)
            return 0

        lax.fori_loop(0, half_steps, body, 0)

    @pl.when(working & (second == 1))
    def _():
        d_pair[step // 2 % 2, :, :lanes] = (dq_turned[...] * score_scale).T.astype(bf16)

    def add_pair():
        item = step // 2 - 1
        slot = item % 2
        pair_copy(item).wait()
        d_n1[...] += dot(d_pair[slot, :own_tokens, :], own_weight[...], 1, 1) + dot(
            d_came[slot], other_weight[...], 1, 1
        )

    @pl.when((step >= 2) & (step <= 2 * pairs) & (second == 0))
    def _():
        add_pair()

    @pl.when(working & (second == 1))
    def _():
        pair_copy(step // 2).start()

    def part_copies(turn):
        rows = pl.ds(pl.multiple_of((seq_at + turn) % n_seq * sub, sub), sub)
        slot = turn % 2
        return (
            pltpu.make_async_copy(start_ref.at[rows], start_part.at[slot], part_sems.at[0, slot]),
            pltpu.make_async_copy(d_middle_ref.at[rows], middle_part.at[slot], part_sems.at[1, slot]),
        )

    @pl.when(step == 2 * pairs)
    def _():
        for copy in part_copies(0):
            copy.start()

        def body(turn, _):
            block = (seq_at + turn) % n_seq

            @pl.when(turn + 1 < n_seq)
            def _():
                for copy in part_copies(turn + 1):
                    copy.start()

            for copy in part_copies(turn):
                copy.wait()
            unit, scale = norm_parts(start_part[turn % 2].astype(f32))
            rows = pl.ds(pl.multiple_of(block * sub, sub), sub)
            grad = norm_back(d_n1[rows, :], gain_ref[...], unit, scale)
            staged[block] = (middle_part[turn % 2] + grad).astype(bf16)
            start_home(block, False)
            return 0

        lax.fori_loop(0, n_seq, body, 0)

    for at, stream in enumerate(streams):
        depth = len(stream.levels)

        def item_at(lag, stream=stream):
            since = step - stream.first - lag
            return since // 2, (since >= 0) & (since % 2 == 0) & (since < 2 * stream.count)

        item, here = item_at(depth + 1 + stream.lag)

        @pl.when(here)
        def _(at=at, item=item):
            core_copy(at, item).wait()
            local_copy(at, item).wait()

        item, here = item_at(depth + stream.lag)

        @pl.when(here)
        def _(at=at, item=item):
            join_copy(at, item).wait()
            core_copy(at, item).start()
            local_copy(at, item).start()

        for level in reversed(range(depth)):
            item, here = item_at(level + stream.lag)

            @pl.when(here)
            def _(at=at, item=item, level=level, stream=stream, depth=depth):
                _, keep, came = levels[at][level]
                slot = item % 2
                level_copy(at, level, item).wait_recv()
                if level == depth - 1:
                    joined[at][item, high] = add(keep[0, 0], came[slot, 0, 0])
                    join_copy(at, item).start()
                    return

                @pl.when(item > 0)
                def _():
                    level_copy(at, level + 1, item - 1).wait_send()

                next_send, next_keep, _ = levels[at][level + 1]
                place = places[stream.levels[level + 1]]
                next_send[...] = add(keep[:, 1 - place], came[slot, :, 1 - place]).reshape(next_send.shape)
                next_keep[...] = add(keep[:, place], came[slot, :, place]).reshape(next_keep.shape)
                level_copy(at, level + 1, item).start()

    def begin_piece(fills):
        for at, fill in fills.items():
            stream = streams[at]
            item = (step - stream.first) // 2

            @pl.when((step % 2 == stream.first % 2) & (step >= stream.first) & (item < stream.count))
            def _(at=at, fill=fill, item=item):
                @pl.when(item > 0)
                def _():
                    level_copy(at, 0, item - 1).wait_send()

                fill(*levels[at][0][:2])
                level_copy(at, 0, item).start()

    def fill_pair(send, keep):
        grad = dot(n1_ref[...], d_pair[step // 2 % 2], 0, 0).astype(bf16)
        grad = grad.reshape(n_seq, 2, send.shape[2], 3 * lanes)
        shape = send.shape[:3] + (3 * lanes,)

        @pl.when(high == 0)
        def _():
            send[:, :, :, : 3 * lanes] = grad[:, 1].reshape(shape)
            keep[:, :, :, : 3 * lanes] = grad[:, 0].reshape(shape)

        @pl.when(high != 0)
        def _():
            send[:, :, :, : 3 * lanes] = grad[:, 0].reshape(shape)
            keep[:, :, :, : 3 * lanes] = grad[:, 1].reshape(shape)

        shape = send.shape[:3] + (lanes,)
        send[:, :, :, 3 * lanes :] = add(out_kept[:, 1 - high], out_came[:, 1 - high]).reshape(shape)
        keep[:, :, :, 3 * lanes :] = add(out_kept[:, high], out_came[:, high]).reshape(shape)

    def fill_from(ref, place):
        def fill(send, keep):
            send[...] = ref[:, 1 - place].reshape(send.shape)
            keep[...] = ref[:, place].reshape(keep.shape)

        return fill

    begin_piece({0: fill_pair, 1: fill_from(down_ref, places["y"]), 2: fill_from(up_ref, high)})

    @pl.when(step == pl.num_programs(0) - 1)
    def _():
        for at, stream in enumerate(streams):
            for level in range(len(stream.levels)):
                level_copy(at, level, stream.count - 1).wait_send()
        wait_home(False)
        wait_home(True)


def back(
    qkv, mixed, d_mixed, lse, key_tags, query_tags, n1, weights, gain, out_kept, out_came, down_part, up_part,
    start, d_middle, outputs, row_count,
):
    tokens = qkv.shape[0]
    width = n1.shape[1]
    own_tokens = tokens // CORES
    lanes = 2 * HDIM
    pairs = qkv.shape[1] // (3 * lanes)
    n_seq = 2 * row_count
    tile = 512
    sub = own_tokens // n_seq
    streams = streams_of(width, down_part.shape[0] * 2, n_seq, pairs)
    last = pairs - 1
    now = lambda i: jnp.minimum(i // 2, last)
    before = lambda i: jnp.clip(i // 2 - 1, 0, last)
    early = lambda i: jnp.clip(i // 2 - 1, 0, down_pieces - 1)
    fixed = lambda shape: pl.BlockSpec(shape, lambda i: (0,) * len(shape), pipeline_mode=pl.Buffered(1))

    def columns(place):
        return pl.BlockSpec((tokens, lanes), lambda i: (0, 3 * now(i) + place))

    pair = pl.BlockSpec((tokens, lanes), lambda i: (0, now(i)))
    weight = pl.BlockSpec((width, 3 * lanes), lambda i: (0, before(i)))
    hbm = pl.BlockSpec(memory_space=pl.ANY)

    rows = streams[0].rows

    def out_piece(value):
        whole = value.reshape(n_seq, 2, rows, value.shape[1])
        return whole, pl.BlockSpec((n_seq, 2, rows, lanes), lambda i: (0, 0, 0, now(i)))

    outs = [out_piece(value) for value in (out_kept, out_came)]
    down = down_part.reshape(n_seq // 2, 2, -1, width // CORES)
    up = up_part.reshape(n_seq // 4, 2, rows, -1)
    down_spec = pl.BlockSpec((n_seq // 2, 2, streams[1].rows, width // CORES), lambda i: (0, 0, early(i), 0))
    up_spec = pl.BlockSpec((n_seq // 4, 2, rows, streams[2].columns), lambda i: (0, 0, 0, early(i)))
    count = len(streams)
    deepest = max(len(stream.levels) for stream in streams)
    return pl.pallas_call(
        functools.partial(back_kernel, pairs, tile, streams, row_count),
        grid=(2 * pairs + deepest + 1 + streams[0].lag,),
        in_specs=[
            fixed((tokens, 1)),
            fixed((1, tokens)),
            columns(0),
            columns(1),
            columns(2),
            pair,
            pair,
            pl.BlockSpec((None, 2, tokens), lambda i: (now(i), 0, 0)),
            fixed((tokens, width)),
            weight,
            weight,
            fixed((1, width)),
            outs[0][1],
            outs[1][1],
            down_spec,
            up_spec,
            hbm,
            hbm,
            hbm,
        ],
        out_specs=[hbm] * 5,
        out_shape=[jax.ShapeDtypeStruct((row_count, CORES, sub, width), bf16)] * 2
        + [jax.ShapeDtypeStruct((stream.count, CORES, 2, stream.rows, stream.columns), bf16) for stream in streams],
        scratch_shapes=[
            pltpu.VMEM((lanes, tokens), bf16),
            pltpu.VMEM((lanes, tokens), f32),
            pltpu.VMEM((2, tokens), f32),
            pltpu.VMEM((2, tokens, 3 * lanes), bf16),
            pltpu.VMEM((2, own_tokens, 3 * lanes), bf16),
            pltpu.VMEM((own_tokens, width), f32),
            pltpu.VMEM((n_seq, sub, width), bf16),
            pltpu.VMEM((2, sub, width), bf16),
            pltpu.VMEM((2, sub, width), f32),
        ]
        + [shape for stream in streams for shape in stream.scratch()]
        + [pltpu.VMEM((stream.count, 2, stream.rows, stream.columns), bf16) for stream in streams]
        + [
            pltpu.SemaphoreType.DMA((count, deepest)),
            pltpu.SemaphoreType.DMA((count, deepest, 2)),
            pltpu.SemaphoreType.DMA((count,)),
            pltpu.SemaphoreType.DMA((count, 2)),
            pltpu.SemaphoreType.DMA((count,)),
            pltpu.SemaphoreType.DMA((count, 2)),
            pltpu.SemaphoreType.DMA((count,)),
            pltpu.SemaphoreType.DMA((2,)),
            pltpu.SemaphoreType.DMA((2,)),
            pltpu.SemaphoreType.DMA((n_seq,)),
            pltpu.SemaphoreType.DMA((row_count, CORES)),
            pltpu.SemaphoreType.DMA,
            pltpu.SemaphoreType.DMA((2, 2)),
            pltpu.SemaphoreType.DMA((n_seq,)),
            pltpu.SemaphoreType.DMA((row_count, CORES)),
            pltpu.SemaphoreType.DMA,
        ],
        compiler_params=pltpu.CompilerParams(
            vmem_limit_bytes=feed_vmem_bytes, collective_id=2, has_side_effects=True
        ),
        cost_estimate=pl.CostEstimate(
            flops=80 * pairs * tokens * tokens * HDIM,
            bytes_accessed=16 * tokens * pairs * lanes,
            transcendentals=2 * pairs * tokens * tokens,
        ),
        name="back",
    )(
        key_tags, query_tags, qkv, qkv, qkv, mixed, d_mixed, lse, n1, weights[0], weights[1],
        gain.reshape(1, width), outs[0][0], outs[1][0], down, up, start, d_middle, outputs,
    )


def collect_kernel(pairs, seq_ref, *refs):
    qkv_parts, down_parts, up_parts = refs[:3]
    qkv_weights, up_weight, first_gain, second_gain = refs[3:9], refs[9], refs[10], refs[11]
    qkv_out, out_out, down_out, up_out, first_out, second_out = refs[12:]
    item = pl.program_id(0)
    lanes = 2 * HDIM
    rows = qkv_parts.shape[2]
    width = out_out.shape[1]
    half = width // CORES
    tile = feed_tile // CORES

    @pl.when(item == 0)
    def _():
        first_out[...] = jnp.zeros_like(first_out)
        second_out[...] = jnp.zeros_like(second_out)

    for core in range(CORES):
        place = pl.multiple_of(core * half + item * lanes, lanes)
        for high in range(2):
            own = slice(high * rows, (high + 1) * rows)
            part = qkv_parts[core, high].astype(f32)
            for kind in range(3):
                value = part[:, kind * lanes : (kind + 1) * lanes]
                qkv_out[own, pl.ds(kind * width + place, lanes)] = value
                weight = qkv_weights[kind * CORES + core][own, :].astype(f32)
                first_out[own, :] += jnp.sum(value * weight, axis=1, keepdims=True)
            out_out[own, pl.ds(place, lanes)] = part[:, 3 * lanes :]

    @pl.when(item < down_pieces)
    def _():
        for core in range(CORES):
            for high in range(2):
                own = slice(high * rows, (high + 1) * rows)
                for at in range(up_parts.shape[3] // lanes):
                    column = item * up_parts.shape[3] + at * lanes
                    column = column // tile * feed_tile + core * tile + column % tile
                    columns = pl.ds(pl.multiple_of(column, lanes), lanes)
                    value = up_parts[core, high, :, at * lanes : (at + 1) * lanes].astype(f32)
                    up_out[own, columns] = value
                    second_out[own, :] += jnp.sum(value * up_weight[own, columns].astype(f32), axis=1, keepdims=True)
                count = down_parts.shape[2] // piece_rows
                for at in range(count):
                    start = ((item * count + at) * 2 + high) * piece_rows
                    value = down_parts[core, high, at * piece_rows : (at + 1) * piece_rows, :].astype(f32)
                    down_out[pl.ds(pl.multiple_of(start, piece_rows), piece_rows), core * half : (core + 1) * half] = value

    @pl.when(item == pairs - 1)
    def _():
        first_out[...] = first_out[...] / first_gain[...]
        second_out[...] = second_out[...] / second_gain[...]


def collect(seq_at, qkv_parts, down_parts, up_parts, qkv_weight, up_weight, first_gain, second_gain):
    pairs, _, _, rows, _ = qkv_parts.shape
    width, lanes = qkv_weight.shape[0], 2 * HDIM
    shard, wide = 2 * rows, up_weight.shape[1]
    down_rows = 2 * down_pieces * down_parts.shape[3]

    def parts(value):
        return pl.BlockSpec(
            (None,) + value.shape[1:], lambda i, seq: (jnp.minimum(i, value.shape[0] - 1), 0, 0, 0, 0)
        )

    def weight(kind, core):
        return pl.BlockSpec((shard, lanes), lambda i, seq: (seq[0], (kind * CORES + core) * pairs + i))

    gain = pl.BlockSpec((shard, 1), lambda i, seq: (seq[0], 0))
    whole = lambda shape: pl.BlockSpec(shape, lambda i, seq: (0, 0))
    return pl.pallas_call(
        functools.partial(collect_kernel, pairs),
        grid_spec=pltpu.PrefetchScalarGridSpec(
            num_scalar_prefetch=1,
            grid=(pairs,),
            in_specs=[parts(qkv_parts), parts(down_parts), parts(up_parts)]
            + [weight(kind, core) for kind in range(3) for core in range(CORES)]
            + [pl.BlockSpec((shard, wide), lambda i, seq: (seq[0], 0)), gain, gain],
            out_specs=[
                whole((shard, 3 * width)),
                whole((shard, width)),
                whole((down_rows, width)),
                whole((shard, wide)),
                whole((shard, 1)),
                whole((shard, 1)),
            ],
        ),
        out_shape=[
            jax.ShapeDtypeStruct((shard, 3 * width), f32),
            jax.ShapeDtypeStruct((shard, width), f32),
            jax.ShapeDtypeStruct((down_rows, width), f32),
            jax.ShapeDtypeStruct((shard, wide), f32),
            jax.ShapeDtypeStruct((shard, 1), f32),
            jax.ShapeDtypeStruct((shard, 1), f32),
        ],
        compiler_params=pltpu.CompilerParams(vmem_limit_bytes=vmem_bytes),
        name="collect",
    )(
        seq_at.reshape(1), qkv_parts, down_parts, up_parts, *[qkv_weight] * 6, up_weight,
        first_gain.reshape(width, 1), second_gain.reshape(width, 1),
    )


def add_split_kernel(has_two, bit_ref, *refs):
    ins, outs = refs[: 2 if has_two else 1], refs[2 if has_two else 1 :]
    value = ins[0][...]
    if has_two:
        value = (value.astype(f32) + ins[1][...].astype(f32)).astype(bf16)
    if len(outs) == 1:
        outs[0][...] = value
    else:
        sends = pl.program_id(0) == 0

        @pl.when(sends)
        def _():
            outs[0][...] = value

        @pl.when(jnp.logical_not(sends))
        def _():
            outs[1][...] = value


def add_split(kept, received, inner, bit):
    rows, columns = kept.shape
    values = [kept] if received is None else [kept, received.reshape(rows, columns)]
    if bit is None:
        if received is None:
            return None, kept
        count = 4 if rows % 64 == 0 else 1
        block = pl.BlockSpec((rows // count, columns), lambda i, bit: (i, 0))
        grid, ins, outs = (count,), [block] * 2, block
        shapes = jax.ShapeDtypeStruct((rows, columns), bf16)
        bit = jnp.zeros((), jnp.int32)
    else:
        outer = rows // (2 * inner)
        cut = 1
        while inner // cut * columns > 2**19 and inner % (32 * cut) == 0:
            cut *= 2
        values = [value.reshape(outer, 2, inner, columns) for value in values]
        ins = [
            pl.BlockSpec(
                (None, None, inner // cut, columns),
                lambda w, i, j, bit: (i, jnp.where(w == 0, 1 - bit[0], bit[0]), j, 0),
            )
        ] * len(values)
        outs = [
            pl.BlockSpec(
                (None, inner // cut, columns),
                lambda w, i, j, bit: (jnp.where(w == 0, i, outer - 1), jnp.where(w == 0, j, cut - 1), 0),
            ),
            pl.BlockSpec(
                (None, inner // cut, columns),
                lambda w, i, j, bit: (jnp.where(w == 0, 0, i), jnp.where(w == 0, 0, j), 0),
            ),
        ]
        grid = (2, outer, cut)
        shapes = [jax.ShapeDtypeStruct((outer, inner, columns), bf16)] * 2
    done = pl.pallas_call(
        functools.partial(add_split_kernel, len(values) == 2),
        grid_spec=pltpu.PrefetchScalarGridSpec(
            num_scalar_prefetch=1, grid=grid, in_specs=ins, out_specs=outs
        ),
        out_shape=shapes,
        cost_estimate=pl.CostEstimate(flops=rows * columns, bytes_accessed=6 * rows * columns, transcendentals=0),
        name="add_split",
    )(bit.reshape(1), *values)
    if not isinstance(done, (list, tuple)):
        return None, done
    return done[0].reshape(rows // 2, columns), done[1].reshape(rows // 2, columns)


def tie(*values):
    return lax.optimization_barrier(values)


def build(n_seq, n_rows):
    highs = n_rows // CORES
    seq_bits = n_seq.bit_length() - 1
    high_bits = highs.bit_length() - 1
    bits = seq_bits + high_bits

    def permute(value, target):
        pairs = []
        for s in range(n_seq):
            for r in range(n_rows):
                to_s, to_r = target(s, r)
                pairs.append((s * n_rows + r, to_s * n_rows + to_r))
        return lax.ppermute(value, AXES, pairs)

    def other_core(value):
        return permute(value, lambda s, r: (s, r ^ 1))

    def pick(value, place, axis):
        return lax.dynamic_index_in_dim(value, place, axis, keepdims=False)

    def bit_of(step):
        name, bit = step
        return (lax.axis_index(name) >> bit) & 1

    def across(value, step):
        name, bit = step
        if name == "rows":
            return permute(value, lambda s, r: (s, r ^ (1 << bit)))
        return permute(value, lambda s, r: (s ^ (1 << bit), r))

    high_steps = [("rows", bit + 1) for bit in reversed(range(high_bits))]
    seq_steps = [("seq", bit) for bit in range(seq_bits)]

    class Sum:
        def __init__(self, kept, received, order):
            self.rows, self.columns = kept.shape
            self.kept, self.received = kept, received
            self.left = [step for step in seq_steps[::-1] + high_steps if step in order]
            self.order = list(order)

        def finish(self):
            step = self.order[0] if self.order else None
            inner = self.rows
            if step is not None:
                axis = self.left.index(step)
                inner = self.rows >> (axis + 1)
            self.sent, self.kept = add_split(self.kept, self.received, inner, step and bit_of(step))
            self.received = None

        def begin(self):
            step = self.order.pop(0)
            self.left.remove(step)
            self.rows //= 2
            self.received = across(self.sent, step)

        def finished(self):
            while self.order:
                self.finish()
                self.begin()
            self.finish()
            return self.kept

    rows_first = high_steps + seq_steps[1:2] + seq_steps[:1] + seq_steps[2:]
    down_order = [step for step in seq_steps + high_steps if step != ("rows", 1)]
    up_order = [step for step in high_steps + seq_steps if step not in (("seq", 0), ("seq", 1))]

    def gather_high(value, pieces=0):
        for step in high_steps[::-1]:
            if pieces and step == ("rows", 1):
                continue
            received = across(value, step)
            value = jnp.where(
                bit_of(step) == 0,
                jnp.concatenate([value, received], 0),
                jnp.concatenate([received, value], 0),
            )
        if pieces:
            value = value.reshape(-1, 1, pieces, value.shape[1])
            received = across(value, ("rows", 1))
            value = jnp.where(
                bit_of(("rows", 1)) == 0,
                jnp.concatenate([value, received], 1),
                jnp.concatenate([received, value], 1),
            )
            value = value.reshape(-1, value.shape[-1])
        return value

    def back_by_steps(
        qkv, mixed, d_mixed, lse, key_tags, query_tags, n1_all, qkv_parts, attention_gain,
        out_kept, out_received, down_part, up_part, start, d_middle, to_member, ordered, from_rows, sizes,
    ):
        group, member, core, pairs, group_width, tokens, width = sizes
        lanes, half = 2 * HDIM, width // CORES
        unit1, scale1 = norm_parts(start)
        down = Sum(down_part, None, down_order)
        up = Sum(up_part, None, up_order)
        out = Sum(out_kept, out_received, rows_first)

        def before_next(*sums):
            nonlocal d_mixed
            for each in sums:
                each.finish()
            values = tie(d_mixed, *[v for each in sums for v in (each.sent, each.kept)])
            d_mixed = values[0]
            for at, each in enumerate(sums):
                each.sent, each.kept = values[1 + 2 * at : 3 + 2 * at]
                each.begin()

        def back_at(at):
            return attend_back(qkv, mixed, d_mixed, lse, key_tags, query_tags, at, 1)

        cut = max(1, 3 * pairs // 5)
        before_next(down, up)
        d_qkv, qkv_sums, d_parts = [], [], [[] for _ in range(group)]

        def take_piece(pieces):
            piece = jnp.concatenate(pieces, axis=1)
            d_parts[0].append(piece[:tokens])
            for hop in range(1, group):
                d_parts[hop].append(to_member(piece[hop * tokens : (hop + 1) * tokens], group - hop))
            return dot(n1_all, piece, 0, 0)

        grads = []
        for at in range(pairs):
            d_qkv.append(back_at(at))
            d_mixed, d_qkv[at] = tie(d_mixed, d_qkv[at])
            if at + 1 == cut:
                grads.append(take_piece(d_qkv))
            if at == min(0, pairs - 1):
                before_next(out)
            if at == min(1, pairs - 1):
                before_next(down, up)
            if at == min(3, pairs - 1):
                before_next(down, up, out)
        if pairs > cut:
            grads.append(take_piece(d_qkv[cut:]))
        if group == CORES:
            qkv_sums = [Sum(grad.astype(bf16), None, rows_first) for grad in grads]
        else:
            grad = jnp.concatenate(grads, 1)
            grad = grad.reshape(width, pairs, 3, lanes).transpose(0, 2, 1, 3)
            grad = grad.reshape(width, 3, 1, pairs * lanes)[..., :group_width]
            grad = lax.dynamic_update_slice_in_dim(
                jnp.zeros((width, 3, group, group_width), f32), grad, member, 2
            ).reshape(width, 3, CORES, half)
            kept = pick(grad, core, 2).astype(bf16).reshape(width, 3 * half)
            sent = pick(grad, 1 - core, 2).astype(bf16).reshape(width, 3 * half)
            qkv_sums = [Sum(kept, other_core(sent), rows_first)]

        d_n1 = jnp.zeros((tokens, width), f32)
        for part, weight in zip(d_parts, qkv_parts):
            d_n1 = d_n1 + dot(jnp.concatenate(part, 1), weight, 1, 1)
        input_grad = d_middle + norm_back(d_n1, attention_gain, unit1, scale1)
        input_grad = from_rows(input_grad.astype(bf16))

        down_total = gather_high(down.finished(), piece_rows)
        down_total = ordered(down_total, other_core(down_total), 1).astype(f32)
        tile = feed_tile // CORES
        up_total = gather_high(up.finished()).reshape(width // n_seq, -1, 1, tile)
        up_total = ordered(up_total, other_core(up_total), 2).reshape(width // n_seq, -1).astype(f32)
        out_total = gather_high(out.finished())
        out_total = ordered(out_total, other_core(out_total), 1).astype(f32)
        qkv_part = gather_high(jnp.concatenate([each.finished() for each in qkv_sums], 1))
        if group == CORES:
            qkv_part = qkv_part.reshape(-1, pairs, 3, lanes).transpose(0, 2, 1, 3)
        qkv_part = qkv_part.reshape(-1, 3, half)
        qkv_total = ordered(qkv_part[:, :, None], other_core(qkv_part)[:, :, None], 2)
        qkv_total = qkv_total.reshape(-1, 3 * width).astype(f32)

        return input_grad, qkv_total, out_total, down_total, up_total

    def per_device(
        inputs, cell_ids, valid_counts, cotangent, attention_gain, qkv_weight, out_weight, feed_gain, up_weight, down_weight
    ):
        row_count, block, width = inputs.shape
        seq_len = cell_ids.shape[1]
        heads = width // HDIM
        lanes = 2 * HDIM
        seq_at, rows_at = lax.axis_index("seq"), lax.axis_index("rows")
        core = rows_at % CORES
        chips = n_seq // (CORES * row_count)
        group = chips * CORES
        sub = block // group
        tokens = n_seq * sub
        member = (seq_at % chips) * CORES + core
        group_heads = heads // group
        pairs = -(-group_heads // 2)
        group_width = group_heads * HDIM
        padded = pairs * lanes - group_width

        def to_member(value, hop):
            def target(s, r):
                place = ((s % chips) * CORES + r % CORES + hop) % group
                return (s // chips * chips + place // CORES, r // CORES * CORES + place % CORES)

            return permute(value, target)

        def ordered(own, received, axis):
            return jnp.where(
                core == 0,
                jnp.concatenate([own, received], axis),
                jnp.concatenate([received, own], axis),
            )

        def to_rows(value):
            halves = value.reshape(row_count, CORES, block // CORES, width)
            received = other_core(pick(halves, 1 - core, 1))
            both = ordered(pick(halves, core, 1), received, 0).reshape(n_seq, sub, width)
            return lax.all_to_all(both, "seq", 0, 0, tiled=True).reshape(tokens, width)

        def from_rows(value):
            both = lax.all_to_all(value.reshape(n_seq, sub, width), "seq", 0, 0, tiled=True)
            both = both.reshape(CORES, row_count, block // CORES, width)
            received = other_core(pick(both, 1 - core, 0))
            own = pick(both, core, 0)
            return ordered(own[:, None], received[:, None], 1).reshape(row_count, block, width)

        places = jnp.arange(seq_len, dtype=jnp.int32)
        tags = jnp.where(places[None, :] < valid_counts[:, None], cell_ids, -1 - places[None, :])
        tags = ordered(tags, other_core(tags), 0)
        tags = pick(tags, seq_at // chips, 0).reshape(n_seq, CORES, chips, sub)
        tags = tags.transpose(2, 1, 0, 3).reshape(group, tokens)
        order = (member - jnp.arange(group, dtype=jnp.int32)) % group
        tags = jnp.take(tags, order, axis=0).reshape(1, seq_len)
        query_tags, key_tags = tags, tags.reshape(seq_len, 1)

        def pad_heads(value, axis):
            if not padded:
                return value
            fill = [(0, 0)] * value.ndim
            fill[axis] = (0, padded)
            return jnp.pad(value, fill)

        def qkv_of(hop):
            if group == CORES:
                return gather_pairs(((core + hop) % CORES).reshape(1), qkv_weight)
            piece = pick(qkv_weight.reshape(width, 3, group, group_width), (member + hop) % group, 2)
            piece = pad_heads(piece, 2).reshape(width, 3, pairs, lanes)
            return piece.transpose(0, 2, 1, 3).reshape(width, 3 * pairs * lanes)

        def out_of(hop):
            at = (member + hop) % group * group_width
            return pad_heads(lax.dynamic_slice_in_dim(out_weight, at, group_width, 0), 0)

        if chips == 1 and highs == 2:
            half = width // CORES
            x_row, n1, qkv, own_weight, other_weight = begin(inputs, qkv_weight, attention_gain)
            start = x_row.reshape(tokens, width)
            mixed, lse, cot, mixed_own = attend_row(qkv, key_tags, query_tags, cotangent)
            middle = start.astype(f32) + dot(mixed_own, out_weight, 1, 0)
            outputs, d_middle, _, d_mixed, out_kept, out_received, down_part, up_part = feed(
                middle, cot.reshape(tokens, width), feed_gain, up_weight, down_weight, mixed_own, out_weight, n_seq
            )
            input_grad, out_low, qkv_out, down_all, up_all = back(
                qkv, mixed, d_mixed, lse, key_tags, query_tags, n1, (own_weight, other_weight), attention_gain,
                out_kept, out_received, down_part, up_part, start, d_middle, outputs, row_count,
            )
            qkv_total, out_total, down_total, up_total, first, second = collect(
                seq_at, qkv_out, down_all, up_all, qkv_weight, up_weight, attention_gain, feed_gain
            )
            return (
                out_low.reshape(inputs.shape),
                input_grad.reshape(inputs.shape),
                first.reshape(-1),
                qkv_total,
                out_total,
                second.reshape(-1),
                up_total,
                down_total,
            )

        start = to_rows(inputs)
        qkv_parts = [qkv_of(hop) for hop in range(group)]
        out_parts = [out_of(hop) for hop in range(group)]
        start = start.astype(f32)
        unit1, scale1 = norm_parts(start)
        n1 = (unit1 * attention_gain).astype(bf16)
        n1_all = jnp.concatenate([n1] + [to_member(n1, hop) for hop in range(1, group)], 0)
        cotangent, _ = tie(cotangent, start[:1])
        cot = to_rows(cotangent)
        qkv = dot(n1_all, qkv_parts[0], 1, 0).astype(bf16)
        mixed, lse = attend(qkv, key_tags, query_tags)
        mixed_parts = [mixed[:tokens]] + [
            to_member(mixed[hop * tokens : (hop + 1) * tokens], group - hop) for hop in range(1, group)
        ]
        middle = start
        for part, weight in zip(mixed_parts, out_parts):
            middle = middle + dot(part, weight, 1, 0)
        if group == CORES:
            mixed_own = ordered(mixed_parts[0], mixed_parts[1], 1)
        else:
            slots = jnp.stack([part[:, :group_width] for part in mixed_parts])
            turn = (jnp.arange(group, dtype=jnp.int32) - member) % group
            mixed_own = jnp.take(slots, turn, axis=0).transpose(1, 0, 2).reshape(tokens, width)
        outputs, d_middle, d_attn, _, _, _, down_part, up_part = feed(
            middle, cot, feed_gain, up_weight, down_weight, mixed_own, out_weight, n_seq
        )

        d_attn_all = jnp.concatenate([d_attn] + [to_member(d_attn, hop) for hop in range(1, group)], 0)


        half = width // CORES
        out_grad = dot(mixed_own, d_attn, 0, 0).astype(bf16)
        out_kept = lax.dynamic_slice_in_dim(out_grad, core * half, half, 1)
        out_received = other_core(lax.dynamic_slice_in_dim(out_grad, (1 - core) * half, half, 1))
        d_mixed = dot(d_attn_all, out_parts[0], 1, 1).astype(bf16)

        out_low = from_rows(outputs)
        input_grad, qkv_total, out_total, down_total, up_total = back_by_steps(
            qkv, mixed, d_mixed, lse, key_tags, query_tags, n1_all, qkv_parts, attention_gain,
            out_kept, out_received, down_part, up_part, start, d_middle, to_member, ordered, from_rows,
            (group, member, core, pairs, group_width, tokens, width),
        )

        shard = width // n_seq

        def gain_total(weight, total, gain):
            rows = lax.dynamic_slice_in_dim(weight, seq_at * shard, shard, 0).astype(f32)
            return jnp.sum(rows * total, axis=1) / lax.dynamic_slice_in_dim(gain, seq_at * shard, shard, 0)

        return (
            out_low,
            input_grad,
            gain_total(qkv_weight, qkv_total, attention_gain),
            qkv_total,
            out_total,
            gain_total(up_weight, up_total, feed_gain),
            up_total,
            down_total,
        )

    return per_device


def solution(mesh):
    placed = (
        P("rows", "seq", None),
        P("rows", None),
        P("rows"),
        P("rows", "seq", None),
        P(),
        P(),
        P(),
        P(),
        P(),
        P(),
    )
    return jax.shard_map(
        build(mesh.shape["seq"], mesh.shape["rows"]),
        mesh=mesh,
        in_specs=placed,
        out_specs=(
            P("rows", "seq", None),
            P("rows", "seq", None),
            P("seq"),
            P("seq", None),
            P("seq", None),
            P("seq"),
            P("seq", None),
            P("seq", None),
        ),
        check_vma=False,
    )
```

```python
import functools

import jax
import jax.numpy as jnp
from jax import lax
from jax.experimental import pallas as pl
from jax.experimental.pallas import tpu as pltpu
from jax.sharding import PartitionSpec as P

HDIM = 64
CORES = 2
epsilon = 1e-05
masked_score = -1e30
score_scale = HDIM ** (-0.5)
log2e = 1.4426950408889634
bf16 = jnp.bfloat16
f32 = jnp.float32
AXES = ("seq", "rows")
vmem_bytes = 60 * 2**20
feed_vmem_bytes = 63 * 2**20
feed_tile = 512
max_cells = 7
MESH = pl.DeviceIdType.MESH


def dot(a, b, ca, cb):
    return lax.dot_general(a, b, (((ca,), (cb,)), ((), ())), preferred_element_type=f32)


def attend_kernel(tile, key_tags, query_tags, q_ref, k_ref, v_ref, o_ref, lse_ref, v_turned):
    tokens = q_ref.shape[0]
    v_turned[...] = v_ref[...].T
    lane = lax.broadcasted_iota(jnp.int32, (tile, 2 * HDIM), 1)

    def body(step, _):
        part = pl.ds(pl.multiple_of(step * tile, tile), tile)
        q = q_ref[part, :]
        allowed = key_tags[...] == query_tags[:, part]
        pieces = []
        for head in range(2):
            own = jnp.where((lane // HDIM) == head, q, bf16(0))
            scores = dot(k_ref[...], own, 1, 1)
            scores = jnp.where(allowed, scores, masked_score)
            peak = jnp.max(scores, axis=0, keepdims=True)
            powers = jnp.exp2((scores - peak) * (score_scale * log2e))
            total = jnp.sum(powers, axis=0, keepdims=True)
            mixed = dot(v_turned[head * HDIM : (head + 1) * HDIM, :], powers.astype(bf16), 1, 0)
            pieces.append(mixed * (1.0 / total))
            lse_ref[head : head + 1, part] = peak * (score_scale * log2e) + jnp.log2(total)
        o_ref[part, :] = jnp.concatenate(pieces, axis=0).T.astype(bf16)
        return 0

    lax.fori_loop(0, tokens // tile, body, 0)


def attend(qkv, key_tags, query_tags):
    tokens, width = qkv.shape
    lanes = 2 * HDIM
    pairs = width // (3 * lanes)
    tile = min(512, tokens)

    def columns(place):
        return pl.BlockSpec((tokens, lanes), lambda i: (0, 3 * i + place))

    return pl.pallas_call(
        functools.partial(attend_kernel, tile),
        grid=(pairs,),
        in_specs=[
            pl.BlockSpec((tokens, 1), lambda i: (0, 0)),
            pl.BlockSpec((1, tokens), lambda i: (0, 0)),
            columns(0),
            columns(1),
            columns(2),
        ],
        out_specs=[
            pl.BlockSpec((tokens, lanes), lambda i: (0, i)),
            pl.BlockSpec((None, 2, tokens), lambda i: (i, 0, 0)),
        ],
        out_shape=[
            jax.ShapeDtypeStruct((tokens, pairs * lanes), bf16),
            jax.ShapeDtypeStruct((pairs, 2, tokens), f32),
        ],
        scratch_shapes=[pltpu.VMEM((lanes, tokens), bf16)],
        compiler_params=pltpu.CompilerParams(vmem_limit_bytes=vmem_bytes),
        cost_estimate=pl.CostEstimate(
            flops=32 * pairs * tokens * tokens * HDIM,
            bytes_accessed=8 * tokens * pairs * lanes,
            transcendentals=2 * pairs * tokens * tokens,
        ),
        name="attend",
    )(key_tags, query_tags, qkv, qkv, qkv)


def attend_back_kernel(
    tile, key_tags, query_tags, q_ref, k_ref, v_ref, o_ref, do_ref, lse_ref, grad_ref, k_turned, dq_turned, delta
):
    tokens = q_ref.shape[0]
    lanes = 2 * HDIM
    k_turned[...] = k_ref[...].T
    dq_turned[...] = (o_ref[...].astype(f32) * do_ref[...].astype(f32)).T
    for head in range(2):
        rows = dq_turned[head * HDIM : (head + 1) * HDIM, :]
        delta[head : head + 1, :] = jnp.sum(rows, axis=0, keepdims=True)
    dq_turned[...] = jnp.zeros_like(dq_turned)
    first = lax.broadcasted_iota(jnp.int32, (tile, lanes), 1) < HDIM

    def body(step, _):
        part = pl.ds(pl.multiple_of(step * tile, tile), tile)
        k, v = k_ref[part, :], v_ref[part, :]
        q, do = q_ref[...], do_ref[...]
        allowed = key_tags[part, :] == query_tags[...]
        dk, dv = [], []
        for head in range(2):
            own = first if head == 0 else jnp.logical_not(first)
            own_rows = slice(head * HDIM, (head + 1) * HDIM)
            scores = dot(jnp.where(own, k, bf16(0)), q, 1, 1)
            scores = jnp.where(allowed, scores, masked_score)
            chances = jnp.exp2(scores * (score_scale * log2e) - lse_ref[head : head + 1, :])
            weight_grad = dot(jnp.where(own, v, bf16(0)), do, 1, 1)
            score_grad = (chances * (weight_grad - delta[head : head + 1, :])).astype(bf16)
            dv.append(dot(chances.astype(bf16), do, 1, 0))
            dk.append(dot(score_grad, q, 1, 0))
            dq_turned[own_rows, :] += dot(k_turned[own_rows, part], score_grad, 1, 0)
        grad_ref[part, lanes : 2 * lanes] = (jnp.where(first, dk[0], dk[1]) * score_scale).astype(bf16)
        grad_ref[part, 2 * lanes :] = jnp.where(first, dv[0], dv[1]).astype(bf16)
        return 0

    lax.fori_loop(0, tokens // tile, body, 0)
    grad_ref[:, :lanes] = (dq_turned[...] * score_scale).T.astype(bf16)


def attend_back(qkv, mixed, d_mixed, lse, key_tags, query_tags, start, count):
    tokens = qkv.shape[0]
    tile = min(512, tokens)
    lanes = 2 * HDIM

    def columns(place):
        return pl.BlockSpec((tokens, lanes), lambda i: (0, 3 * (start + i) + place))

    pair = pl.BlockSpec((tokens, lanes), lambda i: (0, start + i))
    return pl.pallas_call(
        functools.partial(attend_back_kernel, tile),
        grid=(count,),
        in_specs=[
            pl.BlockSpec((tokens, 1), lambda i: (0, 0)),
            pl.BlockSpec((1, tokens), lambda i: (0, 0)),
            columns(0),
            columns(1),
            columns(2),
            pair,
            pair,
            pl.BlockSpec((None, 2, tokens), lambda i: (start + i, 0, 0)),
        ],
        out_specs=pl.BlockSpec((tokens, 3 * lanes), lambda i: (0, i)),
        out_shape=jax.ShapeDtypeStruct((tokens, 3 * count * lanes), bf16),
        scratch_shapes=[
            pltpu.VMEM((lanes, tokens), bf16),
            pltpu.VMEM((lanes, tokens), f32),
            pltpu.VMEM((2, tokens), f32),
        ],
        compiler_params=pltpu.CompilerParams(vmem_limit_bytes=vmem_bytes),
        cost_estimate=pl.CostEstimate(
            flops=80 * count * tokens * tokens * HDIM,
            bytes_accessed=16 * tokens * count * lanes,
            transcendentals=2 * count * tokens * tokens,
        ),
        name="attend_back",
    )(key_tags, query_tags, qkv, qkv, qkv, mixed, d_mixed, lse)


def copy_kernel(core_ref, from_ref, to_ref):
    to_ref[...] = from_ref[...]


def gather_pairs(core, qkv_weight):
    width, lanes = qkv_weight.shape[0], 2 * HDIM
    pairs = width // (CORES * lanes)
    return pl.pallas_call(
        copy_kernel,
        grid_spec=pltpu.PrefetchScalarGridSpec(
            num_scalar_prefetch=1,
            grid=(pairs, 3),
            in_specs=[
                pl.BlockSpec((width, lanes), lambda i, j, core: (0, (j * CORES + core[0]) * pairs + i))
            ],
            out_specs=pl.BlockSpec((width, lanes), lambda i, j, core: (0, 3 * i + j)),
        ),
        out_shape=jax.ShapeDtypeStruct((width, 3 * pairs * lanes), qkv_weight.dtype),
        cost_estimate=pl.CostEstimate(flops=0, bytes_accessed=12 * width * pairs * lanes, transcendentals=0),
        name="gather_pairs",
    )(core, qkv_weight)


def norm_parts(values):
    center = values - jnp.mean(values, axis=-1, keepdims=True)
    spread = jnp.mean(center * center, axis=-1, keepdims=True)
    scale = lax.rsqrt(spread + epsilon)
    return center * scale, scale


def norm_back(grad, gain, unit, scale):
    e = grad * gain
    return scale * (
        e - jnp.mean(e, axis=-1, keepdims=True) - unit * jnp.mean(e * unit, axis=-1, keepdims=True)
    )


def all_signal(n_seq, seq_at, rows_at, extra=()):
    core = rows_at % CORES
    barrier = pltpu.get_barrier_semaphore()
    for s in range(n_seq):
        for c in range(CORES):
            @pl.when(jnp.logical_not((seq_at == s) & (core == c)))
            def _():
                pl.semaphore_signal(barrier, inc=1, device_id=(s, rows_at - core + c), device_id_type=MESH)
    for peer in extra:
        pl.semaphore_signal(barrier, inc=1, device_id=peer, device_id_type=MESH)
    pl.semaphore_wait(barrier, n_seq * CORES - 1 + len(extra))


class ToRows:
    def __init__(self, source, target, send, recv, local, row_count, seq_at, rows_at):
        self.source, self.target, self.send, self.recv, self.local = source, target, send, recv, local
        self.row_count, self.seq_at, self.rows_at = row_count, seq_at, rows_at
        self.core = rows_at % CORES

    def copy(self, row, c):
        chip = self.core * self.row_count + row
        return pltpu.make_async_remote_copy(
            src_ref=self.source.at[row, c],
            dst_ref=self.target.at[self.seq_at],
            send_sem=self.send.at[row, c],
            recv_sem=self.recv.at[self.seq_at],
            device_id=(chip, self.rows_at - self.core + c),
            device_id_type=MESH,
        )

    def own(self, row, c):
        return pltpu.make_async_copy(self.source.at[row, c], self.target.at[self.seq_at], self.local)

    def each(self, own, other):
        for row_turn in range(self.row_count):
            for core_turn in range(CORES):
                row = (row_turn + self.seq_at) % self.row_count
                c = (core_turn + self.seq_at // self.row_count) % CORES
                here = (self.core * self.row_count + row == self.seq_at) & (self.core == c)

                @pl.when(here)
                def _():
                    own(row, c)

                @pl.when(jnp.logical_not(here))
                def _():
                    other(row, c)

    def start(self):
        self.each(lambda row, c: self.own(row, c).start(), lambda row, c: self.copy(row, c).start())

    def wait_block(self, s):
        here = (s == self.seq_at) & (self.seq_at // self.row_count == self.core)

        @pl.when(here)
        def _():
            self.own(0, 0).wait()

        @pl.when(jnp.logical_not(here))
        def _():
            pltpu.make_async_remote_copy(
                src_ref=self.source.at[0, 0],
                dst_ref=self.target.at[s],
                send_sem=self.send.at[0, 0],
                recv_sem=self.recv.at[s],
                device_id=(self.seq_at, self.rows_at + 1 - 2 * self.core),
                device_id_type=MESH,
            ).wait_recv()

    def wait_sends(self):
        self.each(lambda row, c: None, lambda row, c: self.copy(row, c).wait_send())


def begin_kernel(
    row_count, pairs, x_ref, weight_ref, gain_ref, x_out, n1_out, qkv_out, own_out, other_out,
    x_part, n1, qkv, weight, other_weight,
    x_send, x_recv, x_local, n1_send, n1_recv, weight_sems, out_sems, x_sems, qkv_sems, n1_sems,
):
    seq_at, rows_at = lax.axis_index("seq"), lax.axis_index("rows")
    core = rows_at % CORES
    n_seq, sub, width = x_part.shape
    lanes = 2 * HDIM
    tokens = n_seq * sub
    moves = ToRows(x_ref, x_part, x_send, x_recv, x_local, row_count, seq_at, rows_at)

    def weight_copies(item, which):
        pair, kind = item // 3, item % 3
        to = pl.ds(pl.multiple_of(item * lanes, lanes), lanes)

        def columns(c):
            return pl.ds(pl.multiple_of((kind * CORES + c) * pairs * lanes + pair * lanes, lanes), lanes)

        source = weight_ref.at[:, columns(1 - core if which else core)]
        return pltpu.make_async_copy(source, (weight, other_weight)[which].at[:, to], weight_sems.at[which, item])

    def each_weight(act, which):
        def body(item, _):
            act(weight_copies(item, which))
            return 0

        lax.fori_loop(0, 3 * pairs, body, 0)

    each_weight(lambda copy: copy.start(), 0)
    all_signal(n_seq, seq_at, rows_at)
    moves.start()
    each_weight(lambda copy: copy.start(), 1)
    each_weight(lambda copy: copy.wait(), 0)
    weights_out = (
        pltpu.make_async_copy(weight, own_out, out_sems.at[0]),
        pltpu.make_async_copy(other_weight, other_out, out_sems.at[1]),
    )
    weights_out[0].start()
    each_weight(lambda copy: copy.wait(), 1)
    weights_out[1].start()

    def block_of(place):
        near = (place % 2) * ((place + 1) // 2) + (1 - place % 2) * ((n_seq - place // 2) % n_seq)
        return (seq_at + near) % n_seq

    def rows_of(s, other):
        return pl.ds(pl.multiple_of(s * sub + other * tokens, sub), sub)

    def n1_copy(s):
        return pltpu.make_async_remote_copy(
            src_ref=n1.at[rows_of(s, 0)],
            dst_ref=n1.at[rows_of(s, 1)],
            send_sem=n1_send.at[s],
            recv_sem=n1_recv.at[s],
            device_id=(seq_at, rows_at + 1 - 2 * core),
            device_id_type=MESH,
        )

    def x_copy(s):
        return pltpu.make_async_copy(x_part.at[s], x_out.at[s], x_sems.at[s])

    def out_copies(s, other):
        rows = rows_of(s, other)
        return (
            pltpu.make_async_copy(qkv.at[rows], qkv_out.at[rows], qkv_sems.at[other, s]),
            pltpu.make_async_copy(n1.at[rows], n1_out.at[rows], n1_sems.at[other, s]),
        )

    def product(first, second, other):
        both = jnp.concatenate([n1[rows_of(first, other), :], n1[rows_of(second, other), :]], 0)
        found = dot(both, weight[...], 1, 0).astype(bf16)
        for at, s in enumerate((first, second)):
            qkv[rows_of(s, other), :] = found[at * sub : (at + 1) * sub]
            for copy in out_copies(s, other):
                copy.start()

    def body(group, _):
        @pl.when(group < n_seq // 2)
        def _():
            places = block_of(2 * group), block_of(2 * group + 1)
            for s in places:
                moves.wait_block(s)
                x_copy(s).start()
                unit, _s = norm_parts(x_part[s].astype(f32))
                n1[rows_of(s, 0), :] = (unit * gain_ref[...]).astype(bf16)
                n1_copy(s).start()
            product(*places, 0)

        @pl.when(group > 0)
        def _():
            places = block_of(2 * group - 2), block_of(2 * group - 1)
            for s in places:
                n1_copy(s).wait()
            product(*places, 1)

        return 0

    lax.fori_loop(0, n_seq // 2 + 1, body, 0)

    def finish(s, _):
        x_copy(s).wait()
        for other in range(2):
            for copy in out_copies(s, other):
                copy.wait()
        return 0

    lax.fori_loop(0, n_seq, finish, 0)
    moves.wait_sends()
    for copy in weights_out:
        copy.wait()


def begin(inputs, qkv_weight, gain):
    row_count, block, width = inputs.shape
    n_seq = CORES * row_count
    lanes = 2 * HDIM
    pairs = width // (CORES * lanes)
    sub = block // CORES
    tokens = n_seq * sub
    hbm = pl.BlockSpec(memory_space=pl.ANY)
    return pl.pallas_call(
        functools.partial(begin_kernel, row_count, pairs),
        in_specs=[hbm, hbm, pl.BlockSpec(memory_space=pltpu.VMEM)],
        out_specs=[hbm] * 5,
        out_shape=[
            jax.ShapeDtypeStruct((n_seq, sub, width), bf16),
            jax.ShapeDtypeStruct((CORES * tokens, width), bf16),
            jax.ShapeDtypeStruct((CORES * tokens, 3 * pairs * lanes), bf16),
            jax.ShapeDtypeStruct((width, 3 * pairs * lanes), bf16),
            jax.ShapeDtypeStruct((width, 3 * pairs * lanes), bf16),
        ],
        scratch_shapes=[
            pltpu.VMEM((n_seq, sub, width), bf16),
            pltpu.VMEM((CORES * tokens, width), bf16),
            pltpu.VMEM((CORES * tokens, 3 * pairs * lanes), bf16),
            pltpu.VMEM((width, 3 * pairs * lanes), bf16),
            pltpu.VMEM((width, 3 * pairs * lanes), bf16),
            pltpu.SemaphoreType.DMA((row_count, CORES)),
            pltpu.SemaphoreType.DMA((n_seq,)),
            pltpu.SemaphoreType.DMA,
            pltpu.SemaphoreType.DMA((n_seq,)),
            pltpu.SemaphoreType.DMA((n_seq,)),
            pltpu.SemaphoreType.DMA((2, 3 * pairs)),
            pltpu.SemaphoreType.DMA((2,)),
            pltpu.SemaphoreType.DMA((n_seq,)),
            pltpu.SemaphoreType.DMA((CORES, n_seq)),
            pltpu.SemaphoreType.DMA((CORES, n_seq)),
        ],
        compiler_params=pltpu.CompilerParams(
            vmem_limit_bytes=vmem_bytes, collective_id=3, has_side_effects=True
        ),
        name="begin",
    )(inputs.reshape(row_count, CORES, sub, width), qkv_weight, gain.reshape(1, width))


def with_cells(value, tags, head, is_key):
    lane = lax.broadcasted_iota(jnp.int32, value.shape, 1)
    cell = lane - (1 - head) * HDIM
    if is_key:
        marks = jnp.where((cell == tags) | (cell >= max_cells), 0.0, -1.0)
    else:
        marks = jnp.where(cell == tags, -masked_score, 0.0)
    return jnp.where((lane // HDIM) == head, value, marks.astype(bf16))


def attend_row_kernel(
    tile, row_count, tags, row_tags, q_ref, k_ref, v_ref, cot_ref, o_ref, lse_ref, cot_out, own_out,
    v_turned, keys, scores_ref, mixed_ref, parts,
    cot_send, cot_recv, cot_local, part_send, part_recv, part_local,
):
    item, last = pl.program_id(0), pl.num_programs(0) - 1
    seq_at, rows_at = lax.axis_index("seq"), lax.axis_index("rows")
    core = rows_at % CORES
    tokens, lanes = q_ref.shape
    own_tokens = tokens // CORES
    n_seq = cot_out.shape[0]
    moves = ToRows(cot_ref, cot_out, cot_send, cot_recv, cot_local, row_count, seq_at, rows_at)

    def part_copies(at):
        slot = at % 2
        half = pl.num_programs(0) * lanes
        columns = pl.ds(pl.multiple_of(core * half + at * lanes, lanes), lanes)
        return (
            pltpu.make_async_remote_copy(
                src_ref=parts.at[slot, pl.ds(own_tokens, own_tokens)],
                dst_ref=own_out.at[:, columns],
                send_sem=part_send.at[slot],
                recv_sem=part_recv.at[at],
                device_id=(seq_at, rows_at + 1 - 2 * core),
                device_id_type=MESH,
            ),
            pltpu.make_async_copy(parts.at[slot, pl.ds(0, own_tokens)], own_out.at[:, columns], part_local.at[slot]),
        )

    def part_came(at):
        half = pl.num_programs(0) * lanes
        columns = pl.ds(pl.multiple_of((1 - core) * half + at * lanes, lanes), lanes)
        return pltpu.make_async_remote_copy(
            src_ref=parts.at[0, pl.ds(own_tokens, own_tokens)],
            dst_ref=own_out.at[:, columns],
            send_sem=part_send.at[0],
            recv_sem=part_recv.at[at],
            device_id=(seq_at, rows_at + 1 - 2 * core),
            device_id_type=MESH,
        )

    @pl.when(item == 0)
    def _():
        all_signal(n_seq, seq_at, rows_at)
        moves.start()

    for head in range(2):
        keys[head] = with_cells(k_ref[...], tags[...], head, True)
        v_turned[head, :HDIM, :] = v_ref[...].T[head * HDIM : (head + 1) * HDIM, :]
        v_turned[head, HDIM:, :] = jnp.ones((16, tokens), bf16)

    def begin_scores(step, head):
        part = pl.ds(pl.multiple_of(step * tile, tile), tile)
        scores_ref[head] = dot(keys[head], with_cells(q_ref[part, :], tags[part, :], head, False), 1, 1)

    def finish(step, head):
        part = pl.ds(pl.multiple_of(step * tile, tile), tile)
        scores = scores_ref[head]
        peak = jnp.max(scores, axis=0, keepdims=True)
        powers = jnp.exp2((scores - peak) * (score_scale * log2e))
        mixed = dot(v_turned[head], powers.astype(bf16), 1, 0)
        total = mixed[HDIM : HDIM + 1, :]
        mixed_ref[head * HDIM : (head + 1) * HDIM, part] = mixed[:HDIM, :] * (1.0 / total)
        lse = peak * (score_scale * log2e) + jnp.log2(total)
        lse_ref[head : head + 1, part] = jnp.where(row_tags[:, part] < 0, -masked_score, lse)

    steps = tokens // tile
    begin_scores(0, 0)

    def body(step, _):
        begin_scores(step, 1)
        finish(step, 0)
        begin_scores(jnp.minimum(step + 1, steps - 1), 0)
        finish(step, 1)
        return 0

    lax.fori_loop(0, steps, body, 0)
    found = jnp.where(tags[...] < 0, v_ref[...], mixed_ref[...].T.astype(bf16))
    o_ref[...] = found

    @pl.when(item >= 2)
    def _():
        remote, local = part_copies(item - 2)
        remote.wait_send()
        local.wait()

    parts[item % 2] = found
    for copy in part_copies(item):
        copy.start()

    @pl.when(item == last)
    def _():
        for at in range(2):
            remote, local = part_copies(last - at)
            remote.wait_send()
            local.wait()
        for at in range(part_recv.shape[0]):
            part_came(at).wait_recv()
        for s in range(n_seq):
            moves.wait_block(s)
        moves.wait_sends()


def attend_row(qkv, tags, row_tags, cotangent):
    tokens, width = qkv.shape
    row_count, block, model = cotangent.shape
    lanes = 2 * HDIM
    pairs = width // (3 * lanes)
    tile = 512
    n_seq, sub = CORES * row_count, block // CORES
    hbm = pl.BlockSpec(memory_space=pl.ANY)

    def columns(place):
        return pl.BlockSpec((tokens, lanes), lambda i: (0, 3 * i + place))

    return pl.pallas_call(
        functools.partial(attend_row_kernel, tile, row_count),
        grid=(pairs,),
        in_specs=[
            pl.BlockSpec((tokens, 1), lambda i: (0, 0)),
            pl.BlockSpec((1, tokens), lambda i: (0, 0)),
            columns(0),
            columns(1),
            columns(2),
            hbm,
        ],
        out_specs=[
            pl.BlockSpec((tokens, lanes), lambda i: (0, i)),
            pl.BlockSpec((None, 2, tokens), lambda i: (i, 0, 0)),
            hbm,
            hbm,
        ],
        out_shape=[
            jax.ShapeDtypeStruct((tokens, pairs * lanes), bf16),
            jax.ShapeDtypeStruct((pairs, 2, tokens), f32),
            jax.ShapeDtypeStruct((n_seq, sub, model), bf16),
            jax.ShapeDtypeStruct((tokens // CORES, model), bf16),
        ],
        scratch_shapes=[
            pltpu.VMEM((2, HDIM + 16, tokens), bf16),
            pltpu.VMEM((2, tokens, lanes), bf16),
            pltpu.VMEM((2, tokens, tile), f32),
            pltpu.VMEM((lanes, tokens), f32),
            pltpu.VMEM((2, tokens, lanes), bf16),
            pltpu.SemaphoreType.DMA((row_count, CORES)),
            pltpu.SemaphoreType.DMA((n_seq,)),
            pltpu.SemaphoreType.DMA,
            pltpu.SemaphoreType.DMA((2,)),
            pltpu.SemaphoreType.DMA((pairs,)),
            pltpu.SemaphoreType.DMA((2,)),
        ],
        compiler_params=pltpu.CompilerParams(
            vmem_limit_bytes=vmem_bytes, collective_id=4, has_side_effects=True
        ),
        name="attend_row",
    )(tags, row_tags, qkv, qkv, qkv, cotangent.reshape(row_count, CORES, sub, model))


piece_rows = 16


def feed_kernel(
    tiles,
    rows,
    middle_ref,
    cot_ref,
    gain_ref,
    up_ref,
    down_ref,
    mixed_ref,
    out_weight_ref,
    out_ref,
    d_middle_ref,
    d_attn_out,
    d_mixed_out,
    out_kept,
    out_came,
    down_part,
    up_part,
    n2,
    total,
    d_attn,
    out_weight,
    out_keep,
    out_send,
    acts,
    d_ups,
    up_before,
    down_before,
    down_halves,
    down_recv,
    up_halves,
    up_recv,
    down_far_keep,
    down_far_send,
    down_far_recv,
    up_far_keep,
    up_far_send,
    up_far_recv,
    up_last_keep,
    up_last_send,
    up_last_recv,
    core_send_sem,
    core_recv_sem,
    far_send_sem,
    far_recv_sem,
    core_free,
    far_free,
    d_attn_sems,
    last_send_sem,
    last_recv_sem,
    out_sems,
):
    ahead = pl.program_id(0)
    step = ahead - 1
    tokens, width = n2.shape
    half, tile = width // 2, up_ref.shape[1]
    seq_at, rows_at = lax.axis_index("seq"), lax.axis_index("rows")
    core, high, low, mid = rows_at % 2, (rows_at // 2) % 2, seq_at % 2, (seq_at // 2) % 2
    core_peer = (seq_at, rows_at + 1 - 2 * core)
    far_peers = ((seq_at, rows_at + 2 - 4 * high), (seq_at + 1 - 2 * low, rows_at))
    last_peer = (seq_at + 2 - 4 * mid, rows_at)

    def copies(slot, far):
        if far:
            refs = ((down_far_send, down_far_recv), (up_far_send, up_far_recv))
            sems, peers = (far_send_sem, far_recv_sem), far_peers
        else:
            refs = ((down_halves.at[:, 1 - core], down_recv), (up_halves.at[:, 1 - core], up_recv))
            sems, peers = (core_send_sem, core_recv_sem), (core_peer, core_peer)
        return [
            pltpu.make_async_remote_copy(
                src_ref=refs[kind][0].at[slot],
                dst_ref=refs[kind][1].at[slot],
                send_sem=sems[0].at[kind, slot],
                recv_sem=sems[1].at[kind, slot],
                device_id=peers[kind],
                device_id_type=MESH,
            )
            for kind in range(2)
        ]

    def signal(sem, peer):
        pl.semaphore_signal(sem, inc=1, device_id=peer, device_id_type=MESH)

    @pl.when(ahead == 0)
    def _():
        barrier = pltpu.get_barrier_semaphore()
        for peer in (core_peer,) + far_peers + (last_peer,):
            signal(barrier, peer)
        pl.semaphore_wait(barrier, 4)

        def body(i, _):
            part = pl.ds(pl.multiple_of(i * rows, rows), rows)
            unit, _s = norm_parts(middle_ref[part, :])
            n2[part, :] = (unit * gain_ref[...]).astype(bf16)
            return 0

        lax.fori_loop(0, tokens // rows, body, 0)
        total[...] = middle_ref[...]
        d_middle_ref[...] = jnp.zeros_like(d_middle_ref)

    def activate():
        up = dot(n2[...], up_ref[...], 1, 0)
        d_act = dot(cot_ref[...], down_ref[...], 1, 1)
        share = 0.5 + 0.5 * lax.erf(up * (0.5**0.5))
        density = jnp.exp(-0.5 * up * up) * 0.3989422804014327
        acts[ahead % 2] = (up * share).astype(bf16)
        d_ups[ahead % 2] = (d_act * (share + up * density)).astype(bf16)

    def use():
        slot = step % 2
        act, d_up = acts[slot], d_ups[slot]
        total[...] += dot(act, down_before[...], 1, 0)
        d_middle_ref[...] += dot(d_up, up_before[...], 1, 1)
        up_grad = dot(n2[...], d_up, 0, 0).astype(bf16)
        cut = up_grad.shape[1] // 2
        up_halves[slot, 0] = up_grad[:, :cut].reshape(up_halves.shape[2:])
        up_halves[slot, 1] = up_grad[:, cut:].reshape(up_halves.shape[2:])
        down_grad = dot(act, cot_ref[...], 0, 0).astype(bf16)
        down_halves[slot, 0] = down_grad[:, :half].reshape(down_halves.shape[2:])
        down_halves[slot, 1] = down_grad[:, half:].reshape(down_halves.shape[2:])

    @pl.when((step >= 2) & (step < tiles))
    def _():
        for copy in copies(step % 2, False):
            copy.wait_send()

    @pl.when(ahead == 0)
    def _():
        activate()

    @pl.when((ahead > 0) & (ahead < tiles))
    def _():
        activate()
        use()

    @pl.when(ahead == tiles)
    def _():
        use()

    @pl.when(ahead < tiles)
    def _():
        up_before[...] = up_ref[...]
        down_before[...] = down_ref[...]

    def add(a, b):
        return (a.astype(f32) + b.astype(f32)).astype(bf16)

    def last_copy(slot):
        return pltpu.make_async_remote_copy(
            src_ref=up_last_send.at[slot],
            dst_ref=up_last_recv.at[slot],
            send_sem=last_send_sem.at[slot],
            recv_sem=last_recv_sem.at[slot],
            device_id=last_peer,
            device_id_type=MESH,
        )

    def last_add():
        slot = (step + 1) % 2
        last_copy(slot).wait_recv()
        up_part[...] = add(up_last_keep[slot], up_last_recv[slot]).reshape(up_part.shape)

    def far_add():
        slot = step % 2
        for copy in copies(slot, True):
            copy.wait_recv()
        down_part[...] = add(down_far_keep[slot], down_far_recv[slot]).reshape(down_part.shape)

        @pl.when(step >= 4)
        def _():
            last_copy(slot).wait_send()

        up_last_send[slot] = add(up_far_keep[slot, :, 1 - mid], up_far_recv[slot, :, 1 - mid])
        up_last_keep[slot] = add(up_far_keep[slot, :, mid], up_far_recv[slot, :, mid])
        last_copy(slot).start()

        @pl.when(step < tiles)
        def _():
            signal(far_free.at[0], far_peers[0])
            signal(far_free.at[1], far_peers[1])

    def pass_on():
        slot = (step + 1) % 2
        for copy in copies(slot, False):
            copy.wait_recv()

        @pl.when(step >= 3)
        def _():
            for copy in copies(slot, True):
                copy.wait_send()
            pl.semaphore_wait(far_free.at[0], 1)
            pl.semaphore_wait(far_free.at[1], 1)

        down_far_send[slot] = add(down_halves[slot, core, :, 1 - high], down_recv[slot, :, 1 - high])
        down_far_keep[slot] = add(down_halves[slot, core, :, high], down_recv[slot, :, high])
        shape = up_far_send.shape[1:]
        up_far_send[slot] = add(up_halves[slot, core, :, 1 - low], up_recv[slot, :, 1 - low]).reshape(shape)
        up_far_keep[slot] = add(up_halves[slot, core, :, low], up_recv[slot, :, low]).reshape(shape)
        for copy in copies(slot, True):
            copy.start()

        @pl.when(step < tiles - 1)
        def _():
            signal(core_free, core_peer)

    @pl.when((step >= 3) & (step <= tiles + 1))
    def _():
        last_add()

    @pl.when((step >= 2) & (step <= tiles))
    def _():
        far_add()

    @pl.when((step >= 1) & (step <= tiles))
    def _():
        pass_on()

    @pl.when((step >= 0) & (step < tiles))
    def _():
        @pl.when(step >= 2)
        def _():
            pl.semaphore_wait(core_free, 1)

        for copy in copies(step % 2, False):
            copy.start()

    @pl.when(step == tiles)
    def _():
        def body(i, _):
            part = pl.ds(pl.multiple_of(i * rows, rows), rows)
            low_total = total[part, :].astype(bf16)
            for at in range(2):
                acts[at, part, :] = low_total[:, at * tile : (at + 1) * tile]
            d_ups[0, part, : width - 2 * tile] = low_total[:, 2 * tile :]
            unit, scale = norm_parts(middle_ref[part, :])
            grad = cot_ref[part, :].astype(f32) + norm_back(d_middle_ref[part, :], gain_ref[...], unit, scale)
            d_middle_ref[part, :] = grad
            d_attn[part, :] = grad.astype(bf16)
            return 0

        lax.fori_loop(0, tokens // rows, body, 0)

    def to_core(source, target, at):
        return pltpu.make_async_remote_copy(
            src_ref=source,
            dst_ref=target,
            send_sem=d_attn_sems.at[at],
            recv_sem=d_attn_sems.at[at + 1],
            device_id=core_peer,
            device_id_type=MESH,
        )

    d_attn_copy = lambda: to_core(d_attn, d_attn_out.at[1], 0)
    out_copy = lambda: to_core(out_send, out_came, 2)
    mixed_copy = lambda: pltpu.make_async_copy(mixed_ref, n2, out_sems.at[0])
    weight_copy = lambda: pltpu.make_async_copy(
        out_weight_ref.at[pl.ds(pl.multiple_of(core * half, half), half)], out_weight, out_sems.at[1]
    )
    d_attn_save = lambda: pltpu.make_async_copy(d_attn, d_attn_out.at[0], out_sems.at[2])
    out_save = lambda: pltpu.make_async_copy(out_keep, out_kept, out_sems.at[3])
    d_mixed_save = lambda: pltpu.make_async_copy(down_halves, d_mixed_out, out_sems.at[4])

    def in_slots():
        wide = [(acts.at[at], pl.ds(at * tile, tile)) for at in range(2)]
        wide.append((d_ups.at[0, :, pl.ds(0, width - 2 * tile)], pl.ds(2 * tile, width - 2 * tile)))
        return list(enumerate(wide))

    def total_saves():
        return [
            pltpu.make_async_copy(source, out_ref.at[:, columns], out_sems.at[5 + at])
            for at, (source, columns) in in_slots()
        ]

    def d_attn_loads():
        return [
            pltpu.make_async_copy(d_attn_out.at[1, :, columns], target, out_sems.at[8 + at])
            for at, (target, columns) in in_slots()
        ]

    @pl.when(step == tiles)
    def _():
        for copy in total_saves():
            copy.start()
        d_attn_copy().start()
        d_attn_save().start()
        mixed_copy().start()
        weight_copy().start()

    @pl.when(step == tiles + 1)
    def _():
        mixed_copy().wait()
        grad = dot(n2[...], d_attn[...], 0, 0).astype(bf16)

        @pl.when(core == 0)
        def _():
            out_keep[...] = grad[:, :half]
            out_send[...] = grad[:, half:]

        @pl.when(core != 0)
        def _():
            out_keep[...] = grad[:, half:]
            out_send[...] = grad[:, :half]

        out_copy().start()
        out_save().start()
        far_add()

    @pl.when(step == tiles + 2)
    def _():
        for copy in total_saves():
            copy.wait()
        d_attn_copy().wait()
        for copy in d_attn_loads():
            copy.start()
        weight_copy().wait()
        for slot in range(2):
            for copy in copies(slot, False):
                copy.wait_send()

        def keep_d_mixed(at, found):
            found = found.astype(bf16).reshape((-1,) + down_halves.shape[2:])
            down_halves[at, : found.shape[0]] = found

        keep_d_mixed(0, dot(d_attn[...], out_weight[...], 1, 1))
        for copy in d_attn_loads():
            copy.wait()
        other = jnp.concatenate([acts[0], acts[1], d_ups[0, :, : width - 2 * tile]], 1)
        keep_d_mixed(1, dot(other, out_weight[...], 1, 1))
        d_mixed_save().start()
        last_add()
        out_copy().wait()
        for copy in (d_attn_save(), out_save(), d_mixed_save()):
            copy.wait()
        for slot in range(2):
            last_copy(slot).wait_send()
            for copy in copies(slot, True):
                copy.wait_send()


def feed(middle, cot, gain, up_weight, down_weight, mixed_own, out_weight, n_seq):
    tokens, width = middle.shape
    wide = up_weight.shape[1]
    tile = feed_tile
    tiles = wide // tile
    half, shard = width // 2, width // n_seq
    whole = lambda dtype: jax.ShapeDtypeStruct((tokens, width), dtype)
    fixed = lambda shape: pl.BlockSpec(shape, lambda i: (0, 0), pipeline_mode=pl.Buffered(1))
    at = lambda i: jnp.minimum(i, tiles - 1)
    hbm = pl.BlockSpec(memory_space=pl.ANY)
    late = lambda i: jnp.clip(i - 3, 0, tiles - 1)
    down_shape = (2, tile // (2 * piece_rows), 2, piece_rows, half)
    up_shape = (2, n_seq // 2, 2, shard, tile // 2)
    near = [pltpu.VMEM((2, tokens, tile), bf16)] * 2
    near += [pltpu.VMEM((width, tile), bf16), pltpu.VMEM((tile, width), bf16)]
    for shape in (down_shape, up_shape):
        near += [pltpu.VMEM(shape[:1] + (CORES,) + shape[1:], bf16), pltpu.VMEM(shape, bf16)]
    up_far = (2, n_seq // 4, 2, shard, tile // 2)
    far = [pltpu.VMEM(down_shape[:2] + down_shape[3:], bf16)] * 3 + [pltpu.VMEM(up_far, bf16)] * 3
    far += [pltpu.VMEM(up_far[:2] + up_far[3:], bf16)] * 3
    return pl.pallas_call(
        functools.partial(feed_kernel, tiles, 128),
        grid=(tiles + 4,),
        in_specs=[
            fixed((tokens, width)),
            fixed((tokens, width)),
            fixed((1, width)),
            pl.BlockSpec((width, tile), lambda i: (0, at(i))),
            pl.BlockSpec((tile, width), lambda i: (at(i), 0)),
            hbm,
            hbm,
        ],
        out_specs=[
            hbm,
            fixed((tokens, width)),
            hbm,
            hbm,
            hbm,
            hbm,
            pl.BlockSpec((tile // 2, half), lambda i: (late(i), 0)),
            pl.BlockSpec((width // 4, tile // 2), lambda i: (0, jnp.clip(i - 4, 0, tiles - 1))),
        ],
        scratch_shapes=[
            pltpu.VMEM((tokens, width), bf16),
            pltpu.VMEM((tokens, width), f32),
            pltpu.VMEM((tokens, width), bf16),
            pltpu.VMEM((half, width), bf16),
            pltpu.VMEM((width, half), bf16),
            pltpu.VMEM((width, half), bf16),
        ]
        + near
        + far
        + [pltpu.SemaphoreType.DMA((2, 2))] * 4
        + [pltpu.SemaphoreType.REGULAR, pltpu.SemaphoreType.REGULAR((2,)), pltpu.SemaphoreType.DMA((4,))]
        + [pltpu.SemaphoreType.DMA((2,))] * 2
        + [pltpu.SemaphoreType.DMA((11,))],
        out_shape=[
            whole(bf16),
            whole(f32),
            jax.ShapeDtypeStruct((2, tokens, width), bf16),
            jax.ShapeDtypeStruct(down_shape[:1] + (CORES,) + down_shape[1:], bf16),
            jax.ShapeDtypeStruct((width, half), bf16),
            jax.ShapeDtypeStruct((width, half), bf16),
            jax.ShapeDtypeStruct((wide // 2, half), bf16),
            jax.ShapeDtypeStruct((width // 4, wide // 2), bf16),
        ],
        compiler_params=pltpu.CompilerParams(
            vmem_limit_bytes=feed_vmem_bytes, collective_id=1, has_side_effects=True
        ),
        cost_estimate=pl.CostEstimate(
            flops=12 * tokens * width * wide,
            bytes_accessed=16 * tokens * width + 6 * width * wide,
            transcendentals=2 * tokens * wide,
        ),
        name="feed",
    )(middle, cot, gain.reshape(1, width), up_weight, down_weight, mixed_own, out_weight)


class Stream:
    def __init__(self, levels, rows, columns, first, count, lag):
        self.levels, self.rows, self.columns, self.first, self.count = levels, rows, columns, first, count
        self.lag = lag

    def shape(self, level):
        outer = 2 ** (len(self.levels) - 1 - level)
        return (max(outer // 2, 1), min(outer, 2), self.rows, self.columns)

    def scratch(self):
        shapes = []
        for level in range(len(self.levels)):
            shape = self.shape(level)
            shapes += [pltpu.VMEM(shape, bf16), pltpu.VMEM(shape, bf16), pltpu.VMEM((2,) + shape, bf16)]
        return shapes


down_pieces = 4


def streams_of(width, wide, n_seq, pairs):
    lanes = 2 * HDIM
    rows = width // (2 * n_seq)
    return (
        Stream(("x", "y", "z1", "z2"), rows, 4 * lanes, 1, pairs, 2),
        Stream(("y", "z1", "z2"), wide // (2 * n_seq * down_pieces), width // CORES, 2, down_pieces, 1),
        Stream(("x", "z2"), rows, wide // CORES // down_pieces, 2, down_pieces, 1),
    )


def back_kernel(pairs, tile, streams, row_count, *refs):
    (
        key_tags, query_tags, q_ref, k_ref, v_ref, o_ref, do_ref, lse_ref, n1_ref, own_weight, other_weight,
        gain_ref, out_kept, out_came, down_ref, up_ref, start_ref, d_middle_ref, outputs_ref,
    ) = refs[:19]
    grad_out, outputs_out, *gathered = refs[19:24]
    rest = list(refs[24:])
    take = lambda count: [rest.pop(0) for _ in range(count)]
    k_turned, dq_turned, delta, d_pair, d_came, d_n1, staged, start_part, middle_part = take(9)
    levels = []
    for stream in streams:
        levels.append([take(3) for _ in stream.levels])
    joined = take(len(streams))
    (
        send_sems, recv_sems, join_send, join_recv, core_send, core_recv, local_sems,
        pair_send, pair_recv, home_send, home_recv, home_local, part_sems, result_send, result_recv, result_local,
    ) = rest

    step = pl.program_id(0)
    tokens, lanes = q_ref.shape
    own_tokens = tokens // CORES
    seq_at, rows_at = lax.axis_index("seq"), lax.axis_index("rows")
    core, high = rows_at % 2, (rows_at // 2) % 2
    places = {"x": high, "y": seq_at % 2, "z1": (seq_at // 2) % 2, "z2": seq_at // 4}
    peers = {
        "x": (seq_at, rows_at + 2 - 4 * high),
        "y": (seq_at + 1 - 2 * places["y"], rows_at),
        "z1": (seq_at + 2 - 4 * places["z1"], rows_at),
        "z2": (seq_at + 4 - 8 * places["z2"], rows_at),
        "core": (seq_at, rows_at + 1 - 2 * core),
    }
    n_seq = 2 * row_count
    sub = start_part.shape[1]

    def remote(source, target, send, recv, peer):
        return pltpu.make_async_remote_copy(
            src_ref=source, dst_ref=target, send_sem=send, recv_sem=recv, device_id=peer, device_id_type=MESH
        )

    def add(a, b):
        return (a.astype(f32) + b.astype(f32)).astype(bf16)

    def level_copy(at, level, item):
        send, _, came = levels[at][level]
        slot = item % 2
        return remote(
            send, came.at[slot], send_sems.at[at, level], recv_sems.at[at, level, slot], peers[streams[at].levels[level]]
        )

    def join_copy(at, item):
        part = joined[at].at[item, high]
        return remote(part, part, join_send.at[at], join_recv.at[at, item % 2], peers["x"])

    def core_copy(at, item):
        return remote(
            joined[at].at[item],
            gathered[at].at[item, core],
            core_send.at[at],
            core_recv.at[at, item % 2],
            peers["core"],
        )

    def local_copy(at, item):
        return pltpu.make_async_copy(joined[at].at[item], gathered[at].at[item, core], local_sems.at[at])

    def pair_copy(item):
        slot = item % 2
        return remote(
            d_pair.at[slot, pl.ds(own_tokens, own_tokens)],
            d_came.at[slot],
            pair_send.at[slot],
            pair_recv.at[slot],
            peers["core"],
        )

    home = seq_at // row_count

    def to_home(block, own, result):
        if result:
            source, target = outputs_ref.at[pl.ds(pl.multiple_of(block * sub, sub), sub)], outputs_out
            sems = result_send, result_recv, result_local
        else:
            source, target = staged.at[block], grad_out
            sems = home_send, home_recv, home_local
        row = seq_at % row_count
        if own:
            return pltpu.make_async_copy(source, target.at[row, core], sems[2])
        return remote(source, target.at[row, core], sems[0].at[block], sems[1].at[row, core], (block, rows_at - core + home))

    def start_home(block, result):
        @pl.when(is_own(block))
        def _():
            to_home(block, True, result).start()

        @pl.when(jnp.logical_not(is_own(block)))
        def _():
            to_home(block, False, result).start()

    def wait_home(result):
        for block in range(n_seq):
            @pl.when(is_own(block))
            def _():
                to_home(block, True, result).wait()

            @pl.when(jnp.logical_not(is_own(block)))
            def _():
                to_home(block, False, result).wait_send()
        source, target = (outputs_ref.at[pl.ds(0, sub)], outputs_out) if result else (staged.at[0], grad_out)
        sems = (result_send, result_recv) if result else (home_send, home_recv)
        for row in range(row_count):
            for c in range(CORES):
                @pl.when(jnp.logical_not((seq_at == core * row_count + row) & (core == c)))
                def _():
                    remote(source, target.at[row, c], sems[0].at[0], sems[1].at[row, c], peers["core"]).wait_recv()

    def is_own(block):
        return (seq_at == block) & (home == core)

    @pl.when(step == 0)
    def _():
        barrier = pltpu.get_barrier_semaphore()
        for s in range(n_seq):
            for c in range(CORES):
                @pl.when(jnp.logical_not((seq_at == s) & (core == c)))
                def _():
                    pl.semaphore_signal(barrier, inc=1, device_id=(s, rows_at - core + c), device_id_type=MESH)
        pl.semaphore_signal(barrier, inc=1, device_id=peers["x"], device_id_type=MESH)
        pl.semaphore_wait(barrier, n_seq * CORES)
        d_n1[...] = jnp.zeros_like(d_n1)

    @pl.when(step < n_seq)
    def _():
        start_home((seq_at + step) % n_seq, True)

    working, second = step < 2 * pairs, step % 2

    @pl.when(working & (second == 0))
    def _():
        k_turned[...] = k_ref[...].T
        dq_turned[...] = (o_ref[...].astype(f32) * do_ref[...].astype(f32)).T
        for head in range(2):
            own_rows = dq_turned[head * HDIM : (head + 1) * HDIM, :]
            delta[head : head + 1, :] = jnp.sum(own_rows, axis=0, keepdims=True)
        dq_turned[...] = jnp.zeros_like(dq_turned)

    @pl.when(working)
    def _():
        slot = step // 2 % 2
        half_steps = tokens // tile // 2
        first = lax.broadcasted_iota(jnp.int32, (tile, lanes), 1) < HDIM

        def body(i, _):
            part = pl.ds(pl.multiple_of((i + second * half_steps) * tile, tile), tile)
            k, v = k_ref[part, :], v_ref[part, :]
            q, do = q_ref[...], do_ref[...]
            tag = key_tags[part, :]
            allowed = tag == query_tags[...]
            dk, dv = [], []
            for head in range(2):
                own = first if head == 0 else jnp.logical_not(first)
                own_rows = slice(head * HDIM, (head + 1) * HDIM)
                scores = dot(jnp.where(own, k, bf16(0)), q, 1, 1)
                scores = jnp.where(allowed, scores, masked_score)
                chances = jnp.exp2(scores * (score_scale * log2e) - lse_ref[head : head + 1, :])
                weight_grad = dot(jnp.where(own, v, bf16(0)), do, 1, 1)
                score_grad = (chances * (weight_grad - delta[head : head + 1, :])).astype(bf16)
                dv.append(dot(chances.astype(bf16), do, 1, 0))
                dk.append(dot(score_grad, q, 1, 0))
                dq_turned[own_rows, :] += dot(k_turned[own_rows, part], score_grad, 1, 0)
            d_pair[slot, part, lanes : 2 * lanes] = (jnp.where(first, dk[0], dk[1]) * score_scale).astype(bf16)
            d_v = jnp.where(first, dv[0], dv[1]).astype(bf16)
            d_pair[slot, part, 2 * lanes :] = jnp.where(tag < 0, do_ref[part, :], d_v)
            return 0

        lax.fori_loop(0, half_steps, body, 0)

    @pl.when(working & (second == 1))
    def _():
        d_pair[step // 2 % 2, :, :lanes] = (dq_turned[...] * score_scale).T.astype(bf16)

    def add_pair():
        item = step // 2 - 1
        slot = item % 2
        pair_copy(item).wait()
        d_n1[...] += dot(d_pair[slot, :own_tokens, :], own_weight[...], 1, 1) + dot(
            d_came[slot], other_weight[...], 1, 1
        )

    @pl.when((step >= 2) & (step <= 2 * pairs) & (second == 0))
    def _():
        add_pair()

    @pl.when(working & (second == 1))
    def _():
        pair_copy(step // 2).start()

    def part_copies(turn):
        rows = pl.ds(pl.multiple_of((seq_at + turn) % n_seq * sub, sub), sub)
        slot = turn % 2
        return (
            pltpu.make_async_copy(start_ref.at[rows], start_part.at[slot], part_sems.at[0, slot]),
            pltpu.make_async_copy(d_middle_ref.at[rows], middle_part.at[slot], part_sems.at[1, slot]),
        )

    @pl.when(step == 2 * pairs)
    def _():
        for copy in part_copies(0):
            copy.start()

        def body(turn, _):
            block = (seq_at + turn) % n_seq

            @pl.when(turn + 1 < n_seq)
            def _():
                for copy in part_copies(turn + 1):
                    copy.start()

            for copy in part_copies(turn):
                copy.wait()
            unit, scale = norm_parts(start_part[turn % 2].astype(f32))
            rows = pl.ds(pl.multiple_of(block * sub, sub), sub)
            grad = norm_back(d_n1[rows, :], gain_ref[...], unit, scale)
            staged[block] = (middle_part[turn % 2] + grad).astype(bf16)
            start_home(block, False)
            return 0

        lax.fori_loop(0, n_seq, body, 0)

    for at, stream in enumerate(streams):
        depth = len(stream.levels)

        def item_at(lag, stream=stream):
            since = step - stream.first - lag
            return since // 2, (since >= 0) & (since % 2 == 0) & (since < 2 * stream.count)

        item, here = item_at(depth + 1 + stream.lag)

        @pl.when(here)
        def _(at=at, item=item):
            core_copy(at, item).wait()
            local_copy(at, item).wait()

        item, here = item_at(depth + stream.lag)

        @pl.when(here)
        def _(at=at, item=item):
            join_copy(at, item).wait()
            core_copy(at, item).start()
            local_copy(at, item).start()

        for level in reversed(range(depth)):
            item, here = item_at(level + stream.lag)

            @pl.when(here)
            def _(at=at, item=item, level=level, stream=stream, depth=depth):
                _, keep, came = levels[at][level]
                slot = item % 2
                level_copy(at, level, item).wait_recv()
                if level == depth - 1:
                    joined[at][item, high] = add(keep[0, 0], came[slot, 0, 0])
                    join_copy(at, item).start()
                    return

                @pl.when(item > 0)
                def _():
                    level_copy(at, level + 1, item - 1).wait_send()

                next_send, next_keep, _ = levels[at][level + 1]
                place = places[stream.levels[level + 1]]
                next_send[...] = add(keep[:, 1 - place], came[slot, :, 1 - place]).reshape(next_send.shape)
                next_keep[...] = add(keep[:, place], came[slot, :, place]).reshape(next_keep.shape)
                level_copy(at, level + 1, item).start()

    def begin_piece(fills):
        for at, fill in fills.items():
            stream = streams[at]
            item = (step - stream.first) // 2

            @pl.when((step % 2 == stream.first % 2) & (step >= stream.first) & (item < stream.count))
            def _(at=at, fill=fill, item=item):
                @pl.when(item > 0)
                def _():
                    level_copy(at, 0, item - 1).wait_send()

                fill(*levels[at][0][:2])
                level_copy(at, 0, item).start()

    def fill_pair(send, keep):
        grad = dot(n1_ref[...], d_pair[step // 2 % 2], 0, 0).astype(bf16)
        grad = grad.reshape(n_seq, 2, send.shape[2], 3 * lanes)
        shape = send.shape[:3] + (3 * lanes,)

        @pl.when(high == 0)
        def _():
            send[:, :, :, : 3 * lanes] = grad[:, 1].reshape(shape)
            keep[:, :, :, : 3 * lanes] = grad[:, 0].reshape(shape)

        @pl.when(high != 0)
        def _():
            send[:, :, :, : 3 * lanes] = grad[:, 0].reshape(shape)
            keep[:, :, :, : 3 * lanes] = grad[:, 1].reshape(shape)

        shape = send.shape[:3] + (lanes,)
        send[:, :, :, 3 * lanes :] = add(out_kept[:, 1 - high], out_came[:, 1 - high]).reshape(shape)
        keep[:, :, :, 3 * lanes :] = add(out_kept[:, high], out_came[:, high]).reshape(shape)

    def fill_from(ref, place):
        def fill(send, keep):
            send[...] = ref[:, 1 - place].reshape(send.shape)
            keep[...] = ref[:, place].reshape(keep.shape)

        return fill

    begin_piece({0: fill_pair, 1: fill_from(down_ref, places["y"]), 2: fill_from(up_ref, high)})

    @pl.when(step == pl.num_programs(0) - 1)
    def _():
        for at, stream in enumerate(streams):
            for level in range(len(stream.levels)):
                level_copy(at, level, stream.count - 1).wait_send()
        wait_home(False)
        wait_home(True)


def back(
    qkv, mixed, d_mixed, lse, key_tags, query_tags, n1, weights, gain, out_kept, out_came, down_part, up_part,
    start, d_middle, outputs, row_count,
):
    tokens = qkv.shape[0]
    width = n1.shape[1]
    own_tokens = tokens // CORES
    lanes = 2 * HDIM
    pairs = qkv.shape[1] // (3 * lanes)
    n_seq = 2 * row_count
    tile = 512
    sub = own_tokens // n_seq
    streams = streams_of(width, down_part.shape[0] * 2, n_seq, pairs)
    last = pairs - 1
    now = lambda i: jnp.minimum(i // 2, last)
    before = lambda i: jnp.clip(i // 2 - 1, 0, last)
    early = lambda i: jnp.clip(i // 2 - 1, 0, down_pieces - 1)
    fixed = lambda shape: pl.BlockSpec(shape, lambda i: (0,) * len(shape), pipeline_mode=pl.Buffered(1))

    def columns(place):
        return pl.BlockSpec((tokens, lanes), lambda i: (0, 3 * now(i) + place))

    pair = pl.BlockSpec((tokens, lanes), lambda i: (0, now(i)))
    weight = pl.BlockSpec((width, 3 * lanes), lambda i: (0, before(i)))
    hbm = pl.BlockSpec(memory_space=pl.ANY)

    rows = streams[0].rows

    def out_piece(value):
        whole = value.reshape(n_seq, 2, rows, value.shape[1])
        return whole, pl.BlockSpec((n_seq, 2, rows, lanes), lambda i: (0, 0, 0, now(i)))

    outs = [out_piece(value) for value in (out_kept, out_came)]
    down = down_part.reshape(n_seq // 2, 2, -1, width // CORES)
    up = up_part.reshape(n_seq // 4, 2, rows, -1)
    down_spec = pl.BlockSpec((n_seq // 2, 2, streams[1].rows, width // CORES), lambda i: (0, 0, early(i), 0))
    up_spec = pl.BlockSpec((n_seq // 4, 2, rows, streams[2].columns), lambda i: (0, 0, 0, early(i)))
    count = len(streams)
    deepest = max(len(stream.levels) for stream in streams)
    return pl.pallas_call(
        functools.partial(back_kernel, pairs, tile, streams, row_count),
        grid=(2 * pairs + deepest + 1 + streams[0].lag,),
        in_specs=[
            fixed((tokens, 1)),
            fixed((1, tokens)),
            columns(0),
            columns(1),
            columns(2),
            pair,
            pair,
            pl.BlockSpec((None, 2, tokens), lambda i: (now(i), 0, 0)),
            fixed((tokens, width)),
            weight,
            weight,
            fixed((1, width)),
            outs[0][1],
            outs[1][1],
            down_spec,
            up_spec,
            hbm,
            hbm,
            hbm,
        ],
        out_specs=[hbm] * 5,
        out_shape=[jax.ShapeDtypeStruct((row_count, CORES, sub, width), bf16)] * 2
        + [jax.ShapeDtypeStruct((stream.count, CORES, 2, stream.rows, stream.columns), bf16) for stream in streams],
        scratch_shapes=[
            pltpu.VMEM((lanes, tokens), bf16),
            pltpu.VMEM((lanes, tokens), f32),
            pltpu.VMEM((2, tokens), f32),
            pltpu.VMEM((2, tokens, 3 * lanes), bf16),
            pltpu.VMEM((2, own_tokens, 3 * lanes), bf16),
            pltpu.VMEM((own_tokens, width), f32),
            pltpu.VMEM((n_seq, sub, width), bf16),
            pltpu.VMEM((2, sub, width), bf16),
            pltpu.VMEM((2, sub, width), f32),
        ]
        + [shape for stream in streams for shape in stream.scratch()]
        + [pltpu.VMEM((stream.count, 2, stream.rows, stream.columns), bf16) for stream in streams]
        + [
            pltpu.SemaphoreType.DMA((count, deepest)),
            pltpu.SemaphoreType.DMA((count, deepest, 2)),
            pltpu.SemaphoreType.DMA((count,)),
            pltpu.SemaphoreType.DMA((count, 2)),
            pltpu.SemaphoreType.DMA((count,)),
            pltpu.SemaphoreType.DMA((count, 2)),
            pltpu.SemaphoreType.DMA((count,)),
            pltpu.SemaphoreType.DMA((2,)),
            pltpu.SemaphoreType.DMA((2,)),
            pltpu.SemaphoreType.DMA((n_seq,)),
            pltpu.SemaphoreType.DMA((row_count, CORES)),
            pltpu.SemaphoreType.DMA,
            pltpu.SemaphoreType.DMA((2, 2)),
            pltpu.SemaphoreType.DMA((n_seq,)),
            pltpu.SemaphoreType.DMA((row_count, CORES)),
            pltpu.SemaphoreType.DMA,
        ],
        compiler_params=pltpu.CompilerParams(
            vmem_limit_bytes=feed_vmem_bytes, collective_id=2, has_side_effects=True
        ),
        cost_estimate=pl.CostEstimate(
            flops=80 * pairs * tokens * tokens * HDIM,
            bytes_accessed=16 * tokens * pairs * lanes,
            transcendentals=2 * pairs * tokens * tokens,
        ),
        name="back",
    )(
        key_tags, query_tags, qkv, qkv, qkv, mixed, d_mixed, lse, n1, weights[0], weights[1],
        gain.reshape(1, width), outs[0][0], outs[1][0], down, up, start, d_middle, outputs,
    )


def collect_kernel(pairs, seq_ref, *refs):
    qkv_parts, down_parts, up_parts = refs[:3]
    qkv_weights, up_weight = refs[3:9], refs[9]
    qkv_out, out_out, down_out, up_out, first_out, second_out, first_sum, second_sum = refs[10:]
    item = pl.program_id(0)
    lanes = 2 * HDIM
    rows = qkv_parts.shape[2]
    width = out_out.shape[1]
    half = width // CORES
    tile = feed_tile // CORES

    @pl.when(item == 0)
    def _():
        first_sum[...] = jnp.zeros_like(first_sum)
        second_sum[...] = jnp.zeros_like(second_sum)

    for core in range(CORES):
        place = pl.multiple_of(core * half + item * lanes, lanes)
        for high in range(2):
            own = slice(high * rows, (high + 1) * rows)
            part = qkv_parts[core, high].astype(f32)
            for kind in range(3):
                value = part[:, kind * lanes : (kind + 1) * lanes]
                qkv_out[own, pl.ds(kind * width + place, lanes)] = value
                weight = qkv_weights[kind * CORES + core][own, :].astype(f32)
                first_sum[own, :] += value * weight
            out_out[own, pl.ds(place, lanes)] = part[:, 3 * lanes :]

    @pl.when(item < down_pieces)
    def _():
        for core in range(CORES):
            for high in range(2):
                own = slice(high * rows, (high + 1) * rows)
                for at in range(up_parts.shape[3] // lanes):
                    column = item * up_parts.shape[3] + at * lanes
                    column = column // tile * feed_tile + core * tile + column % tile
                    columns = pl.ds(pl.multiple_of(column, lanes), lanes)
                    value = up_parts[core, high, :, at * lanes : (at + 1) * lanes].astype(f32)
                    up_out[own, columns] = value
                    second_sum[own, :] += value * up_weight[own, columns].astype(f32)
                count = down_parts.shape[2] // piece_rows
                for at in range(count):
                    start = ((item * count + at) * 2 + high) * piece_rows
                    value = down_parts[core, high, at * piece_rows : (at + 1) * piece_rows, :].astype(f32)
                    down_out[pl.ds(pl.multiple_of(start, piece_rows), piece_rows), core * half : (core + 1) * half] = value

    @pl.when(item == pairs - 1)
    def _():
        first_out[...] = jnp.sum(first_sum[...].T, axis=0, keepdims=True)
        second_out[...] = jnp.sum(second_sum[...].T, axis=0, keepdims=True)


def collect(seq_at, qkv_parts, down_parts, up_parts, qkv_weight, up_weight):
    pairs, _, _, rows, _ = qkv_parts.shape
    width, lanes = qkv_weight.shape[0], 2 * HDIM
    shard, wide = 2 * rows, up_weight.shape[1]
    down_rows = 2 * down_pieces * down_parts.shape[3]

    def parts(value):
        return pl.BlockSpec(
            (None,) + value.shape[1:], lambda i, seq: (jnp.minimum(i, value.shape[0] - 1), 0, 0, 0, 0)
        )

    def weight(kind, core):
        return pl.BlockSpec((shard, lanes), lambda i, seq: (seq[0], (kind * CORES + core) * pairs + i))

    whole = lambda shape: pl.BlockSpec(shape, lambda i, seq: (0, 0))
    return pl.pallas_call(
        functools.partial(collect_kernel, pairs),
        grid_spec=pltpu.PrefetchScalarGridSpec(
            num_scalar_prefetch=1,
            grid=(pairs,),
            in_specs=[parts(qkv_parts), parts(down_parts), parts(up_parts)]
            + [weight(kind, core) for kind in range(3) for core in range(CORES)]
            + [pl.BlockSpec((shard, wide), lambda i, seq: (seq[0], 0))],
            out_specs=[
                whole((shard, 3 * width)),
                whole((shard, width)),
                whole((down_rows, width)),
                whole((shard, wide)),
                whole((1, shard)),
                whole((1, shard)),
            ],
            scratch_shapes=[pltpu.VMEM((shard, lanes), f32)] * 2,
        ),
        out_shape=[
            jax.ShapeDtypeStruct((shard, 3 * width), f32),
            jax.ShapeDtypeStruct((shard, width), f32),
            jax.ShapeDtypeStruct((down_rows, width), f32),
            jax.ShapeDtypeStruct((shard, wide), f32),
            jax.ShapeDtypeStruct((1, shard), f32),
            jax.ShapeDtypeStruct((1, shard), f32),
        ],
        compiler_params=pltpu.CompilerParams(vmem_limit_bytes=vmem_bytes),
        name="collect",
    )(
        seq_at.reshape(1), qkv_parts, down_parts, up_parts, *[qkv_weight] * 6, up_weight,
    )


def add_split_kernel(has_two, bit_ref, *refs):
    ins, outs = refs[: 2 if has_two else 1], refs[2 if has_two else 1 :]
    value = ins[0][...]
    if has_two:
        value = (value.astype(f32) + ins[1][...].astype(f32)).astype(bf16)
    if len(outs) == 1:
        outs[0][...] = value
    else:
        sends = pl.program_id(0) == 0

        @pl.when(sends)
        def _():
            outs[0][...] = value

        @pl.when(jnp.logical_not(sends))
        def _():
            outs[1][...] = value


def add_split(kept, received, inner, bit):
    rows, columns = kept.shape
    values = [kept] if received is None else [kept, received.reshape(rows, columns)]
    if bit is None:
        if received is None:
            return None, kept
        count = 4 if rows % 64 == 0 else 1
        block = pl.BlockSpec((rows // count, columns), lambda i, bit: (i, 0))
        grid, ins, outs = (count,), [block] * 2, block
        shapes = jax.ShapeDtypeStruct((rows, columns), bf16)
        bit = jnp.zeros((), jnp.int32)
    else:
        outer = rows // (2 * inner)
        cut = 1
        while inner // cut * columns > 2**19 and inner % (32 * cut) == 0:
            cut *= 2
        values = [value.reshape(outer, 2, inner, columns) for value in values]
        ins = [
            pl.BlockSpec(
                (None, None, inner // cut, columns),
                lambda w, i, j, bit: (i, jnp.where(w == 0, 1 - bit[0], bit[0]), j, 0),
            )
        ] * len(values)
        outs = [
            pl.BlockSpec(
                (None, inner // cut, columns),
                lambda w, i, j, bit: (jnp.where(w == 0, i, outer - 1), jnp.where(w == 0, j, cut - 1), 0),
            ),
            pl.BlockSpec(
                (None, inner // cut, columns),
                lambda w, i, j, bit: (jnp.where(w == 0, 0, i), jnp.where(w == 0, 0, j), 0),
            ),
        ]
        grid = (2, outer, cut)
        shapes = [jax.ShapeDtypeStruct((outer, inner, columns), bf16)] * 2
    done = pl.pallas_call(
        functools.partial(add_split_kernel, len(values) == 2),
        grid_spec=pltpu.PrefetchScalarGridSpec(
            num_scalar_prefetch=1, grid=grid, in_specs=ins, out_specs=outs
        ),
        out_shape=shapes,
        cost_estimate=pl.CostEstimate(flops=rows * columns, bytes_accessed=6 * rows * columns, transcendentals=0),
        name="add_split",
    )(bit.reshape(1), *values)
    if not isinstance(done, (list, tuple)):
        return None, done
    return done[0].reshape(rows // 2, columns), done[1].reshape(rows // 2, columns)


def tie(*values):
    return lax.optimization_barrier(values)


def build(n_seq, n_rows):
    highs = n_rows // CORES
    seq_bits = n_seq.bit_length() - 1
    high_bits = highs.bit_length() - 1
    bits = seq_bits + high_bits

    def permute(value, target):
        pairs = []
        for s in range(n_seq):
            for r in range(n_rows):
                to_s, to_r = target(s, r)
                pairs.append((s * n_rows + r, to_s * n_rows + to_r))
        return lax.ppermute(value, AXES, pairs)

    def other_core(value):
        return permute(value, lambda s, r: (s, r ^ 1))

    def pick(value, place, axis):
        return lax.dynamic_index_in_dim(value, place, axis, keepdims=False)

    def bit_of(step):
        name, bit = step
        return (lax.axis_index(name) >> bit) & 1

    def across(value, step):
        name, bit = step
        if name == "rows":
            return permute(value, lambda s, r: (s, r ^ (1 << bit)))
        return permute(value, lambda s, r: (s ^ (1 << bit), r))

    high_steps = [("rows", bit + 1) for bit in reversed(range(high_bits))]
    seq_steps = [("seq", bit) for bit in range(seq_bits)]

    class Sum:
        def __init__(self, kept, received, order):
            self.rows, self.columns = kept.shape
            self.kept, self.received = kept, received
            self.left = [step for step in seq_steps[::-1] + high_steps if step in order]
            self.order = list(order)

        def finish(self):
            step = self.order[0] if self.order else None
            inner = self.rows
            if step is not None:
                axis = self.left.index(step)
                inner = self.rows >> (axis + 1)
            self.sent, self.kept = add_split(self.kept, self.received, inner, step and bit_of(step))
            self.received = None

        def begin(self):
            step = self.order.pop(0)
            self.left.remove(step)
            self.rows //= 2
            self.received = across(self.sent, step)

        def finished(self):
            while self.order:
                self.finish()
                self.begin()
            self.finish()
            return self.kept

    rows_first = high_steps + seq_steps[1:2] + seq_steps[:1] + seq_steps[2:]
    down_order = [step for step in seq_steps + high_steps if step != ("rows", 1)]
    up_order = [step for step in high_steps + seq_steps if step not in (("seq", 0), ("seq", 1))]

    def gather_high(value, pieces=0):
        for step in high_steps[::-1]:
            if pieces and step == ("rows", 1):
                continue
            received = across(value, step)
            value = jnp.where(
                bit_of(step) == 0,
                jnp.concatenate([value, received], 0),
                jnp.concatenate([received, value], 0),
            )
        if pieces:
            value = value.reshape(-1, 1, pieces, value.shape[1])
            received = across(value, ("rows", 1))
            value = jnp.where(
                bit_of(("rows", 1)) == 0,
                jnp.concatenate([value, received], 1),
                jnp.concatenate([received, value], 1),
            )
            value = value.reshape(-1, value.shape[-1])
        return value

    def back_by_steps(
        qkv, mixed, d_mixed, lse, key_tags, query_tags, n1_all, qkv_parts, attention_gain,
        out_kept, out_received, down_part, up_part, start, d_middle, to_member, ordered, from_rows, sizes,
    ):
        group, member, core, pairs, group_width, tokens, width = sizes
        lanes, half = 2 * HDIM, width // CORES
        unit1, scale1 = norm_parts(start)
        down = Sum(down_part, None, down_order)
        up = Sum(up_part, None, up_order)
        out = Sum(out_kept, out_received, rows_first)

        def before_next(*sums):
            nonlocal d_mixed
            for each in sums:
                each.finish()
            values = tie(d_mixed, *[v for each in sums for v in (each.sent, each.kept)])
            d_mixed = values[0]
            for at, each in enumerate(sums):
                each.sent, each.kept = values[1 + 2 * at : 3 + 2 * at]
                each.begin()

        def back_at(at):
            return attend_back(qkv, mixed, d_mixed, lse, key_tags, query_tags, at, 1)

        cut = max(1, 3 * pairs // 5)
        before_next(down, up)
        d_qkv, qkv_sums, d_parts = [], [], [[] for _ in range(group)]

        def take_piece(pieces):
            piece = jnp.concatenate(pieces, axis=1)
            d_parts[0].append(piece[:tokens])
            for hop in range(1, group):
                d_parts[hop].append(to_member(piece[hop * tokens : (hop + 1) * tokens], group - hop))
            return dot(n1_all, piece, 0, 0)

        grads = []
        for at in range(pairs):
            d_qkv.append(back_at(at))
            d_mixed, d_qkv[at] = tie(d_mixed, d_qkv[at])
            if at + 1 == cut:
                grads.append(take_piece(d_qkv))
            if at == min(0, pairs - 1):
                before_next(out)
            if at == min(1, pairs - 1):
                before_next(down, up)
            if at == min(3, pairs - 1):
                before_next(down, up, out)
        if pairs > cut:
            grads.append(take_piece(d_qkv[cut:]))
        if group == CORES:
            qkv_sums = [Sum(grad.astype(bf16), None, rows_first) for grad in grads]
        else:
            grad = jnp.concatenate(grads, 1)
            grad = grad.reshape(width, pairs, 3, lanes).transpose(0, 2, 1, 3)
            grad = grad.reshape(width, 3, 1, pairs * lanes)[..., :group_width]
            grad = lax.dynamic_update_slice_in_dim(
                jnp.zeros((width, 3, group, group_width), f32), grad, member, 2
            ).reshape(width, 3, CORES, half)
            kept = pick(grad, core, 2).astype(bf16).reshape(width, 3 * half)
            sent = pick(grad, 1 - core, 2).astype(bf16).reshape(width, 3 * half)
            qkv_sums = [Sum(kept, other_core(sent), rows_first)]

        d_n1 = jnp.zeros((tokens, width), f32)
        for part, weight in zip(d_parts, qkv_parts):
            d_n1 = d_n1 + dot(jnp.concatenate(part, 1), weight, 1, 1)
        input_grad = d_middle + norm_back(d_n1, attention_gain, unit1, scale1)
        input_grad = from_rows(input_grad.astype(bf16))

        down_total = gather_high(down.finished(), piece_rows)
        down_total = ordered(down_total, other_core(down_total), 1).astype(f32)
        tile = feed_tile // CORES
        up_total = gather_high(up.finished()).reshape(width // n_seq, -1, 1, tile)
        up_total = ordered(up_total, other_core(up_total), 2).reshape(width // n_seq, -1).astype(f32)
        out_total = gather_high(out.finished())
        out_total = ordered(out_total, other_core(out_total), 1).astype(f32)
        qkv_part = gather_high(jnp.concatenate([each.finished() for each in qkv_sums], 1))
        if group == CORES:
            qkv_part = qkv_part.reshape(-1, pairs, 3, lanes).transpose(0, 2, 1, 3)
        qkv_part = qkv_part.reshape(-1, 3, half)
        qkv_total = ordered(qkv_part[:, :, None], other_core(qkv_part)[:, :, None], 2)
        qkv_total = qkv_total.reshape(-1, 3 * width).astype(f32)

        return input_grad, qkv_total, out_total, down_total, up_total

    def per_device(
        inputs, cell_ids, valid_counts, cotangent, attention_gain, qkv_weight, out_weight, feed_gain, up_weight, down_weight
    ):
        row_count, block, width = inputs.shape
        seq_len = cell_ids.shape[1]
        heads = width // HDIM
        lanes = 2 * HDIM
        seq_at, rows_at = lax.axis_index("seq"), lax.axis_index("rows")
        core = rows_at % CORES
        chips = n_seq // (CORES * row_count)
        group = chips * CORES
        sub = block // group
        tokens = n_seq * sub
        member = (seq_at % chips) * CORES + core
        group_heads = heads // group
        pairs = -(-group_heads // 2)
        group_width = group_heads * HDIM
        padded = pairs * lanes - group_width

        def to_member(value, hop):
            def target(s, r):
                place = ((s % chips) * CORES + r % CORES + hop) % group
                return (s // chips * chips + place // CORES, r // CORES * CORES + place % CORES)

            return permute(value, target)

        def ordered(own, received, axis):
            return jnp.where(
                core == 0,
                jnp.concatenate([own, received], axis),
                jnp.concatenate([received, own], axis),
            )

        def to_rows(value):
            halves = value.reshape(row_count, CORES, block // CORES, width)
            received = other_core(pick(halves, 1 - core, 1))
            both = ordered(pick(halves, core, 1), received, 0).reshape(n_seq, sub, width)
            return lax.all_to_all(both, "seq", 0, 0, tiled=True).reshape(tokens, width)

        def from_rows(value):
            both = lax.all_to_all(value.reshape(n_seq, sub, width), "seq", 0, 0, tiled=True)
            both = both.reshape(CORES, row_count, block // CORES, width)
            received = other_core(pick(both, 1 - core, 0))
            own = pick(both, core, 0)
            return ordered(own[:, None], received[:, None], 1).reshape(row_count, block, width)

        places = jnp.arange(seq_len, dtype=jnp.int32)
        tags = jnp.where(places[None, :] < valid_counts[:, None], cell_ids, -1 - places[None, :])
        tags = ordered(tags, other_core(tags), 0)
        tags = pick(tags, seq_at // chips, 0).reshape(n_seq, CORES, chips, sub)
        tags = tags.transpose(2, 1, 0, 3).reshape(group, tokens)
        order = (member - jnp.arange(group, dtype=jnp.int32)) % group
        tags = jnp.take(tags, order, axis=0).reshape(1, seq_len)
        query_tags, key_tags = tags, tags.reshape(seq_len, 1)

        def pad_heads(value, axis):
            if not padded:
                return value
            fill = [(0, 0)] * value.ndim
            fill[axis] = (0, padded)
            return jnp.pad(value, fill)

        def qkv_of(hop):
            if group == CORES:
                return gather_pairs(((core + hop) % CORES).reshape(1), qkv_weight)
            piece = pick(qkv_weight.reshape(width, 3, group, group_width), (member + hop) % group, 2)
            piece = pad_heads(piece, 2).reshape(width, 3, pairs, lanes)
            return piece.transpose(0, 2, 1, 3).reshape(width, 3 * pairs * lanes)

        def out_of(hop):
            at = (member + hop) % group * group_width
            return pad_heads(lax.dynamic_slice_in_dim(out_weight, at, group_width, 0), 0)

        if chips == 1 and highs == 2:
            half = width // CORES
            x_row, n1, qkv, own_weight, other_weight = begin(inputs, qkv_weight, attention_gain)
            start = x_row.reshape(tokens, width)
            mixed, lse, cot, mixed_own = attend_row(qkv, key_tags, query_tags, cotangent)
            middle = start.astype(f32) + dot(mixed_own, out_weight, 1, 0)
            outputs, d_middle, _, d_mixed, out_kept, out_received, down_part, up_part = feed(
                middle, cot.reshape(tokens, width), feed_gain, up_weight, down_weight, mixed_own, out_weight, n_seq
            )
            input_grad, out_low, qkv_out, down_all, up_all = back(
                qkv, mixed, d_mixed.reshape(seq_len, half), lse, key_tags, query_tags, n1, (own_weight, other_weight), attention_gain,
                out_kept, out_received, down_part, up_part, start, d_middle, outputs, row_count,
            )
            qkv_total, out_total, down_total, up_total, first, second = collect(
                seq_at, qkv_out, down_all, up_all, qkv_weight, up_weight
            )
            shard = width // n_seq

            def gain_grad(sums, gain):
                return sums.reshape(shard) / lax.dynamic_slice_in_dim(gain, seq_at * shard, shard, 0)

            return (
                out_low.reshape(inputs.shape),
                input_grad.reshape(inputs.shape),
                gain_grad(first, attention_gain),
                qkv_total,
                out_total,
                gain_grad(second, feed_gain),
                up_total,
                down_total,
            )

        start = to_rows(inputs)
        qkv_parts = [qkv_of(hop) for hop in range(group)]
        out_parts = [out_of(hop) for hop in range(group)]
        start = start.astype(f32)
        unit1, scale1 = norm_parts(start)
        n1 = (unit1 * attention_gain).astype(bf16)
        n1_all = jnp.concatenate([n1] + [to_member(n1, hop) for hop in range(1, group)], 0)
        cotangent, _ = tie(cotangent, start[:1])
        cot = to_rows(cotangent)
        qkv = dot(n1_all, qkv_parts[0], 1, 0).astype(bf16)
        mixed, lse = attend(qkv, key_tags, query_tags)
        mixed_parts = [mixed[:tokens]] + [
            to_member(mixed[hop * tokens : (hop + 1) * tokens], group - hop) for hop in range(1, group)
        ]
        middle = start
        for part, weight in zip(mixed_parts, out_parts):
            middle = middle + dot(part, weight, 1, 0)
        if group == CORES:
            mixed_own = ordered(mixed_parts[0], mixed_parts[1], 1)
        else:
            slots = jnp.stack([part[:, :group_width] for part in mixed_parts])
            turn = (jnp.arange(group, dtype=jnp.int32) - member) % group
            mixed_own = jnp.take(slots, turn, axis=0).transpose(1, 0, 2).reshape(tokens, width)
        outputs, d_middle, d_attn, _, _, _, down_part, up_part = feed(
            middle, cot, feed_gain, up_weight, down_weight, mixed_own, out_weight, n_seq
        )
        d_attn = d_attn[0]

        d_attn_all = jnp.concatenate([d_attn] + [to_member(d_attn, hop) for hop in range(1, group)], 0)


        half = width // CORES
        out_grad = dot(mixed_own, d_attn, 0, 0).astype(bf16)
        out_kept = lax.dynamic_slice_in_dim(out_grad, core * half, half, 1)
        out_received = other_core(lax.dynamic_slice_in_dim(out_grad, (1 - core) * half, half, 1))
        d_mixed = dot(d_attn_all, out_parts[0], 1, 1).astype(bf16)

        out_low = from_rows(outputs)
        input_grad, qkv_total, out_total, down_total, up_total = back_by_steps(
            qkv, mixed, d_mixed, lse, key_tags, query_tags, n1_all, qkv_parts, attention_gain,
            out_kept, out_received, down_part, up_part, start, d_middle, to_member, ordered, from_rows,
            (group, member, core, pairs, group_width, tokens, width),
        )

        shard = width // n_seq

        def gain_total(weight, total, gain):
            rows = lax.dynamic_slice_in_dim(weight, seq_at * shard, shard, 0).astype(f32)
            return jnp.sum(rows * total, axis=1) / lax.dynamic_slice_in_dim(gain, seq_at * shard, shard, 0)

        return (
            out_low,
            input_grad,
            gain_total(qkv_weight, qkv_total, attention_gain),
            qkv_total,
            out_total,
            gain_total(up_weight, up_total, feed_gain),
            up_total,
            down_total,
        )

    return per_device


def solution(mesh):
    placed = (
        P("rows", "seq", None),
        P("rows", None),
        P("rows"),
        P("rows", "seq", None),
        P(),
        P(),
        P(),
        P(),
        P(),
        P(),
    )
    return jax.shard_map(
        build(mesh.shape["seq"], mesh.shape["rows"]),
        mesh=mesh,
        in_specs=placed,
        out_specs=(
            P("rows", "seq", None),
            P("rows", "seq", None),
            P("seq"),
            P("seq", None),
            P("seq", None),
            P("seq"),
            P("seq", None),
            P("seq", None),
        ),
        check_vma=False,
    )
```

```python
import functools

import jax
import jax.numpy as jnp
from jax import lax
from jax.experimental import pallas as pl
from jax.experimental.pallas import tpu as pltpu
from jax.sharding import PartitionSpec as P

HDIM = 64
CORES = 2
epsilon = 1e-05
masked_score = -1e30
score_scale = HDIM ** (-0.5)
log2e = 1.4426950408889634
bf16 = jnp.bfloat16
f32 = jnp.float32
AXES = ("seq", "rows")
vmem_bytes = 60 * 2**20
feed_vmem_bytes = 63 * 2**20
feed_tile = 512
max_cells = 7
MESH = pl.DeviceIdType.MESH


def dot(a, b, ca, cb):
    return lax.dot_general(a, b, (((ca,), (cb,)), ((), ())), preferred_element_type=f32)


def attend_kernel(tile, key_tags, query_tags, q_ref, k_ref, v_ref, o_ref, lse_ref, v_turned):
    tokens = q_ref.shape[0]
    v_turned[...] = v_ref[...].T
    lane = lax.broadcasted_iota(jnp.int32, (tile, 2 * HDIM), 1)

    def body(step, _):
        part = pl.ds(pl.multiple_of(step * tile, tile), tile)
        q = q_ref[part, :]
        allowed = key_tags[...] == query_tags[:, part]
        pieces = []
        for head in range(2):
            own = jnp.where((lane // HDIM) == head, q, bf16(0))
            scores = dot(k_ref[...], own, 1, 1)
            scores = jnp.where(allowed, scores, masked_score)
            peak = jnp.max(scores, axis=0, keepdims=True)
            powers = jnp.exp2((scores - peak) * (score_scale * log2e))
            total = jnp.sum(powers, axis=0, keepdims=True)
            mixed = dot(v_turned[head * HDIM : (head + 1) * HDIM, :], powers.astype(bf16), 1, 0)
            pieces.append(mixed * (1.0 / total))
            lse_ref[head : head + 1, part] = peak * (score_scale * log2e) + jnp.log2(total)
        o_ref[part, :] = jnp.concatenate(pieces, axis=0).T.astype(bf16)
        return 0

    lax.fori_loop(0, tokens // tile, body, 0)


def attend(qkv, key_tags, query_tags):
    tokens, width = qkv.shape
    lanes = 2 * HDIM
    pairs = width // (3 * lanes)
    tile = min(512, tokens)

    def columns(place):
        return pl.BlockSpec((tokens, lanes), lambda i: (0, 3 * i + place))

    return pl.pallas_call(
        functools.partial(attend_kernel, tile),
        grid=(pairs,),
        in_specs=[
            pl.BlockSpec((tokens, 1), lambda i: (0, 0)),
            pl.BlockSpec((1, tokens), lambda i: (0, 0)),
            columns(0),
            columns(1),
            columns(2),
        ],
        out_specs=[
            pl.BlockSpec((tokens, lanes), lambda i: (0, i)),
            pl.BlockSpec((None, 2, tokens), lambda i: (i, 0, 0)),
        ],
        out_shape=[
            jax.ShapeDtypeStruct((tokens, pairs * lanes), bf16),
            jax.ShapeDtypeStruct((pairs, 2, tokens), f32),
        ],
        scratch_shapes=[pltpu.VMEM((lanes, tokens), bf16)],
        compiler_params=pltpu.CompilerParams(vmem_limit_bytes=vmem_bytes),
        cost_estimate=pl.CostEstimate(
            flops=32 * pairs * tokens * tokens * HDIM,
            bytes_accessed=8 * tokens * pairs * lanes,
            transcendentals=2 * pairs * tokens * tokens,
        ),
        name="attend",
    )(key_tags, query_tags, qkv, qkv, qkv)


def attend_back_kernel(
    tile, key_tags, query_tags, q_ref, k_ref, v_ref, o_ref, do_ref, lse_ref, grad_ref, k_turned, dq_turned, delta
):
    tokens = q_ref.shape[0]
    lanes = 2 * HDIM
    k_turned[...] = k_ref[...].T
    dq_turned[...] = (o_ref[...].astype(f32) * do_ref[...].astype(f32)).T
    for head in range(2):
        rows = dq_turned[head * HDIM : (head + 1) * HDIM, :]
        delta[head : head + 1, :] = jnp.sum(rows, axis=0, keepdims=True)
    dq_turned[...] = jnp.zeros_like(dq_turned)
    first = lax.broadcasted_iota(jnp.int32, (tile, lanes), 1) < HDIM

    def body(step, _):
        part = pl.ds(pl.multiple_of(step * tile, tile), tile)
        k, v = k_ref[part, :], v_ref[part, :]
        q, do = q_ref[...], do_ref[...]
        allowed = key_tags[part, :] == query_tags[...]
        dk, dv = [], []
        for head in range(2):
            own = first if head == 0 else jnp.logical_not(first)
            own_rows = slice(head * HDIM, (head + 1) * HDIM)
            scores = dot(jnp.where(own, k, bf16(0)), q, 1, 1)
            scores = jnp.where(allowed, scores, masked_score)
            chances = jnp.exp2(scores * (score_scale * log2e) - lse_ref[head : head + 1, :])
            weight_grad = dot(jnp.where(own, v, bf16(0)), do, 1, 1)
            score_grad = (chances * (weight_grad - delta[head : head + 1, :])).astype(bf16)
            dv.append(dot(chances.astype(bf16), do, 1, 0))
            dk.append(dot(score_grad, q, 1, 0))
            dq_turned[own_rows, :] += dot(k_turned[own_rows, part], score_grad, 1, 0)
        grad_ref[part, lanes : 2 * lanes] = (jnp.where(first, dk[0], dk[1]) * score_scale).astype(bf16)
        grad_ref[part, 2 * lanes :] = jnp.where(first, dv[0], dv[1]).astype(bf16)
        return 0

    lax.fori_loop(0, tokens // tile, body, 0)
    grad_ref[:, :lanes] = (dq_turned[...] * score_scale).T.astype(bf16)


def attend_back(qkv, mixed, d_mixed, lse, key_tags, query_tags, start, count):
    tokens = qkv.shape[0]
    tile = min(512, tokens)
    lanes = 2 * HDIM

    def columns(place):
        return pl.BlockSpec((tokens, lanes), lambda i: (0, 3 * (start + i) + place))

    pair = pl.BlockSpec((tokens, lanes), lambda i: (0, start + i))
    return pl.pallas_call(
        functools.partial(attend_back_kernel, tile),
        grid=(count,),
        in_specs=[
            pl.BlockSpec((tokens, 1), lambda i: (0, 0)),
            pl.BlockSpec((1, tokens), lambda i: (0, 0)),
            columns(0),
            columns(1),
            columns(2),
            pair,
            pair,
            pl.BlockSpec((None, 2, tokens), lambda i: (start + i, 0, 0)),
        ],
        out_specs=pl.BlockSpec((tokens, 3 * lanes), lambda i: (0, i)),
        out_shape=jax.ShapeDtypeStruct((tokens, 3 * count * lanes), bf16),
        scratch_shapes=[
            pltpu.VMEM((lanes, tokens), bf16),
            pltpu.VMEM((lanes, tokens), f32),
            pltpu.VMEM((2, tokens), f32),
        ],
        compiler_params=pltpu.CompilerParams(vmem_limit_bytes=vmem_bytes),
        cost_estimate=pl.CostEstimate(
            flops=80 * count * tokens * tokens * HDIM,
            bytes_accessed=16 * tokens * count * lanes,
            transcendentals=2 * count * tokens * tokens,
        ),
        name="attend_back",
    )(key_tags, query_tags, qkv, qkv, qkv, mixed, d_mixed, lse)


def copy_kernel(core_ref, from_ref, to_ref):
    to_ref[...] = from_ref[...]


def gather_pairs(core, qkv_weight):
    width, lanes = qkv_weight.shape[0], 2 * HDIM
    pairs = width // (CORES * lanes)
    return pl.pallas_call(
        copy_kernel,
        grid_spec=pltpu.PrefetchScalarGridSpec(
            num_scalar_prefetch=1,
            grid=(pairs, 3),
            in_specs=[
                pl.BlockSpec((width, lanes), lambda i, j, core: (0, (j * CORES + core[0]) * pairs + i))
            ],
            out_specs=pl.BlockSpec((width, lanes), lambda i, j, core: (0, 3 * i + j)),
        ),
        out_shape=jax.ShapeDtypeStruct((width, 3 * pairs * lanes), qkv_weight.dtype),
        cost_estimate=pl.CostEstimate(flops=0, bytes_accessed=12 * width * pairs * lanes, transcendentals=0),
        name="gather_pairs",
    )(core, qkv_weight)


def norm_parts(values):
    center = values - jnp.mean(values, axis=-1, keepdims=True)
    spread = jnp.mean(center * center, axis=-1, keepdims=True)
    scale = lax.rsqrt(spread + epsilon)
    return center * scale, scale


def norm_back(grad, gain, unit, scale):
    e = grad * gain
    return scale * (
        e - jnp.mean(e, axis=-1, keepdims=True) - unit * jnp.mean(e * unit, axis=-1, keepdims=True)
    )


def all_signal(n_seq, seq_at, rows_at, extra=()):
    core = rows_at % CORES
    barrier = pltpu.get_barrier_semaphore()
    for s in range(n_seq):
        for c in range(CORES):
            @pl.when(jnp.logical_not((seq_at == s) & (core == c)))
            def _():
                pl.semaphore_signal(barrier, inc=1, device_id=(s, rows_at - core + c), device_id_type=MESH)
    for peer in extra:
        pl.semaphore_signal(barrier, inc=1, device_id=peer, device_id_type=MESH)
    pl.semaphore_wait(barrier, n_seq * CORES - 1 + len(extra))


class ToRows:
    def __init__(self, source, target, send, recv, local, row_count, seq_at, rows_at):
        self.source, self.target, self.send, self.recv, self.local = source, target, send, recv, local
        self.row_count, self.seq_at, self.rows_at = row_count, seq_at, rows_at
        self.core = rows_at % CORES

    def copy(self, row, c):
        chip = self.core * self.row_count + row
        return pltpu.make_async_remote_copy(
            src_ref=self.source.at[row, c],
            dst_ref=self.target.at[self.seq_at],
            send_sem=self.send.at[row, c],
            recv_sem=self.recv.at[self.seq_at],
            device_id=(chip, self.rows_at - self.core + c),
            device_id_type=MESH,
        )

    def own(self, row, c):
        return pltpu.make_async_copy(self.source.at[row, c], self.target.at[self.seq_at], self.local)

    def each(self, own, other):
        for row_turn in range(self.row_count):
            for core_turn in range(CORES):
                row = (row_turn + self.seq_at) % self.row_count
                c = (core_turn + self.seq_at // self.row_count) % CORES
                here = (self.core * self.row_count + row == self.seq_at) & (self.core == c)

                @pl.when(here)
                def _():
                    own(row, c)

                @pl.when(jnp.logical_not(here))
                def _():
                    other(row, c)

    def start(self):
        self.each(lambda row, c: self.own(row, c).start(), lambda row, c: self.copy(row, c).start())

    def wait_block(self, s):
        here = (s == self.seq_at) & (self.seq_at // self.row_count == self.core)

        @pl.when(here)
        def _():
            self.own(0, 0).wait()

        @pl.when(jnp.logical_not(here))
        def _():
            pltpu.make_async_remote_copy(
                src_ref=self.source.at[0, 0],
                dst_ref=self.target.at[s],
                send_sem=self.send.at[0, 0],
                recv_sem=self.recv.at[s],
                device_id=(self.seq_at, self.rows_at + 1 - 2 * self.core),
                device_id_type=MESH,
            ).wait_recv()

    def wait_sends(self):
        self.each(lambda row, c: None, lambda row, c: self.copy(row, c).wait_send())


def begin_kernel(
    row_count, pairs, x_ref, weight_ref, gain_ref, x_out, n1_out, qkv_out, own_out, other_out,
    x_part, n1, qkv, weight, other_weight,
    x_send, x_recv, x_local, n1_send, n1_recv, weight_sems, out_sems, x_sems, qkv_sems, n1_sems,
):
    seq_at, rows_at = lax.axis_index("seq"), lax.axis_index("rows")
    core = rows_at % CORES
    n_seq, sub, width = x_part.shape
    lanes = 2 * HDIM
    tokens = n_seq * sub
    moves = ToRows(x_ref, x_part, x_send, x_recv, x_local, row_count, seq_at, rows_at)

    def weight_copies(item, which):
        pair, kind = item // 3, item % 3
        to = pl.ds(pl.multiple_of(item * lanes, lanes), lanes)

        def columns(c):
            return pl.ds(pl.multiple_of((kind * CORES + c) * pairs * lanes + pair * lanes, lanes), lanes)

        source = weight_ref.at[:, columns(1 - core if which else core)]
        return pltpu.make_async_copy(source, (weight, other_weight)[which].at[:, to], weight_sems.at[which, item])

    def each_weight(act, which):
        def body(item, _):
            act(weight_copies(item, which))
            return 0

        lax.fori_loop(0, 3 * pairs, body, 0)

    each_weight(lambda copy: copy.start(), 0)
    all_signal(n_seq, seq_at, rows_at)
    moves.start()
    each_weight(lambda copy: copy.start(), 1)
    each_weight(lambda copy: copy.wait(), 0)
    weights_out = (
        pltpu.make_async_copy(weight, own_out, out_sems.at[0]),
        pltpu.make_async_copy(other_weight, other_out, out_sems.at[1]),
    )
    weights_out[0].start()
    each_weight(lambda copy: copy.wait(), 1)
    weights_out[1].start()

    def block_of(place):
        near = (place % 2) * ((place + 1) // 2) + (1 - place % 2) * ((n_seq - place // 2) % n_seq)
        return (seq_at + near) % n_seq

    def rows_of(s, other):
        return pl.ds(pl.multiple_of(s * sub + other * tokens, sub), sub)

    def n1_copy(s):
        return pltpu.make_async_remote_copy(
            src_ref=n1.at[rows_of(s, 0)],
            dst_ref=n1.at[rows_of(s, 1)],
            send_sem=n1_send.at[s],
            recv_sem=n1_recv.at[s],
            device_id=(seq_at, rows_at + 1 - 2 * core),
            device_id_type=MESH,
        )

    def x_copy(s):
        return pltpu.make_async_copy(x_part.at[s], x_out.at[s], x_sems.at[s])

    def out_copies(s, other):
        rows = rows_of(s, other)
        return (
            pltpu.make_async_copy(qkv.at[rows], qkv_out.at[rows], qkv_sems.at[other, s]),
            pltpu.make_async_copy(n1.at[rows], n1_out.at[rows], n1_sems.at[other, s]),
        )

    def product(first, second, other):
        both = jnp.concatenate([n1[rows_of(first, other), :], n1[rows_of(second, other), :]], 0)
        found = dot(both, weight[...], 1, 0).astype(bf16)
        for at, s in enumerate((first, second)):
            qkv[rows_of(s, other), :] = found[at * sub : (at + 1) * sub]
            for copy in out_copies(s, other):
                copy.start()

    def body(group, _):
        @pl.when(group < n_seq // 2)
        def _():
            places = block_of(2 * group), block_of(2 * group + 1)
            for s in places:
                moves.wait_block(s)
                x_copy(s).start()
                unit, _s = norm_parts(x_part[s].astype(f32))
                n1[rows_of(s, 0), :] = (unit * gain_ref[...]).astype(bf16)
                n1_copy(s).start()
            product(*places, 0)

        @pl.when(group > 0)
        def _():
            places = block_of(2 * group - 2), block_of(2 * group - 1)
            for s in places:
                n1_copy(s).wait()
            product(*places, 1)

        return 0

    lax.fori_loop(0, n_seq // 2 + 1, body, 0)

    def finish(s, _):
        x_copy(s).wait()
        for other in range(2):
            for copy in out_copies(s, other):
                copy.wait()
        return 0

    lax.fori_loop(0, n_seq, finish, 0)
    moves.wait_sends()
    for copy in weights_out:
        copy.wait()


def begin(inputs, qkv_weight, gain):
    row_count, block, width = inputs.shape
    n_seq = CORES * row_count
    lanes = 2 * HDIM
    pairs = width // (CORES * lanes)
    sub = block // CORES
    tokens = n_seq * sub
    hbm = pl.BlockSpec(memory_space=pl.ANY)
    return pl.pallas_call(
        functools.partial(begin_kernel, row_count, pairs),
        in_specs=[hbm, hbm, pl.BlockSpec(memory_space=pltpu.VMEM)],
        out_specs=[hbm] * 5,
        out_shape=[
            jax.ShapeDtypeStruct((n_seq, sub, width), bf16),
            jax.ShapeDtypeStruct((CORES * tokens, width), bf16),
            jax.ShapeDtypeStruct((CORES * tokens, 3 * pairs * lanes), bf16),
            jax.ShapeDtypeStruct((width, 3 * pairs * lanes), bf16),
            jax.ShapeDtypeStruct((width, 3 * pairs * lanes), bf16),
        ],
        scratch_shapes=[
            pltpu.VMEM((n_seq, sub, width), bf16),
            pltpu.VMEM((CORES * tokens, width), bf16),
            pltpu.VMEM((CORES * tokens, 3 * pairs * lanes), bf16),
            pltpu.VMEM((width, 3 * pairs * lanes), bf16),
            pltpu.VMEM((width, 3 * pairs * lanes), bf16),
            pltpu.SemaphoreType.DMA((row_count, CORES)),
            pltpu.SemaphoreType.DMA((n_seq,)),
            pltpu.SemaphoreType.DMA,
            pltpu.SemaphoreType.DMA((n_seq,)),
            pltpu.SemaphoreType.DMA((n_seq,)),
            pltpu.SemaphoreType.DMA((2, 3 * pairs)),
            pltpu.SemaphoreType.DMA((2,)),
            pltpu.SemaphoreType.DMA((n_seq,)),
            pltpu.SemaphoreType.DMA((CORES, n_seq)),
            pltpu.SemaphoreType.DMA((CORES, n_seq)),
        ],
        compiler_params=pltpu.CompilerParams(
            vmem_limit_bytes=vmem_bytes, collective_id=3, has_side_effects=True
        ),
        name="begin",
    )(inputs.reshape(row_count, CORES, sub, width), qkv_weight, gain.reshape(1, width))


def with_cells(value, tags, head, is_key):
    lane = lax.broadcasted_iota(jnp.int32, value.shape, 1)
    cell = lane - (1 - head) * HDIM
    if is_key:
        marks = jnp.where((cell == tags) | (cell >= max_cells), 0.0, -1.0)
    else:
        marks = jnp.where(cell == tags, -masked_score, 0.0)
    return jnp.where((lane // HDIM) == head, value, marks.astype(bf16))


def attend_row_kernel(
    tile, row_count, tags, row_tags, q_ref, k_ref, v_ref, cot_ref, x_ref, weight_ref, o_ref, lse_ref, cot_out, own_out,
    middle_out, v_turned, keys, scores_ref, mixed_ref, parts, x_part, weight, own, middle,
    cot_send, cot_recv, cot_local, part_send, part_recv, part_local, in_sems, out_sems,
):
    item, last = pl.program_id(0), pl.num_programs(0) - 1
    seq_at, rows_at = lax.axis_index("seq"), lax.axis_index("rows")
    core = rows_at % CORES
    tokens, lanes = q_ref.shape
    own_tokens = tokens // CORES
    n_seq, sub, _w = cot_out.shape
    moves = ToRows(cot_ref, cot_out, cot_send, cot_recv, cot_local, row_count, seq_at, rows_at)

    def part_copies(at):
        slot = at % 2
        half = pl.num_programs(0) * lanes
        columns = pl.ds(pl.multiple_of(core * half + at * lanes, lanes), lanes)
        return (
            pltpu.make_async_remote_copy(
                src_ref=parts.at[slot, pl.ds(own_tokens, own_tokens)],
                dst_ref=own_out.at[:, columns],
                send_sem=part_send.at[slot],
                recv_sem=part_recv.at[at],
                device_id=(seq_at, rows_at + 1 - 2 * core),
                device_id_type=MESH,
            ),
            pltpu.make_async_copy(parts.at[slot, pl.ds(0, own_tokens)], own_out.at[:, columns], part_local.at[slot]),
        )

    def part_came(at):
        half = pl.num_programs(0) * lanes
        columns = pl.ds(pl.multiple_of((1 - core) * half + at * lanes, lanes), lanes)
        return pltpu.make_async_remote_copy(
            src_ref=parts.at[0, pl.ds(own_tokens, own_tokens)],
            dst_ref=own_out.at[:, columns],
            send_sem=part_send.at[0],
            recv_sem=part_recv.at[at],
            device_id=(seq_at, rows_at + 1 - 2 * core),
            device_id_type=MESH,
        )

    def in_copies():
        return [
            pltpu.make_async_copy(x_ref, x_part, in_sems.at[0]),
            pltpu.make_async_copy(weight_ref, weight, in_sems.at[1]),
        ]

    def own_copy():
        return pltpu.make_async_copy(own_out, own, in_sems.at[2])

    def middle_copy(at):
        rows = pl.ds(at * sub, sub)
        return pltpu.make_async_copy(middle.at[rows], middle_out.at[rows], out_sems.at[at])

    @pl.when(item == 0)
    def _():
        all_signal(n_seq, seq_at, rows_at)
        moves.start()
        for copy in in_copies():
            copy.start()

    for head in range(2):
        keys[head] = with_cells(k_ref[...], tags[...], head, True)
        v_turned[head, :HDIM, :] = v_ref[...].T[head * HDIM : (head + 1) * HDIM, :]
        v_turned[head, HDIM:, :] = jnp.ones((16, tokens), bf16)

    def begin_scores(step, head):
        part = pl.ds(pl.multiple_of(step * tile, tile), tile)
        scores_ref[head] = dot(keys[head], with_cells(q_ref[part, :], tags[part, :], head, False), 1, 1)

    def finish(step, head):
        part = pl.ds(pl.multiple_of(step * tile, tile), tile)
        scores = scores_ref[head]
        peak = jnp.max(scores, axis=0, keepdims=True)
        powers = jnp.exp2((scores - peak) * (score_scale * log2e))
        mixed = dot(v_turned[head], powers.astype(bf16), 1, 0)
        total = mixed[HDIM : HDIM + 1, :]
        mixed_ref[head * HDIM : (head + 1) * HDIM, part] = mixed[:HDIM, :] * (1.0 / total)
        lse = peak * (score_scale * log2e) + jnp.log2(total)
        lse_ref[head : head + 1, part] = jnp.where(row_tags[:, part] < 0, -masked_score, lse)

    steps = tokens // tile
    begin_scores(0, 0)

    def body(step, _):
        begin_scores(step, 1)
        finish(step, 0)
        begin_scores(jnp.minimum(step + 1, steps - 1), 0)
        finish(step, 1)
        return 0

    lax.fori_loop(0, steps, body, 0)
    found = jnp.where(tags[...] < 0, v_ref[...], mixed_ref[...].T.astype(bf16))
    o_ref[...] = found

    @pl.when(item >= 2)
    def _():
        remote, local = part_copies(item - 2)
        remote.wait_send()
        local.wait()

    parts[item % 2] = found
    for copy in part_copies(item):
        copy.start()

    @pl.when(item == last)
    def _():
        for at in range(2):
            remote, local = part_copies(last - at)
            remote.wait_send()
            local.wait()
        for at in range(part_recv.shape[0]):
            part_came(at).wait_recv()
        own_copy().start()
        for copy in in_copies() + [own_copy()]:
            copy.wait()
        for at in range(n_seq // 2):
            rows = slice(2 * at * sub, 2 * (at + 1) * sub)
            middle[rows, :] = x_part[rows, :].astype(f32) + dot(own[rows, :], weight[...], 1, 0)
            middle_copy(2 * at).start()
            middle_copy(2 * at + 1).start()
        for s in range(n_seq):
            moves.wait_block(s)
        moves.wait_sends()
        for at in range(n_seq):
            middle_copy(at).wait()


def attend_row(qkv, tags, row_tags, cotangent, start, out_weight):
    tokens, width = qkv.shape
    row_count, block, model = cotangent.shape
    lanes = 2 * HDIM
    pairs = width // (3 * lanes)
    tile = 512
    n_seq, sub = CORES * row_count, block // CORES
    hbm = pl.BlockSpec(memory_space=pl.ANY)

    def columns(place):
        return pl.BlockSpec((tokens, lanes), lambda i: (0, 3 * i + place))

    return pl.pallas_call(
        functools.partial(attend_row_kernel, tile, row_count),
        grid=(pairs,),
        in_specs=[
            pl.BlockSpec((tokens, 1), lambda i: (0, 0)),
            pl.BlockSpec((1, tokens), lambda i: (0, 0)),
            columns(0),
            columns(1),
            columns(2),
            hbm,
            hbm,
            hbm,
        ],
        out_specs=[
            pl.BlockSpec((tokens, lanes), lambda i: (0, i)),
            pl.BlockSpec((None, 2, tokens), lambda i: (i, 0, 0)),
            hbm,
            hbm,
            hbm,
        ],
        out_shape=[
            jax.ShapeDtypeStruct((tokens, pairs * lanes), bf16),
            jax.ShapeDtypeStruct((pairs, 2, tokens), f32),
            jax.ShapeDtypeStruct((n_seq, sub, model), bf16),
            jax.ShapeDtypeStruct((tokens // CORES, model), bf16),
            jax.ShapeDtypeStruct((tokens // CORES, model), f32),
        ],
        scratch_shapes=[
            pltpu.VMEM((2, HDIM + 16, tokens), bf16),
            pltpu.VMEM((2, tokens, lanes), bf16),
            pltpu.VMEM((2, tokens, tile), f32),
            pltpu.VMEM((lanes, tokens), f32),
            pltpu.VMEM((2, tokens, lanes), bf16),
            pltpu.VMEM((tokens // CORES, model), bf16),
            pltpu.VMEM((model, model), bf16),
            pltpu.VMEM((tokens // CORES, model), bf16),
            pltpu.VMEM((tokens // CORES, model), f32),
            pltpu.SemaphoreType.DMA((row_count, CORES)),
            pltpu.SemaphoreType.DMA((n_seq,)),
            pltpu.SemaphoreType.DMA,
            pltpu.SemaphoreType.DMA((2,)),
            pltpu.SemaphoreType.DMA((pairs,)),
            pltpu.SemaphoreType.DMA((2,)),
            pltpu.SemaphoreType.DMA((3,)),
            pltpu.SemaphoreType.DMA((n_seq,)),
        ],
        compiler_params=pltpu.CompilerParams(
            vmem_limit_bytes=vmem_bytes, collective_id=4, has_side_effects=True
        ),
        name="attend_row",
    )(tags, row_tags, qkv, qkv, qkv, cotangent.reshape(row_count, CORES, sub, model), start, out_weight)


piece_rows = 16


def feed_kernel(
    tiles,
    rows,
    middle_ref,
    cot_ref,
    gain_ref,
    up_ref,
    down_ref,
    mixed_ref,
    out_weight_ref,
    out_ref,
    d_middle_ref,
    d_attn_out,
    d_mixed_out,
    out_kept,
    out_came,
    down_part,
    up_part,
    n2,
    total,
    d_attn,
    out_weight,
    out_keep,
    out_send,
    acts,
    d_ups,
    up_before,
    down_before,
    down_halves,
    down_recv,
    up_halves,
    up_recv,
    down_far_keep,
    down_far_send,
    down_far_recv,
    up_far_keep,
    up_far_send,
    up_far_recv,
    up_last_keep,
    up_last_send,
    up_last_recv,
    core_send_sem,
    core_recv_sem,
    far_send_sem,
    far_recv_sem,
    core_free,
    far_free,
    d_attn_sems,
    last_send_sem,
    last_recv_sem,
    out_sems,
):
    ahead = pl.program_id(0)
    step = ahead - 1
    tokens, width = n2.shape
    half, tile = width // 2, up_ref.shape[1]
    seq_at, rows_at = lax.axis_index("seq"), lax.axis_index("rows")
    core, high, low, mid = rows_at % 2, (rows_at // 2) % 2, seq_at % 2, (seq_at // 2) % 2
    core_peer = (seq_at, rows_at + 1 - 2 * core)
    far_peers = ((seq_at, rows_at + 2 - 4 * high), (seq_at + 1 - 2 * low, rows_at))
    last_peer = (seq_at + 2 - 4 * mid, rows_at)

    def copies(slot, far):
        if far:
            refs = ((down_far_send, down_far_recv), (up_far_send, up_far_recv))
            sems, peers = (far_send_sem, far_recv_sem), far_peers
        else:
            refs = ((down_halves.at[:, 1 - core], down_recv), (up_halves.at[:, 1 - core], up_recv))
            sems, peers = (core_send_sem, core_recv_sem), (core_peer, core_peer)
        return [
            pltpu.make_async_remote_copy(
                src_ref=refs[kind][0].at[slot],
                dst_ref=refs[kind][1].at[slot],
                send_sem=sems[0].at[kind, slot],
                recv_sem=sems[1].at[kind, slot],
                device_id=peers[kind],
                device_id_type=MESH,
            )
            for kind in range(2)
        ]

    def signal(sem, peer):
        pl.semaphore_signal(sem, inc=1, device_id=peer, device_id_type=MESH)

    @pl.when(ahead == 0)
    def _():
        barrier = pltpu.get_barrier_semaphore()
        for peer in (core_peer,) + far_peers + (last_peer,):
            signal(barrier, peer)
        pl.semaphore_wait(barrier, 4)

        def body(i, _):
            part = pl.ds(pl.multiple_of(i * rows, rows), rows)
            unit, _s = norm_parts(middle_ref[part, :])
            n2[part, :] = (unit * gain_ref[...]).astype(bf16)
            return 0

        lax.fori_loop(0, tokens // rows, body, 0)
        total[...] = middle_ref[...]
        d_middle_ref[...] = jnp.zeros_like(d_middle_ref)

    def activate():
        up = dot(n2[...], up_ref[...], 1, 0)
        d_act = dot(cot_ref[...], down_ref[...], 1, 1)
        share = 0.5 + 0.5 * lax.erf(up * (0.5**0.5))
        density = jnp.exp(-0.5 * up * up) * 0.3989422804014327
        acts[ahead % 2] = (up * share).astype(bf16)
        d_ups[ahead % 2] = (d_act * (share + up * density)).astype(bf16)

    def use():
        slot = step % 2
        act, d_up = acts[slot], d_ups[slot]
        total[...] += dot(act, down_before[...], 1, 0)
        d_middle_ref[...] += dot(d_up, up_before[...], 1, 1)
        up_grad = dot(n2[...], d_up, 0, 0).astype(bf16)
        cut = up_grad.shape[1] // 2
        up_halves[slot, 0] = up_grad[:, :cut].reshape(up_halves.shape[2:])
        up_halves[slot, 1] = up_grad[:, cut:].reshape(up_halves.shape[2:])
        down_grad = dot(act, cot_ref[...], 0, 0).astype(bf16)
        down_halves[slot, 0] = down_grad[:, :half].reshape(down_halves.shape[2:])
        down_halves[slot, 1] = down_grad[:, half:].reshape(down_halves.shape[2:])

    @pl.when((step >= 2) & (step < tiles))
    def _():
        for copy in copies(step % 2, False):
            copy.wait_send()

    @pl.when(ahead == 0)
    def _():
        activate()

    @pl.when((ahead > 0) & (ahead < tiles))
    def _():
        activate()
        use()

    @pl.when(ahead == tiles)
    def _():
        use()

    @pl.when(ahead < tiles)
    def _():
        up_before[...] = up_ref[...]
        down_before[...] = down_ref[...]

    def add(a, b):
        return (a.astype(f32) + b.astype(f32)).astype(bf16)

    def last_copy(slot):
        return pltpu.make_async_remote_copy(
            src_ref=up_last_send.at[slot],
            dst_ref=up_last_recv.at[slot],
            send_sem=last_send_sem.at[slot],
            recv_sem=last_recv_sem.at[slot],
            device_id=last_peer,
            device_id_type=MESH,
        )

    def last_add():
        slot = (step + 1) % 2
        last_copy(slot).wait_recv()
        up_part[...] = add(up_last_keep[slot], up_last_recv[slot]).reshape(up_part.shape)

    def far_add():
        slot = step % 2
        for copy in copies(slot, True):
            copy.wait_recv()
        down_part[...] = add(down_far_keep[slot], down_far_recv[slot]).reshape(down_part.shape)

        @pl.when(step >= 4)
        def _():
            last_copy(slot).wait_send()

        up_last_send[slot] = add(up_far_keep[slot, :, 1 - mid], up_far_recv[slot, :, 1 - mid])
        up_last_keep[slot] = add(up_far_keep[slot, :, mid], up_far_recv[slot, :, mid])
        last_copy(slot).start()

        @pl.when(step < tiles)
        def _():
            signal(far_free.at[0], far_peers[0])
            signal(far_free.at[1], far_peers[1])

    def pass_on():
        slot = (step + 1) % 2
        for copy in copies(slot, False):
            copy.wait_recv()

        @pl.when(step >= 3)
        def _():
            for copy in copies(slot, True):
                copy.wait_send()
            pl.semaphore_wait(far_free.at[0], 1)
            pl.semaphore_wait(far_free.at[1], 1)

        down_far_send[slot] = add(down_halves[slot, core, :, 1 - high], down_recv[slot, :, 1 - high])
        down_far_keep[slot] = add(down_halves[slot, core, :, high], down_recv[slot, :, high])
        shape = up_far_send.shape[1:]
        up_far_send[slot] = add(up_halves[slot, core, :, 1 - low], up_recv[slot, :, 1 - low]).reshape(shape)
        up_far_keep[slot] = add(up_halves[slot, core, :, low], up_recv[slot, :, low]).reshape(shape)
        for copy in copies(slot, True):
            copy.start()

        @pl.when(step < tiles - 1)
        def _():
            signal(core_free, core_peer)

    @pl.when((step >= 3) & (step <= tiles + 1))
    def _():
        last_add()

    @pl.when((step >= 2) & (step <= tiles))
    def _():
        far_add()

    @pl.when((step >= 1) & (step <= tiles))
    def _():
        pass_on()

    @pl.when((step >= 0) & (step < tiles))
    def _():
        @pl.when(step >= 2)
        def _():
            pl.semaphore_wait(core_free, 1)

        for copy in copies(step % 2, False):
            copy.start()

    @pl.when(step == tiles)
    def _():
        def body(i, _):
            part = pl.ds(pl.multiple_of(i * rows, rows), rows)
            low_total = total[part, :].astype(bf16)
            for at in range(2):
                acts[at, part, :] = low_total[:, at * tile : (at + 1) * tile]
            d_ups[0, part, : width - 2 * tile] = low_total[:, 2 * tile :]
            unit, scale = norm_parts(middle_ref[part, :])
            grad = cot_ref[part, :].astype(f32) + norm_back(d_middle_ref[part, :], gain_ref[...], unit, scale)
            d_middle_ref[part, :] = grad
            d_attn[part, :] = grad.astype(bf16)
            return 0

        lax.fori_loop(0, tokens // rows, body, 0)

    def to_core(source, target, at):
        return pltpu.make_async_remote_copy(
            src_ref=source,
            dst_ref=target,
            send_sem=d_attn_sems.at[at],
            recv_sem=d_attn_sems.at[at + 1],
            device_id=core_peer,
            device_id_type=MESH,
        )

    d_attn_copy = lambda: to_core(d_attn, d_attn_out.at[1], 0)
    out_copy = lambda: to_core(out_send, out_came, 2)
    mixed_copy = lambda: pltpu.make_async_copy(mixed_ref, n2, out_sems.at[0])
    weight_copy = lambda: pltpu.make_async_copy(
        out_weight_ref.at[pl.ds(pl.multiple_of(core * half, half), half)], out_weight, out_sems.at[1]
    )
    d_attn_save = lambda: pltpu.make_async_copy(d_attn, d_attn_out.at[0], out_sems.at[2])
    out_save = lambda: pltpu.make_async_copy(out_keep, out_kept, out_sems.at[3])
    d_mixed_save = lambda: pltpu.make_async_copy(down_halves, d_mixed_out, out_sems.at[4])

    def in_slots():
        wide = [(acts.at[at], pl.ds(at * tile, tile)) for at in range(2)]
        wide.append((d_ups.at[0, :, pl.ds(0, width - 2 * tile)], pl.ds(2 * tile, width - 2 * tile)))
        return list(enumerate(wide))

    def total_saves():
        return [
            pltpu.make_async_copy(source, out_ref.at[:, columns], out_sems.at[5 + at])
            for at, (source, columns) in in_slots()
        ]

    def d_attn_loads():
        return [
            pltpu.make_async_copy(d_attn_out.at[1, :, columns], target, out_sems.at[8 + at])
            for at, (target, columns) in in_slots()
        ]

    @pl.when(step == tiles)
    def _():
        for copy in total_saves():
            copy.start()
        d_attn_copy().start()
        d_attn_save().start()
        mixed_copy().start()
        weight_copy().start()

    @pl.when(step == tiles + 1)
    def _():
        mixed_copy().wait()
        grad = dot(n2[...], d_attn[...], 0, 0).astype(bf16)

        @pl.when(core == 0)
        def _():
            out_keep[...] = grad[:, :half]
            out_send[...] = grad[:, half:]

        @pl.when(core != 0)
        def _():
            out_keep[...] = grad[:, half:]
            out_send[...] = grad[:, :half]

        out_copy().start()
        out_save().start()
        far_add()

    @pl.when(step == tiles + 2)
    def _():
        for copy in total_saves():
            copy.wait()
        d_attn_copy().wait()
        for copy in d_attn_loads():
            copy.start()
        weight_copy().wait()
        for slot in range(2):
            for copy in copies(slot, False):
                copy.wait_send()

        def keep_d_mixed(at, found):
            found = found.astype(bf16).reshape((-1,) + down_halves.shape[2:])
            down_halves[at, : found.shape[0]] = found

        keep_d_mixed(0, dot(d_attn[...], out_weight[...], 1, 1))
        for copy in d_attn_loads():
            copy.wait()
        other = jnp.concatenate([acts[0], acts[1], d_ups[0, :, : width - 2 * tile]], 1)
        keep_d_mixed(1, dot(other, out_weight[...], 1, 1))
        d_mixed_save().start()
        last_add()
        out_copy().wait()
        for copy in (d_attn_save(), out_save(), d_mixed_save()):
            copy.wait()
        for slot in range(2):
            last_copy(slot).wait_send()
            for copy in copies(slot, True):
                copy.wait_send()


def feed(middle, cot, gain, up_weight, down_weight, mixed_own, out_weight, n_seq):
    tokens, width = middle.shape
    wide = up_weight.shape[1]
    tile = feed_tile
    tiles = wide // tile
    half, shard = width // 2, width // n_seq
    whole = lambda dtype: jax.ShapeDtypeStruct((tokens, width), dtype)
    fixed = lambda shape: pl.BlockSpec(shape, lambda i: (0, 0), pipeline_mode=pl.Buffered(1))
    at = lambda i: jnp.minimum(i, tiles - 1)
    hbm = pl.BlockSpec(memory_space=pl.ANY)
    late = lambda i: jnp.clip(i - 3, 0, tiles - 1)
    down_shape = (2, tile // (2 * piece_rows), 2, piece_rows, half)
    up_shape = (2, n_seq // 2, 2, shard, tile // 2)
    near = [pltpu.VMEM((2, tokens, tile), bf16)] * 2
    near += [pltpu.VMEM((width, tile), bf16), pltpu.VMEM((tile, width), bf16)]
    for shape in (down_shape, up_shape):
        near += [pltpu.VMEM(shape[:1] + (CORES,) + shape[1:], bf16), pltpu.VMEM(shape, bf16)]
    up_far = (2, n_seq // 4, 2, shard, tile // 2)
    far = [pltpu.VMEM(down_shape[:2] + down_shape[3:], bf16)] * 3 + [pltpu.VMEM(up_far, bf16)] * 3
    far += [pltpu.VMEM(up_far[:2] + up_far[3:], bf16)] * 3
    return pl.pallas_call(
        functools.partial(feed_kernel, tiles, 128),
        grid=(tiles + 4,),
        in_specs=[
            fixed((tokens, width)),
            fixed((tokens, width)),
            fixed((1, width)),
            pl.BlockSpec((width, tile), lambda i: (0, at(i))),
            pl.BlockSpec((tile, width), lambda i: (at(i), 0)),
            hbm,
            hbm,
        ],
        out_specs=[
            hbm,
            fixed((tokens, width)),
            hbm,
            hbm,
            hbm,
            hbm,
            pl.BlockSpec((tile // 2, half), lambda i: (late(i), 0)),
            pl.BlockSpec((width // 4, tile // 2), lambda i: (0, jnp.clip(i - 4, 0, tiles - 1))),
        ],
        scratch_shapes=[
            pltpu.VMEM((tokens, width), bf16),
            pltpu.VMEM((tokens, width), f32),
            pltpu.VMEM((tokens, width), bf16),
            pltpu.VMEM((half, width), bf16),
            pltpu.VMEM((width, half), bf16),
            pltpu.VMEM((width, half), bf16),
        ]
        + near
        + far
        + [pltpu.SemaphoreType.DMA((2, 2))] * 4
        + [pltpu.SemaphoreType.REGULAR, pltpu.SemaphoreType.REGULAR((2,)), pltpu.SemaphoreType.DMA((4,))]
        + [pltpu.SemaphoreType.DMA((2,))] * 2
        + [pltpu.SemaphoreType.DMA((11,))],
        out_shape=[
            whole(bf16),
            whole(f32),
            jax.ShapeDtypeStruct((2, tokens, width), bf16),
            jax.ShapeDtypeStruct(down_shape[:1] + (CORES,) + down_shape[1:], bf16),
            jax.ShapeDtypeStruct((width, half), bf16),
            jax.ShapeDtypeStruct((width, half), bf16),
            jax.ShapeDtypeStruct((wide // 2, half), bf16),
            jax.ShapeDtypeStruct((width // 4, wide // 2), bf16),
        ],
        compiler_params=pltpu.CompilerParams(
            vmem_limit_bytes=feed_vmem_bytes, collective_id=1, has_side_effects=True
        ),
        cost_estimate=pl.CostEstimate(
            flops=12 * tokens * width * wide,
            bytes_accessed=16 * tokens * width + 6 * width * wide,
            transcendentals=2 * tokens * wide,
        ),
        name="feed",
    )(middle, cot, gain.reshape(1, width), up_weight, down_weight, mixed_own, out_weight)


class Stream:
    def __init__(self, levels, rows, columns, first, count, lag):
        self.levels, self.rows, self.columns, self.first, self.count = levels, rows, columns, first, count
        self.lag = lag

    def shape(self, level):
        outer = 2 ** (len(self.levels) - 1 - level)
        return (max(outer // 2, 1), min(outer, 2), self.rows, self.columns)

    def scratch(self):
        shapes = []
        for level in range(len(self.levels)):
            shape = self.shape(level)
            shapes += [pltpu.VMEM(shape, bf16), pltpu.VMEM(shape, bf16), pltpu.VMEM((2,) + shape, bf16)]
        return shapes


down_pieces = 4


def streams_of(width, wide, n_seq, pairs):
    lanes = 2 * HDIM
    rows = width // (2 * n_seq)
    return (
        Stream(("x", "y", "z1", "z2"), rows, 4 * lanes, 1, pairs, 2),
        Stream(("y", "z1", "z2"), wide // (2 * n_seq * down_pieces), width // CORES, 2, down_pieces, 1),
        Stream(("x", "z2"), rows, wide // CORES // down_pieces, 2, down_pieces, 1),
    )


def back_kernel(pairs, tile, streams, row_count, *refs):
    (
        key_tags, query_tags, q_ref, k_ref, v_ref, o_ref, do_ref, lse_ref, n1_ref, own_weight, other_weight,
        gain_ref, out_kept, out_came, down_ref, up_ref, start_ref, d_middle_ref, outputs_ref,
    ) = refs[:19]
    grad_out, outputs_out, *gathered = refs[19:24]
    rest = list(refs[24:])
    take = lambda count: [rest.pop(0) for _ in range(count)]
    k_turned, dq_turned, delta, d_pair, d_came, d_n1, staged, start_part, middle_part = take(9)
    levels = []
    for stream in streams:
        levels.append([take(3) for _ in stream.levels])
    joined = take(len(streams))
    (
        send_sems, recv_sems, join_send, join_recv, core_send, core_recv, local_sems,
        pair_send, pair_recv, home_send, home_recv, home_local, part_sems, result_send, result_recv, result_local,
    ) = rest

    step = pl.program_id(0)
    tokens, lanes = q_ref.shape
    own_tokens = tokens // CORES
    seq_at, rows_at = lax.axis_index("seq"), lax.axis_index("rows")
    core, high = rows_at % 2, (rows_at // 2) % 2
    places = {"x": high, "y": seq_at % 2, "z1": (seq_at // 2) % 2, "z2": seq_at // 4}
    peers = {
        "x": (seq_at, rows_at + 2 - 4 * high),
        "y": (seq_at + 1 - 2 * places["y"], rows_at),
        "z1": (seq_at + 2 - 4 * places["z1"], rows_at),
        "z2": (seq_at + 4 - 8 * places["z2"], rows_at),
        "core": (seq_at, rows_at + 1 - 2 * core),
    }
    n_seq = 2 * row_count
    sub = start_part.shape[1]

    def remote(source, target, send, recv, peer):
        return pltpu.make_async_remote_copy(
            src_ref=source, dst_ref=target, send_sem=send, recv_sem=recv, device_id=peer, device_id_type=MESH
        )

    def add(a, b):
        return (a.astype(f32) + b.astype(f32)).astype(bf16)

    def level_copy(at, level, item):
        send, _, came = levels[at][level]
        slot = item % 2
        return remote(
            send, came.at[slot], send_sems.at[at, level], recv_sems.at[at, level, slot], peers[streams[at].levels[level]]
        )

    def join_copy(at, item):
        part = joined[at].at[item, high]
        return remote(part, part, join_send.at[at], join_recv.at[at, item % 2], peers["x"])

    def core_copy(at, item):
        return remote(
            joined[at].at[item],
            gathered[at].at[item, core],
            core_send.at[at],
            core_recv.at[at, item % 2],
            peers["core"],
        )

    def local_copy(at, item):
        return pltpu.make_async_copy(joined[at].at[item], gathered[at].at[item, core], local_sems.at[at])

    def pair_copy(item):
        slot = item % 2
        return remote(
            d_pair.at[slot, pl.ds(own_tokens, own_tokens)],
            d_came.at[slot],
            pair_send.at[slot],
            pair_recv.at[slot],
            peers["core"],
        )

    home = seq_at // row_count

    def to_home(block, own, result):
        if result:
            source, target = outputs_ref.at[pl.ds(pl.multiple_of(block * sub, sub), sub)], outputs_out
            sems = result_send, result_recv, result_local
        else:
            source, target = staged.at[block], grad_out
            sems = home_send, home_recv, home_local
        row = seq_at % row_count
        if own:
            return pltpu.make_async_copy(source, target.at[row, core], sems[2])
        return remote(source, target.at[row, core], sems[0].at[block], sems[1].at[row, core], (block, rows_at - core + home))

    def start_home(block, result):
        @pl.when(is_own(block))
        def _():
            to_home(block, True, result).start()

        @pl.when(jnp.logical_not(is_own(block)))
        def _():
            to_home(block, False, result).start()

    def wait_home(result):
        for block in range(n_seq):
            @pl.when(is_own(block))
            def _():
                to_home(block, True, result).wait()

            @pl.when(jnp.logical_not(is_own(block)))
            def _():
                to_home(block, False, result).wait_send()
        source, target = (outputs_ref.at[pl.ds(0, sub)], outputs_out) if result else (staged.at[0], grad_out)
        sems = (result_send, result_recv) if result else (home_send, home_recv)
        for row in range(row_count):
            for c in range(CORES):
                @pl.when(jnp.logical_not((seq_at == core * row_count + row) & (core == c)))
                def _():
                    remote(source, target.at[row, c], sems[0].at[0], sems[1].at[row, c], peers["core"]).wait_recv()

    def is_own(block):
        return (seq_at == block) & (home == core)

    @pl.when(step == 0)
    def _():
        barrier = pltpu.get_barrier_semaphore()
        for s in range(n_seq):
            for c in range(CORES):
                @pl.when(jnp.logical_not((seq_at == s) & (core == c)))
                def _():
                    pl.semaphore_signal(barrier, inc=1, device_id=(s, rows_at - core + c), device_id_type=MESH)
        pl.semaphore_signal(barrier, inc=1, device_id=peers["x"], device_id_type=MESH)
        pl.semaphore_wait(barrier, n_seq * CORES)
        d_n1[...] = jnp.zeros_like(d_n1)

    @pl.when(step < n_seq)
    def _():
        start_home((seq_at + step) % n_seq, True)

    working, second = step < 2 * pairs, step % 2

    @pl.when(working & (second == 0))
    def _():
        k_turned[...] = k_ref[...].T
        dq_turned[...] = (o_ref[...].astype(f32) * do_ref[...].astype(f32)).T
        for head in range(2):
            own_rows = dq_turned[head * HDIM : (head + 1) * HDIM, :]
            delta[head : head + 1, :] = jnp.sum(own_rows, axis=0, keepdims=True)
        dq_turned[...] = jnp.zeros_like(dq_turned)

    @pl.when(working)
    def _():
        slot = step // 2 % 2
        half_steps = tokens // tile // 2
        first = lax.broadcasted_iota(jnp.int32, (tile, lanes), 1) < HDIM

        def body(i, _):
            part = pl.ds(pl.multiple_of((i + second * half_steps) * tile, tile), tile)
            k, v = k_ref[part, :], v_ref[part, :]
            q, do = q_ref[...], do_ref[...]
            tag = key_tags[part, :]
            allowed = tag == query_tags[...]
            dk, dv = [], []
            for head in range(2):
                own = first if head == 0 else jnp.logical_not(first)
                own_rows = slice(head * HDIM, (head + 1) * HDIM)
                scores = dot(jnp.where(own, k, bf16(0)), q, 1, 1)
                scores = jnp.where(allowed, scores, masked_score)
                chances = jnp.exp2(scores * (score_scale * log2e) - lse_ref[head : head + 1, :])
                weight_grad = dot(jnp.where(own, v, bf16(0)), do, 1, 1)
                score_grad = (chances * (weight_grad - delta[head : head + 1, :])).astype(bf16)
                dv.append(dot(chances.astype(bf16), do, 1, 0))
                dk.append(dot(score_grad, q, 1, 0))
                dq_turned[own_rows, :] += dot(k_turned[own_rows, part], score_grad, 1, 0)
            d_pair[slot, part, lanes : 2 * lanes] = (jnp.where(first, dk[0], dk[1]) * score_scale).astype(bf16)
            d_v = jnp.where(first, dv[0], dv[1]).astype(bf16)
            d_pair[slot, part, 2 * lanes :] = jnp.where(tag < 0, do_ref[part, :], d_v)
            return 0

        lax.fori_loop(0, half_steps, body, 0)

    @pl.when(working & (second == 1))
    def _():
        d_pair[step // 2 % 2, :, :lanes] = (dq_turned[...] * score_scale).T.astype(bf16)

    def add_pair():
        item = step // 2 - 1
        slot = item % 2
        pair_copy(item).wait()
        d_n1[...] += dot(d_pair[slot, :own_tokens, :], own_weight[...], 1, 1) + dot(
            d_came[slot], other_weight[...], 1, 1
        )

    @pl.when((step >= 2) & (step <= 2 * pairs) & (second == 0))
    def _():
        add_pair()

    @pl.when(working & (second == 1))
    def _():
        pair_copy(step // 2).start()

    def part_copies(turn):
        rows = pl.ds(pl.multiple_of((seq_at + turn) % n_seq * sub, sub), sub)
        slot = turn % 2
        return (
            pltpu.make_async_copy(start_ref.at[rows], start_part.at[slot], part_sems.at[0, slot]),
            pltpu.make_async_copy(d_middle_ref.at[rows], middle_part.at[slot], part_sems.at[1, slot]),
        )

    @pl.when(step == 2 * pairs)
    def _():
        for copy in part_copies(0):
            copy.start()

        def body(turn, _):
            block = (seq_at + turn) % n_seq

            @pl.when(turn + 1 < n_seq)
            def _():
                for copy in part_copies(turn + 1):
                    copy.start()

            for copy in part_copies(turn):
                copy.wait()
            unit, scale = norm_parts(start_part[turn % 2].astype(f32))
            rows = pl.ds(pl.multiple_of(block * sub, sub), sub)
            grad = norm_back(d_n1[rows, :], gain_ref[...], unit, scale)
            staged[block] = (middle_part[turn % 2] + grad).astype(bf16)
            start_home(block, False)
            return 0

        lax.fori_loop(0, n_seq, body, 0)

    for at, stream in enumerate(streams):
        depth = len(stream.levels)

        def item_at(lag, stream=stream):
            since = step - stream.first - lag
            return since // 2, (since >= 0) & (since % 2 == 0) & (since < 2 * stream.count)

        item, here = item_at(depth + 1 + stream.lag)

        @pl.when(here)
        def _(at=at, item=item):
            core_copy(at, item).wait()
            local_copy(at, item).wait()

        item, here = item_at(depth + stream.lag)

        @pl.when(here)
        def _(at=at, item=item):
            join_copy(at, item).wait()
            core_copy(at, item).start()
            local_copy(at, item).start()

        for level in reversed(range(depth)):
            item, here = item_at(level + stream.lag)

            @pl.when(here)
            def _(at=at, item=item, level=level, stream=stream, depth=depth):
                _, keep, came = levels[at][level]
                slot = item % 2
                level_copy(at, level, item).wait_recv()
                if level == depth - 1:
                    joined[at][item, high] = add(keep[0, 0], came[slot, 0, 0])
                    join_copy(at, item).start()
                    return

                @pl.when(item > 0)
                def _():
                    level_copy(at, level + 1, item - 1).wait_send()

                next_send, next_keep, _ = levels[at][level + 1]
                place = places[stream.levels[level + 1]]
                next_send[...] = add(keep[:, 1 - place], came[slot, :, 1 - place]).reshape(next_send.shape)
                next_keep[...] = add(keep[:, place], came[slot, :, place]).reshape(next_keep.shape)
                level_copy(at, level + 1, item).start()

    def begin_piece(fills):
        for at, fill in fills.items():
            stream = streams[at]
            item = (step - stream.first) // 2

            @pl.when((step % 2 == stream.first % 2) & (step >= stream.first) & (item < stream.count))
            def _(at=at, fill=fill, item=item):
                @pl.when(item > 0)
                def _():
                    level_copy(at, 0, item - 1).wait_send()

                fill(*levels[at][0][:2])
                level_copy(at, 0, item).start()

    def fill_pair(send, keep):
        grad = dot(n1_ref[...], d_pair[step // 2 % 2], 0, 0).astype(bf16)
        grad = grad.reshape(n_seq, 2, send.shape[2], 3 * lanes)
        shape = send.shape[:3] + (3 * lanes,)

        @pl.when(high == 0)
        def _():
            send[:, :, :, : 3 * lanes] = grad[:, 1].reshape(shape)
            keep[:, :, :, : 3 * lanes] = grad[:, 0].reshape(shape)

        @pl.when(high != 0)
        def _():
            send[:, :, :, : 3 * lanes] = grad[:, 0].reshape(shape)
            keep[:, :, :, : 3 * lanes] = grad[:, 1].reshape(shape)

        shape = send.shape[:3] + (lanes,)
        send[:, :, :, 3 * lanes :] = add(out_kept[:, 1 - high], out_came[:, 1 - high]).reshape(shape)
        keep[:, :, :, 3 * lanes :] = add(out_kept[:, high], out_came[:, high]).reshape(shape)

    def fill_from(ref, place):
        def fill(send, keep):
            send[...] = ref[:, 1 - place].reshape(send.shape)
            keep[...] = ref[:, place].reshape(keep.shape)

        return fill

    begin_piece({0: fill_pair, 1: fill_from(down_ref, places["y"]), 2: fill_from(up_ref, high)})

    @pl.when(step == pl.num_programs(0) - 1)
    def _():
        for at, stream in enumerate(streams):
            for level in range(len(stream.levels)):
                level_copy(at, level, stream.count - 1).wait_send()
        wait_home(False)
        wait_home(True)


def back(
    qkv, mixed, d_mixed, lse, key_tags, query_tags, n1, weights, gain, out_kept, out_came, down_part, up_part,
    start, d_middle, outputs, row_count,
):
    tokens = qkv.shape[0]
    width = n1.shape[1]
    own_tokens = tokens // CORES
    lanes = 2 * HDIM
    pairs = qkv.shape[1] // (3 * lanes)
    n_seq = 2 * row_count
    tile = 512
    sub = own_tokens // n_seq
    streams = streams_of(width, down_part.shape[0] * 2, n_seq, pairs)
    last = pairs - 1
    now = lambda i: jnp.minimum(i // 2, last)
    before = lambda i: jnp.clip(i // 2 - 1, 0, last)
    early = lambda i: jnp.clip(i // 2 - 1, 0, down_pieces - 1)
    fixed = lambda shape: pl.BlockSpec(shape, lambda i: (0,) * len(shape), pipeline_mode=pl.Buffered(1))

    def columns(place):
        return pl.BlockSpec((tokens, lanes), lambda i: (0, 3 * now(i) + place))

    pair = pl.BlockSpec((tokens, lanes), lambda i: (0, now(i)))
    weight = pl.BlockSpec((width, 3 * lanes), lambda i: (0, before(i)))
    hbm = pl.BlockSpec(memory_space=pl.ANY)

    rows = streams[0].rows

    def out_piece(value):
        whole = value.reshape(n_seq, 2, rows, value.shape[1])
        return whole, pl.BlockSpec((n_seq, 2, rows, lanes), lambda i: (0, 0, 0, now(i)))

    outs = [out_piece(value) for value in (out_kept, out_came)]
    down = down_part.reshape(n_seq // 2, 2, -1, width // CORES)
    up = up_part.reshape(n_seq // 4, 2, rows, -1)
    down_spec = pl.BlockSpec((n_seq // 2, 2, streams[1].rows, width // CORES), lambda i: (0, 0, early(i), 0))
    up_spec = pl.BlockSpec((n_seq // 4, 2, rows, streams[2].columns), lambda i: (0, 0, 0, early(i)))
    count = len(streams)
    deepest = max(len(stream.levels) for stream in streams)
    return pl.pallas_call(
        functools.partial(back_kernel, pairs, tile, streams, row_count),
        grid=(2 * pairs + deepest + 1 + streams[0].lag,),
        in_specs=[
            fixed((tokens, 1)),
            fixed((1, tokens)),
            columns(0),
            columns(1),
            columns(2),
            pair,
            pair,
            pl.BlockSpec((None, 2, tokens), lambda i: (now(i), 0, 0)),
            fixed((tokens, width)),
            weight,
            weight,
            fixed((1, width)),
            outs[0][1],
            outs[1][1],
            down_spec,
            up_spec,
            hbm,
            hbm,
            hbm,
        ],
        out_specs=[hbm] * 5,
        out_shape=[jax.ShapeDtypeStruct((row_count, CORES, sub, width), bf16)] * 2
        + [jax.ShapeDtypeStruct((stream.count, CORES, 2, stream.rows, stream.columns), bf16) for stream in streams],
        scratch_shapes=[
            pltpu.VMEM((lanes, tokens), bf16),
            pltpu.VMEM((lanes, tokens), f32),
            pltpu.VMEM((2, tokens), f32),
            pltpu.VMEM((2, tokens, 3 * lanes), bf16),
            pltpu.VMEM((2, own_tokens, 3 * lanes), bf16),
            pltpu.VMEM((own_tokens, width), f32),
            pltpu.VMEM((n_seq, sub, width), bf16),
            pltpu.VMEM((2, sub, width), bf16),
            pltpu.VMEM((2, sub, width), f32),
        ]
        + [shape for stream in streams for shape in stream.scratch()]
        + [pltpu.VMEM((stream.count, 2, stream.rows, stream.columns), bf16) for stream in streams]
        + [
            pltpu.SemaphoreType.DMA((count, deepest)),
            pltpu.SemaphoreType.DMA((count, deepest, 2)),
            pltpu.SemaphoreType.DMA((count,)),
            pltpu.SemaphoreType.DMA((count, 2)),
            pltpu.SemaphoreType.DMA((count,)),
            pltpu.SemaphoreType.DMA((count, 2)),
            pltpu.SemaphoreType.DMA((count,)),
            pltpu.SemaphoreType.DMA((2,)),
            pltpu.SemaphoreType.DMA((2,)),
            pltpu.SemaphoreType.DMA((n_seq,)),
            pltpu.SemaphoreType.DMA((row_count, CORES)),
            pltpu.SemaphoreType.DMA,
            pltpu.SemaphoreType.DMA((2, 2)),
            pltpu.SemaphoreType.DMA((n_seq,)),
            pltpu.SemaphoreType.DMA((row_count, CORES)),
            pltpu.SemaphoreType.DMA,
        ],
        compiler_params=pltpu.CompilerParams(
            vmem_limit_bytes=feed_vmem_bytes, collective_id=2, has_side_effects=True
        ),
        cost_estimate=pl.CostEstimate(
            flops=80 * pairs * tokens * tokens * HDIM,
            bytes_accessed=16 * tokens * pairs * lanes,
            transcendentals=2 * pairs * tokens * tokens,
        ),
        name="back",
    )(
        key_tags, query_tags, qkv, qkv, qkv, mixed, d_mixed, lse, n1, weights[0], weights[1],
        gain.reshape(1, width), outs[0][0], outs[1][0], down, up, start, d_middle, outputs,
    )


def collect_kernel(pairs, seq_ref, *refs):
    qkv_parts, down_parts, up_parts = refs[:3]
    qkv_weights, up_weight = refs[3:9], refs[9]
    qkv_out, out_out, down_out, up_out, first_out, second_out, first_sum, second_sum = refs[10:]
    item = pl.program_id(0)
    lanes = 2 * HDIM
    rows = qkv_parts.shape[2]
    width = out_out.shape[1]
    half = width // CORES
    tile = feed_tile // CORES

    @pl.when(item == 0)
    def _():
        first_sum[...] = jnp.zeros_like(first_sum)
        second_sum[...] = jnp.zeros_like(second_sum)

    for core in range(CORES):
        place = pl.multiple_of(core * half + item * lanes, lanes)
        for high in range(2):
            own = slice(high * rows, (high + 1) * rows)
            part = qkv_parts[core, high].astype(f32)
            for kind in range(3):
                value = part[:, kind * lanes : (kind + 1) * lanes]
                qkv_out[own, pl.ds(kind * width + place, lanes)] = value
                weight = qkv_weights[kind * CORES + core][own, :].astype(f32)
                first_sum[own, :] += value * weight
            out_out[own, pl.ds(place, lanes)] = part[:, 3 * lanes :]

    @pl.when(item < down_pieces)
    def _():
        for core in range(CORES):
            for high in range(2):
                own = slice(high * rows, (high + 1) * rows)
                for at in range(up_parts.shape[3] // lanes):
                    column = item * up_parts.shape[3] + at * lanes
                    column = column // tile * feed_tile + core * tile + column % tile
                    columns = pl.ds(pl.multiple_of(column, lanes), lanes)
                    value = up_parts[core, high, :, at * lanes : (at + 1) * lanes].astype(f32)
                    up_out[own, columns] = value
                    second_sum[own, :] += value * up_weight[own, columns].astype(f32)
                count = down_parts.shape[2] // piece_rows
                for at in range(count):
                    start = ((item * count + at) * 2 + high) * piece_rows
                    value = down_parts[core, high, at * piece_rows : (at + 1) * piece_rows, :].astype(f32)
                    down_out[pl.ds(pl.multiple_of(start, piece_rows), piece_rows), core * half : (core + 1) * half] = value

    @pl.when(item == pairs - 1)
    def _():
        first_out[...] = jnp.sum(first_sum[...].T, axis=0, keepdims=True)
        second_out[...] = jnp.sum(second_sum[...].T, axis=0, keepdims=True)


def collect(seq_at, qkv_parts, down_parts, up_parts, qkv_weight, up_weight):
    pairs, _, _, rows, _ = qkv_parts.shape
    width, lanes = qkv_weight.shape[0], 2 * HDIM
    shard, wide = 2 * rows, up_weight.shape[1]
    down_rows = 2 * down_pieces * down_parts.shape[3]

    def parts(value):
        return pl.BlockSpec(
            (None,) + value.shape[1:], lambda i, seq: (jnp.minimum(i, value.shape[0] - 1), 0, 0, 0, 0)
        )

    def weight(kind, core):
        return pl.BlockSpec((shard, lanes), lambda i, seq: (seq[0], (kind * CORES + core) * pairs + i))

    whole = lambda shape: pl.BlockSpec(shape, lambda i, seq: (0, 0))
    return pl.pallas_call(
        functools.partial(collect_kernel, pairs),
        grid_spec=pltpu.PrefetchScalarGridSpec(
            num_scalar_prefetch=1,
            grid=(pairs,),
            in_specs=[parts(qkv_parts), parts(down_parts), parts(up_parts)]
            + [weight(kind, core) for kind in range(3) for core in range(CORES)]
            + [pl.BlockSpec((shard, wide), lambda i, seq: (seq[0], 0))],
            out_specs=[
                whole((shard, 3 * width)),
                whole((shard, width)),
                whole((down_rows, width)),
                whole((shard, wide)),
                whole((1, shard)),
                whole((1, shard)),
            ],
            scratch_shapes=[pltpu.VMEM((shard, lanes), f32)] * 2,
        ),
        out_shape=[
            jax.ShapeDtypeStruct((shard, 3 * width), f32),
            jax.ShapeDtypeStruct((shard, width), f32),
            jax.ShapeDtypeStruct((down_rows, width), f32),
            jax.ShapeDtypeStruct((shard, wide), f32),
            jax.ShapeDtypeStruct((1, shard), f32),
            jax.ShapeDtypeStruct((1, shard), f32),
        ],
        compiler_params=pltpu.CompilerParams(vmem_limit_bytes=vmem_bytes),
        name="collect",
    )(
        seq_at.reshape(1), qkv_parts, down_parts, up_parts, *[qkv_weight] * 6, up_weight,
    )


def add_split_kernel(has_two, bit_ref, *refs):
    ins, outs = refs[: 2 if has_two else 1], refs[2 if has_two else 1 :]
    value = ins[0][...]
    if has_two:
        value = (value.astype(f32) + ins[1][...].astype(f32)).astype(bf16)
    if len(outs) == 1:
        outs[0][...] = value
    else:
        sends = pl.program_id(0) == 0

        @pl.when(sends)
        def _():
            outs[0][...] = value

        @pl.when(jnp.logical_not(sends))
        def _():
            outs[1][...] = value


def add_split(kept, received, inner, bit):
    rows, columns = kept.shape
    values = [kept] if received is None else [kept, received.reshape(rows, columns)]
    if bit is None:
        if received is None:
            return None, kept
        count = 4 if rows % 64 == 0 else 1
        block = pl.BlockSpec((rows // count, columns), lambda i, bit: (i, 0))
        grid, ins, outs = (count,), [block] * 2, block
        shapes = jax.ShapeDtypeStruct((rows, columns), bf16)
        bit = jnp.zeros((), jnp.int32)
    else:
        outer = rows // (2 * inner)
        cut = 1
        while inner // cut * columns > 2**19 and inner % (32 * cut) == 0:
            cut *= 2
        values = [value.reshape(outer, 2, inner, columns) for value in values]
        ins = [
            pl.BlockSpec(
                (None, None, inner // cut, columns),
                lambda w, i, j, bit: (i, jnp.where(w == 0, 1 - bit[0], bit[0]), j, 0),
            )
        ] * len(values)
        outs = [
            pl.BlockSpec(
                (None, inner // cut, columns),
                lambda w, i, j, bit: (jnp.where(w == 0, i, outer - 1), jnp.where(w == 0, j, cut - 1), 0),
            ),
            pl.BlockSpec(
                (None, inner // cut, columns),
                lambda w, i, j, bit: (jnp.where(w == 0, 0, i), jnp.where(w == 0, 0, j), 0),
            ),
        ]
        grid = (2, outer, cut)
        shapes = [jax.ShapeDtypeStruct((outer, inner, columns), bf16)] * 2
    done = pl.pallas_call(
        functools.partial(add_split_kernel, len(values) == 2),
        grid_spec=pltpu.PrefetchScalarGridSpec(
            num_scalar_prefetch=1, grid=grid, in_specs=ins, out_specs=outs
        ),
        out_shape=shapes,
        cost_estimate=pl.CostEstimate(flops=rows * columns, bytes_accessed=6 * rows * columns, transcendentals=0),
        name="add_split",
    )(bit.reshape(1), *values)
    if not isinstance(done, (list, tuple)):
        return None, done
    return done[0].reshape(rows // 2, columns), done[1].reshape(rows // 2, columns)


def tie(*values):
    return lax.optimization_barrier(values)


def build(n_seq, n_rows):
    highs = n_rows // CORES
    seq_bits = n_seq.bit_length() - 1
    high_bits = highs.bit_length() - 1
    bits = seq_bits + high_bits

    def permute(value, target):
        pairs = []
        for s in range(n_seq):
            for r in range(n_rows):
                to_s, to_r = target(s, r)
                pairs.append((s * n_rows + r, to_s * n_rows + to_r))
        return lax.ppermute(value, AXES, pairs)

    def other_core(value):
        return permute(value, lambda s, r: (s, r ^ 1))

    def pick(value, place, axis):
        return lax.dynamic_index_in_dim(value, place, axis, keepdims=False)

    def bit_of(step):
        name, bit = step
        return (lax.axis_index(name) >> bit) & 1

    def across(value, step):
        name, bit = step
        if name == "rows":
            return permute(value, lambda s, r: (s, r ^ (1 << bit)))
        return permute(value, lambda s, r: (s ^ (1 << bit), r))

    high_steps = [("rows", bit + 1) for bit in reversed(range(high_bits))]
    seq_steps = [("seq", bit) for bit in range(seq_bits)]

    class Sum:
        def __init__(self, kept, received, order):
            self.rows, self.columns = kept.shape
            self.kept, self.received = kept, received
            self.left = [step for step in seq_steps[::-1] + high_steps if step in order]
            self.order = list(order)

        def finish(self):
            step = self.order[0] if self.order else None
            inner = self.rows
            if step is not None:
                axis = self.left.index(step)
                inner = self.rows >> (axis + 1)
            self.sent, self.kept = add_split(self.kept, self.received, inner, step and bit_of(step))
            self.received = None

        def begin(self):
            step = self.order.pop(0)
            self.left.remove(step)
            self.rows //= 2
            self.received = across(self.sent, step)

        def finished(self):
            while self.order:
                self.finish()
                self.begin()
            self.finish()
            return self.kept

    rows_first = high_steps + seq_steps[1:2] + seq_steps[:1] + seq_steps[2:]
    down_order = [step for step in seq_steps + high_steps if step != ("rows", 1)]
    up_order = [step for step in high_steps + seq_steps if step not in (("seq", 0), ("seq", 1))]

    def gather_high(value, pieces=0):
        for step in high_steps[::-1]:
            if pieces and step == ("rows", 1):
                continue
            received = across(value, step)
            value = jnp.where(
                bit_of(step) == 0,
                jnp.concatenate([value, received], 0),
                jnp.concatenate([received, value], 0),
            )
        if pieces:
            value = value.reshape(-1, 1, pieces, value.shape[1])
            received = across(value, ("rows", 1))
            value = jnp.where(
                bit_of(("rows", 1)) == 0,
                jnp.concatenate([value, received], 1),
                jnp.concatenate([received, value], 1),
            )
            value = value.reshape(-1, value.shape[-1])
        return value

    def back_by_steps(
        qkv, mixed, d_mixed, lse, key_tags, query_tags, n1_all, qkv_parts, attention_gain,
        out_kept, out_received, down_part, up_part, start, d_middle, to_member, ordered, from_rows, sizes,
    ):
        group, member, core, pairs, group_width, tokens, width = sizes
        lanes, half = 2 * HDIM, width // CORES
        unit1, scale1 = norm_parts(start)
        down = Sum(down_part, None, down_order)
        up = Sum(up_part, None, up_order)
        out = Sum(out_kept, out_received, rows_first)

        def before_next(*sums):
            nonlocal d_mixed
            for each in sums:
                each.finish()
            values = tie(d_mixed, *[v for each in sums for v in (each.sent, each.kept)])
            d_mixed = values[0]
            for at, each in enumerate(sums):
                each.sent, each.kept = values[1 + 2 * at : 3 + 2 * at]
                each.begin()

        def back_at(at):
            return attend_back(qkv, mixed, d_mixed, lse, key_tags, query_tags, at, 1)

        cut = max(1, 3 * pairs // 5)
        before_next(down, up)
        d_qkv, qkv_sums, d_parts = [], [], [[] for _ in range(group)]

        def take_piece(pieces):
            piece = jnp.concatenate(pieces, axis=1)
            d_parts[0].append(piece[:tokens])
            for hop in range(1, group):
                d_parts[hop].append(to_member(piece[hop * tokens : (hop + 1) * tokens], group - hop))
            return dot(n1_all, piece, 0, 0)

        grads = []
        for at in range(pairs):
            d_qkv.append(back_at(at))
            d_mixed, d_qkv[at] = tie(d_mixed, d_qkv[at])
            if at + 1 == cut:
                grads.append(take_piece(d_qkv))
            if at == min(0, pairs - 1):
                before_next(out)
            if at == min(1, pairs - 1):
                before_next(down, up)
            if at == min(3, pairs - 1):
                before_next(down, up, out)
        if pairs > cut:
            grads.append(take_piece(d_qkv[cut:]))
        if group == CORES:
            qkv_sums = [Sum(grad.astype(bf16), None, rows_first) for grad in grads]
        else:
            grad = jnp.concatenate(grads, 1)
            grad = grad.reshape(width, pairs, 3, lanes).transpose(0, 2, 1, 3)
            grad = grad.reshape(width, 3, 1, pairs * lanes)[..., :group_width]
            grad = lax.dynamic_update_slice_in_dim(
                jnp.zeros((width, 3, group, group_width), f32), grad, member, 2
            ).reshape(width, 3, CORES, half)
            kept = pick(grad, core, 2).astype(bf16).reshape(width, 3 * half)
            sent = pick(grad, 1 - core, 2).astype(bf16).reshape(width, 3 * half)
            qkv_sums = [Sum(kept, other_core(sent), rows_first)]

        d_n1 = jnp.zeros((tokens, width), f32)
        for part, weight in zip(d_parts, qkv_parts):
            d_n1 = d_n1 + dot(jnp.concatenate(part, 1), weight, 1, 1)
        input_grad = d_middle + norm_back(d_n1, attention_gain, unit1, scale1)
        input_grad = from_rows(input_grad.astype(bf16))

        down_total = gather_high(down.finished(), piece_rows)
        down_total = ordered(down_total, other_core(down_total), 1).astype(f32)
        tile = feed_tile // CORES
        up_total = gather_high(up.finished()).reshape(width // n_seq, -1, 1, tile)
        up_total = ordered(up_total, other_core(up_total), 2).reshape(width // n_seq, -1).astype(f32)
        out_total = gather_high(out.finished())
        out_total = ordered(out_total, other_core(out_total), 1).astype(f32)
        qkv_part = gather_high(jnp.concatenate([each.finished() for each in qkv_sums], 1))
        if group == CORES:
            qkv_part = qkv_part.reshape(-1, pairs, 3, lanes).transpose(0, 2, 1, 3)
        qkv_part = qkv_part.reshape(-1, 3, half)
        qkv_total = ordered(qkv_part[:, :, None], other_core(qkv_part)[:, :, None], 2)
        qkv_total = qkv_total.reshape(-1, 3 * width).astype(f32)

        return input_grad, qkv_total, out_total, down_total, up_total

    def per_device(
        inputs, cell_ids, valid_counts, cotangent, attention_gain, qkv_weight, out_weight, feed_gain, up_weight, down_weight
    ):
        row_count, block, width = inputs.shape
        seq_len = cell_ids.shape[1]
        heads = width // HDIM
        lanes = 2 * HDIM
        seq_at, rows_at = lax.axis_index("seq"), lax.axis_index("rows")
        core = rows_at % CORES
        chips = n_seq // (CORES * row_count)
        group = chips * CORES
        sub = block // group
        tokens = n_seq * sub
        member = (seq_at % chips) * CORES + core
        group_heads = heads // group
        pairs = -(-group_heads // 2)
        group_width = group_heads * HDIM
        padded = pairs * lanes - group_width

        def to_member(value, hop):
            def target(s, r):
                place = ((s % chips) * CORES + r % CORES + hop) % group
                return (s // chips * chips + place // CORES, r // CORES * CORES + place % CORES)

            return permute(value, target)

        def ordered(own, received, axis):
            return jnp.where(
                core == 0,
                jnp.concatenate([own, received], axis),
                jnp.concatenate([received, own], axis),
            )

        def to_rows(value):
            halves = value.reshape(row_count, CORES, block // CORES, width)
            received = other_core(pick(halves, 1 - core, 1))
            both = ordered(pick(halves, core, 1), received, 0).reshape(n_seq, sub, width)
            return lax.all_to_all(both, "seq", 0, 0, tiled=True).reshape(tokens, width)

        def from_rows(value):
            both = lax.all_to_all(value.reshape(n_seq, sub, width), "seq", 0, 0, tiled=True)
            both = both.reshape(CORES, row_count, block // CORES, width)
            received = other_core(pick(both, 1 - core, 0))
            own = pick(both, core, 0)
            return ordered(own[:, None], received[:, None], 1).reshape(row_count, block, width)

        places = jnp.arange(seq_len, dtype=jnp.int32)
        tags = jnp.where(places[None, :] < valid_counts[:, None], cell_ids, -1 - places[None, :])
        tags = ordered(tags, other_core(tags), 0)
        tags = pick(tags, seq_at // chips, 0).reshape(n_seq, CORES, chips, sub)
        tags = tags.transpose(2, 1, 0, 3).reshape(group, tokens)
        order = (member - jnp.arange(group, dtype=jnp.int32)) % group
        tags = jnp.take(tags, order, axis=0).reshape(1, seq_len)
        query_tags, key_tags = tags, tags.reshape(seq_len, 1)

        def pad_heads(value, axis):
            if not padded:
                return value
            fill = [(0, 0)] * value.ndim
            fill[axis] = (0, padded)
            return jnp.pad(value, fill)

        def qkv_of(hop):
            if group == CORES:
                return gather_pairs(((core + hop) % CORES).reshape(1), qkv_weight)
            piece = pick(qkv_weight.reshape(width, 3, group, group_width), (member + hop) % group, 2)
            piece = pad_heads(piece, 2).reshape(width, 3, pairs, lanes)
            return piece.transpose(0, 2, 1, 3).reshape(width, 3 * pairs * lanes)

        def out_of(hop):
            at = (member + hop) % group * group_width
            return pad_heads(lax.dynamic_slice_in_dim(out_weight, at, group_width, 0), 0)

        if chips == 1 and highs == 2:
            half = width // CORES
            x_row, n1, qkv, own_weight, other_weight = begin(inputs, qkv_weight, attention_gain)
            start = x_row.reshape(tokens, width)
            mixed, lse, cot, mixed_own, middle = attend_row(qkv, key_tags, query_tags, cotangent, start, out_weight)
            outputs, d_middle, _, d_mixed, out_kept, out_received, down_part, up_part = feed(
                middle, cot.reshape(tokens, width), feed_gain, up_weight, down_weight, mixed_own, out_weight, n_seq
            )
            input_grad, out_low, qkv_out, down_all, up_all = back(
                qkv, mixed, d_mixed.reshape(seq_len, half), lse, key_tags, query_tags, n1, (own_weight, other_weight), attention_gain,
                out_kept, out_received, down_part, up_part, start, d_middle, outputs, row_count,
            )
            qkv_total, out_total, down_total, up_total, first, second = collect(
                seq_at, qkv_out, down_all, up_all, qkv_weight, up_weight
            )
            shard = width // n_seq

            def gain_grad(sums, gain):
                return sums.reshape(shard) / lax.dynamic_slice_in_dim(gain, seq_at * shard, shard, 0)

            return (
                out_low.reshape(inputs.shape),
                input_grad.reshape(inputs.shape),
                gain_grad(first, attention_gain),
                qkv_total,
                out_total,
                gain_grad(second, feed_gain),
                up_total,
                down_total,
            )

        start = to_rows(inputs)
        qkv_parts = [qkv_of(hop) for hop in range(group)]
        out_parts = [out_of(hop) for hop in range(group)]
        start = start.astype(f32)
        unit1, scale1 = norm_parts(start)
        n1 = (unit1 * attention_gain).astype(bf16)
        n1_all = jnp.concatenate([n1] + [to_member(n1, hop) for hop in range(1, group)], 0)
        cotangent, _ = tie(cotangent, start[:1])
        cot = to_rows(cotangent)
        qkv = dot(n1_all, qkv_parts[0], 1, 0).astype(bf16)
        mixed, lse = attend(qkv, key_tags, query_tags)
        mixed_parts = [mixed[:tokens]] + [
            to_member(mixed[hop * tokens : (hop + 1) * tokens], group - hop) for hop in range(1, group)
        ]
        middle = start
        for part, weight in zip(mixed_parts, out_parts):
            middle = middle + dot(part, weight, 1, 0)
        if group == CORES:
            mixed_own = ordered(mixed_parts[0], mixed_parts[1], 1)
        else:
            slots = jnp.stack([part[:, :group_width] for part in mixed_parts])
            turn = (jnp.arange(group, dtype=jnp.int32) - member) % group
            mixed_own = jnp.take(slots, turn, axis=0).transpose(1, 0, 2).reshape(tokens, width)
        outputs, d_middle, d_attn, _, _, _, down_part, up_part = feed(
            middle, cot, feed_gain, up_weight, down_weight, mixed_own, out_weight, n_seq
        )
        d_attn = d_attn[0]

        d_attn_all = jnp.concatenate([d_attn] + [to_member(d_attn, hop) for hop in range(1, group)], 0)


        half = width // CORES
        out_grad = dot(mixed_own, d_attn, 0, 0).astype(bf16)
        out_kept = lax.dynamic_slice_in_dim(out_grad, core * half, half, 1)
        out_received = other_core(lax.dynamic_slice_in_dim(out_grad, (1 - core) * half, half, 1))
        d_mixed = dot(d_attn_all, out_parts[0], 1, 1).astype(bf16)

        out_low = from_rows(outputs)
        input_grad, qkv_total, out_total, down_total, up_total = back_by_steps(
            qkv, mixed, d_mixed, lse, key_tags, query_tags, n1_all, qkv_parts, attention_gain,
            out_kept, out_received, down_part, up_part, start, d_middle, to_member, ordered, from_rows,
            (group, member, core, pairs, group_width, tokens, width),
        )

        shard = width // n_seq

        def gain_total(weight, total, gain):
            rows = lax.dynamic_slice_in_dim(weight, seq_at * shard, shard, 0).astype(f32)
            return jnp.sum(rows * total, axis=1) / lax.dynamic_slice_in_dim(gain, seq_at * shard, shard, 0)

        return (
            out_low,
            input_grad,
            gain_total(qkv_weight, qkv_total, attention_gain),
            qkv_total,
            out_total,
            gain_total(up_weight, up_total, feed_gain),
            up_total,
            down_total,
        )

    return per_device


def solution(mesh):
    placed = (
        P("rows", "seq", None),
        P("rows", None),
        P("rows"),
        P("rows", "seq", None),
        P(),
        P(),
        P(),
        P(),
        P(),
        P(),
    )
    return jax.shard_map(
        build(mesh.shape["seq"], mesh.shape["rows"]),
        mesh=mesh,
        in_specs=placed,
        out_specs=(
            P("rows", "seq", None),
            P("rows", "seq", None),
            P("seq"),
            P("seq", None),
            P("seq", None),
            P("seq"),
            P("seq", None),
            P("seq", None),
        ),
        check_vma=False,
    )
```

```python
import functools

import jax
import jax.numpy as jnp
from jax import lax
from jax.experimental import pallas as pl
from jax.experimental.pallas import tpu as pltpu
from jax.sharding import PartitionSpec as P

HDIM = 64
CORES = 2
epsilon = 1e-05
masked_score = -1e30
score_scale = HDIM ** (-0.5)
log2e = 1.4426950408889634
bf16 = jnp.bfloat16
f32 = jnp.float32
AXES = ("seq", "rows")
vmem_bytes = 60 * 2**20
feed_vmem_bytes = 63 * 2**20
feed_tile = 512
max_cells = 7
MESH = pl.DeviceIdType.MESH


def dot(a, b, ca, cb):
    return lax.dot_general(a, b, (((ca,), (cb,)), ((), ())), preferred_element_type=f32)


def attend_kernel(tile, key_tags, query_tags, q_ref, k_ref, v_ref, o_ref, lse_ref, v_turned):
    tokens = q_ref.shape[0]
    v_turned[...] = v_ref[...].T
    lane = lax.broadcasted_iota(jnp.int32, (tile, 2 * HDIM), 1)

    def body(step, _):
        part = pl.ds(pl.multiple_of(step * tile, tile), tile)
        q = q_ref[part, :]
        allowed = key_tags[...] == query_tags[:, part]
        pieces = []
        for head in range(2):
            own = jnp.where((lane // HDIM) == head, q, bf16(0))
            scores = dot(k_ref[...], own, 1, 1)
            scores = jnp.where(allowed, scores, masked_score)
            peak = jnp.max(scores, axis=0, keepdims=True)
            powers = jnp.exp2((scores - peak) * (score_scale * log2e))
            total = jnp.sum(powers, axis=0, keepdims=True)
            mixed = dot(v_turned[head * HDIM : (head + 1) * HDIM, :], powers.astype(bf16), 1, 0)
            pieces.append(mixed * (1.0 / total))
            lse_ref[head : head + 1, part] = peak * (score_scale * log2e) + jnp.log2(total)
        o_ref[part, :] = jnp.concatenate(pieces, axis=0).T.astype(bf16)
        return 0

    lax.fori_loop(0, tokens // tile, body, 0)


def attend(qkv, key_tags, query_tags):
    tokens, width = qkv.shape
    lanes = 2 * HDIM
    pairs = width // (3 * lanes)
    tile = min(512, tokens)

    def columns(place):
        return pl.BlockSpec((tokens, lanes), lambda i: (0, 3 * i + place))

    return pl.pallas_call(
        functools.partial(attend_kernel, tile),
        grid=(pairs,),
        in_specs=[
            pl.BlockSpec((tokens, 1), lambda i: (0, 0)),
            pl.BlockSpec((1, tokens), lambda i: (0, 0)),
            columns(0),
            columns(1),
            columns(2),
        ],
        out_specs=[
            pl.BlockSpec((tokens, lanes), lambda i: (0, i)),
            pl.BlockSpec((None, 2, tokens), lambda i: (i, 0, 0)),
        ],
        out_shape=[
            jax.ShapeDtypeStruct((tokens, pairs * lanes), bf16),
            jax.ShapeDtypeStruct((pairs, 2, tokens), f32),
        ],
        scratch_shapes=[pltpu.VMEM((lanes, tokens), bf16)],
        compiler_params=pltpu.CompilerParams(vmem_limit_bytes=vmem_bytes),
        cost_estimate=pl.CostEstimate(
            flops=32 * pairs * tokens * tokens * HDIM,
            bytes_accessed=8 * tokens * pairs * lanes,
            transcendentals=2 * pairs * tokens * tokens,
        ),
        name="attend",
    )(key_tags, query_tags, qkv, qkv, qkv)


def attend_back_kernel(
    tile, key_tags, query_tags, q_ref, k_ref, v_ref, o_ref, do_ref, lse_ref, grad_ref, k_turned, dq_turned, delta
):
    tokens = q_ref.shape[0]
    lanes = 2 * HDIM
    k_turned[...] = k_ref[...].T
    dq_turned[...] = (o_ref[...].astype(f32) * do_ref[...].astype(f32)).T
    for head in range(2):
        rows = dq_turned[head * HDIM : (head + 1) * HDIM, :]
        delta[head : head + 1, :] = jnp.sum(rows, axis=0, keepdims=True)
    dq_turned[...] = jnp.zeros_like(dq_turned)
    first = lax.broadcasted_iota(jnp.int32, (tile, lanes), 1) < HDIM

    def body(step, _):
        part = pl.ds(pl.multiple_of(step * tile, tile), tile)
        k, v = k_ref[part, :], v_ref[part, :]
        q, do = q_ref[...], do_ref[...]
        allowed = key_tags[part, :] == query_tags[...]
        dk, dv = [], []
        for head in range(2):
            own = first if head == 0 else jnp.logical_not(first)
            own_rows = slice(head * HDIM, (head + 1) * HDIM)
            scores = dot(jnp.where(own, k, bf16(0)), q, 1, 1)
            scores = jnp.where(allowed, scores, masked_score)
            chances = jnp.exp2(scores * (score_scale * log2e) - lse_ref[head : head + 1, :])
            weight_grad = dot(jnp.where(own, v, bf16(0)), do, 1, 1)
            score_grad = (chances * (weight_grad - delta[head : head + 1, :])).astype(bf16)
            dv.append(dot(chances.astype(bf16), do, 1, 0))
            dk.append(dot(score_grad, q, 1, 0))
            dq_turned[own_rows, :] += dot(k_turned[own_rows, part], score_grad, 1, 0)
        grad_ref[part, lanes : 2 * lanes] = (jnp.where(first, dk[0], dk[1]) * score_scale).astype(bf16)
        grad_ref[part, 2 * lanes :] = jnp.where(first, dv[0], dv[1]).astype(bf16)
        return 0

    lax.fori_loop(0, tokens // tile, body, 0)
    grad_ref[:, :lanes] = (dq_turned[...] * score_scale).T.astype(bf16)


def attend_back(qkv, mixed, d_mixed, lse, key_tags, query_tags, start, count):
    tokens = qkv.shape[0]
    tile = min(512, tokens)
    lanes = 2 * HDIM

    def columns(place):
        return pl.BlockSpec((tokens, lanes), lambda i: (0, 3 * (start + i) + place))

    pair = pl.BlockSpec((tokens, lanes), lambda i: (0, start + i))
    return pl.pallas_call(
        functools.partial(attend_back_kernel, tile),
        grid=(count,),
        in_specs=[
            pl.BlockSpec((tokens, 1), lambda i: (0, 0)),
            pl.BlockSpec((1, tokens), lambda i: (0, 0)),
            columns(0),
            columns(1),
            columns(2),
            pair,
            pair,
            pl.BlockSpec((None, 2, tokens), lambda i: (start + i, 0, 0)),
        ],
        out_specs=pl.BlockSpec((tokens, 3 * lanes), lambda i: (0, i)),
        out_shape=jax.ShapeDtypeStruct((tokens, 3 * count * lanes), bf16),
        scratch_shapes=[
            pltpu.VMEM((lanes, tokens), bf16),
            pltpu.VMEM((lanes, tokens), f32),
            pltpu.VMEM((2, tokens), f32),
        ],
        compiler_params=pltpu.CompilerParams(vmem_limit_bytes=vmem_bytes),
        cost_estimate=pl.CostEstimate(
            flops=80 * count * tokens * tokens * HDIM,
            bytes_accessed=16 * tokens * count * lanes,
            transcendentals=2 * count * tokens * tokens,
        ),
        name="attend_back",
    )(key_tags, query_tags, qkv, qkv, qkv, mixed, d_mixed, lse)


def copy_kernel(core_ref, from_ref, to_ref):
    to_ref[...] = from_ref[...]


def gather_pairs(core, qkv_weight):
    width, lanes = qkv_weight.shape[0], 2 * HDIM
    pairs = width // (CORES * lanes)
    return pl.pallas_call(
        copy_kernel,
        grid_spec=pltpu.PrefetchScalarGridSpec(
            num_scalar_prefetch=1,
            grid=(pairs, 3),
            in_specs=[
                pl.BlockSpec((width, lanes), lambda i, j, core: (0, (j * CORES + core[0]) * pairs + i))
            ],
            out_specs=pl.BlockSpec((width, lanes), lambda i, j, core: (0, 3 * i + j)),
        ),
        out_shape=jax.ShapeDtypeStruct((width, 3 * pairs * lanes), qkv_weight.dtype),
        cost_estimate=pl.CostEstimate(flops=0, bytes_accessed=12 * width * pairs * lanes, transcendentals=0),
        name="gather_pairs",
    )(core, qkv_weight)


def norm_parts(values):
    center = values - jnp.mean(values, axis=-1, keepdims=True)
    spread = jnp.mean(center * center, axis=-1, keepdims=True)
    scale = lax.rsqrt(spread + epsilon)
    return center * scale, scale


def norm_back(grad, gain, unit, scale):
    e = grad * gain
    return scale * (
        e - jnp.mean(e, axis=-1, keepdims=True) - unit * jnp.mean(e * unit, axis=-1, keepdims=True)
    )


def all_signal(n_seq, seq_at, rows_at, extra=()):
    core = rows_at % CORES
    barrier = pltpu.get_barrier_semaphore()
    for s in range(n_seq):
        for c in range(CORES):
            @pl.when(jnp.logical_not((seq_at == s) & (core == c)))
            def _():
                pl.semaphore_signal(barrier, inc=1, device_id=(s, rows_at - core + c), device_id_type=MESH)
    for peer in extra:
        pl.semaphore_signal(barrier, inc=1, device_id=peer, device_id_type=MESH)
    pl.semaphore_wait(barrier, n_seq * CORES - 1 + len(extra))


class ToRows:
    def __init__(self, source, target, send, recv, local, row_count, seq_at, rows_at):
        self.source, self.target, self.send, self.recv, self.local = source, target, send, recv, local
        self.row_count, self.seq_at, self.rows_at = row_count, seq_at, rows_at
        self.core = rows_at % CORES

    def copy(self, row, c):
        chip = self.core * self.row_count + row
        return pltpu.make_async_remote_copy(
            src_ref=self.source.at[row, c],
            dst_ref=self.target.at[self.seq_at],
            send_sem=self.send.at[row, c],
            recv_sem=self.recv.at[self.seq_at],
            device_id=(chip, self.rows_at - self.core + c),
            device_id_type=MESH,
        )

    def own(self, row, c):
        return pltpu.make_async_copy(self.source.at[row, c], self.target.at[self.seq_at], self.local)

    def each(self, own, other):
        for row_turn in range(self.row_count):
            for core_turn in range(CORES):
                row = (row_turn + self.seq_at) % self.row_count
                c = (core_turn + self.seq_at // self.row_count) % CORES
                here = (self.core * self.row_count + row == self.seq_at) & (self.core == c)

                @pl.when(here)
                def _():
                    own(row, c)

                @pl.when(jnp.logical_not(here))
                def _():
                    other(row, c)

    def start(self):
        self.each(lambda row, c: self.own(row, c).start(), lambda row, c: self.copy(row, c).start())

    def wait_block(self, s):
        here = (s == self.seq_at) & (self.seq_at // self.row_count == self.core)

        @pl.when(here)
        def _():
            self.own(0, 0).wait()

        @pl.when(jnp.logical_not(here))
        def _():
            pltpu.make_async_remote_copy(
                src_ref=self.source.at[0, 0],
                dst_ref=self.target.at[s],
                send_sem=self.send.at[0, 0],
                recv_sem=self.recv.at[s],
                device_id=(self.seq_at, self.rows_at + 1 - 2 * self.core),
                device_id_type=MESH,
            ).wait_recv()

    def wait_sends(self):
        self.each(lambda row, c: None, lambda row, c: self.copy(row, c).wait_send())


def begin_kernel(
    row_count, pairs, x_ref, weight_ref, gain_ref, x_out, n1_out, qkv_out, own_out, other_out,
    x_part, n1, qkv, weight, other_weight,
    x_send, x_recv, x_local, n1_send, n1_recv, weight_sems, out_sems, x_sems, qkv_sems, n1_sems,
):
    seq_at, rows_at = lax.axis_index("seq"), lax.axis_index("rows")
    core = rows_at % CORES
    n_seq, sub, width = x_part.shape
    lanes = 2 * HDIM
    tokens = n_seq * sub
    moves = ToRows(x_ref, x_part, x_send, x_recv, x_local, row_count, seq_at, rows_at)

    def weight_copies(item, which):
        pair, kind = item // 3, item % 3
        to = pl.ds(pl.multiple_of(item * lanes, lanes), lanes)

        def columns(c):
            return pl.ds(pl.multiple_of((kind * CORES + c) * pairs * lanes + pair * lanes, lanes), lanes)

        source = weight_ref.at[:, columns(1 - core if which else core)]
        return pltpu.make_async_copy(source, (weight, other_weight)[which].at[:, to], weight_sems.at[which, item])

    def each_weight(act, which):
        def body(item, _):
            act(weight_copies(item, which))
            return 0

        lax.fori_loop(0, 3 * pairs, body, 0)

    each_weight(lambda copy: copy.start(), 0)
    all_signal(n_seq, seq_at, rows_at)
    moves.start()
    each_weight(lambda copy: copy.start(), 1)
    each_weight(lambda copy: copy.wait(), 0)
    weights_out = (
        pltpu.make_async_copy(weight, own_out, out_sems.at[0]),
        pltpu.make_async_copy(other_weight, other_out, out_sems.at[1]),
    )
    weights_out[0].start()
    each_weight(lambda copy: copy.wait(), 1)
    weights_out[1].start()

    def block_of(place):
        near = (place % 2) * ((place + 1) // 2) + (1 - place % 2) * ((n_seq - place // 2) % n_seq)
        return (seq_at + near) % n_seq

    def rows_of(s, other):
        return pl.ds(pl.multiple_of(s * sub + other * tokens, sub), sub)

    def n1_copy(s):
        return pltpu.make_async_remote_copy(
            src_ref=n1.at[rows_of(s, 0)],
            dst_ref=n1.at[rows_of(s, 1)],
            send_sem=n1_send.at[s],
            recv_sem=n1_recv.at[s],
            device_id=(seq_at, rows_at + 1 - 2 * core),
            device_id_type=MESH,
        )

    def x_copy(s):
        return pltpu.make_async_copy(x_part.at[s], x_out.at[s], x_sems.at[s])

    def out_copies(s, other):
        rows = rows_of(s, other)
        return (
            pltpu.make_async_copy(qkv.at[rows], qkv_out.at[rows], qkv_sems.at[other, s]),
            pltpu.make_async_copy(n1.at[rows], n1_out.at[rows], n1_sems.at[other, s]),
        )

    def product(first, second, other):
        both = jnp.concatenate([n1[rows_of(first, other), :], n1[rows_of(second, other), :]], 0)
        found = dot(both, weight[...], 1, 0).astype(bf16)
        for at, s in enumerate((first, second)):
            qkv[rows_of(s, other), :] = found[at * sub : (at + 1) * sub]
            for copy in out_copies(s, other):
                copy.start()

    def body(group, _):
        @pl.when(group < n_seq // 2)
        def _():
            places = block_of(2 * group), block_of(2 * group + 1)
            for s in places:
                moves.wait_block(s)
                x_copy(s).start()
                unit, _s = norm_parts(x_part[s].astype(f32))
                n1[rows_of(s, 0), :] = (unit * gain_ref[...]).astype(bf16)
                n1_copy(s).start()
            product(*places, 0)

        @pl.when(group > 0)
        def _():
            places = block_of(2 * group - 2), block_of(2 * group - 1)
            for s in places:
                n1_copy(s).wait()
            product(*places, 1)

        return 0

    lax.fori_loop(0, n_seq // 2 + 1, body, 0)

    def finish(s, _):
        x_copy(s).wait()
        for other in range(2):
            for copy in out_copies(s, other):
                copy.wait()
        return 0

    lax.fori_loop(0, n_seq, finish, 0)
    moves.wait_sends()
    for copy in weights_out:
        copy.wait()


def begin(inputs, qkv_weight, gain):
    row_count, block, width = inputs.shape
    n_seq = CORES * row_count
    lanes = 2 * HDIM
    pairs = width // (CORES * lanes)
    sub = block // CORES
    tokens = n_seq * sub
    hbm = pl.BlockSpec(memory_space=pl.ANY)
    return pl.pallas_call(
        functools.partial(begin_kernel, row_count, pairs),
        in_specs=[hbm, hbm, pl.BlockSpec(memory_space=pltpu.VMEM)],
        out_specs=[hbm] * 5,
        out_shape=[
            jax.ShapeDtypeStruct((n_seq, sub, width), bf16),
            jax.ShapeDtypeStruct((CORES * tokens, width), bf16),
            jax.ShapeDtypeStruct((CORES * tokens, 3 * pairs * lanes), bf16),
            jax.ShapeDtypeStruct((width, 3 * pairs * lanes), bf16),
            jax.ShapeDtypeStruct((width, 3 * pairs * lanes), bf16),
        ],
        scratch_shapes=[
            pltpu.VMEM((n_seq, sub, width), bf16),
            pltpu.VMEM((CORES * tokens, width), bf16),
            pltpu.VMEM((CORES * tokens, 3 * pairs * lanes), bf16),
            pltpu.VMEM((width, 3 * pairs * lanes), bf16),
            pltpu.VMEM((width, 3 * pairs * lanes), bf16),
            pltpu.SemaphoreType.DMA((row_count, CORES)),
            pltpu.SemaphoreType.DMA((n_seq,)),
            pltpu.SemaphoreType.DMA,
            pltpu.SemaphoreType.DMA((n_seq,)),
            pltpu.SemaphoreType.DMA((n_seq,)),
            pltpu.SemaphoreType.DMA((2, 3 * pairs)),
            pltpu.SemaphoreType.DMA((2,)),
            pltpu.SemaphoreType.DMA((n_seq,)),
            pltpu.SemaphoreType.DMA((CORES, n_seq)),
            pltpu.SemaphoreType.DMA((CORES, n_seq)),
        ],
        compiler_params=pltpu.CompilerParams(
            vmem_limit_bytes=vmem_bytes, collective_id=3, has_side_effects=True
        ),
        name="begin",
    )(inputs.reshape(row_count, CORES, sub, width), qkv_weight, gain.reshape(1, width))


def with_cells(value, tags, head, is_key):
    lane = lax.broadcasted_iota(jnp.int32, value.shape, 1)
    cell = lane - (1 - head) * HDIM
    if is_key:
        marks = jnp.where((cell == tags) | (cell >= max_cells), 0.0, -1.0)
    else:
        marks = jnp.where(cell == tags, -masked_score, 0.0)
    return jnp.where((lane // HDIM) == head, value, marks.astype(bf16))


def attend_row_kernel(
    tile, row_count, tags, row_tags, q_ref, k_ref, v_ref, cot_ref, x_ref, weight_ref, o_ref, lse_ref, cot_out, own_out,
    middle_out, v_turned, keys, scores_ref, mixed_ref, parts, x_part, weight, own, middle,
    cot_send, cot_recv, cot_local, part_send, part_recv, part_local, in_sems, out_sems,
):
    item, last = pl.program_id(0), pl.num_programs(0) - 1
    seq_at, rows_at = lax.axis_index("seq"), lax.axis_index("rows")
    core = rows_at % CORES
    tokens, lanes = q_ref.shape
    own_tokens = tokens // CORES
    n_seq, sub, _w = cot_out.shape
    moves = ToRows(cot_ref, cot_out, cot_send, cot_recv, cot_local, row_count, seq_at, rows_at)

    def part_copies(at):
        slot = at % 2
        half = pl.num_programs(0) * lanes
        columns = pl.ds(pl.multiple_of(core * half + at * lanes, lanes), lanes)
        return (
            pltpu.make_async_remote_copy(
                src_ref=parts.at[slot, pl.ds(own_tokens, own_tokens)],
                dst_ref=own_out.at[:, columns],
                send_sem=part_send.at[slot],
                recv_sem=part_recv.at[at],
                device_id=(seq_at, rows_at + 1 - 2 * core),
                device_id_type=MESH,
            ),
            pltpu.make_async_copy(parts.at[slot, pl.ds(0, own_tokens)], own_out.at[:, columns], part_local.at[slot]),
        )

    def part_came(at):
        half = pl.num_programs(0) * lanes
        columns = pl.ds(pl.multiple_of((1 - core) * half + at * lanes, lanes), lanes)
        return pltpu.make_async_remote_copy(
            src_ref=parts.at[0, pl.ds(own_tokens, own_tokens)],
            dst_ref=own_out.at[:, columns],
            send_sem=part_send.at[0],
            recv_sem=part_recv.at[at],
            device_id=(seq_at, rows_at + 1 - 2 * core),
            device_id_type=MESH,
        )

    def in_copies():
        return [
            pltpu.make_async_copy(x_ref, x_part, in_sems.at[0]),
            pltpu.make_async_copy(weight_ref, weight, in_sems.at[1]),
        ]

    def own_copy():
        return pltpu.make_async_copy(own_out, own, in_sems.at[2])

    def middle_copy(at):
        rows = pl.ds(at * sub, sub)
        return pltpu.make_async_copy(middle.at[rows], middle_out.at[rows], out_sems.at[at])

    @pl.when(item == 0)
    def _():
        all_signal(n_seq, seq_at, rows_at)
        moves.start()
        for copy in in_copies():
            copy.start()

    for head in range(2):
        keys[head] = with_cells(k_ref[...], tags[...], head, True)
        v_turned[head, :HDIM, :] = v_ref[...].T[head * HDIM : (head + 1) * HDIM, :]
        v_turned[head, HDIM:, :] = jnp.ones((16, tokens), bf16)

    def begin_scores(step, head):
        part = pl.ds(pl.multiple_of(step * tile, tile), tile)
        scores_ref[head] = dot(keys[head], with_cells(q_ref[part, :], tags[part, :], head, False), 1, 1)

    def finish(step, head):
        part = pl.ds(pl.multiple_of(step * tile, tile), tile)
        scores = scores_ref[head]
        peak = jnp.max(scores, axis=0, keepdims=True)
        powers = jnp.exp2((scores - peak) * (score_scale * log2e))
        mixed = dot(v_turned[head], powers.astype(bf16), 1, 0)
        total = mixed[HDIM : HDIM + 1, :]
        mixed_ref[head * HDIM : (head + 1) * HDIM, part] = mixed[:HDIM, :] * (1.0 / total)
        lse = peak * (score_scale * log2e) + jnp.log2(total)
        lse_ref[head : head + 1, part] = jnp.where(row_tags[:, part] < 0, -masked_score, lse)

    steps = tokens // tile
    begin_scores(0, 0)

    def body(step, _):
        begin_scores(step, 1)
        finish(step, 0)
        begin_scores(jnp.minimum(step + 1, steps - 1), 0)
        finish(step, 1)
        return 0

    lax.fori_loop(0, steps, body, 0)
    found = jnp.where(tags[...] < 0, v_ref[...], mixed_ref[...].T.astype(bf16))
    o_ref[...] = found

    @pl.when(item >= 2)
    def _():
        remote, local = part_copies(item - 2)
        remote.wait_send()
        local.wait()

    parts[item % 2] = found
    for copy in part_copies(item):
        copy.start()

    @pl.when(item == last)
    def _():
        for at in range(2):
            remote, local = part_copies(last - at)
            remote.wait_send()
            local.wait()
        for at in range(part_recv.shape[0]):
            part_came(at).wait_recv()
        own_copy().start()
        for copy in in_copies() + [own_copy()]:
            copy.wait()
        for at in range(n_seq // 2):
            rows = slice(2 * at * sub, 2 * (at + 1) * sub)
            middle[rows, :] = x_part[rows, :].astype(f32) + dot(own[rows, :], weight[...], 1, 0)
            middle_copy(2 * at).start()
            middle_copy(2 * at + 1).start()
        for s in range(n_seq):
            moves.wait_block(s)
        moves.wait_sends()
        for at in range(n_seq):
            middle_copy(at).wait()


def attend_row(qkv, tags, row_tags, cotangent, start, out_weight):
    tokens, width = qkv.shape
    row_count, block, model = cotangent.shape
    lanes = 2 * HDIM
    pairs = width // (3 * lanes)
    tile = 512
    n_seq, sub = CORES * row_count, block // CORES
    hbm = pl.BlockSpec(memory_space=pl.ANY)

    def columns(place):
        return pl.BlockSpec((tokens, lanes), lambda i: (0, 3 * i + place))

    return pl.pallas_call(
        functools.partial(attend_row_kernel, tile, row_count),
        grid=(pairs,),
        in_specs=[
            pl.BlockSpec((tokens, 1), lambda i: (0, 0)),
            pl.BlockSpec((1, tokens), lambda i: (0, 0)),
            columns(0),
            columns(1),
            columns(2),
            hbm,
            hbm,
            hbm,
        ],
        out_specs=[
            pl.BlockSpec((tokens, lanes), lambda i: (0, i)),
            pl.BlockSpec((None, 2, tokens), lambda i: (i, 0, 0)),
            hbm,
            hbm,
            hbm,
        ],
        out_shape=[
            jax.ShapeDtypeStruct((tokens, pairs * lanes), bf16),
            jax.ShapeDtypeStruct((pairs, 2, tokens), f32),
            jax.ShapeDtypeStruct((n_seq, sub, model), bf16),
            jax.ShapeDtypeStruct((tokens // CORES, model), bf16),
            jax.ShapeDtypeStruct((tokens // CORES, model), f32),
        ],
        scratch_shapes=[
            pltpu.VMEM((2, HDIM + 16, tokens), bf16),
            pltpu.VMEM((2, tokens, lanes), bf16),
            pltpu.VMEM((2, tokens, tile), f32),
            pltpu.VMEM((lanes, tokens), f32),
            pltpu.VMEM((2, tokens, lanes), bf16),
            pltpu.VMEM((tokens // CORES, model), bf16),
            pltpu.VMEM((model, model), bf16),
            pltpu.VMEM((tokens // CORES, model), bf16),
            pltpu.VMEM((tokens // CORES, model), f32),
            pltpu.SemaphoreType.DMA((row_count, CORES)),
            pltpu.SemaphoreType.DMA((n_seq,)),
            pltpu.SemaphoreType.DMA,
            pltpu.SemaphoreType.DMA((2,)),
            pltpu.SemaphoreType.DMA((pairs,)),
            pltpu.SemaphoreType.DMA((2,)),
            pltpu.SemaphoreType.DMA((3,)),
            pltpu.SemaphoreType.DMA((n_seq,)),
        ],
        compiler_params=pltpu.CompilerParams(
            vmem_limit_bytes=vmem_bytes, collective_id=4, has_side_effects=True
        ),
        name="attend_row",
    )(tags, row_tags, qkv, qkv, qkv, cotangent.reshape(row_count, CORES, sub, model), start, out_weight)


piece_rows = 16


def feed_kernel(
    tiles,
    rows,
    middle_ref,
    cot_ref,
    gain_ref,
    up_ref,
    down_ref,
    mixed_ref,
    out_weight_ref,
    out_ref,
    d_middle_ref,
    d_attn_out,
    d_mixed_out,
    out_kept,
    out_came,
    down_part,
    up_part,
    n2,
    total,
    d_attn,
    out_weight,
    out_keep,
    out_send,
    acts,
    d_ups,
    up_before,
    down_before,
    down_halves,
    down_recv,
    up_halves,
    up_recv,
    down_far_keep,
    down_far_send,
    down_far_recv,
    up_far_keep,
    up_far_send,
    up_far_recv,
    up_last_keep,
    up_last_send,
    up_last_recv,
    core_send_sem,
    core_recv_sem,
    far_send_sem,
    far_recv_sem,
    core_free,
    far_free,
    d_attn_sems,
    last_send_sem,
    last_recv_sem,
    out_sems,
):
    ahead = pl.program_id(0)
    step = ahead - 1
    tokens, width = n2.shape
    half, tile = width // 2, up_ref.shape[1]
    seq_at, rows_at = lax.axis_index("seq"), lax.axis_index("rows")
    core, high, low, mid = rows_at % 2, (rows_at // 2) % 2, seq_at % 2, (seq_at // 2) % 2
    core_peer = (seq_at, rows_at + 1 - 2 * core)
    far_peers = ((seq_at, rows_at + 2 - 4 * high), (seq_at + 1 - 2 * low, rows_at))
    last_peer = (seq_at + 2 - 4 * mid, rows_at)

    def copies(slot, far):
        if far:
            refs = ((down_far_send, down_far_recv), (up_far_send, up_far_recv))
            sems, peers = (far_send_sem, far_recv_sem), far_peers
        else:
            refs = ((down_halves.at[:, 1 - core], down_recv), (up_halves.at[:, 1 - core], up_recv))
            sems, peers = (core_send_sem, core_recv_sem), (core_peer, core_peer)
        return [
            pltpu.make_async_remote_copy(
                src_ref=refs[kind][0].at[slot],
                dst_ref=refs[kind][1].at[slot],
                send_sem=sems[0].at[kind, slot],
                recv_sem=sems[1].at[kind, slot],
                device_id=peers[kind],
                device_id_type=MESH,
            )
            for kind in range(2)
        ]

    def signal(sem, peer):
        pl.semaphore_signal(sem, inc=1, device_id=peer, device_id_type=MESH)

    @pl.when(ahead == 0)
    def _():
        barrier = pltpu.get_barrier_semaphore()
        for peer in (core_peer,) + far_peers + (last_peer,):
            signal(barrier, peer)
        pl.semaphore_wait(barrier, 4)

        def body(i, _):
            part = pl.ds(pl.multiple_of(i * rows, rows), rows)
            unit, _s = norm_parts(middle_ref[part, :])
            n2[part, :] = (unit * gain_ref[...]).astype(bf16)
            return 0

        lax.fori_loop(0, tokens // rows, body, 0)
        total[...] = middle_ref[...]
        d_middle_ref[...] = jnp.zeros_like(d_middle_ref)

    def activate():
        up = dot(n2[...], up_ref[...], 1, 0)
        d_act = dot(cot_ref[...], down_ref[...], 1, 1)
        share = 0.5 + 0.5 * lax.erf(up * (0.5**0.5))
        density = jnp.exp(-0.5 * up * up) * 0.3989422804014327
        acts[ahead % 2] = (up * share).astype(bf16)
        d_ups[ahead % 2] = (d_act * (share + up * density)).astype(bf16)

    def use():
        slot = step % 2
        act, d_up = acts[slot], d_ups[slot]
        total[...] += dot(act, down_before[...], 1, 0)
        d_middle_ref[...] += dot(d_up, up_before[...], 1, 1)
        up_grad = dot(n2[...], d_up, 0, 0).astype(bf16)
        cut = up_grad.shape[1] // 2
        up_halves[slot, 0] = up_grad[:, :cut].reshape(up_halves.shape[2:])
        up_halves[slot, 1] = up_grad[:, cut:].reshape(up_halves.shape[2:])
        down_grad = dot(act, cot_ref[...], 0, 0).astype(bf16)
        down_halves[slot, 0] = down_grad[:, :half].reshape(down_halves.shape[2:])
        down_halves[slot, 1] = down_grad[:, half:].reshape(down_halves.shape[2:])

    @pl.when((step >= 2) & (step < tiles))
    def _():
        for copy in copies(step % 2, False):
            copy.wait_send()

    @pl.when(ahead == 0)
    def _():
        activate()

    @pl.when((ahead > 0) & (ahead < tiles))
    def _():
        activate()
        use()

    @pl.when(ahead == tiles)
    def _():
        use()

    @pl.when(ahead < tiles)
    def _():
        up_before[...] = up_ref[...]
        down_before[...] = down_ref[...]

    def add(a, b):
        return (a.astype(f32) + b.astype(f32)).astype(bf16)

    def last_copy(slot):
        return pltpu.make_async_remote_copy(
            src_ref=up_last_send.at[slot],
            dst_ref=up_last_recv.at[slot],
            send_sem=last_send_sem.at[slot],
            recv_sem=last_recv_sem.at[slot],
            device_id=last_peer,
            device_id_type=MESH,
        )

    def last_add():
        slot = (step + 1) % 2
        last_copy(slot).wait_recv()
        up_part[...] = add(up_last_keep[slot], up_last_recv[slot]).reshape(up_part.shape)

    def far_add():
        slot = step % 2
        for copy in copies(slot, True):
            copy.wait_recv()
        down_part[...] = add(down_far_keep[slot], down_far_recv[slot]).reshape(down_part.shape)

        @pl.when(step >= 4)
        def _():
            last_copy(slot).wait_send()

        up_last_send[slot] = add(up_far_keep[slot, :, 1 - mid], up_far_recv[slot, :, 1 - mid])
        up_last_keep[slot] = add(up_far_keep[slot, :, mid], up_far_recv[slot, :, mid])
        last_copy(slot).start()

        @pl.when(step < tiles)
        def _():
            signal(far_free.at[0], far_peers[0])
            signal(far_free.at[1], far_peers[1])

    def pass_on():
        slot = (step + 1) % 2
        for copy in copies(slot, False):
            copy.wait_recv()

        @pl.when(step >= 3)
        def _():
            for copy in copies(slot, True):
                copy.wait_send()
            pl.semaphore_wait(far_free.at[0], 1)
            pl.semaphore_wait(far_free.at[1], 1)

        down_far_send[slot] = add(down_halves[slot, core, :, 1 - high], down_recv[slot, :, 1 - high])
        down_far_keep[slot] = add(down_halves[slot, core, :, high], down_recv[slot, :, high])
        shape = up_far_send.shape[1:]
        up_far_send[slot] = add(up_halves[slot, core, :, 1 - low], up_recv[slot, :, 1 - low]).reshape(shape)
        up_far_keep[slot] = add(up_halves[slot, core, :, low], up_recv[slot, :, low]).reshape(shape)
        for copy in copies(slot, True):
            copy.start()

        @pl.when(step < tiles - 1)
        def _():
            signal(core_free, core_peer)

    @pl.when((step >= 3) & (step <= tiles + 1))
    def _():
        last_add()

    @pl.when((step >= 2) & (step <= tiles))
    def _():
        far_add()

    @pl.when((step >= 1) & (step <= tiles))
    def _():
        pass_on()

    @pl.when((step >= 0) & (step < tiles))
    def _():
        @pl.when(step >= 2)
        def _():
            pl.semaphore_wait(core_free, 1)

        for copy in copies(step % 2, False):
            copy.start()

    @pl.when(step == tiles)
    def _():
        def body(i, _):
            part = pl.ds(pl.multiple_of(i * rows, rows), rows)
            low_total = total[part, :].astype(bf16)
            for at in range(2):
                acts[at, part, :] = low_total[:, at * tile : (at + 1) * tile]
            d_ups[0, part, : width - 2 * tile] = low_total[:, 2 * tile :]
            unit, scale = norm_parts(middle_ref[part, :])
            grad = cot_ref[part, :].astype(f32) + norm_back(d_middle_ref[part, :], gain_ref[...], unit, scale)
            d_middle_ref[part, :] = grad
            d_attn[part, :] = grad.astype(bf16)
            return 0

        lax.fori_loop(0, tokens // rows, body, 0)

    def to_core(source, target, at):
        return pltpu.make_async_remote_copy(
            src_ref=source,
            dst_ref=target,
            send_sem=d_attn_sems.at[at],
            recv_sem=d_attn_sems.at[at + 1],
            device_id=core_peer,
            device_id_type=MESH,
        )

    d_attn_copy = lambda: to_core(d_attn, d_attn_out.at[1], 0)
    out_copy = lambda: to_core(out_send, out_came, 2)
    mixed_copy = lambda: pltpu.make_async_copy(mixed_ref, n2, out_sems.at[0])
    weight_copy = lambda: pltpu.make_async_copy(
        out_weight_ref.at[pl.ds(pl.multiple_of(core * half, half), half)], out_weight, out_sems.at[1]
    )
    d_attn_save = lambda: pltpu.make_async_copy(d_attn, d_attn_out.at[0], out_sems.at[2])
    out_save = lambda: pltpu.make_async_copy(out_keep, out_kept, out_sems.at[3])
    d_mixed_save = lambda: pltpu.make_async_copy(down_halves, d_mixed_out, out_sems.at[4])

    def in_slots():
        wide = [(acts.at[at], pl.ds(at * tile, tile)) for at in range(2)]
        wide.append((d_ups.at[0, :, pl.ds(0, width - 2 * tile)], pl.ds(2 * tile, width - 2 * tile)))
        return list(enumerate(wide))

    def total_saves():
        return [
            pltpu.make_async_copy(source, out_ref.at[:, columns], out_sems.at[5 + at])
            for at, (source, columns) in in_slots()
        ]

    def d_attn_loads():
        return [
            pltpu.make_async_copy(d_attn_out.at[1, :, columns], target, out_sems.at[8 + at])
            for at, (target, columns) in in_slots()
        ]

    @pl.when(step == tiles)
    def _():
        for copy in total_saves():
            copy.start()
        d_attn_copy().start()
        d_attn_save().start()
        mixed_copy().start()
        weight_copy().start()

    @pl.when(step == tiles + 1)
    def _():
        mixed_copy().wait()
        grad = dot(n2[...], d_attn[...], 0, 0).astype(bf16)

        @pl.when(core == 0)
        def _():
            out_keep[...] = grad[:, :half]
            out_send[...] = grad[:, half:]

        @pl.when(core != 0)
        def _():
            out_keep[...] = grad[:, half:]
            out_send[...] = grad[:, :half]

        out_copy().start()
        out_save().start()
        far_add()

    @pl.when(step == tiles + 2)
    def _():
        for copy in total_saves():
            copy.wait()
        d_attn_copy().wait()
        for copy in d_attn_loads():
            copy.start()
        weight_copy().wait()
        for slot in range(2):
            for copy in copies(slot, False):
                copy.wait_send()

        def keep_d_mixed(at, found):
            found = found.astype(bf16).reshape((-1,) + down_halves.shape[2:])
            down_halves[at, : found.shape[0]] = found

        keep_d_mixed(0, dot(d_attn[...], out_weight[...], 1, 1))
        for copy in d_attn_loads():
            copy.wait()
        other = jnp.concatenate([acts[0], acts[1], d_ups[0, :, : width - 2 * tile]], 1)
        keep_d_mixed(1, dot(other, out_weight[...], 1, 1))
        d_mixed_save().start()
        last_add()
        out_copy().wait()
        for copy in (d_attn_save(), out_save(), d_mixed_save()):
            copy.wait()
        for slot in range(2):
            last_copy(slot).wait_send()
            for copy in copies(slot, True):
                copy.wait_send()


def feed(middle, cot, gain, up_weight, down_weight, mixed_own, out_weight, n_seq):
    tokens, width = middle.shape
    wide = up_weight.shape[1]
    tile = feed_tile
    tiles = wide // tile
    half, shard = width // 2, width // n_seq
    whole = lambda dtype: jax.ShapeDtypeStruct((tokens, width), dtype)
    fixed = lambda shape: pl.BlockSpec(shape, lambda i: (0, 0), pipeline_mode=pl.Buffered(1))
    at = lambda i: jnp.minimum(i, tiles - 1)
    hbm = pl.BlockSpec(memory_space=pl.ANY)
    late = lambda i: jnp.clip(i - 3, 0, tiles - 1)
    down_shape = (2, tile // (2 * piece_rows), 2, piece_rows, half)
    up_shape = (2, n_seq // 2, 2, shard, tile // 2)
    near = [pltpu.VMEM((2, tokens, tile), bf16)] * 2
    near += [pltpu.VMEM((width, tile), bf16), pltpu.VMEM((tile, width), bf16)]
    for shape in (down_shape, up_shape):
        near += [pltpu.VMEM(shape[:1] + (CORES,) + shape[1:], bf16), pltpu.VMEM(shape, bf16)]
    up_far = (2, n_seq // 4, 2, shard, tile // 2)
    far = [pltpu.VMEM(down_shape[:2] + down_shape[3:], bf16)] * 3 + [pltpu.VMEM(up_far, bf16)] * 3
    far += [pltpu.VMEM(up_far[:2] + up_far[3:], bf16)] * 3
    return pl.pallas_call(
        functools.partial(feed_kernel, tiles, 128),
        grid=(tiles + 4,),
        in_specs=[
            fixed((tokens, width)),
            fixed((tokens, width)),
            fixed((1, width)),
            pl.BlockSpec((width, tile), lambda i: (0, at(i))),
            pl.BlockSpec((tile, width), lambda i: (at(i), 0)),
            hbm,
            hbm,
        ],
        out_specs=[
            hbm,
            fixed((tokens, width)),
            hbm,
            hbm,
            hbm,
            hbm,
            pl.BlockSpec((tile // 2, half), lambda i: (late(i), 0)),
            pl.BlockSpec((width // 4, tile // 2), lambda i: (0, jnp.clip(i - 4, 0, tiles - 1))),
        ],
        scratch_shapes=[
            pltpu.VMEM((tokens, width), bf16),
            pltpu.VMEM((tokens, width), f32),
            pltpu.VMEM((tokens, width), bf16),
            pltpu.VMEM((half, width), bf16),
            pltpu.VMEM((width, half), bf16),
            pltpu.VMEM((width, half), bf16),
        ]
        + near
        + far
        + [pltpu.SemaphoreType.DMA((2, 2))] * 4
        + [pltpu.SemaphoreType.REGULAR, pltpu.SemaphoreType.REGULAR((2,)), pltpu.SemaphoreType.DMA((4,))]
        + [pltpu.SemaphoreType.DMA((2,))] * 2
        + [pltpu.SemaphoreType.DMA((11,))],
        out_shape=[
            whole(bf16),
            whole(f32),
            jax.ShapeDtypeStruct((2, tokens, width), bf16),
            jax.ShapeDtypeStruct(down_shape[:1] + (CORES,) + down_shape[1:], bf16),
            jax.ShapeDtypeStruct((width, half), bf16),
            jax.ShapeDtypeStruct((width, half), bf16),
            jax.ShapeDtypeStruct((wide // 2, half), bf16),
            jax.ShapeDtypeStruct((width // 4, wide // 2), bf16),
        ],
        compiler_params=pltpu.CompilerParams(
            vmem_limit_bytes=feed_vmem_bytes, collective_id=1, has_side_effects=True
        ),
        cost_estimate=pl.CostEstimate(
            flops=12 * tokens * width * wide,
            bytes_accessed=16 * tokens * width + 6 * width * wide,
            transcendentals=2 * tokens * wide,
        ),
        name="feed",
    )(middle, cot, gain.reshape(1, width), up_weight, down_weight, mixed_own, out_weight)


class Stream:
    def __init__(self, levels, rows, columns, first, count, lag):
        self.levels, self.rows, self.columns, self.first, self.count = levels, rows, columns, first, count
        self.lag = lag

    def shape(self, level):
        outer = 2 ** (len(self.levels) - 1 - level)
        return (max(outer // 2, 1), min(outer, 2), self.rows, self.columns)

    def scratch(self):
        shapes = []
        for level in range(len(self.levels)):
            shape = self.shape(level)
            shapes += [pltpu.VMEM(shape, bf16), pltpu.VMEM(shape, bf16), pltpu.VMEM((2,) + shape, bf16)]
        return shapes


down_pieces = 4


def streams_of(width, wide, n_seq, pairs):
    lanes = 2 * HDIM
    rows = width // (2 * n_seq)
    return (
        Stream(("x", "y", "z1", "z2"), rows, 4 * lanes, 1, pairs, 2),
        Stream(("y", "z1", "z2"), wide // (2 * n_seq * down_pieces), width // CORES, 2, down_pieces, 2),
        Stream(("x", "z2"), rows, wide // CORES // down_pieces, 2, down_pieces, 1),
    )


def back_kernel(pairs, tile, streams, row_count, *refs):
    (
        key_tags, query_tags, q_ref, k_ref, v_ref, o_ref, do_ref, lse_ref, n1_ref, own_weight, other_weight,
        gain_ref, out_kept, out_came, down_ref, up_ref, start_ref, d_middle_ref, outputs_ref,
    ) = refs[:19]
    grad_out, outputs_out, *gathered = refs[19:24]
    rest = list(refs[24:])
    take = lambda count: [rest.pop(0) for _ in range(count)]
    k_turned, dq_turned, delta, d_pair, d_came, d_n1, staged, start_part, middle_part = take(9)
    levels = []
    for stream in streams:
        levels.append([take(3) for _ in stream.levels])
    joined = take(len(streams))
    (
        send_sems, recv_sems, join_send, join_recv, core_send, core_recv, local_sems,
        pair_send, pair_recv, home_send, home_recv, home_local, part_sems, result_send, result_recv, result_local,
    ) = rest

    step = pl.program_id(0)
    tokens, lanes = q_ref.shape
    own_tokens = tokens // CORES
    seq_at, rows_at = lax.axis_index("seq"), lax.axis_index("rows")
    core, high = rows_at % 2, (rows_at // 2) % 2
    places = {"x": high, "y": seq_at % 2, "z1": (seq_at // 2) % 2, "z2": seq_at // 4}
    peers = {
        "x": (seq_at, rows_at + 2 - 4 * high),
        "y": (seq_at + 1 - 2 * places["y"], rows_at),
        "z1": (seq_at + 2 - 4 * places["z1"], rows_at),
        "z2": (seq_at + 4 - 8 * places["z2"], rows_at),
        "core": (seq_at, rows_at + 1 - 2 * core),
    }
    n_seq = 2 * row_count
    sub = start_part.shape[1]

    def remote(source, target, send, recv, peer):
        return pltpu.make_async_remote_copy(
            src_ref=source, dst_ref=target, send_sem=send, recv_sem=recv, device_id=peer, device_id_type=MESH
        )

    def add(a, b):
        return (a.astype(f32) + b.astype(f32)).astype(bf16)

    def level_copy(at, level, item):
        send, _, came = levels[at][level]
        slot = item % 2
        return remote(
            send, came.at[slot], send_sems.at[at, level], recv_sems.at[at, level, slot], peers[streams[at].levels[level]]
        )

    def join_copy(at, item):
        part = joined[at].at[item, high]
        return remote(part, part, join_send.at[at], join_recv.at[at, item % 2], peers["x"])

    def core_copy(at, item):
        return remote(
            joined[at].at[item],
            gathered[at].at[item, core],
            core_send.at[at],
            core_recv.at[at, item % 2],
            peers["core"],
        )

    def local_copy(at, item):
        return pltpu.make_async_copy(joined[at].at[item], gathered[at].at[item, core], local_sems.at[at])

    def pair_copy(item):
        slot = item % 2
        return remote(
            d_pair.at[slot, pl.ds(own_tokens, own_tokens)],
            d_came.at[slot],
            pair_send.at[slot],
            pair_recv.at[slot],
            peers["core"],
        )

    home = seq_at // row_count

    def to_home(block, own, result):
        if result:
            source, target = outputs_ref.at[pl.ds(pl.multiple_of(block * sub, sub), sub)], outputs_out
            sems = result_send, result_recv, result_local
        else:
            source, target = staged.at[block], grad_out
            sems = home_send, home_recv, home_local
        row = seq_at % row_count
        if own:
            return pltpu.make_async_copy(source, target.at[row, core], sems[2])
        return remote(source, target.at[row, core], sems[0].at[block], sems[1].at[row, core], (block, rows_at - core + home))

    def start_home(block, result):
        @pl.when(is_own(block))
        def _():
            to_home(block, True, result).start()

        @pl.when(jnp.logical_not(is_own(block)))
        def _():
            to_home(block, False, result).start()

    def wait_home(result):
        for block in range(n_seq):
            @pl.when(is_own(block))
            def _():
                to_home(block, True, result).wait()

            @pl.when(jnp.logical_not(is_own(block)))
            def _():
                to_home(block, False, result).wait_send()
        source, target = (outputs_ref.at[pl.ds(0, sub)], outputs_out) if result else (staged.at[0], grad_out)
        sems = (result_send, result_recv) if result else (home_send, home_recv)
        for row in range(row_count):
            for c in range(CORES):
                @pl.when(jnp.logical_not((seq_at == core * row_count + row) & (core == c)))
                def _():
                    remote(source, target.at[row, c], sems[0].at[0], sems[1].at[row, c], peers["core"]).wait_recv()

    def is_own(block):
        return (seq_at == block) & (home == core)

    @pl.when(step == 0)
    def _():
        barrier = pltpu.get_barrier_semaphore()
        for s in range(n_seq):
            for c in range(CORES):
                @pl.when(jnp.logical_not((seq_at == s) & (core == c)))
                def _():
                    pl.semaphore_signal(barrier, inc=1, device_id=(s, rows_at - core + c), device_id_type=MESH)
        pl.semaphore_signal(barrier, inc=1, device_id=peers["x"], device_id_type=MESH)
        pl.semaphore_wait(barrier, n_seq * CORES)
        d_n1[...] = jnp.zeros_like(d_n1)

    @pl.when(step < n_seq // 2)
    def _():
        for turn in range(2):
            start_home((seq_at + 2 * step + turn) % n_seq, True)

    working, second = step < 2 * pairs, step % 2

    @pl.when(working & (second == 0))
    def _():
        k_turned[...] = k_ref[...].T
        dq_turned[...] = (o_ref[...].astype(f32) * do_ref[...].astype(f32)).T
        for head in range(2):
            own_rows = dq_turned[head * HDIM : (head + 1) * HDIM, :]
            delta[head : head + 1, :] = jnp.sum(own_rows, axis=0, keepdims=True)
        dq_turned[...] = jnp.zeros_like(dq_turned)

    @pl.when(working)
    def _():
        slot = step // 2 % 2
        half_steps = tokens // tile // 2
        first = lax.broadcasted_iota(jnp.int32, (tile, lanes), 1) < HDIM

        def body(i, _):
            part = pl.ds(pl.multiple_of((i + second * half_steps) * tile, tile), tile)
            k, v = k_ref[part, :], v_ref[part, :]
            q, do = q_ref[...], do_ref[...]
            tag = key_tags[part, :]
            allowed = tag == query_tags[...]
            dk, dv = [], []
            for head in range(2):
                own = first if head == 0 else jnp.logical_not(first)
                own_rows = slice(head * HDIM, (head + 1) * HDIM)
                scores = dot(jnp.where(own, k, bf16(0)), q, 1, 1)
                scores = jnp.where(allowed, scores, masked_score)
                chances = jnp.exp2(scores * (score_scale * log2e) - lse_ref[head : head + 1, :])
                weight_grad = dot(jnp.where(own, v, bf16(0)), do, 1, 1)
                score_grad = (chances * (weight_grad - delta[head : head + 1, :])).astype(bf16)
                dv.append(dot(chances.astype(bf16), do, 1, 0))
                dk.append(dot(score_grad, q, 1, 0))
                dq_turned[own_rows, :] += dot(k_turned[own_rows, part], score_grad, 1, 0)
            d_pair[slot, part, lanes : 2 * lanes] = (jnp.where(first, dk[0], dk[1]) * score_scale).astype(bf16)
            d_v = jnp.where(first, dv[0], dv[1]).astype(bf16)
            d_pair[slot, part, 2 * lanes :] = jnp.where(tag < 0, do_ref[part, :], d_v)
            return 0

        lax.fori_loop(0, half_steps, body, 0)

    @pl.when(working & (second == 1))
    def _():
        d_pair[step // 2 % 2, :, :lanes] = (dq_turned[...] * score_scale).T.astype(bf16)

    def add_pair():
        item = step // 2 - 1
        slot = item % 2
        pair_copy(item).wait()
        d_n1[...] += dot(d_pair[slot, :own_tokens, :], own_weight[...], 1, 1) + dot(
            d_came[slot], other_weight[...], 1, 1
        )

    @pl.when((step >= 2) & (step <= 2 * pairs) & (second == 0))
    def _():
        add_pair()

    @pl.when(working & (second == 1))
    def _():
        pair_copy(step // 2).start()

    def part_copies(turn):
        rows = pl.ds(pl.multiple_of((seq_at + turn) % n_seq * sub, sub), sub)
        slot = turn % 2
        return (
            pltpu.make_async_copy(start_ref.at[rows], start_part.at[slot], part_sems.at[0, slot]),
            pltpu.make_async_copy(d_middle_ref.at[rows], middle_part.at[slot], part_sems.at[1, slot]),
        )

    @pl.when(step == 2 * pairs)
    def _():
        for copy in part_copies(0):
            copy.start()

        def body(turn, _):
            block = (seq_at + turn) % n_seq

            @pl.when(turn + 1 < n_seq)
            def _():
                for copy in part_copies(turn + 1):
                    copy.start()

            for copy in part_copies(turn):
                copy.wait()
            unit, scale = norm_parts(start_part[turn % 2].astype(f32))
            rows = pl.ds(pl.multiple_of(block * sub, sub), sub)
            grad = norm_back(d_n1[rows, :], gain_ref[...], unit, scale)
            staged[block] = (middle_part[turn % 2] + grad).astype(bf16)
            start_home(block, False)
            return 0

        lax.fori_loop(0, n_seq, body, 0)

    for at, stream in enumerate(streams):
        depth = len(stream.levels)

        def item_at(lag, stream=stream):
            since = step - stream.first - lag
            return since // 2, (since >= 0) & (since % 2 == 0) & (since < 2 * stream.count)

        item, here = item_at(depth + 1 + stream.lag)

        @pl.when(here)
        def _(at=at, item=item):
            core_copy(at, item).wait()
            local_copy(at, item).wait()

        item, here = item_at(depth + stream.lag)

        @pl.when(here)
        def _(at=at, item=item):
            join_copy(at, item).wait()
            core_copy(at, item).start()
            local_copy(at, item).start()

        for level in reversed(range(depth)):
            item, here = item_at(level + stream.lag)

            @pl.when(here)
            def _(at=at, item=item, level=level, stream=stream, depth=depth):
                _, keep, came = levels[at][level]
                slot = item % 2
                level_copy(at, level, item).wait_recv()
                if level == depth - 1:
                    joined[at][item, high] = add(keep[0, 0], came[slot, 0, 0])
                    join_copy(at, item).start()
                    return

                @pl.when(item > 0)
                def _():
                    level_copy(at, level + 1, item - 1).wait_send()

                next_send, next_keep, _ = levels[at][level + 1]
                place = places[stream.levels[level + 1]]
                next_send[...] = add(keep[:, 1 - place], came[slot, :, 1 - place]).reshape(next_send.shape)
                next_keep[...] = add(keep[:, place], came[slot, :, place]).reshape(next_keep.shape)
                level_copy(at, level + 1, item).start()

    def begin_piece(fills):
        for at, fill in fills.items():
            stream = streams[at]
            item = (step - stream.first) // 2

            @pl.when((step % 2 == stream.first % 2) & (step >= stream.first) & (item < stream.count))
            def _(at=at, fill=fill, item=item):
                @pl.when(item > 0)
                def _():
                    level_copy(at, 0, item - 1).wait_send()

                fill(*levels[at][0][:2])
                level_copy(at, 0, item).start()

    def fill_pair(send, keep):
        grad = dot(n1_ref[...], d_pair[step // 2 % 2], 0, 0).astype(bf16)
        grad = grad.reshape(n_seq, 2, send.shape[2], 3 * lanes)
        shape = send.shape[:3] + (3 * lanes,)

        @pl.when(high == 0)
        def _():
            send[:, :, :, : 3 * lanes] = grad[:, 1].reshape(shape)
            keep[:, :, :, : 3 * lanes] = grad[:, 0].reshape(shape)

        @pl.when(high != 0)
        def _():
            send[:, :, :, : 3 * lanes] = grad[:, 0].reshape(shape)
            keep[:, :, :, : 3 * lanes] = grad[:, 1].reshape(shape)

        shape = send.shape[:3] + (lanes,)
        send[:, :, :, 3 * lanes :] = add(out_kept[:, 1 - high], out_came[:, 1 - high]).reshape(shape)
        keep[:, :, :, 3 * lanes :] = add(out_kept[:, high], out_came[:, high]).reshape(shape)

    def fill_from(ref, place):
        def fill(send, keep):
            send[...] = ref[:, 1 - place].reshape(send.shape)
            keep[...] = ref[:, place].reshape(keep.shape)

        return fill

    begin_piece({0: fill_pair, 1: fill_from(down_ref, places["y"]), 2: fill_from(up_ref, high)})

    @pl.when(step == pl.num_programs(0) - 1)
    def _():
        for at, stream in enumerate(streams):
            for level in range(len(stream.levels)):
                level_copy(at, level, stream.count - 1).wait_send()
        wait_home(False)
        wait_home(True)


def back(
    qkv, mixed, d_mixed, lse, key_tags, query_tags, n1, weights, gain, out_kept, out_came, down_part, up_part,
    start, d_middle, outputs, row_count,
):
    tokens = qkv.shape[0]
    width = n1.shape[1]
    own_tokens = tokens // CORES
    lanes = 2 * HDIM
    pairs = qkv.shape[1] // (3 * lanes)
    n_seq = 2 * row_count
    tile = 512
    sub = own_tokens // n_seq
    streams = streams_of(width, down_part.shape[0] * 2, n_seq, pairs)
    last = pairs - 1
    now = lambda i: jnp.minimum(i // 2, last)
    before = lambda i: jnp.clip(i // 2 - 1, 0, last)
    early = lambda i: jnp.clip(i // 2 - 1, 0, down_pieces - 1)
    fixed = lambda shape: pl.BlockSpec(shape, lambda i: (0,) * len(shape), pipeline_mode=pl.Buffered(1))

    def columns(place):
        return pl.BlockSpec((tokens, lanes), lambda i: (0, 3 * now(i) + place))

    pair = pl.BlockSpec((tokens, lanes), lambda i: (0, now(i)))
    weight = pl.BlockSpec((width, 3 * lanes), lambda i: (0, before(i)))
    hbm = pl.BlockSpec(memory_space=pl.ANY)

    rows = streams[0].rows

    def out_piece(value):
        whole = value.reshape(n_seq, 2, rows, value.shape[1])
        return whole, pl.BlockSpec((n_seq, 2, rows, lanes), lambda i: (0, 0, 0, now(i)))

    outs = [out_piece(value) for value in (out_kept, out_came)]
    down = down_part.reshape(n_seq // 2, 2, -1, width // CORES)
    up = up_part.reshape(n_seq // 4, 2, rows, -1)
    down_spec = pl.BlockSpec((n_seq // 2, 2, streams[1].rows, width // CORES), lambda i: (0, 0, early(i), 0))
    up_spec = pl.BlockSpec((n_seq // 4, 2, rows, streams[2].columns), lambda i: (0, 0, 0, early(i)))
    count = len(streams)
    deepest = max(len(stream.levels) for stream in streams)
    return pl.pallas_call(
        functools.partial(back_kernel, pairs, tile, streams, row_count),
        grid=(2 * pairs + deepest + 1 + streams[0].lag,),
        in_specs=[
            fixed((tokens, 1)),
            fixed((1, tokens)),
            columns(0),
            columns(1),
            columns(2),
            pair,
            pair,
            pl.BlockSpec((None, 2, tokens), lambda i: (now(i), 0, 0)),
            fixed((tokens, width)),
            weight,
            weight,
            fixed((1, width)),
            outs[0][1],
            outs[1][1],
            down_spec,
            up_spec,
            hbm,
            hbm,
            hbm,
        ],
        out_specs=[hbm] * 5,
        out_shape=[jax.ShapeDtypeStruct((row_count, CORES, sub, width), bf16)] * 2
        + [jax.ShapeDtypeStruct((stream.count, CORES, 2, stream.rows, stream.columns), bf16) for stream in streams],
        scratch_shapes=[
            pltpu.VMEM((lanes, tokens), bf16),
            pltpu.VMEM((lanes, tokens), f32),
            pltpu.VMEM((2, tokens), f32),
            pltpu.VMEM((2, tokens, 3 * lanes), bf16),
            pltpu.VMEM((2, own_tokens, 3 * lanes), bf16),
            pltpu.VMEM((own_tokens, width), f32),
            pltpu.VMEM((n_seq, sub, width), bf16),
            pltpu.VMEM((2, sub, width), bf16),
            pltpu.VMEM((2, sub, width), f32),
        ]
        + [shape for stream in streams for shape in stream.scratch()]
        + [pltpu.VMEM((stream.count, 2, stream.rows, stream.columns), bf16) for stream in streams]
        + [
            pltpu.SemaphoreType.DMA((count, deepest)),
            pltpu.SemaphoreType.DMA((count, deepest, 2)),
            pltpu.SemaphoreType.DMA((count,)),
            pltpu.SemaphoreType.DMA((count, 2)),
            pltpu.SemaphoreType.DMA((count,)),
            pltpu.SemaphoreType.DMA((count, 2)),
            pltpu.SemaphoreType.DMA((count,)),
            pltpu.SemaphoreType.DMA((2,)),
            pltpu.SemaphoreType.DMA((2,)),
            pltpu.SemaphoreType.DMA((n_seq,)),
            pltpu.SemaphoreType.DMA((row_count, CORES)),
            pltpu.SemaphoreType.DMA,
            pltpu.SemaphoreType.DMA((2, 2)),
            pltpu.SemaphoreType.DMA((n_seq,)),
            pltpu.SemaphoreType.DMA((row_count, CORES)),
            pltpu.SemaphoreType.DMA,
        ],
        compiler_params=pltpu.CompilerParams(
            vmem_limit_bytes=feed_vmem_bytes, collective_id=2, has_side_effects=True
        ),
        cost_estimate=pl.CostEstimate(
            flops=80 * pairs * tokens * tokens * HDIM,
            bytes_accessed=16 * tokens * pairs * lanes,
            transcendentals=2 * pairs * tokens * tokens,
        ),
        name="back",
    )(
        key_tags, query_tags, qkv, qkv, qkv, mixed, d_mixed, lse, n1, weights[0], weights[1],
        gain.reshape(1, width), outs[0][0], outs[1][0], down, up, start, d_middle, outputs,
    )


def collect_kernel(pairs, seq_ref, *refs):
    qkv_parts, down_parts, up_parts = refs[:3]
    qkv_weights, up_weight = refs[3:9], refs[9]
    qkv_out, out_out, down_out, up_out, first_out, second_out, first_sum, second_sum = refs[10:]
    item = pl.program_id(0)
    lanes = 2 * HDIM
    rows = qkv_parts.shape[2]
    width = out_out.shape[1]
    half = width // CORES
    tile = feed_tile // CORES

    @pl.when(item == 0)
    def _():
        first_sum[...] = jnp.zeros_like(first_sum)
        second_sum[...] = jnp.zeros_like(second_sum)

    for core in range(CORES):
        place = pl.multiple_of(core * half + item * lanes, lanes)
        for high in range(2):
            own = slice(high * rows, (high + 1) * rows)
            part = qkv_parts[core, high].astype(f32)
            for kind in range(3):
                value = part[:, kind * lanes : (kind + 1) * lanes]
                qkv_out[own, pl.ds(kind * width + place, lanes)] = value
                weight = qkv_weights[kind * CORES + core][own, :].astype(f32)
                first_sum[own, :] += value * weight
            out_out[own, pl.ds(place, lanes)] = part[:, 3 * lanes :]

    @pl.when(item < down_pieces)
    def _():
        for core in range(CORES):
            for high in range(2):
                own = slice(high * rows, (high + 1) * rows)
                for at in range(up_parts.shape[3] // lanes):
                    column = item * up_parts.shape[3] + at * lanes
                    column = column // tile * feed_tile + core * tile + column % tile
                    columns = pl.ds(pl.multiple_of(column, lanes), lanes)
                    value = up_parts[core, high, :, at * lanes : (at + 1) * lanes].astype(f32)
                    up_out[own, columns] = value
                    second_sum[own, :] += value * up_weight[own, columns].astype(f32)
                count = down_parts.shape[2] // piece_rows
                for at in range(count):
                    start = ((item * count + at) * 2 + high) * piece_rows
                    value = down_parts[core, high, at * piece_rows : (at + 1) * piece_rows, :].astype(f32)
                    down_out[pl.ds(pl.multiple_of(start, piece_rows), piece_rows), core * half : (core + 1) * half] = value

    @pl.when(item == pairs - 1)
    def _():
        first_out[...] = jnp.sum(first_sum[...].T, axis=0, keepdims=True)
        second_out[...] = jnp.sum(second_sum[...].T, axis=0, keepdims=True)


def collect(seq_at, qkv_parts, down_parts, up_parts, qkv_weight, up_weight):
    pairs, _, _, rows, _ = qkv_parts.shape
    width, lanes = qkv_weight.shape[0], 2 * HDIM
    shard, wide = 2 * rows, up_weight.shape[1]
    down_rows = 2 * down_pieces * down_parts.shape[3]

    def parts(value):
        return pl.BlockSpec(
            (None,) + value.shape[1:], lambda i, seq: (jnp.minimum(i, value.shape[0] - 1), 0, 0, 0, 0)
        )

    def weight(kind, core):
        return pl.BlockSpec((shard, lanes), lambda i, seq: (seq[0], (kind * CORES + core) * pairs + i))

    whole = lambda shape: pl.BlockSpec(shape, lambda i, seq: (0, 0))
    return pl.pallas_call(
        functools.partial(collect_kernel, pairs),
        grid_spec=pltpu.PrefetchScalarGridSpec(
            num_scalar_prefetch=1,
            grid=(pairs,),
            in_specs=[parts(qkv_parts), parts(down_parts), parts(up_parts)]
            + [weight(kind, core) for kind in range(3) for core in range(CORES)]
            + [pl.BlockSpec((shard, wide), lambda i, seq: (seq[0], 0))],
            out_specs=[
                whole((shard, 3 * width)),
                whole((shard, width)),
                whole((down_rows, width)),
                whole((shard, wide)),
                whole((1, shard)),
                whole((1, shard)),
            ],
            scratch_shapes=[pltpu.VMEM((shard, lanes), f32)] * 2,
        ),
        out_shape=[
            jax.ShapeDtypeStruct((shard, 3 * width), f32),
            jax.ShapeDtypeStruct((shard, width), f32),
            jax.ShapeDtypeStruct((down_rows, width), f32),
            jax.ShapeDtypeStruct((shard, wide), f32),
            jax.ShapeDtypeStruct((1, shard), f32),
            jax.ShapeDtypeStruct((1, shard), f32),
        ],
        compiler_params=pltpu.CompilerParams(vmem_limit_bytes=vmem_bytes),
        name="collect",
    )(
        seq_at.reshape(1), qkv_parts, down_parts, up_parts, *[qkv_weight] * 6, up_weight,
    )


def add_split_kernel(has_two, bit_ref, *refs):
    ins, outs = refs[: 2 if has_two else 1], refs[2 if has_two else 1 :]
    value = ins[0][...]
    if has_two:
        value = (value.astype(f32) + ins[1][...].astype(f32)).astype(bf16)
    if len(outs) == 1:
        outs[0][...] = value
    else:
        sends = pl.program_id(0) == 0

        @pl.when(sends)
        def _():
            outs[0][...] = value

        @pl.when(jnp.logical_not(sends))
        def _():
            outs[1][...] = value


def add_split(kept, received, inner, bit):
    rows, columns = kept.shape
    values = [kept] if received is None else [kept, received.reshape(rows, columns)]
    if bit is None:
        if received is None:
            return None, kept
        count = 4 if rows % 64 == 0 else 1
        block = pl.BlockSpec((rows // count, columns), lambda i, bit: (i, 0))
        grid, ins, outs = (count,), [block] * 2, block
        shapes = jax.ShapeDtypeStruct((rows, columns), bf16)
        bit = jnp.zeros((), jnp.int32)
    else:
        outer = rows // (2 * inner)
        cut = 1
        while inner // cut * columns > 2**19 and inner % (32 * cut) == 0:
            cut *= 2
        values = [value.reshape(outer, 2, inner, columns) for value in values]
        ins = [
            pl.BlockSpec(
                (None, None, inner // cut, columns),
                lambda w, i, j, bit: (i, jnp.where(w == 0, 1 - bit[0], bit[0]), j, 0),
            )
        ] * len(values)
        outs = [
            pl.BlockSpec(
                (None, inner // cut, columns),
                lambda w, i, j, bit: (jnp.where(w == 0, i, outer - 1), jnp.where(w == 0, j, cut - 1), 0),
            ),
            pl.BlockSpec(
                (None, inner // cut, columns),
                lambda w, i, j, bit: (jnp.where(w == 0, 0, i), jnp.where(w == 0, 0, j), 0),
            ),
        ]
        grid = (2, outer, cut)
        shapes = [jax.ShapeDtypeStruct((outer, inner, columns), bf16)] * 2
    done = pl.pallas_call(
        functools.partial(add_split_kernel, len(values) == 2),
        grid_spec=pltpu.PrefetchScalarGridSpec(
            num_scalar_prefetch=1, grid=grid, in_specs=ins, out_specs=outs
        ),
        out_shape=shapes,
        cost_estimate=pl.CostEstimate(flops=rows * columns, bytes_accessed=6 * rows * columns, transcendentals=0),
        name="add_split",
    )(bit.reshape(1), *values)
    if not isinstance(done, (list, tuple)):
        return None, done
    return done[0].reshape(rows // 2, columns), done[1].reshape(rows // 2, columns)


def tie(*values):
    return lax.optimization_barrier(values)


def build(n_seq, n_rows):
    highs = n_rows // CORES
    seq_bits = n_seq.bit_length() - 1
    high_bits = highs.bit_length() - 1
    bits = seq_bits + high_bits

    def permute(value, target):
        pairs = []
        for s in range(n_seq):
            for r in range(n_rows):
                to_s, to_r = target(s, r)
                pairs.append((s * n_rows + r, to_s * n_rows + to_r))
        return lax.ppermute(value, AXES, pairs)

    def other_core(value):
        return permute(value, lambda s, r: (s, r ^ 1))

    def pick(value, place, axis):
        return lax.dynamic_index_in_dim(value, place, axis, keepdims=False)

    def bit_of(step):
        name, bit = step
        return (lax.axis_index(name) >> bit) & 1

    def across(value, step):
        name, bit = step
        if name == "rows":
            return permute(value, lambda s, r: (s, r ^ (1 << bit)))
        return permute(value, lambda s, r: (s ^ (1 << bit), r))

    high_steps = [("rows", bit + 1) for bit in reversed(range(high_bits))]
    seq_steps = [("seq", bit) for bit in range(seq_bits)]

    class Sum:
        def __init__(self, kept, received, order):
            self.rows, self.columns = kept.shape
            self.kept, self.received = kept, received
            self.left = [step for step in seq_steps[::-1] + high_steps if step in order]
            self.order = list(order)

        def finish(self):
            step = self.order[0] if self.order else None
            inner = self.rows
            if step is not None:
                axis = self.left.index(step)
                inner = self.rows >> (axis + 1)
            self.sent, self.kept = add_split(self.kept, self.received, inner, step and bit_of(step))
            self.received = None

        def begin(self):
            step = self.order.pop(0)
            self.left.remove(step)
            self.rows //= 2
            self.received = across(self.sent, step)

        def finished(self):
            while self.order:
                self.finish()
                self.begin()
            self.finish()
            return self.kept

    rows_first = high_steps + seq_steps[1:2] + seq_steps[:1] + seq_steps[2:]
    down_order = [step for step in seq_steps + high_steps if step != ("rows", 1)]
    up_order = [step for step in high_steps + seq_steps if step not in (("seq", 0), ("seq", 1))]

    def gather_high(value, pieces=0):
        for step in high_steps[::-1]:
            if pieces and step == ("rows", 1):
                continue
            received = across(value, step)
            value = jnp.where(
                bit_of(step) == 0,
                jnp.concatenate([value, received], 0),
                jnp.concatenate([received, value], 0),
            )
        if pieces:
            value = value.reshape(-1, 1, pieces, value.shape[1])
            received = across(value, ("rows", 1))
            value = jnp.where(
                bit_of(("rows", 1)) == 0,
                jnp.concatenate([value, received], 1),
                jnp.concatenate([received, value], 1),
            )
            value = value.reshape(-1, value.shape[-1])
        return value

    def back_by_steps(
        qkv, mixed, d_mixed, lse, key_tags, query_tags, n1_all, qkv_parts, attention_gain,
        out_kept, out_received, down_part, up_part, start, d_middle, to_member, ordered, from_rows, sizes,
    ):
        group, member, core, pairs, group_width, tokens, width = sizes
        lanes, half = 2 * HDIM, width // CORES
        unit1, scale1 = norm_parts(start)
        down = Sum(down_part, None, down_order)
        up = Sum(up_part, None, up_order)
        out = Sum(out_kept, out_received, rows_first)

        def before_next(*sums):
            nonlocal d_mixed
            for each in sums:
                each.finish()
            values = tie(d_mixed, *[v for each in sums for v in (each.sent, each.kept)])
            d_mixed = values[0]
            for at, each in enumerate(sums):
                each.sent, each.kept = values[1 + 2 * at : 3 + 2 * at]
                each.begin()

        def back_at(at):
            return attend_back(qkv, mixed, d_mixed, lse, key_tags, query_tags, at, 1)

        cut = max(1, 3 * pairs // 5)
        before_next(down, up)
        d_qkv, qkv_sums, d_parts = [], [], [[] for _ in range(group)]

        def take_piece(pieces):
            piece = jnp.concatenate(pieces, axis=1)
            d_parts[0].append(piece[:tokens])
            for hop in range(1, group):
                d_parts[hop].append(to_member(piece[hop * tokens : (hop + 1) * tokens], group - hop))
            return dot(n1_all, piece, 0, 0)

        grads = []
        for at in range(pairs):
            d_qkv.append(back_at(at))
            d_mixed, d_qkv[at] = tie(d_mixed, d_qkv[at])
            if at + 1 == cut:
                grads.append(take_piece(d_qkv))
            if at == min(0, pairs - 1):
                before_next(out)
            if at == min(1, pairs - 1):
                before_next(down, up)
            if at == min(3, pairs - 1):
                before_next(down, up, out)
        if pairs > cut:
            grads.append(take_piece(d_qkv[cut:]))
        if group == CORES:
            qkv_sums = [Sum(grad.astype(bf16), None, rows_first) for grad in grads]
        else:
            grad = jnp.concatenate(grads, 1)
            grad = grad.reshape(width, pairs, 3, lanes).transpose(0, 2, 1, 3)
            grad = grad.reshape(width, 3, 1, pairs * lanes)[..., :group_width]
            grad = lax.dynamic_update_slice_in_dim(
                jnp.zeros((width, 3, group, group_width), f32), grad, member, 2
            ).reshape(width, 3, CORES, half)
            kept = pick(grad, core, 2).astype(bf16).reshape(width, 3 * half)
            sent = pick(grad, 1 - core, 2).astype(bf16).reshape(width, 3 * half)
            qkv_sums = [Sum(kept, other_core(sent), rows_first)]

        d_n1 = jnp.zeros((tokens, width), f32)
        for part, weight in zip(d_parts, qkv_parts):
            d_n1 = d_n1 + dot(jnp.concatenate(part, 1), weight, 1, 1)
        input_grad = d_middle + norm_back(d_n1, attention_gain, unit1, scale1)
        input_grad = from_rows(input_grad.astype(bf16))

        down_total = gather_high(down.finished(), piece_rows)
        down_total = ordered(down_total, other_core(down_total), 1).astype(f32)
        tile = feed_tile // CORES
        up_total = gather_high(up.finished()).reshape(width // n_seq, -1, 1, tile)
        up_total = ordered(up_total, other_core(up_total), 2).reshape(width // n_seq, -1).astype(f32)
        out_total = gather_high(out.finished())
        out_total = ordered(out_total, other_core(out_total), 1).astype(f32)
        qkv_part = gather_high(jnp.concatenate([each.finished() for each in qkv_sums], 1))
        if group == CORES:
            qkv_part = qkv_part.reshape(-1, pairs, 3, lanes).transpose(0, 2, 1, 3)
        qkv_part = qkv_part.reshape(-1, 3, half)
        qkv_total = ordered(qkv_part[:, :, None], other_core(qkv_part)[:, :, None], 2)
        qkv_total = qkv_total.reshape(-1, 3 * width).astype(f32)

        return input_grad, qkv_total, out_total, down_total, up_total

    def per_device(
        inputs, cell_ids, valid_counts, cotangent, attention_gain, qkv_weight, out_weight, feed_gain, up_weight, down_weight
    ):
        row_count, block, width = inputs.shape
        seq_len = cell_ids.shape[1]
        heads = width // HDIM
        lanes = 2 * HDIM
        seq_at, rows_at = lax.axis_index("seq"), lax.axis_index("rows")
        core = rows_at % CORES
        chips = n_seq // (CORES * row_count)
        group = chips * CORES
        sub = block // group
        tokens = n_seq * sub
        member = (seq_at % chips) * CORES + core
        group_heads = heads // group
        pairs = -(-group_heads // 2)
        group_width = group_heads * HDIM
        padded = pairs * lanes - group_width

        def to_member(value, hop):
            def target(s, r):
                place = ((s % chips) * CORES + r % CORES + hop) % group
                return (s // chips * chips + place // CORES, r // CORES * CORES + place % CORES)

            return permute(value, target)

        def ordered(own, received, axis):
            return jnp.where(
                core == 0,
                jnp.concatenate([own, received], axis),
                jnp.concatenate([received, own], axis),
            )

        def to_rows(value):
            halves = value.reshape(row_count, CORES, block // CORES, width)
            received = other_core(pick(halves, 1 - core, 1))
            both = ordered(pick(halves, core, 1), received, 0).reshape(n_seq, sub, width)
            return lax.all_to_all(both, "seq", 0, 0, tiled=True).reshape(tokens, width)

        def from_rows(value):
            both = lax.all_to_all(value.reshape(n_seq, sub, width), "seq", 0, 0, tiled=True)
            both = both.reshape(CORES, row_count, block // CORES, width)
            received = other_core(pick(both, 1 - core, 0))
            own = pick(both, core, 0)
            return ordered(own[:, None], received[:, None], 1).reshape(row_count, block, width)

        places = jnp.arange(seq_len, dtype=jnp.int32)
        tags = jnp.where(places[None, :] < valid_counts[:, None], cell_ids, -1 - places[None, :])
        tags = ordered(tags, other_core(tags), 0)
        tags = pick(tags, seq_at // chips, 0).reshape(n_seq, CORES, chips, sub)
        tags = tags.transpose(2, 1, 0, 3).reshape(group, tokens)
        order = (member - jnp.arange(group, dtype=jnp.int32)) % group
        tags = jnp.take(tags, order, axis=0).reshape(1, seq_len)
        query_tags, key_tags = tags, tags.reshape(seq_len, 1)

        def pad_heads(value, axis):
            if not padded:
                return value
            fill = [(0, 0)] * value.ndim
            fill[axis] = (0, padded)
            return jnp.pad(value, fill)

        def qkv_of(hop):
            if group == CORES:
                return gather_pairs(((core + hop) % CORES).reshape(1), qkv_weight)
            piece = pick(qkv_weight.reshape(width, 3, group, group_width), (member + hop) % group, 2)
            piece = pad_heads(piece, 2).reshape(width, 3, pairs, lanes)
            return piece.transpose(0, 2, 1, 3).reshape(width, 3 * pairs * lanes)

        def out_of(hop):
            at = (member + hop) % group * group_width
            return pad_heads(lax.dynamic_slice_in_dim(out_weight, at, group_width, 0), 0)

        if chips == 1 and highs == 2:
            half = width // CORES
            x_row, n1, qkv, own_weight, other_weight = begin(inputs, qkv_weight, attention_gain)
            start = x_row.reshape(tokens, width)
            mixed, lse, cot, mixed_own, middle = attend_row(qkv, key_tags, query_tags, cotangent, start, out_weight)
            outputs, d_middle, _, d_mixed, out_kept, out_received, down_part, up_part = feed(
                middle, cot.reshape(tokens, width), feed_gain, up_weight, down_weight, mixed_own, out_weight, n_seq
            )
            input_grad, out_low, qkv_out, down_all, up_all = back(
                qkv, mixed, d_mixed.reshape(seq_len, half), lse, key_tags, query_tags, n1, (own_weight, other_weight), attention_gain,
                out_kept, out_received, down_part, up_part, start, d_middle, outputs, row_count,
            )
            qkv_total, out_total, down_total, up_total, first, second = collect(
                seq_at, qkv_out, down_all, up_all, qkv_weight, up_weight
            )
            shard = width // n_seq

            def gain_grad(sums, gain):
                return sums.reshape(shard) / lax.dynamic_slice_in_dim(gain, seq_at * shard, shard, 0)

            return (
                out_low.reshape(inputs.shape),
                input_grad.reshape(inputs.shape),
                gain_grad(first, attention_gain),
                qkv_total,
                out_total,
                gain_grad(second, feed_gain),
                up_total,
                down_total,
            )

        start = to_rows(inputs)
        qkv_parts = [qkv_of(hop) for hop in range(group)]
        out_parts = [out_of(hop) for hop in range(group)]
        start = start.astype(f32)
        unit1, scale1 = norm_parts(start)
        n1 = (unit1 * attention_gain).astype(bf16)
        n1_all = jnp.concatenate([n1] + [to_member(n1, hop) for hop in range(1, group)], 0)
        cotangent, _ = tie(cotangent, start[:1])
        cot = to_rows(cotangent)
        qkv = dot(n1_all, qkv_parts[0], 1, 0).astype(bf16)
        mixed, lse = attend(qkv, key_tags, query_tags)
        mixed_parts = [mixed[:tokens]] + [
            to_member(mixed[hop * tokens : (hop + 1) * tokens], group - hop) for hop in range(1, group)
        ]
        middle = start
        for part, weight in zip(mixed_parts, out_parts):
            middle = middle + dot(part, weight, 1, 0)
        if group == CORES:
            mixed_own = ordered(mixed_parts[0], mixed_parts[1], 1)
        else:
            slots = jnp.stack([part[:, :group_width] for part in mixed_parts])
            turn = (jnp.arange(group, dtype=jnp.int32) - member) % group
            mixed_own = jnp.take(slots, turn, axis=0).transpose(1, 0, 2).reshape(tokens, width)
        outputs, d_middle, d_attn, _, _, _, down_part, up_part = feed(
            middle, cot, feed_gain, up_weight, down_weight, mixed_own, out_weight, n_seq
        )
        d_attn = d_attn[0]

        d_attn_all = jnp.concatenate([d_attn] + [to_member(d_attn, hop) for hop in range(1, group)], 0)


        half = width // CORES
        out_grad = dot(mixed_own, d_attn, 0, 0).astype(bf16)
        out_kept = lax.dynamic_slice_in_dim(out_grad, core * half, half, 1)
        out_received = other_core(lax.dynamic_slice_in_dim(out_grad, (1 - core) * half, half, 1))
        d_mixed = dot(d_attn_all, out_parts[0], 1, 1).astype(bf16)

        out_low = from_rows(outputs)
        input_grad, qkv_total, out_total, down_total, up_total = back_by_steps(
            qkv, mixed, d_mixed, lse, key_tags, query_tags, n1_all, qkv_parts, attention_gain,
            out_kept, out_received, down_part, up_part, start, d_middle, to_member, ordered, from_rows,
            (group, member, core, pairs, group_width, tokens, width),
        )

        shard = width // n_seq

        def gain_total(weight, total, gain):
            rows = lax.dynamic_slice_in_dim(weight, seq_at * shard, shard, 0).astype(f32)
            return jnp.sum(rows * total, axis=1) / lax.dynamic_slice_in_dim(gain, seq_at * shard, shard, 0)

        return (
            out_low,
            input_grad,
            gain_total(qkv_weight, qkv_total, attention_gain),
            qkv_total,
            out_total,
            gain_total(up_weight, up_total, feed_gain),
            up_total,
            down_total,
        )

    return per_device


def solution(mesh):
    placed = (
        P("rows", "seq", None),
        P("rows", None),
        P("rows"),
        P("rows", "seq", None),
        P(),
        P(),
        P(),
        P(),
        P(),
        P(),
    )
    return jax.shard_map(
        build(mesh.shape["seq"], mesh.shape["rows"]),
        mesh=mesh,
        in_specs=placed,
        out_specs=(
            P("rows", "seq", None),
            P("rows", "seq", None),
            P("seq"),
            P("seq", None),
            P("seq", None),
            P("seq"),
            P("seq", None),
            P("seq", None),
        ),
        check_vma=False,
    )
```

```python
import functools

import jax
import jax.numpy as jnp
from jax import lax
from jax.experimental import pallas as pl
from jax.experimental.pallas import tpu as pltpu
from jax.sharding import PartitionSpec as P

HDIM = 64
CORES = 2
epsilon = 1e-05
masked_score = -1e30
score_scale = HDIM ** (-0.5)
log2e = 1.4426950408889634
bf16 = jnp.bfloat16
f32 = jnp.float32
AXES = ("seq", "rows")
vmem_bytes = 60 * 2**20
feed_vmem_bytes = 63 * 2**20
feed_tile = 512
max_cells = 7
MESH = pl.DeviceIdType.MESH


def dot(a, b, ca, cb):
    return lax.dot_general(a, b, (((ca,), (cb,)), ((), ())), preferred_element_type=f32)


def attend_kernel(tile, key_tags, query_tags, q_ref, k_ref, v_ref, o_ref, lse_ref, v_turned):
    tokens = q_ref.shape[0]
    v_turned[...] = v_ref[...].T
    lane = lax.broadcasted_iota(jnp.int32, (tile, 2 * HDIM), 1)

    def body(step, _):
        part = pl.ds(pl.multiple_of(step * tile, tile), tile)
        q = q_ref[part, :]
        allowed = key_tags[...] == query_tags[:, part]
        pieces = []
        for head in range(2):
            own = jnp.where((lane // HDIM) == head, q, bf16(0))
            scores = dot(k_ref[...], own, 1, 1)
            scores = jnp.where(allowed, scores, masked_score)
            peak = jnp.max(scores, axis=0, keepdims=True)
            powers = jnp.exp2((scores - peak) * (score_scale * log2e))
            total = jnp.sum(powers, axis=0, keepdims=True)
            mixed = dot(v_turned[head * HDIM : (head + 1) * HDIM, :], powers.astype(bf16), 1, 0)
            pieces.append(mixed * (1.0 / total))
            lse_ref[head : head + 1, part] = peak * (score_scale * log2e) + jnp.log2(total)
        o_ref[part, :] = jnp.concatenate(pieces, axis=0).T.astype(bf16)
        return 0

    lax.fori_loop(0, tokens // tile, body, 0)


def attend(qkv, key_tags, query_tags):
    tokens, width = qkv.shape
    lanes = 2 * HDIM
    pairs = width // (3 * lanes)
    tile = min(512, tokens)

    def columns(place):
        return pl.BlockSpec((tokens, lanes), lambda i: (0, 3 * i + place))

    return pl.pallas_call(
        functools.partial(attend_kernel, tile),
        grid=(pairs,),
        in_specs=[
            pl.BlockSpec((tokens, 1), lambda i: (0, 0)),
            pl.BlockSpec((1, tokens), lambda i: (0, 0)),
            columns(0),
            columns(1),
            columns(2),
        ],
        out_specs=[
            pl.BlockSpec((tokens, lanes), lambda i: (0, i)),
            pl.BlockSpec((None, 2, tokens), lambda i: (i, 0, 0)),
        ],
        out_shape=[
            jax.ShapeDtypeStruct((tokens, pairs * lanes), bf16),
            jax.ShapeDtypeStruct((pairs, 2, tokens), f32),
        ],
        scratch_shapes=[pltpu.VMEM((lanes, tokens), bf16)],
        compiler_params=pltpu.CompilerParams(vmem_limit_bytes=vmem_bytes),
        cost_estimate=pl.CostEstimate(
            flops=32 * pairs * tokens * tokens * HDIM,
            bytes_accessed=8 * tokens * pairs * lanes,
            transcendentals=2 * pairs * tokens * tokens,
        ),
        name="attend",
    )(key_tags, query_tags, qkv, qkv, qkv)


def attend_back_kernel(
    tile, key_tags, query_tags, q_ref, k_ref, v_ref, o_ref, do_ref, lse_ref, grad_ref, k_turned, dq_turned, delta
):
    tokens = q_ref.shape[0]
    lanes = 2 * HDIM
    k_turned[...] = k_ref[...].T
    dq_turned[...] = (o_ref[...].astype(f32) * do_ref[...].astype(f32)).T
    for head in range(2):
        rows = dq_turned[head * HDIM : (head + 1) * HDIM, :]
        delta[head : head + 1, :] = jnp.sum(rows, axis=0, keepdims=True)
    dq_turned[...] = jnp.zeros_like(dq_turned)
    first = lax.broadcasted_iota(jnp.int32, (tile, lanes), 1) < HDIM

    def body(step, _):
        part = pl.ds(pl.multiple_of(step * tile, tile), tile)
        k, v = k_ref[part, :], v_ref[part, :]
        q, do = q_ref[...], do_ref[...]
        allowed = key_tags[part, :] == query_tags[...]
        dk, dv = [], []
        for head in range(2):
            own = first if head == 0 else jnp.logical_not(first)
            own_rows = slice(head * HDIM, (head + 1) * HDIM)
            scores = dot(jnp.where(own, k, bf16(0)), q, 1, 1)
            scores = jnp.where(allowed, scores, masked_score)
            chances = jnp.exp2(scores * (score_scale * log2e) - lse_ref[head : head + 1, :])
            weight_grad = dot(jnp.where(own, v, bf16(0)), do, 1, 1)
            score_grad = (chances * (weight_grad - delta[head : head + 1, :])).astype(bf16)
            dv.append(dot(chances.astype(bf16), do, 1, 0))
            dk.append(dot(score_grad, q, 1, 0))
            dq_turned[own_rows, :] += dot(k_turned[own_rows, part], score_grad, 1, 0)
        grad_ref[part, lanes : 2 * lanes] = (jnp.where(first, dk[0], dk[1]) * score_scale).astype(bf16)
        grad_ref[part, 2 * lanes :] = jnp.where(first, dv[0], dv[1]).astype(bf16)
        return 0

    lax.fori_loop(0, tokens // tile, body, 0)
    grad_ref[:, :lanes] = (dq_turned[...] * score_scale).T.astype(bf16)


def attend_back(qkv, mixed, d_mixed, lse, key_tags, query_tags, start, count):
    tokens = qkv.shape[0]
    tile = min(512, tokens)
    lanes = 2 * HDIM

    def columns(place):
        return pl.BlockSpec((tokens, lanes), lambda i: (0, 3 * (start + i) + place))

    pair = pl.BlockSpec((tokens, lanes), lambda i: (0, start + i))
    return pl.pallas_call(
        functools.partial(attend_back_kernel, tile),
        grid=(count,),
        in_specs=[
            pl.BlockSpec((tokens, 1), lambda i: (0, 0)),
            pl.BlockSpec((1, tokens), lambda i: (0, 0)),
            columns(0),
            columns(1),
            columns(2),
            pair,
            pair,
            pl.BlockSpec((None, 2, tokens), lambda i: (start + i, 0, 0)),
        ],
        out_specs=pl.BlockSpec((tokens, 3 * lanes), lambda i: (0, i)),
        out_shape=jax.ShapeDtypeStruct((tokens, 3 * count * lanes), bf16),
        scratch_shapes=[
            pltpu.VMEM((lanes, tokens), bf16),
            pltpu.VMEM((lanes, tokens), f32),
            pltpu.VMEM((2, tokens), f32),
        ],
        compiler_params=pltpu.CompilerParams(vmem_limit_bytes=vmem_bytes),
        cost_estimate=pl.CostEstimate(
            flops=80 * count * tokens * tokens * HDIM,
            bytes_accessed=16 * tokens * count * lanes,
            transcendentals=2 * count * tokens * tokens,
        ),
        name="attend_back",
    )(key_tags, query_tags, qkv, qkv, qkv, mixed, d_mixed, lse)


def copy_kernel(core_ref, from_ref, to_ref):
    to_ref[...] = from_ref[...]


def gather_pairs(core, qkv_weight):
    width, lanes = qkv_weight.shape[0], 2 * HDIM
    pairs = width // (CORES * lanes)
    return pl.pallas_call(
        copy_kernel,
        grid_spec=pltpu.PrefetchScalarGridSpec(
            num_scalar_prefetch=1,
            grid=(pairs, 3),
            in_specs=[
                pl.BlockSpec((width, lanes), lambda i, j, core: (0, (j * CORES + core[0]) * pairs + i))
            ],
            out_specs=pl.BlockSpec((width, lanes), lambda i, j, core: (0, 3 * i + j)),
        ),
        out_shape=jax.ShapeDtypeStruct((width, 3 * pairs * lanes), qkv_weight.dtype),
        cost_estimate=pl.CostEstimate(flops=0, bytes_accessed=12 * width * pairs * lanes, transcendentals=0),
        name="gather_pairs",
    )(core, qkv_weight)


def norm_parts(values):
    center = values - jnp.mean(values, axis=-1, keepdims=True)
    spread = jnp.mean(center * center, axis=-1, keepdims=True)
    scale = lax.rsqrt(spread + epsilon)
    return center * scale, scale


def norm_back(grad, gain, unit, scale):
    e = grad * gain
    return scale * (
        e - jnp.mean(e, axis=-1, keepdims=True) - unit * jnp.mean(e * unit, axis=-1, keepdims=True)
    )


def all_signal(n_seq, seq_at, rows_at, extra=()):
    core = rows_at % CORES
    barrier = pltpu.get_barrier_semaphore()
    for s in range(n_seq):
        for c in range(CORES):
            @pl.when(jnp.logical_not((seq_at == s) & (core == c)))
            def _():
                pl.semaphore_signal(barrier, inc=1, device_id=(s, rows_at - core + c), device_id_type=MESH)
    for peer in extra:
        pl.semaphore_signal(barrier, inc=1, device_id=peer, device_id_type=MESH)
    pl.semaphore_wait(barrier, n_seq * CORES - 1 + len(extra))


class ToRows:
    def __init__(self, source, target, send, recv, local, row_count, seq_at, rows_at):
        self.source, self.target, self.send, self.recv, self.local = source, target, send, recv, local
        self.row_count, self.seq_at, self.rows_at = row_count, seq_at, rows_at
        self.core = rows_at % CORES

    def copy(self, row, c):
        chip = self.core * self.row_count + row
        return pltpu.make_async_remote_copy(
            src_ref=self.source.at[row, c],
            dst_ref=self.target.at[self.seq_at],
            send_sem=self.send.at[row, c],
            recv_sem=self.recv.at[self.seq_at],
            device_id=(chip, self.rows_at - self.core + c),
            device_id_type=MESH,
        )

    def own(self, row, c):
        return pltpu.make_async_copy(self.source.at[row, c], self.target.at[self.seq_at], self.local)

    def each(self, own, other):
        for row_turn in range(self.row_count):
            for core_turn in range(CORES):
                row = (row_turn + self.seq_at) % self.row_count
                c = (core_turn + self.seq_at // self.row_count) % CORES
                here = (self.core * self.row_count + row == self.seq_at) & (self.core == c)

                @pl.when(here)
                def _():
                    own(row, c)

                @pl.when(jnp.logical_not(here))
                def _():
                    other(row, c)

    def start(self):
        self.each(lambda row, c: self.own(row, c).start(), lambda row, c: self.copy(row, c).start())

    def wait_block(self, s):
        here = (s == self.seq_at) & (self.seq_at // self.row_count == self.core)

        @pl.when(here)
        def _():
            self.own(0, 0).wait()

        @pl.when(jnp.logical_not(here))
        def _():
            pltpu.make_async_remote_copy(
                src_ref=self.source.at[0, 0],
                dst_ref=self.target.at[s],
                send_sem=self.send.at[0, 0],
                recv_sem=self.recv.at[s],
                device_id=(self.seq_at, self.rows_at + 1 - 2 * self.core),
                device_id_type=MESH,
            ).wait_recv()

    def wait_sends(self):
        self.each(lambda row, c: None, lambda row, c: self.copy(row, c).wait_send())


def begin_kernel(
    row_count, pairs, x_ref, weight_ref, gain_ref, x_out, n1_out, qkv_out, own_out, other_out,
    x_part, n1, qkv, weight, other_weight,
    x_send, x_recv, x_local, n1_send, n1_recv, weight_sems, out_sems, x_sems, qkv_sems, n1_sems,
):
    seq_at, rows_at = lax.axis_index("seq"), lax.axis_index("rows")
    core = rows_at % CORES
    n_seq, sub, width = x_part.shape
    lanes = 2 * HDIM
    tokens = n_seq * sub
    moves = ToRows(x_ref, x_part, x_send, x_recv, x_local, row_count, seq_at, rows_at)

    def weight_copies(item, which):
        pair, kind = item // 3, item % 3
        to = pl.ds(pl.multiple_of(item * lanes, lanes), lanes)

        def columns(c):
            return pl.ds(pl.multiple_of((kind * CORES + c) * pairs * lanes + pair * lanes, lanes), lanes)

        source = weight_ref.at[:, columns(1 - core if which else core)]
        return pltpu.make_async_copy(source, (weight, other_weight)[which].at[:, to], weight_sems.at[which, item])

    def each_weight(act, which):
        def body(item, _):
            act(weight_copies(item, which))
            return 0

        lax.fori_loop(0, 3 * pairs, body, 0)

    each_weight(lambda copy: copy.start(), 0)
    all_signal(n_seq, seq_at, rows_at)
    moves.start()
    each_weight(lambda copy: copy.start(), 1)
    each_weight(lambda copy: copy.wait(), 0)
    weights_out = (
        pltpu.make_async_copy(weight, own_out, out_sems.at[0]),
        pltpu.make_async_copy(other_weight, other_out, out_sems.at[1]),
    )
    weights_out[0].start()
    each_weight(lambda copy: copy.wait(), 1)
    weights_out[1].start()

    def block_of(place):
        near = (place % 2) * ((place + 1) // 2) + (1 - place % 2) * ((n_seq - place // 2) % n_seq)
        return (seq_at + near) % n_seq

    def rows_of(s, other):
        return pl.ds(pl.multiple_of(s * sub + other * tokens, sub), sub)

    def n1_copy(s):
        return pltpu.make_async_remote_copy(
            src_ref=n1.at[rows_of(s, 0)],
            dst_ref=n1.at[rows_of(s, 1)],
            send_sem=n1_send.at[s],
            recv_sem=n1_recv.at[s],
            device_id=(seq_at, rows_at + 1 - 2 * core),
            device_id_type=MESH,
        )

    def x_copy(s):
        return pltpu.make_async_copy(x_part.at[s], x_out.at[s], x_sems.at[s])

    def out_copies(s, other):
        rows = rows_of(s, other)
        return (
            pltpu.make_async_copy(qkv.at[rows], qkv_out.at[rows], qkv_sems.at[other, s]),
            pltpu.make_async_copy(n1.at[rows], n1_out.at[rows], n1_sems.at[other, s]),
        )

    def product(first, second, other):
        both = jnp.concatenate([n1[rows_of(first, other), :], n1[rows_of(second, other), :]], 0)
        found = dot(both, weight[...], 1, 0).astype(bf16)
        for at, s in enumerate((first, second)):
            qkv[rows_of(s, other), :] = found[at * sub : (at + 1) * sub]
            for copy in out_copies(s, other):
                copy.start()

    def body(group, _):
        @pl.when(group < n_seq // 2)
        def _():
            places = block_of(2 * group), block_of(2 * group + 1)
            for s in places:
                moves.wait_block(s)
                x_copy(s).start()
                unit, _s = norm_parts(x_part[s].astype(f32))
                n1[rows_of(s, 0), :] = (unit * gain_ref[...]).astype(bf16)
                n1_copy(s).start()
            product(*places, 0)

        @pl.when(group > 0)
        def _():
            places = block_of(2 * group - 2), block_of(2 * group - 1)
            for s in places:
                n1_copy(s).wait()
            product(*places, 1)

        return 0

    lax.fori_loop(0, n_seq // 2 + 1, body, 0)

    def finish(s, _):
        x_copy(s).wait()
        for other in range(2):
            for copy in out_copies(s, other):
                copy.wait()
        return 0

    lax.fori_loop(0, n_seq, finish, 0)
    moves.wait_sends()
    for copy in weights_out:
        copy.wait()


def begin(inputs, qkv_weight, gain):
    row_count, block, width = inputs.shape
    n_seq = CORES * row_count
    lanes = 2 * HDIM
    pairs = width // (CORES * lanes)
    sub = block // CORES
    tokens = n_seq * sub
    hbm = pl.BlockSpec(memory_space=pl.ANY)
    return pl.pallas_call(
        functools.partial(begin_kernel, row_count, pairs),
        in_specs=[hbm, hbm, pl.BlockSpec(memory_space=pltpu.VMEM)],
        out_specs=[hbm] * 5,
        out_shape=[
            jax.ShapeDtypeStruct((n_seq, sub, width), bf16),
            jax.ShapeDtypeStruct((CORES * tokens, width), bf16),
            jax.ShapeDtypeStruct((CORES * tokens, 3 * pairs * lanes), bf16),
            jax.ShapeDtypeStruct((width, 3 * pairs * lanes), bf16),
            jax.ShapeDtypeStruct((width, 3 * pairs * lanes), bf16),
        ],
        scratch_shapes=[
            pltpu.VMEM((n_seq, sub, width), bf16),
            pltpu.VMEM((CORES * tokens, width), bf16),
            pltpu.VMEM((CORES * tokens, 3 * pairs * lanes), bf16),
            pltpu.VMEM((width, 3 * pairs * lanes), bf16),
            pltpu.VMEM((width, 3 * pairs * lanes), bf16),
            pltpu.SemaphoreType.DMA((row_count, CORES)),
            pltpu.SemaphoreType.DMA((n_seq,)),
            pltpu.SemaphoreType.DMA,
            pltpu.SemaphoreType.DMA((n_seq,)),
            pltpu.SemaphoreType.DMA((n_seq,)),
            pltpu.SemaphoreType.DMA((2, 3 * pairs)),
            pltpu.SemaphoreType.DMA((2,)),
            pltpu.SemaphoreType.DMA((n_seq,)),
            pltpu.SemaphoreType.DMA((CORES, n_seq)),
            pltpu.SemaphoreType.DMA((CORES, n_seq)),
        ],
        compiler_params=pltpu.CompilerParams(
            vmem_limit_bytes=vmem_bytes, collective_id=3, has_side_effects=True
        ),
        name="begin",
    )(inputs.reshape(row_count, CORES, sub, width), qkv_weight, gain)


def with_cells(value, tags, head, is_key):
    lane = lax.broadcasted_iota(jnp.int32, value.shape, 1)
    cell = lane - (1 - head) * HDIM
    if is_key:
        marks = jnp.where((cell == tags) | (cell >= max_cells), 0.0, -1.0)
    else:
        marks = jnp.where(cell == tags, -masked_score, 0.0)
    return jnp.where((lane // HDIM) == head, value, marks.astype(bf16))


def attend_row_kernel(
    tile, row_count, tags, row_tags, q_ref, k_ref, v_ref, cot_ref, x_ref, weight_ref, o_ref, lse_ref, cot_out, own_out,
    middle_out, v_turned, keys, scores_ref, mixed_ref, parts, x_part, weight, own, middle,
    cot_send, cot_recv, cot_local, part_send, part_recv, part_local, in_sems, out_sems,
):
    item, last = pl.program_id(0), pl.num_programs(0) - 1
    seq_at, rows_at = lax.axis_index("seq"), lax.axis_index("rows")
    core = rows_at % CORES
    tokens, lanes = q_ref.shape
    own_tokens = tokens // CORES
    n_seq, sub, _w = cot_out.shape
    moves = ToRows(cot_ref, cot_out, cot_send, cot_recv, cot_local, row_count, seq_at, rows_at)

    def part_copies(at):
        slot = at % 2
        half = pl.num_programs(0) * lanes
        columns = pl.ds(pl.multiple_of(core * half + at * lanes, lanes), lanes)
        return (
            pltpu.make_async_remote_copy(
                src_ref=parts.at[slot, pl.ds(own_tokens, own_tokens)],
                dst_ref=own_out.at[:, columns],
                send_sem=part_send.at[slot],
                recv_sem=part_recv.at[at],
                device_id=(seq_at, rows_at + 1 - 2 * core),
                device_id_type=MESH,
            ),
            pltpu.make_async_copy(parts.at[slot, pl.ds(0, own_tokens)], own_out.at[:, columns], part_local.at[slot]),
        )

    def part_came(at):
        half = pl.num_programs(0) * lanes
        columns = pl.ds(pl.multiple_of((1 - core) * half + at * lanes, lanes), lanes)
        return pltpu.make_async_remote_copy(
            src_ref=parts.at[0, pl.ds(own_tokens, own_tokens)],
            dst_ref=own_out.at[:, columns],
            send_sem=part_send.at[0],
            recv_sem=part_recv.at[at],
            device_id=(seq_at, rows_at + 1 - 2 * core),
            device_id_type=MESH,
        )

    def in_copies():
        return [
            pltpu.make_async_copy(x_ref, x_part, in_sems.at[0]),
            pltpu.make_async_copy(weight_ref, weight, in_sems.at[1]),
        ]

    def own_copy():
        return pltpu.make_async_copy(own_out, own, in_sems.at[2])

    def middle_copy(at):
        rows = pl.ds(at * sub, sub)
        return pltpu.make_async_copy(middle.at[rows], middle_out.at[rows], out_sems.at[at])

    @pl.when(item == 0)
    def _():
        all_signal(n_seq, seq_at, rows_at)
        moves.start()
        for copy in in_copies():
            copy.start()

    for head in range(2):
        keys[head] = with_cells(k_ref[...], tags[...], head, True)
        v_turned[head, :HDIM, :] = v_ref[...].T[head * HDIM : (head + 1) * HDIM, :]
        v_turned[head, HDIM:, :] = jnp.ones((16, tokens), bf16)

    def begin_scores(step, head):
        part = pl.ds(pl.multiple_of(step * tile, tile), tile)
        scores_ref[head] = dot(keys[head], with_cells(q_ref[part, :], tags[part, :], head, False), 1, 1)

    def finish(step, head):
        part = pl.ds(pl.multiple_of(step * tile, tile), tile)
        scores = scores_ref[head]
        peak = jnp.max(scores, axis=0, keepdims=True)
        powers = jnp.exp2((scores - peak) * (score_scale * log2e))
        mixed = dot(v_turned[head], powers.astype(bf16), 1, 0)
        total = mixed[HDIM : HDIM + 1, :]
        mixed_ref[head * HDIM : (head + 1) * HDIM, part] = mixed[:HDIM, :] * (1.0 / total)
        lse = peak * (score_scale * log2e) + jnp.log2(total)
        lse_ref[head : head + 1, part] = jnp.where(row_tags[:, part] < 0, -masked_score, lse)

    steps = tokens // tile
    begin_scores(0, 0)

    def body(step, _):
        begin_scores(step, 1)
        finish(step, 0)
        begin_scores(jnp.minimum(step + 1, steps - 1), 0)
        finish(step, 1)
        return 0

    lax.fori_loop(0, steps, body, 0)
    found = jnp.where(tags[...] < 0, v_ref[...], mixed_ref[...].T.astype(bf16))
    o_ref[...] = found

    @pl.when(item >= 2)
    def _():
        remote, local = part_copies(item - 2)
        remote.wait_send()
        local.wait()

    parts[item % 2] = found
    for copy in part_copies(item):
        copy.start()

    @pl.when(item == last)
    def _():
        for at in range(2):
            remote, local = part_copies(last - at)
            remote.wait_send()
            local.wait()
        for at in range(part_recv.shape[0]):
            part_came(at).wait_recv()
        own_copy().start()
        for copy in in_copies() + [own_copy()]:
            copy.wait()
        for at in range(n_seq // 2):
            rows = slice(2 * at * sub, 2 * (at + 1) * sub)
            middle[rows, :] = x_part[rows, :].astype(f32) + dot(own[rows, :], weight[...], 1, 0)
            middle_copy(2 * at).start()
            middle_copy(2 * at + 1).start()
        for s in range(n_seq):
            moves.wait_block(s)
        moves.wait_sends()
        for at in range(n_seq):
            middle_copy(at).wait()


def attend_row(qkv, tags, row_tags, cotangent, start, out_weight):
    tokens, width = qkv.shape
    row_count, block, model = cotangent.shape
    lanes = 2 * HDIM
    pairs = width // (3 * lanes)
    tile = 512
    n_seq, sub = CORES * row_count, block // CORES
    hbm = pl.BlockSpec(memory_space=pl.ANY)

    def columns(place):
        return pl.BlockSpec((tokens, lanes), lambda i: (0, 3 * i + place))

    return pl.pallas_call(
        functools.partial(attend_row_kernel, tile, row_count),
        grid=(pairs,),
        in_specs=[
            pl.BlockSpec((tokens, 1), lambda i: (0, 0)),
            pl.BlockSpec((1, tokens), lambda i: (0, 0)),
            columns(0),
            columns(1),
            columns(2),
            hbm,
            hbm,
            hbm,
        ],
        out_specs=[
            pl.BlockSpec((tokens, lanes), lambda i: (0, i)),
            pl.BlockSpec((None, 2, tokens), lambda i: (i, 0, 0)),
            hbm,
            hbm,
            hbm,
        ],
        out_shape=[
            jax.ShapeDtypeStruct((tokens, pairs * lanes), bf16),
            jax.ShapeDtypeStruct((pairs, 2, tokens), f32),
            jax.ShapeDtypeStruct((n_seq, sub, model), bf16),
            jax.ShapeDtypeStruct((tokens // CORES, model), bf16),
            jax.ShapeDtypeStruct((tokens // CORES, model), f32),
        ],
        scratch_shapes=[
            pltpu.VMEM((2, HDIM + 16, tokens), bf16),
            pltpu.VMEM((2, tokens, lanes), bf16),
            pltpu.VMEM((2, tokens, tile), f32),
            pltpu.VMEM((lanes, tokens), f32),
            pltpu.VMEM((2, tokens, lanes), bf16),
            pltpu.VMEM((tokens // CORES, model), bf16),
            pltpu.VMEM((model, model), bf16),
            pltpu.VMEM((tokens // CORES, model), bf16),
            pltpu.VMEM((tokens // CORES, model), f32),
            pltpu.SemaphoreType.DMA((row_count, CORES)),
            pltpu.SemaphoreType.DMA((n_seq,)),
            pltpu.SemaphoreType.DMA,
            pltpu.SemaphoreType.DMA((2,)),
            pltpu.SemaphoreType.DMA((pairs,)),
            pltpu.SemaphoreType.DMA((2,)),
            pltpu.SemaphoreType.DMA((3,)),
            pltpu.SemaphoreType.DMA((n_seq,)),
        ],
        compiler_params=pltpu.CompilerParams(
            vmem_limit_bytes=vmem_bytes, collective_id=4, has_side_effects=True
        ),
        name="attend_row",
    )(tags, row_tags, qkv, qkv, qkv, cotangent.reshape(row_count, CORES, sub, model), start, out_weight)


piece_rows = 16


def feed_kernel(
    tiles,
    rows,
    middle_ref,
    cot_ref,
    gain_ref,
    up_ref,
    down_ref,
    mixed_ref,
    out_weight_ref,
    out_ref,
    d_middle_ref,
    d_attn_out,
    d_mixed_out,
    out_kept,
    out_came,
    down_part,
    up_part,
    n2,
    total,
    d_attn,
    out_weight,
    out_keep,
    out_send,
    acts,
    d_ups,
    up_before,
    down_before,
    down_halves,
    down_recv,
    up_halves,
    up_recv,
    down_far_keep,
    down_far_send,
    down_far_recv,
    up_far_keep,
    up_far_send,
    up_far_recv,
    up_last_keep,
    up_last_send,
    up_last_recv,
    core_send_sem,
    core_recv_sem,
    far_send_sem,
    far_recv_sem,
    core_free,
    far_free,
    d_attn_sems,
    last_send_sem,
    last_recv_sem,
    out_sems,
):
    ahead = pl.program_id(0)
    step = ahead - 1
    tokens, width = n2.shape
    half, tile = width // 2, up_ref.shape[1]
    seq_at, rows_at = lax.axis_index("seq"), lax.axis_index("rows")
    core, high, low, mid = rows_at % 2, (rows_at // 2) % 2, seq_at % 2, (seq_at // 2) % 2
    core_peer = (seq_at, rows_at + 1 - 2 * core)
    far_peers = ((seq_at, rows_at + 2 - 4 * high), (seq_at + 1 - 2 * low, rows_at))
    last_peer = (seq_at + 2 - 4 * mid, rows_at)

    def copies(slot, far):
        if far:
            refs = ((down_far_send, down_far_recv), (up_far_send, up_far_recv))
            sems, peers = (far_send_sem, far_recv_sem), far_peers
        else:
            refs = ((down_halves.at[:, 1 - core], down_recv), (up_halves.at[:, 1 - core], up_recv))
            sems, peers = (core_send_sem, core_recv_sem), (core_peer, core_peer)
        return [
            pltpu.make_async_remote_copy(
                src_ref=refs[kind][0].at[slot],
                dst_ref=refs[kind][1].at[slot],
                send_sem=sems[0].at[kind, slot],
                recv_sem=sems[1].at[kind, slot],
                device_id=peers[kind],
                device_id_type=MESH,
            )
            for kind in range(2)
        ]

    def signal(sem, peer):
        pl.semaphore_signal(sem, inc=1, device_id=peer, device_id_type=MESH)

    @pl.when(ahead == 0)
    def _():
        barrier = pltpu.get_barrier_semaphore()
        for peer in (core_peer,) + far_peers + (last_peer,):
            signal(barrier, peer)
        pl.semaphore_wait(barrier, 4)

        def body(i, _):
            part = pl.ds(pl.multiple_of(i * rows, rows), rows)
            unit, _s = norm_parts(middle_ref[part, :])
            n2[part, :] = (unit * gain_ref[...]).astype(bf16)
            return 0

        lax.fori_loop(0, tokens // rows, body, 0)
        total[...] = middle_ref[...]
        d_middle_ref[...] = jnp.zeros_like(d_middle_ref)

    def activate():
        up = dot(n2[...], up_ref[...], 1, 0)
        d_act = dot(cot_ref[...], down_ref[...], 1, 1)
        share = 0.5 + 0.5 * lax.erf(up * (0.5**0.5))
        density = jnp.exp(-0.5 * up * up) * 0.3989422804014327
        acts[ahead % 2] = (up * share).astype(bf16)
        d_ups[ahead % 2] = (d_act * (share + up * density)).astype(bf16)

    def use():
        slot = step % 2
        act, d_up = acts[slot], d_ups[slot]
        total[...] += dot(act, down_before[...], 1, 0)
        d_middle_ref[...] += dot(d_up, up_before[...], 1, 1)
        up_grad = dot(n2[...], d_up, 0, 0).astype(bf16)
        cut = up_grad.shape[1] // 2
        up_halves[slot, 0] = up_grad[:, :cut].reshape(up_halves.shape[2:])
        up_halves[slot, 1] = up_grad[:, cut:].reshape(up_halves.shape[2:])
        down_grad = dot(act, cot_ref[...], 0, 0).astype(bf16)
        down_halves[slot, 0] = down_grad[:, :half].reshape(down_halves.shape[2:])
        down_halves[slot, 1] = down_grad[:, half:].reshape(down_halves.shape[2:])

    @pl.when((step >= 2) & (step < tiles))
    def _():
        for copy in copies(step % 2, False):
            copy.wait_send()

    @pl.when(ahead == 0)
    def _():
        activate()

    @pl.when((ahead > 0) & (ahead < tiles))
    def _():
        activate()
        use()

    @pl.when(ahead == tiles)
    def _():
        use()

    @pl.when(ahead < tiles)
    def _():
        up_before[...] = up_ref[...]
        down_before[...] = down_ref[...]

    def add(a, b):
        return (a.astype(f32) + b.astype(f32)).astype(bf16)

    def last_copy(slot):
        return pltpu.make_async_remote_copy(
            src_ref=up_last_send.at[slot],
            dst_ref=up_last_recv.at[slot],
            send_sem=last_send_sem.at[slot],
            recv_sem=last_recv_sem.at[slot],
            device_id=last_peer,
            device_id_type=MESH,
        )

    def last_add():
        slot = (step + 1) % 2
        last_copy(slot).wait_recv()
        up_part[...] = add(up_last_keep[slot], up_last_recv[slot]).reshape(up_part.shape)

    def far_add():
        slot = step % 2
        for copy in copies(slot, True):
            copy.wait_recv()
        down_part[...] = add(down_far_keep[slot], down_far_recv[slot]).reshape(down_part.shape)

        @pl.when(step >= 4)
        def _():
            last_copy(slot).wait_send()

        up_last_send[slot] = add(up_far_keep[slot, :, 1 - mid], up_far_recv[slot, :, 1 - mid])
        up_last_keep[slot] = add(up_far_keep[slot, :, mid], up_far_recv[slot, :, mid])
        last_copy(slot).start()

        @pl.when(step < tiles)
        def _():
            signal(far_free.at[0], far_peers[0])
            signal(far_free.at[1], far_peers[1])

    def pass_on():
        slot = (step + 1) % 2
        for copy in copies(slot, False):
            copy.wait_recv()

        @pl.when(step >= 3)
        def _():
            for copy in copies(slot, True):
                copy.wait_send()
            pl.semaphore_wait(far_free.at[0], 1)
            pl.semaphore_wait(far_free.at[1], 1)

        down_far_send[slot] = add(down_halves[slot, core, :, 1 - high], down_recv[slot, :, 1 - high])
        down_far_keep[slot] = add(down_halves[slot, core, :, high], down_recv[slot, :, high])
        shape = up_far_send.shape[1:]
        up_far_send[slot] = add(up_halves[slot, core, :, 1 - low], up_recv[slot, :, 1 - low]).reshape(shape)
        up_far_keep[slot] = add(up_halves[slot, core, :, low], up_recv[slot, :, low]).reshape(shape)
        for copy in copies(slot, True):
            copy.start()

        @pl.when(step < tiles - 1)
        def _():
            signal(core_free, core_peer)

    @pl.when((step >= 3) & (step <= tiles + 1))
    def _():
        last_add()

    @pl.when((step >= 2) & (step <= tiles))
    def _():
        far_add()

    @pl.when((step >= 1) & (step <= tiles))
    def _():
        pass_on()

    @pl.when((step >= 0) & (step < tiles))
    def _():
        @pl.when(step >= 2)
        def _():
            pl.semaphore_wait(core_free, 1)

        for copy in copies(step % 2, False):
            copy.start()

    @pl.when(step == tiles)
    def _():
        def body(i, _):
            part = pl.ds(pl.multiple_of(i * rows, rows), rows)
            low_total = total[part, :].astype(bf16)
            for at in range(2):
                acts[at, part, :] = low_total[:, at * tile : (at + 1) * tile]
            d_ups[0, part, : width - 2 * tile] = low_total[:, 2 * tile :]
            unit, scale = norm_parts(middle_ref[part, :])
            grad = cot_ref[part, :].astype(f32) + norm_back(d_middle_ref[part, :], gain_ref[...], unit, scale)
            d_middle_ref[part, :] = grad
            d_attn[part, :] = grad.astype(bf16)
            return 0

        lax.fori_loop(0, tokens // rows, body, 0)

    def to_core(source, target, at):
        return pltpu.make_async_remote_copy(
            src_ref=source,
            dst_ref=target,
            send_sem=d_attn_sems.at[at],
            recv_sem=d_attn_sems.at[at + 1],
            device_id=core_peer,
            device_id_type=MESH,
        )

    d_attn_copy = lambda: to_core(d_attn, d_attn_out.at[1], 0)
    out_copy = lambda: to_core(out_send, out_came, 2)
    mixed_copy = lambda: pltpu.make_async_copy(mixed_ref, n2, out_sems.at[0])
    weight_copy = lambda: pltpu.make_async_copy(
        out_weight_ref.at[pl.ds(pl.multiple_of(core * half, half), half)], out_weight, out_sems.at[1]
    )
    d_attn_save = lambda: pltpu.make_async_copy(d_attn, d_attn_out.at[0], out_sems.at[2])
    out_save = lambda: pltpu.make_async_copy(out_keep, out_kept, out_sems.at[3])
    d_mixed_save = lambda: pltpu.make_async_copy(down_halves, d_mixed_out, out_sems.at[4])

    def in_slots():
        wide = [(acts.at[at], pl.ds(at * tile, tile)) for at in range(2)]
        wide.append((d_ups.at[0, :, pl.ds(0, width - 2 * tile)], pl.ds(2 * tile, width - 2 * tile)))
        return list(enumerate(wide))

    def total_saves():
        return [
            pltpu.make_async_copy(source, out_ref.at[:, columns], out_sems.at[5 + at])
            for at, (source, columns) in in_slots()
        ]

    def d_attn_loads():
        return [
            pltpu.make_async_copy(d_attn_out.at[1, :, columns], target, out_sems.at[8 + at])
            for at, (target, columns) in in_slots()
        ]

    @pl.when(step == tiles)
    def _():
        for copy in total_saves():
            copy.start()
        d_attn_copy().start()
        d_attn_save().start()
        mixed_copy().start()
        weight_copy().start()

    @pl.when(step == tiles + 1)
    def _():
        mixed_copy().wait()
        grad = dot(n2[...], d_attn[...], 0, 0).astype(bf16)

        @pl.when(core == 0)
        def _():
            out_keep[...] = grad[:, :half]
            out_send[...] = grad[:, half:]

        @pl.when(core != 0)
        def _():
            out_keep[...] = grad[:, half:]
            out_send[...] = grad[:, :half]

        out_copy().start()
        out_save().start()
        far_add()

    @pl.when(step == tiles + 2)
    def _():
        for copy in total_saves():
            copy.wait()
        d_attn_copy().wait()
        for copy in d_attn_loads():
            copy.start()
        weight_copy().wait()
        for slot in range(2):
            for copy in copies(slot, False):
                copy.wait_send()

        def keep_d_mixed(at, found):
            found = found.astype(bf16).reshape((-1,) + down_halves.shape[2:])
            down_halves[at, : found.shape[0]] = found

        keep_d_mixed(0, dot(d_attn[...], out_weight[...], 1, 1))
        for copy in d_attn_loads():
            copy.wait()
        other = jnp.concatenate([acts[0], acts[1], d_ups[0, :, : width - 2 * tile]], 1)
        keep_d_mixed(1, dot(other, out_weight[...], 1, 1))
        d_mixed_save().start()
        last_add()
        out_copy().wait()
        for copy in (d_attn_save(), out_save(), d_mixed_save()):
            copy.wait()
        for slot in range(2):
            last_copy(slot).wait_send()
            for copy in copies(slot, True):
                copy.wait_send()


def feed(middle, cot, gain, up_weight, down_weight, mixed_own, out_weight, n_seq):
    tokens, width = middle.shape
    wide = up_weight.shape[1]
    tile = feed_tile
    tiles = wide // tile
    half, shard = width // 2, width // n_seq
    whole = lambda dtype: jax.ShapeDtypeStruct((tokens, width), dtype)
    fixed = lambda shape: pl.BlockSpec(shape, lambda i: (0, 0), pipeline_mode=pl.Buffered(1))
    at = lambda i: jnp.minimum(i, tiles - 1)
    hbm = pl.BlockSpec(memory_space=pl.ANY)
    late = lambda i: jnp.clip(i - 3, 0, tiles - 1)
    down_shape = (2, tile // (2 * piece_rows), 2, piece_rows, half)
    up_shape = (2, n_seq // 2, 2, shard, tile // 2)
    near = [pltpu.VMEM((2, tokens, tile), bf16)] * 2
    near += [pltpu.VMEM((width, tile), bf16), pltpu.VMEM((tile, width), bf16)]
    for shape in (down_shape, up_shape):
        near += [pltpu.VMEM(shape[:1] + (CORES,) + shape[1:], bf16), pltpu.VMEM(shape, bf16)]
    up_far = (2, n_seq // 4, 2, shard, tile // 2)
    far = [pltpu.VMEM(down_shape[:2] + down_shape[3:], bf16)] * 3 + [pltpu.VMEM(up_far, bf16)] * 3
    far += [pltpu.VMEM(up_far[:2] + up_far[3:], bf16)] * 3
    return pl.pallas_call(
        functools.partial(feed_kernel, tiles, 128),
        grid=(tiles + 4,),
        in_specs=[
            fixed((tokens, width)),
            fixed((tokens, width)),
            pl.BlockSpec((width,), lambda i: (0,), pipeline_mode=pl.Buffered(1)),
            pl.BlockSpec((width, tile), lambda i: (0, at(i))),
            pl.BlockSpec((tile, width), lambda i: (at(i), 0)),
            hbm,
            hbm,
        ],
        out_specs=[
            hbm,
            fixed((tokens, width)),
            hbm,
            hbm,
            hbm,
            hbm,
            pl.BlockSpec((tile // 2, half), lambda i: (late(i), 0)),
            pl.BlockSpec((width // 4, tile // 2), lambda i: (0, jnp.clip(i - 4, 0, tiles - 1))),
        ],
        scratch_shapes=[
            pltpu.VMEM((tokens, width), bf16),
            pltpu.VMEM((tokens, width), f32),
            pltpu.VMEM((tokens, width), bf16),
            pltpu.VMEM((half, width), bf16),
            pltpu.VMEM((width, half), bf16),
            pltpu.VMEM((width, half), bf16),
        ]
        + near
        + far
        + [pltpu.SemaphoreType.DMA((2, 2))] * 4
        + [pltpu.SemaphoreType.REGULAR, pltpu.SemaphoreType.REGULAR((2,)), pltpu.SemaphoreType.DMA((4,))]
        + [pltpu.SemaphoreType.DMA((2,))] * 2
        + [pltpu.SemaphoreType.DMA((11,))],
        out_shape=[
            whole(bf16),
            whole(f32),
            jax.ShapeDtypeStruct((2, tokens, width), bf16),
            jax.ShapeDtypeStruct(down_shape[:1] + (CORES,) + down_shape[1:], bf16),
            jax.ShapeDtypeStruct((width, half), bf16),
            jax.ShapeDtypeStruct((width, half), bf16),
            jax.ShapeDtypeStruct((wide // 2, half), bf16),
            jax.ShapeDtypeStruct((width // 4, wide // 2), bf16),
        ],
        compiler_params=pltpu.CompilerParams(
            vmem_limit_bytes=feed_vmem_bytes, collective_id=1, has_side_effects=True
        ),
        cost_estimate=pl.CostEstimate(
            flops=12 * tokens * width * wide,
            bytes_accessed=16 * tokens * width + 6 * width * wide,
            transcendentals=2 * tokens * wide,
        ),
        name="feed",
    )(middle, cot, gain, up_weight, down_weight, mixed_own, out_weight)


class Stream:
    def __init__(self, levels, rows, columns, first, count, lag):
        self.levels, self.rows, self.columns, self.first, self.count = levels, rows, columns, first, count
        self.lag = lag

    def shape(self, level):
        outer = 2 ** (len(self.levels) - 1 - level)
        return (max(outer // 2, 1), min(outer, 2), self.rows, self.columns)

    def scratch(self):
        shapes = []
        for level in range(len(self.levels)):
            shape = self.shape(level)
            shapes += [pltpu.VMEM(shape, bf16), pltpu.VMEM(shape, bf16), pltpu.VMEM((2,) + shape, bf16)]
        return shapes


down_pieces = 4


def streams_of(width, wide, n_seq, pairs):
    lanes = 2 * HDIM
    rows = width // (2 * n_seq)
    return (
        Stream(("x", "y", "z1", "z2"), rows, 4 * lanes, 1, pairs, 2),
        Stream(("y", "z1", "z2"), wide // (2 * n_seq * down_pieces), width // CORES, 2, down_pieces, 2),
        Stream(("x", "z2"), rows, wide // CORES // down_pieces, 2, down_pieces, 1),
    )


def back_kernel(pairs, tile, streams, row_count, *refs):
    (
        key_tags, query_tags, q_ref, k_ref, v_ref, o_ref, do_ref, lse_ref, n1_ref, own_weight, other_weight,
        gain_ref, out_kept, out_came, down_ref, up_ref, start_ref, d_middle_ref, outputs_ref,
    ) = refs[:19]
    grad_out, outputs_out, *gathered = refs[19:24]
    rest = list(refs[24:])
    take = lambda count: [rest.pop(0) for _ in range(count)]
    k_turned, dq_turned, delta, d_pair, d_came, d_n1, staged, start_part, middle_part = take(9)
    levels = []
    for stream in streams:
        levels.append([take(3) for _ in stream.levels])
    joined = take(len(streams))
    (
        send_sems, recv_sems, join_send, join_recv, core_send, core_recv, local_sems,
        pair_send, pair_recv, home_send, home_recv, home_local, part_sems, result_send, result_recv, result_local,
    ) = rest

    step = pl.program_id(0)
    tokens, lanes = q_ref.shape
    own_tokens = tokens // CORES
    seq_at, rows_at = lax.axis_index("seq"), lax.axis_index("rows")
    core, high = rows_at % 2, (rows_at // 2) % 2
    places = {"x": high, "y": seq_at % 2, "z1": (seq_at // 2) % 2, "z2": seq_at // 4}
    peers = {
        "x": (seq_at, rows_at + 2 - 4 * high),
        "y": (seq_at + 1 - 2 * places["y"], rows_at),
        "z1": (seq_at + 2 - 4 * places["z1"], rows_at),
        "z2": (seq_at + 4 - 8 * places["z2"], rows_at),
        "core": (seq_at, rows_at + 1 - 2 * core),
    }
    n_seq = 2 * row_count
    sub = start_part.shape[1]

    def remote(source, target, send, recv, peer):
        return pltpu.make_async_remote_copy(
            src_ref=source, dst_ref=target, send_sem=send, recv_sem=recv, device_id=peer, device_id_type=MESH
        )

    def add(a, b):
        return (a.astype(f32) + b.astype(f32)).astype(bf16)

    def level_copy(at, level, item):
        send, _, came = levels[at][level]
        slot = item % 2
        return remote(
            send, came.at[slot], send_sems.at[at, level], recv_sems.at[at, level, slot], peers[streams[at].levels[level]]
        )

    def join_copy(at, item):
        part = joined[at].at[item, high]
        return remote(part, part, join_send.at[at], join_recv.at[at, item % 2], peers["x"])

    def core_copy(at, item):
        return remote(
            joined[at].at[item],
            gathered[at].at[item, core],
            core_send.at[at],
            core_recv.at[at, item % 2],
            peers["core"],
        )

    def local_copy(at, item):
        return pltpu.make_async_copy(joined[at].at[item], gathered[at].at[item, core], local_sems.at[at])

    def pair_copy(item):
        slot = item % 2
        return remote(
            d_pair.at[slot, pl.ds(own_tokens, own_tokens)],
            d_came.at[slot],
            pair_send.at[slot],
            pair_recv.at[slot],
            peers["core"],
        )

    home = seq_at // row_count

    def to_home(block, own, result):
        if result:
            source, target = outputs_ref.at[pl.ds(pl.multiple_of(block * sub, sub), sub)], outputs_out
            sems = result_send, result_recv, result_local
        else:
            source, target = staged.at[block], grad_out
            sems = home_send, home_recv, home_local
        row = seq_at % row_count
        if own:
            return pltpu.make_async_copy(source, target.at[row, core], sems[2])
        return remote(source, target.at[row, core], sems[0].at[block], sems[1].at[row, core], (block, rows_at - core + home))

    def start_home(block, result):
        @pl.when(is_own(block))
        def _():
            to_home(block, True, result).start()

        @pl.when(jnp.logical_not(is_own(block)))
        def _():
            to_home(block, False, result).start()

    def wait_home(result):
        for block in range(n_seq):
            @pl.when(is_own(block))
            def _():
                to_home(block, True, result).wait()

            @pl.when(jnp.logical_not(is_own(block)))
            def _():
                to_home(block, False, result).wait_send()
        source, target = (outputs_ref.at[pl.ds(0, sub)], outputs_out) if result else (staged.at[0], grad_out)
        sems = (result_send, result_recv) if result else (home_send, home_recv)
        for row in range(row_count):
            for c in range(CORES):
                @pl.when(jnp.logical_not((seq_at == core * row_count + row) & (core == c)))
                def _():
                    remote(source, target.at[row, c], sems[0].at[0], sems[1].at[row, c], peers["core"]).wait_recv()

    def is_own(block):
        return (seq_at == block) & (home == core)

    @pl.when(step == 0)
    def _():
        barrier = pltpu.get_barrier_semaphore()
        for s in range(n_seq):
            for c in range(CORES):
                @pl.when(jnp.logical_not((seq_at == s) & (core == c)))
                def _():
                    pl.semaphore_signal(barrier, inc=1, device_id=(s, rows_at - core + c), device_id_type=MESH)
        pl.semaphore_signal(barrier, inc=1, device_id=peers["x"], device_id_type=MESH)
        pl.semaphore_wait(barrier, n_seq * CORES)
        d_n1[...] = jnp.zeros_like(d_n1)

    @pl.when(step < n_seq // 2)
    def _():
        for turn in range(2):
            start_home((seq_at + 2 * step + turn) % n_seq, True)

    working, second = step < 2 * pairs, step % 2

    @pl.when(working & (second == 0))
    def _():
        k_turned[...] = k_ref[...].T
        dq_turned[...] = (o_ref[...].astype(f32) * do_ref[...].astype(f32)).T
        for head in range(2):
            own_rows = dq_turned[head * HDIM : (head + 1) * HDIM, :]
            delta[head : head + 1, :] = jnp.sum(own_rows, axis=0, keepdims=True)
        dq_turned[...] = jnp.zeros_like(dq_turned)

    @pl.when(working)
    def _():
        slot = step // 2 % 2
        half_steps = tokens // tile // 2
        first = lax.broadcasted_iota(jnp.int32, (tile, lanes), 1) < HDIM

        def body(i, _):
            part = pl.ds(pl.multiple_of((i + second * half_steps) * tile, tile), tile)
            k, v = k_ref[part, :], v_ref[part, :]
            q, do = q_ref[...], do_ref[...]
            tag = key_tags[part, :]
            allowed = tag == query_tags[...]
            dk, dv = [], []
            for head in range(2):
                own = first if head == 0 else jnp.logical_not(first)
                own_rows = slice(head * HDIM, (head + 1) * HDIM)
                scores = dot(jnp.where(own, k, bf16(0)), q, 1, 1)
                scores = jnp.where(allowed, scores, masked_score)
                chances = jnp.exp2(scores * (score_scale * log2e) - lse_ref[head : head + 1, :])
                weight_grad = dot(jnp.where(own, v, bf16(0)), do, 1, 1)
                score_grad = (chances * (weight_grad - delta[head : head + 1, :])).astype(bf16)
                dv.append(dot(chances.astype(bf16), do, 1, 0))
                dk.append(dot(score_grad, q, 1, 0))
                dq_turned[own_rows, :] += dot(k_turned[own_rows, part], score_grad, 1, 0)
            d_pair[slot, part, lanes : 2 * lanes] = (jnp.where(first, dk[0], dk[1]) * score_scale).astype(bf16)
            d_v = jnp.where(first, dv[0], dv[1]).astype(bf16)
            d_pair[slot, part, 2 * lanes :] = jnp.where(tag < 0, do_ref[part, :], d_v)
            return 0

        lax.fori_loop(0, half_steps, body, 0)

    @pl.when(working & (second == 1))
    def _():
        d_pair[step // 2 % 2, :, :lanes] = (dq_turned[...] * score_scale).T.astype(bf16)

    def add_pair():
        item = step // 2 - 1
        slot = item % 2
        pair_copy(item).wait()
        d_n1[...] += dot(d_pair[slot, :own_tokens, :], own_weight[...], 1, 1) + dot(
            d_came[slot], other_weight[...], 1, 1
        )

    @pl.when((step >= 2) & (step <= 2 * pairs) & (second == 0))
    def _():
        add_pair()

    @pl.when(working & (second == 1))
    def _():
        pair_copy(step // 2).start()

    def part_copies(turn):
        rows = pl.ds(pl.multiple_of((seq_at + turn) % n_seq * sub, sub), sub)
        slot = turn % 2
        return (
            pltpu.make_async_copy(start_ref.at[rows], start_part.at[slot], part_sems.at[0, slot]),
            pltpu.make_async_copy(d_middle_ref.at[rows], middle_part.at[slot], part_sems.at[1, slot]),
        )

    @pl.when(step == 2 * pairs)
    def _():
        for copy in part_copies(0):
            copy.start()

        def body(turn, _):
            block = (seq_at + turn) % n_seq

            @pl.when(turn + 1 < n_seq)
            def _():
                for copy in part_copies(turn + 1):
                    copy.start()

            for copy in part_copies(turn):
                copy.wait()
            unit, scale = norm_parts(start_part[turn % 2].astype(f32))
            rows = pl.ds(pl.multiple_of(block * sub, sub), sub)
            grad = norm_back(d_n1[rows, :], gain_ref[...], unit, scale)
            staged[block] = (middle_part[turn % 2] + grad).astype(bf16)
            start_home(block, False)
            return 0

        lax.fori_loop(0, n_seq, body, 0)

    for at, stream in enumerate(streams):
        depth = len(stream.levels)

        def item_at(lag, stream=stream):
            since = step - stream.first - lag
            return since // 2, (since >= 0) & (since % 2 == 0) & (since < 2 * stream.count)

        item, here = item_at(depth + 1 + stream.lag)

        @pl.when(here)
        def _(at=at, item=item):
            core_copy(at, item).wait()
            local_copy(at, item).wait()

        item, here = item_at(depth + stream.lag)

        @pl.when(here)
        def _(at=at, item=item):
            join_copy(at, item).wait()
            core_copy(at, item).start()
            local_copy(at, item).start()

        for level in reversed(range(depth)):
            item, here = item_at(level + stream.lag)

            @pl.when(here)
            def _(at=at, item=item, level=level, stream=stream, depth=depth):
                _, keep, came = levels[at][level]
                slot = item % 2
                level_copy(at, level, item).wait_recv()
                if level == depth - 1:
                    joined[at][item, high] = add(keep[0, 0], came[slot, 0, 0])
                    join_copy(at, item).start()
                    return

                @pl.when(item > 0)
                def _():
                    level_copy(at, level + 1, item - 1).wait_send()

                next_send, next_keep, _ = levels[at][level + 1]
                place = places[stream.levels[level + 1]]
                next_send[...] = add(keep[:, 1 - place], came[slot, :, 1 - place]).reshape(next_send.shape)
                next_keep[...] = add(keep[:, place], came[slot, :, place]).reshape(next_keep.shape)
                level_copy(at, level + 1, item).start()

    def begin_piece(fills):
        for at, fill in fills.items():
            stream = streams[at]
            item = (step - stream.first) // 2

            @pl.when((step % 2 == stream.first % 2) & (step >= stream.first) & (item < stream.count))
            def _(at=at, fill=fill, item=item):
                @pl.when(item > 0)
                def _():
                    level_copy(at, 0, item - 1).wait_send()

                fill(*levels[at][0][:2])
                level_copy(at, 0, item).start()

    def fill_pair(send, keep):
        grad = dot(n1_ref[...], d_pair[step // 2 % 2], 0, 0).astype(bf16)
        grad = grad.reshape(n_seq, 2, send.shape[2], 3 * lanes)
        shape = send.shape[:3] + (3 * lanes,)

        @pl.when(high == 0)
        def _():
            send[:, :, :, : 3 * lanes] = grad[:, 1].reshape(shape)
            keep[:, :, :, : 3 * lanes] = grad[:, 0].reshape(shape)

        @pl.when(high != 0)
        def _():
            send[:, :, :, : 3 * lanes] = grad[:, 0].reshape(shape)
            keep[:, :, :, : 3 * lanes] = grad[:, 1].reshape(shape)

        shape = send.shape[:3] + (lanes,)
        send[:, :, :, 3 * lanes :] = add(out_kept[:, 1 - high], out_came[:, 1 - high]).reshape(shape)
        keep[:, :, :, 3 * lanes :] = add(out_kept[:, high], out_came[:, high]).reshape(shape)

    def fill_from(ref, place):
        def fill(send, keep):
            send[...] = ref[:, 1 - place].reshape(send.shape)
            keep[...] = ref[:, place].reshape(keep.shape)

        return fill

    begin_piece({0: fill_pair, 1: fill_from(down_ref, places["y"]), 2: fill_from(up_ref, high)})

    @pl.when(step == pl.num_programs(0) - 1)
    def _():
        for at, stream in enumerate(streams):
            for level in range(len(stream.levels)):
                level_copy(at, level, stream.count - 1).wait_send()
        wait_home(False)
        wait_home(True)


def back(
    qkv, mixed, d_mixed, lse, key_tags, query_tags, n1, weights, gain, out_kept, out_came, down_part, up_part,
    start, d_middle, outputs, row_count,
):
    tokens = qkv.shape[0]
    width = n1.shape[1]
    own_tokens = tokens // CORES
    lanes = 2 * HDIM
    pairs = qkv.shape[1] // (3 * lanes)
    n_seq = 2 * row_count
    tile = 512
    sub = own_tokens // n_seq
    streams = streams_of(width, down_part.shape[0] * 2, n_seq, pairs)
    last = pairs - 1
    now = lambda i: jnp.minimum(i // 2, last)
    before = lambda i: jnp.clip(i // 2 - 1, 0, last)
    early = lambda i: jnp.clip(i // 2 - 1, 0, down_pieces - 1)
    fixed = lambda shape: pl.BlockSpec(shape, lambda i: (0,) * len(shape), pipeline_mode=pl.Buffered(1))

    def columns(place):
        return pl.BlockSpec((tokens, lanes), lambda i: (0, 3 * now(i) + place))

    pair = pl.BlockSpec((tokens, lanes), lambda i: (0, now(i)))
    weight = pl.BlockSpec((width, 3 * lanes), lambda i: (0, before(i)))
    hbm = pl.BlockSpec(memory_space=pl.ANY)

    rows = streams[0].rows

    def out_piece(value):
        whole = value.reshape(n_seq, 2, rows, value.shape[1])
        return whole, pl.BlockSpec((n_seq, 2, rows, lanes), lambda i: (0, 0, 0, now(i)))

    outs = [out_piece(value) for value in (out_kept, out_came)]
    down = down_part.reshape(n_seq // 2, 2, -1, width // CORES)
    up = up_part.reshape(n_seq // 4, 2, rows, -1)
    down_spec = pl.BlockSpec((n_seq // 2, 2, streams[1].rows, width // CORES), lambda i: (0, 0, early(i), 0))
    up_spec = pl.BlockSpec((n_seq // 4, 2, rows, streams[2].columns), lambda i: (0, 0, 0, early(i)))
    count = len(streams)
    deepest = max(len(stream.levels) for stream in streams)
    return pl.pallas_call(
        functools.partial(back_kernel, pairs, tile, streams, row_count),
        grid=(2 * pairs + deepest + 1 + streams[0].lag,),
        in_specs=[
            fixed((tokens, 1)),
            fixed((1, tokens)),
            columns(0),
            columns(1),
            columns(2),
            pair,
            pair,
            pl.BlockSpec((None, 2, tokens), lambda i: (now(i), 0, 0)),
            fixed((tokens, width)),
            weight,
            weight,
            pl.BlockSpec((width,), lambda i: (0,), pipeline_mode=pl.Buffered(1)),
            outs[0][1],
            outs[1][1],
            down_spec,
            up_spec,
            hbm,
            hbm,
            hbm,
        ],
        out_specs=[hbm] * 5,
        out_shape=[jax.ShapeDtypeStruct((row_count, CORES, sub, width), bf16)] * 2
        + [jax.ShapeDtypeStruct((stream.count, CORES, 2, stream.rows, stream.columns), bf16) for stream in streams],
        scratch_shapes=[
            pltpu.VMEM((lanes, tokens), bf16),
            pltpu.VMEM((lanes, tokens), f32),
            pltpu.VMEM((2, tokens), f32),
            pltpu.VMEM((2, tokens, 3 * lanes), bf16),
            pltpu.VMEM((2, own_tokens, 3 * lanes), bf16),
            pltpu.VMEM((own_tokens, width), f32),
            pltpu.VMEM((n_seq, sub, width), bf16),
            pltpu.VMEM((2, sub, width), bf16),
            pltpu.VMEM((2, sub, width), f32),
        ]
        + [shape for stream in streams for shape in stream.scratch()]
        + [pltpu.VMEM((stream.count, 2, stream.rows, stream.columns), bf16) for stream in streams]
        + [
            pltpu.SemaphoreType.DMA((count, deepest)),
            pltpu.SemaphoreType.DMA((count, deepest, 2)),
            pltpu.SemaphoreType.DMA((count,)),
            pltpu.SemaphoreType.DMA((count, 2)),
            pltpu.SemaphoreType.DMA((count,)),
            pltpu.SemaphoreType.DMA((count, 2)),
            pltpu.SemaphoreType.DMA((count,)),
            pltpu.SemaphoreType.DMA((2,)),
            pltpu.SemaphoreType.DMA((2,)),
            pltpu.SemaphoreType.DMA((n_seq,)),
            pltpu.SemaphoreType.DMA((row_count, CORES)),
            pltpu.SemaphoreType.DMA,
            pltpu.SemaphoreType.DMA((2, 2)),
            pltpu.SemaphoreType.DMA((n_seq,)),
            pltpu.SemaphoreType.DMA((row_count, CORES)),
            pltpu.SemaphoreType.DMA,
        ],
        compiler_params=pltpu.CompilerParams(
            vmem_limit_bytes=feed_vmem_bytes, collective_id=2, has_side_effects=True
        ),
        cost_estimate=pl.CostEstimate(
            flops=80 * pairs * tokens * tokens * HDIM,
            bytes_accessed=16 * tokens * pairs * lanes,
            transcendentals=2 * pairs * tokens * tokens,
        ),
        name="back",
    )(
        key_tags, query_tags, qkv, qkv, qkv, mixed, d_mixed, lse, n1, weights[0], weights[1],
        gain, outs[0][0], outs[1][0], down, up, start, d_middle, outputs,
    )


def collect_kernel(pairs, seq_ref, *refs):
    qkv_parts, down_parts, up_parts = refs[:3]
    qkv_weights, up_weight = refs[3:9], refs[9]
    qkv_out, out_out, down_out, up_out, first_out, second_out, first_sum, second_sum = refs[10:]
    item = pl.program_id(0)
    lanes = 2 * HDIM
    rows = qkv_parts.shape[2]
    width = out_out.shape[1]
    half = width // CORES
    tile = feed_tile // CORES

    @pl.when(item == 0)
    def _():
        first_sum[...] = jnp.zeros_like(first_sum)
        second_sum[...] = jnp.zeros_like(second_sum)

    for core in range(CORES):
        place = pl.multiple_of(core * half + item * lanes, lanes)
        for high in range(2):
            own = slice(high * rows, (high + 1) * rows)
            part = qkv_parts[core, high].astype(f32)
            for kind in range(3):
                value = part[:, kind * lanes : (kind + 1) * lanes]
                qkv_out[own, pl.ds(kind * width + place, lanes)] = value
                weight = qkv_weights[kind * CORES + core][own, :].astype(f32)
                first_sum[own, :] += value * weight
            out_out[own, pl.ds(place, lanes)] = part[:, 3 * lanes :]

    @pl.when(item < down_pieces)
    def _():
        for core in range(CORES):
            for high in range(2):
                own = slice(high * rows, (high + 1) * rows)
                for at in range(up_parts.shape[3] // lanes):
                    column = item * up_parts.shape[3] + at * lanes
                    column = column // tile * feed_tile + core * tile + column % tile
                    columns = pl.ds(pl.multiple_of(column, lanes), lanes)
                    value = up_parts[core, high, :, at * lanes : (at + 1) * lanes].astype(f32)
                    up_out[own, columns] = value
                    second_sum[own, :] += value * up_weight[own, columns].astype(f32)
                count = down_parts.shape[2] // piece_rows
                for at in range(count):
                    start = ((item * count + at) * 2 + high) * piece_rows
                    value = down_parts[core, high, at * piece_rows : (at + 1) * piece_rows, :].astype(f32)
                    down_out[pl.ds(pl.multiple_of(start, piece_rows), piece_rows), core * half : (core + 1) * half] = value

    @pl.when(item == pairs - 1)
    def _():
        first_out[...] = jnp.sum(first_sum[...].T, axis=0, keepdims=True)
        second_out[...] = jnp.sum(second_sum[...].T, axis=0, keepdims=True)


def collect(seq_at, qkv_parts, down_parts, up_parts, qkv_weight, up_weight):
    pairs, _, _, rows, _ = qkv_parts.shape
    width, lanes = qkv_weight.shape[0], 2 * HDIM
    shard, wide = 2 * rows, up_weight.shape[1]
    down_rows = 2 * down_pieces * down_parts.shape[3]

    def parts(value):
        return pl.BlockSpec(
            (None,) + value.shape[1:], lambda i, seq: (jnp.minimum(i, value.shape[0] - 1), 0, 0, 0, 0)
        )

    def weight(kind, core):
        return pl.BlockSpec((shard, lanes), lambda i, seq: (seq[0], (kind * CORES + core) * pairs + i))

    whole = lambda shape: pl.BlockSpec(shape, lambda i, seq: (0, 0))
    return pl.pallas_call(
        functools.partial(collect_kernel, pairs),
        grid_spec=pltpu.PrefetchScalarGridSpec(
            num_scalar_prefetch=1,
            grid=(pairs,),
            in_specs=[parts(qkv_parts), parts(down_parts), parts(up_parts)]
            + [weight(kind, core) for kind in range(3) for core in range(CORES)]
            + [pl.BlockSpec((shard, wide), lambda i, seq: (seq[0], 0))],
            out_specs=[
                whole((shard, 3 * width)),
                whole((shard, width)),
                whole((down_rows, width)),
                whole((shard, wide)),
                whole((1, shard)),
                whole((1, shard)),
            ],
            scratch_shapes=[pltpu.VMEM((shard, lanes), f32)] * 2,
        ),
        out_shape=[
            jax.ShapeDtypeStruct((shard, 3 * width), f32),
            jax.ShapeDtypeStruct((shard, width), f32),
            jax.ShapeDtypeStruct((down_rows, width), f32),
            jax.ShapeDtypeStruct((shard, wide), f32),
            jax.ShapeDtypeStruct((1, shard), f32),
            jax.ShapeDtypeStruct((1, shard), f32),
        ],
        compiler_params=pltpu.CompilerParams(vmem_limit_bytes=vmem_bytes),
        name="collect",
    )(
        seq_at.reshape(1), qkv_parts, down_parts, up_parts, *[qkv_weight] * 6, up_weight,
    )


def add_split_kernel(has_two, bit_ref, *refs):
    ins, outs = refs[: 2 if has_two else 1], refs[2 if has_two else 1 :]
    value = ins[0][...]
    if has_two:
        value = (value.astype(f32) + ins[1][...].astype(f32)).astype(bf16)
    if len(outs) == 1:
        outs[0][...] = value
    else:
        sends = pl.program_id(0) == 0

        @pl.when(sends)
        def _():
            outs[0][...] = value

        @pl.when(jnp.logical_not(sends))
        def _():
            outs[1][...] = value


def add_split(kept, received, inner, bit):
    rows, columns = kept.shape
    values = [kept] if received is None else [kept, received.reshape(rows, columns)]
    if bit is None:
        if received is None:
            return None, kept
        count = 4 if rows % 64 == 0 else 1
        block = pl.BlockSpec((rows // count, columns), lambda i, bit: (i, 0))
        grid, ins, outs = (count,), [block] * 2, block
        shapes = jax.ShapeDtypeStruct((rows, columns), bf16)
        bit = jnp.zeros((), jnp.int32)
    else:
        outer = rows // (2 * inner)
        cut = 1
        while inner // cut * columns > 2**19 and inner % (32 * cut) == 0:
            cut *= 2
        values = [value.reshape(outer, 2, inner, columns) for value in values]
        ins = [
            pl.BlockSpec(
                (None, None, inner // cut, columns),
                lambda w, i, j, bit: (i, jnp.where(w == 0, 1 - bit[0], bit[0]), j, 0),
            )
        ] * len(values)
        outs = [
            pl.BlockSpec(
                (None, inner // cut, columns),
                lambda w, i, j, bit: (jnp.where(w == 0, i, outer - 1), jnp.where(w == 0, j, cut - 1), 0),
            ),
            pl.BlockSpec(
                (None, inner // cut, columns),
                lambda w, i, j, bit: (jnp.where(w == 0, 0, i), jnp.where(w == 0, 0, j), 0),
            ),
        ]
        grid = (2, outer, cut)
        shapes = [jax.ShapeDtypeStruct((outer, inner, columns), bf16)] * 2
    done = pl.pallas_call(
        functools.partial(add_split_kernel, len(values) == 2),
        grid_spec=pltpu.PrefetchScalarGridSpec(
            num_scalar_prefetch=1, grid=grid, in_specs=ins, out_specs=outs
        ),
        out_shape=shapes,
        cost_estimate=pl.CostEstimate(flops=rows * columns, bytes_accessed=6 * rows * columns, transcendentals=0),
        name="add_split",
    )(bit.reshape(1), *values)
    if not isinstance(done, (list, tuple)):
        return None, done
    return done[0].reshape(rows // 2, columns), done[1].reshape(rows // 2, columns)


def tie(*values):
    return lax.optimization_barrier(values)


def build(n_seq, n_rows):
    highs = n_rows // CORES
    seq_bits = n_seq.bit_length() - 1
    high_bits = highs.bit_length() - 1
    bits = seq_bits + high_bits

    def permute(value, target):
        pairs = []
        for s in range(n_seq):
            for r in range(n_rows):
                to_s, to_r = target(s, r)
                pairs.append((s * n_rows + r, to_s * n_rows + to_r))
        return lax.ppermute(value, AXES, pairs)

    def other_core(value):
        return permute(value, lambda s, r: (s, r ^ 1))

    def pick(value, place, axis):
        return lax.dynamic_index_in_dim(value, place, axis, keepdims=False)

    def bit_of(step):
        name, bit = step
        return (lax.axis_index(name) >> bit) & 1

    def across(value, step):
        name, bit = step
        if name == "rows":
            return permute(value, lambda s, r: (s, r ^ (1 << bit)))
        return permute(value, lambda s, r: (s ^ (1 << bit), r))

    high_steps = [("rows", bit + 1) for bit in reversed(range(high_bits))]
    seq_steps = [("seq", bit) for bit in range(seq_bits)]

    class Sum:
        def __init__(self, kept, received, order):
            self.rows, self.columns = kept.shape
            self.kept, self.received = kept, received
            self.left = [step for step in seq_steps[::-1] + high_steps if step in order]
            self.order = list(order)

        def finish(self):
            step = self.order[0] if self.order else None
            inner = self.rows
            if step is not None:
                axis = self.left.index(step)
                inner = self.rows >> (axis + 1)
            self.sent, self.kept = add_split(self.kept, self.received, inner, step and bit_of(step))
            self.received = None

        def begin(self):
            step = self.order.pop(0)
            self.left.remove(step)
            self.rows //= 2
            self.received = across(self.sent, step)

        def finished(self):
            while self.order:
                self.finish()
                self.begin()
            self.finish()
            return self.kept

    rows_first = high_steps + seq_steps[1:2] + seq_steps[:1] + seq_steps[2:]
    down_order = [step for step in seq_steps + high_steps if step != ("rows", 1)]
    up_order = [step for step in high_steps + seq_steps if step not in (("seq", 0), ("seq", 1))]

    def gather_high(value, pieces=0):
        for step in high_steps[::-1]:
            if pieces and step == ("rows", 1):
                continue
            received = across(value, step)
            value = jnp.where(
                bit_of(step) == 0,
                jnp.concatenate([value, received], 0),
                jnp.concatenate([received, value], 0),
            )
        if pieces:
            value = value.reshape(-1, 1, pieces, value.shape[1])
            received = across(value, ("rows", 1))
            value = jnp.where(
                bit_of(("rows", 1)) == 0,
                jnp.concatenate([value, received], 1),
                jnp.concatenate([received, value], 1),
            )
            value = value.reshape(-1, value.shape[-1])
        return value

    def back_by_steps(
        qkv, mixed, d_mixed, lse, key_tags, query_tags, n1_all, qkv_parts, attention_gain,
        out_kept, out_received, down_part, up_part, start, d_middle, to_member, ordered, from_rows, sizes,
    ):
        group, member, core, pairs, group_width, tokens, width = sizes
        lanes, half = 2 * HDIM, width // CORES
        unit1, scale1 = norm_parts(start)
        down = Sum(down_part, None, down_order)
        up = Sum(up_part, None, up_order)
        out = Sum(out_kept, out_received, rows_first)

        def before_next(*sums):
            nonlocal d_mixed
            for each in sums:
                each.finish()
            values = tie(d_mixed, *[v for each in sums for v in (each.sent, each.kept)])
            d_mixed = values[0]
            for at, each in enumerate(sums):
                each.sent, each.kept = values[1 + 2 * at : 3 + 2 * at]
                each.begin()

        def back_at(at):
            return attend_back(qkv, mixed, d_mixed, lse, key_tags, query_tags, at, 1)

        cut = max(1, 3 * pairs // 5)
        before_next(down, up)
        d_qkv, qkv_sums, d_parts = [], [], [[] for _ in range(group)]

        def take_piece(pieces):
            piece = jnp.concatenate(pieces, axis=1)
            d_parts[0].append(piece[:tokens])
            for hop in range(1, group):
                d_parts[hop].append(to_member(piece[hop * tokens : (hop + 1) * tokens], group - hop))
            return dot(n1_all, piece, 0, 0)

        grads = []
        for at in range(pairs):
            d_qkv.append(back_at(at))
            d_mixed, d_qkv[at] = tie(d_mixed, d_qkv[at])
            if at + 1 == cut:
                grads.append(take_piece(d_qkv))
            if at == min(0, pairs - 1):
                before_next(out)
            if at == min(1, pairs - 1):
                before_next(down, up)
            if at == min(3, pairs - 1):
                before_next(down, up, out)
        if pairs > cut:
            grads.append(take_piece(d_qkv[cut:]))
        if group == CORES:
            qkv_sums = [Sum(grad.astype(bf16), None, rows_first) for grad in grads]
        else:
            grad = jnp.concatenate(grads, 1)
            grad = grad.reshape(width, pairs, 3, lanes).transpose(0, 2, 1, 3)
            grad = grad.reshape(width, 3, 1, pairs * lanes)[..., :group_width]
            grad = lax.dynamic_update_slice_in_dim(
                jnp.zeros((width, 3, group, group_width), f32), grad, member, 2
            ).reshape(width, 3, CORES, half)
            kept = pick(grad, core, 2).astype(bf16).reshape(width, 3 * half)
            sent = pick(grad, 1 - core, 2).astype(bf16).reshape(width, 3 * half)
            qkv_sums = [Sum(kept, other_core(sent), rows_first)]

        d_n1 = jnp.zeros((tokens, width), f32)
        for part, weight in zip(d_parts, qkv_parts):
            d_n1 = d_n1 + dot(jnp.concatenate(part, 1), weight, 1, 1)
        input_grad = d_middle + norm_back(d_n1, attention_gain, unit1, scale1)
        input_grad = from_rows(input_grad.astype(bf16))

        down_total = gather_high(down.finished(), piece_rows)
        down_total = ordered(down_total, other_core(down_total), 1).astype(f32)
        tile = feed_tile // CORES
        up_total = gather_high(up.finished()).reshape(width // n_seq, -1, 1, tile)
        up_total = ordered(up_total, other_core(up_total), 2).reshape(width // n_seq, -1).astype(f32)
        out_total = gather_high(out.finished())
        out_total = ordered(out_total, other_core(out_total), 1).astype(f32)
        qkv_part = gather_high(jnp.concatenate([each.finished() for each in qkv_sums], 1))
        if group == CORES:
            qkv_part = qkv_part.reshape(-1, pairs, 3, lanes).transpose(0, 2, 1, 3)
        qkv_part = qkv_part.reshape(-1, 3, half)
        qkv_total = ordered(qkv_part[:, :, None], other_core(qkv_part)[:, :, None], 2)
        qkv_total = qkv_total.reshape(-1, 3 * width).astype(f32)

        return input_grad, qkv_total, out_total, down_total, up_total

    def per_device(
        inputs, cell_ids, valid_counts, cotangent, attention_gain, qkv_weight, out_weight, feed_gain, up_weight, down_weight
    ):
        row_count, block, width = inputs.shape
        seq_len = cell_ids.shape[1]
        heads = width // HDIM
        lanes = 2 * HDIM
        seq_at, rows_at = lax.axis_index("seq"), lax.axis_index("rows")
        core = rows_at % CORES
        chips = n_seq // (CORES * row_count)
        group = chips * CORES
        sub = block // group
        tokens = n_seq * sub
        member = (seq_at % chips) * CORES + core
        group_heads = heads // group
        pairs = -(-group_heads // 2)
        group_width = group_heads * HDIM
        padded = pairs * lanes - group_width

        def to_member(value, hop):
            def target(s, r):
                place = ((s % chips) * CORES + r % CORES + hop) % group
                return (s // chips * chips + place // CORES, r // CORES * CORES + place % CORES)

            return permute(value, target)

        def ordered(own, received, axis):
            return jnp.where(
                core == 0,
                jnp.concatenate([own, received], axis),
                jnp.concatenate([received, own], axis),
            )

        def to_rows(value):
            halves = value.reshape(row_count, CORES, block // CORES, width)
            received = other_core(pick(halves, 1 - core, 1))
            both = ordered(pick(halves, core, 1), received, 0).reshape(n_seq, sub, width)
            return lax.all_to_all(both, "seq", 0, 0, tiled=True).reshape(tokens, width)

        def from_rows(value):
            both = lax.all_to_all(value.reshape(n_seq, sub, width), "seq", 0, 0, tiled=True)
            both = both.reshape(CORES, row_count, block // CORES, width)
            received = other_core(pick(both, 1 - core, 0))
            own = pick(both, core, 0)
            return ordered(own[:, None], received[:, None], 1).reshape(row_count, block, width)

        places = jnp.arange(seq_len, dtype=jnp.int32)
        tags = jnp.where(places[None, :] < valid_counts[:, None], cell_ids, -1 - places[None, :])
        tags = ordered(tags, other_core(tags), 0)
        tags = pick(tags, seq_at // chips, 0).reshape(n_seq, CORES, chips, sub)
        tags = tags.transpose(2, 1, 0, 3).reshape(group, tokens)
        order = (member - jnp.arange(group, dtype=jnp.int32)) % group
        tags = jnp.take(tags, order, axis=0).reshape(1, seq_len)
        query_tags, key_tags = tags, tags.reshape(seq_len, 1)

        def pad_heads(value, axis):
            if not padded:
                return value
            fill = [(0, 0)] * value.ndim
            fill[axis] = (0, padded)
            return jnp.pad(value, fill)

        def qkv_of(hop):
            if group == CORES:
                return gather_pairs(((core + hop) % CORES).reshape(1), qkv_weight)
            piece = pick(qkv_weight.reshape(width, 3, group, group_width), (member + hop) % group, 2)
            piece = pad_heads(piece, 2).reshape(width, 3, pairs, lanes)
            return piece.transpose(0, 2, 1, 3).reshape(width, 3 * pairs * lanes)

        def out_of(hop):
            at = (member + hop) % group * group_width
            return pad_heads(lax.dynamic_slice_in_dim(out_weight, at, group_width, 0), 0)

        if chips == 1 and highs == 2:
            half = width // CORES
            x_row, n1, qkv, own_weight, other_weight = begin(inputs, qkv_weight, attention_gain)
            start = x_row.reshape(tokens, width)
            mixed, lse, cot, mixed_own, middle = attend_row(qkv, key_tags, query_tags, cotangent, start, out_weight)
            outputs, d_middle, _, d_mixed, out_kept, out_received, down_part, up_part = feed(
                middle, cot.reshape(tokens, width), feed_gain, up_weight, down_weight, mixed_own, out_weight, n_seq
            )
            input_grad, out_low, qkv_out, down_all, up_all = back(
                qkv, mixed, d_mixed.reshape(seq_len, half), lse, key_tags, query_tags, n1, (own_weight, other_weight), attention_gain,
                out_kept, out_received, down_part, up_part, start, d_middle, outputs, row_count,
            )
            qkv_total, out_total, down_total, up_total, first, second = collect(
                seq_at, qkv_out, down_all, up_all, qkv_weight, up_weight
            )
            shard = width // n_seq

            def gain_grad(sums, gain):
                return sums.reshape(shard) / lax.dynamic_slice_in_dim(gain, seq_at * shard, shard, 0)

            return (
                out_low.reshape(inputs.shape),
                input_grad.reshape(inputs.shape),
                gain_grad(first, attention_gain),
                qkv_total,
                out_total,
                gain_grad(second, feed_gain),
                up_total,
                down_total,
            )

        start = to_rows(inputs)
        qkv_parts = [qkv_of(hop) for hop in range(group)]
        out_parts = [out_of(hop) for hop in range(group)]
        start = start.astype(f32)
        unit1, scale1 = norm_parts(start)
        n1 = (unit1 * attention_gain).astype(bf16)
        n1_all = jnp.concatenate([n1] + [to_member(n1, hop) for hop in range(1, group)], 0)
        cotangent, _ = tie(cotangent, start[:1])
        cot = to_rows(cotangent)
        qkv = dot(n1_all, qkv_parts[0], 1, 0).astype(bf16)
        mixed, lse = attend(qkv, key_tags, query_tags)
        mixed_parts = [mixed[:tokens]] + [
            to_member(mixed[hop * tokens : (hop + 1) * tokens], group - hop) for hop in range(1, group)
        ]
        middle = start
        for part, weight in zip(mixed_parts, out_parts):
            middle = middle + dot(part, weight, 1, 0)
        if group == CORES:
            mixed_own = ordered(mixed_parts[0], mixed_parts[1], 1)
        else:
            slots = jnp.stack([part[:, :group_width] for part in mixed_parts])
            turn = (jnp.arange(group, dtype=jnp.int32) - member) % group
            mixed_own = jnp.take(slots, turn, axis=0).transpose(1, 0, 2).reshape(tokens, width)
        outputs, d_middle, d_attn, _, _, _, down_part, up_part = feed(
            middle, cot, feed_gain, up_weight, down_weight, mixed_own, out_weight, n_seq
        )
        d_attn = d_attn[0]

        d_attn_all = jnp.concatenate([d_attn] + [to_member(d_attn, hop) for hop in range(1, group)], 0)


        half = width // CORES
        out_grad = dot(mixed_own, d_attn, 0, 0).astype(bf16)
        out_kept = lax.dynamic_slice_in_dim(out_grad, core * half, half, 1)
        out_received = other_core(lax.dynamic_slice_in_dim(out_grad, (1 - core) * half, half, 1))
        d_mixed = dot(d_attn_all, out_parts[0], 1, 1).astype(bf16)

        out_low = from_rows(outputs)
        input_grad, qkv_total, out_total, down_total, up_total = back_by_steps(
            qkv, mixed, d_mixed, lse, key_tags, query_tags, n1_all, qkv_parts, attention_gain,
            out_kept, out_received, down_part, up_part, start, d_middle, to_member, ordered, from_rows,
            (group, member, core, pairs, group_width, tokens, width),
        )

        shard = width // n_seq

        def gain_total(weight, total, gain):
            rows = lax.dynamic_slice_in_dim(weight, seq_at * shard, shard, 0).astype(f32)
            return jnp.sum(rows * total, axis=1) / lax.dynamic_slice_in_dim(gain, seq_at * shard, shard, 0)

        return (
            out_low,
            input_grad,
            gain_total(qkv_weight, qkv_total, attention_gain),
            qkv_total,
            out_total,
            gain_total(up_weight, up_total, feed_gain),
            up_total,
            down_total,
        )

    return per_device


def solution(mesh):
    placed = (
        P("rows", "seq", None),
        P("rows", None),
        P("rows"),
        P("rows", "seq", None),
        P(),
        P(),
        P(),
        P(),
        P(),
        P(),
    )
    return jax.shard_map(
        build(mesh.shape["seq"], mesh.shape["rows"]),
        mesh=mesh,
        in_specs=placed,
        out_specs=(
            P("rows", "seq", None),
            P("rows", "seq", None),
            P("seq"),
            P("seq", None),
            P("seq", None),
            P("seq"),
            P("seq", None),
            P("seq", None),
        ),
        check_vma=False,
    )
```
